32 devices in a mesh: seq: 16 (over z, y, x), ch: 2 (over core).
Axes of the slice: x: 2, y: 2, z: 4, core: 2. Of those that a mesh axis runs over, the one named last changes fastest.
Arguments:
- inputs: bfloat16 [4096, 2560], P('seq'), may hold values from -30 to 30
- norm_gain: float32 [2560], replicated, may hold values from 0.5 to 1.5
- branch_weight: bfloat16 [2560, 2560], P('seq', 'ch'), may hold values from -0.125 to 0.125
- input_weight: bfloat16 [2560, 2560], P('seq', 'ch'), may hold values from -0.125 to 0.125
- channel_params: float32 [8, 2560], P(None, 'ch'), may hold values from -16 to 4, as said below
- gate_x_blocks: bfloat16 [10, 256, 256], P('ch', 'seq'), may hold values from -0.375 to 0.375
- gate_a_blocks: bfloat16 [10, 256, 256], P('ch', 'seq'), may hold values from -0.375 to 0.375
- out_weight: bfloat16 [2560, 2560], P('ch', 'seq'), may hold values from -0.125 to 0.125
- ffn_gain: float32 [2560], replicated, may hold values from 0.5 to 1.5
- ffn_gate: bfloat16 [2560, 7680], P('seq', 'ch'), may hold values from -0.125 to 0.125
- ffn_up: bfloat16 [2560, 7680], P('seq', 'ch'), may hold values from -0.125 to 0.125
- ffn_down: bfloat16 [7680, 2560], P('ch', 'seq'), may hold values from -0.0625 to 0.0625
- cotangent: bfloat16 [4096, 2560], P('seq'), may hold values from -6 to 6
Outputs:
- block_out: bfloat16 [4096, 2560], P('seq')
- d_inputs: float32 [4096, 2560], P('seq')
- d_norm_gain: float32 [2560], replicated
- d_branch: float32 [2560, 2560], P('seq', 'ch')
- d_input_w: float32 [2560, 2560], P('seq', 'ch')
- d_channel: float32 [8, 2560], P(None, 'ch')
- d_gate_x: float32 [10, 256, 256], P('ch', 'seq')
- d_gate_a: float32 [10, 256, 256], P('ch', 'seq')
- d_out_weight: float32 [2560, 2560], P('ch', 'seq')
- d_ffn_gain: float32 [2560], replicated
- d_ffn_gate: float32 [2560, 7680], P('seq', 'ch')
- d_ffn_up: float32 [2560, 7680], P('seq', 'ch')
- d_ffn_down: float32 [7680, 2560], P('ch', 'seq')
The draws below stay inside these ranges and needn't reach their ends.
Inputs may be any that keep to these rules, and one draw needn't show every extreme that they name: Rows 0 to 3 of channel_params are the conv taps, row 4 the conv bias, rows 5 and 6 the gate biases, row 7 the decay parameter of each channel.
All inputs are finite; a program needn't handle non-finite values.
Results may differ from the reference program's by a relative error of at most 0.012.
Values may be sent and summed in bfloat16 or wider, within the bound.
A program may use at most 384 MiB of HBM per device.

```python
import jax
import jax.numpy as jnp
from jax import lax

D = 2560
H = 10
B = 256
F = 7680
W = 2560
TOKENS = 4096


def draw_inputs(key, part):
    key = jax.random.fold_in(key, 11)
    k_base, k_rows, k_cols = jax.random.split(key, 3)
    base = jax.random.normal(k_base, (TOKENS, D), jnp.float32)
    row_scale = jnp.exp(jax.random.uniform(k_rows, (TOKENS, 1), jnp.float32, -0.7, 1.6))
    col_scale = jnp.exp(jax.random.uniform(k_cols, (1, D), jnp.float32, -0.7, 0.7))
    return jnp.clip(base * row_scale * col_scale, -30.0, 30.0).astype(jnp.bfloat16)


def draw_channel_params(key, part):
    key = jax.random.fold_in(key, 23)
    k_taps, k_bias, k_gx, k_ga, k_heads, k_slow, k_fast = jax.random.split(key, 7)
    taps = jnp.clip(0.5 * jax.random.normal(k_taps, (4, W), jnp.float32), -2.0, 2.0)
    conv_bias = jnp.clip(0.3 * jax.random.normal(k_bias, (1, W), jnp.float32), -1.5, 1.5)
    bias_x = jnp.clip(0.5 * jax.random.normal(k_gx, (1, W), jnp.float32), -2.5, 2.5)
    bias_a = jnp.clip(0.5 * jax.random.normal(k_ga, (1, W), jnp.float32), -2.5, 2.5)
    share = 0.5
    slow_heads = jax.random.uniform(k_heads, (H, 1), jnp.float32) < share
    slow_rate = jnp.exp(jax.random.uniform(k_slow, (H, B), jnp.float32, jnp.log(0.025), jnp.log(0.125))) / TOKENS
    fast_rate = jnp.exp(jax.random.uniform(k_fast, (H, B), jnp.float32, jnp.log(1.0 / 320.0), jnp.log(1.0 / 80.0)))
    rate = jnp.where(slow_heads, slow_rate, fast_rate)
    decay_param = jnp.clip(jnp.log(jnp.expm1(rate)), -16.0, 4.0).reshape(1, W)
    return jnp.concatenate([taps, conv_bias, bias_x, bias_a, decay_param], axis=0)


def shard_levels(stream_key, extent, shards, least, high):
    def one(axis_at, parts):
        draws = jax.random.uniform(jax.random.fold_in(jax.random.fold_in(stream_key, 6), axis_at), (parts,), jnp.float32, least / len(shards), high / len(shards))
        return jnp.repeat(jnp.exp(draws), extent[axis_at] // parts).reshape((-1,) + (1,) * (len(extent) - axis_at - 1))

    factor_of = one(*shards[0])
    for cut in shards[1:]:
        factor_of = factor_of * one(*cut)
    return factor_of


def noise(own_key, shape, spread, most, cuts=(), kind=jnp.bfloat16):
    loudness = shard_levels(own_key, shape, cuts, -0.22, 0.18) if cuts else 1.0
    entries = jax.random.normal(own_key, shape, jnp.float32) * spread * loudness
    return jnp.minimum(jnp.maximum(entries, -most), most).astype(kind)


def setup_inputs(seed: int = 0) -> dict:
    key_of = jax.random.split(jax.random.key(seed), 14)
    inputs = draw_inputs(jax.random.fold_in(key_of[13], 71), 0)
    norm_gain = jnp.clip(1.0 + 0.1 * jax.random.normal(key_of[1], (D,), jnp.float32), 0.5, 1.5)
    branch_weight = noise(key_of[2], (D, W), D ** -0.5, 0.125, ((0, 16), (1, 2)))
    input_weight = noise(key_of[3], (D, W), D ** -0.5, 0.125, ((0, 16), (1, 2)))
    channel_params = draw_channel_params(jax.random.fold_in(key_of[13], 71), 0)
    gate_x_blocks = noise(key_of[5], (H, B, B), B ** -0.5, 0.375, ((0, 2), (1, 16)))
    gate_a_blocks = noise(key_of[6], (H, B, B), B ** -0.5, 0.375, ((0, 2), (1, 16)))
    out_weight = noise(key_of[7], (W, D), W ** -0.5, 0.125, ((0, 2), (1, 16)))
    ffn_gain = jnp.clip(1.0 + 0.1 * jax.random.normal(key_of[8], (D,), jnp.float32), 0.5, 1.5)
    ffn_gate = noise(key_of[9], (D, F), D ** -0.5, 0.125, ((0, 16), (1, 2)))
    ffn_up = noise(key_of[10], (D, F), D ** -0.5, 0.125, ((0, 16), (1, 2)))
    ffn_down = noise(key_of[11], (F, D), F ** -0.5, 0.0625, ((0, 2), (1, 16)))
    cotangent = noise(key_of[12], (TOKENS, D), 1.0, 6.0, ((0, 16),))
    return {"inputs": inputs, "norm_gain": norm_gain, "branch_weight": branch_weight, "input_weight": input_weight, "channel_params": channel_params, "gate_x_blocks": gate_x_blocks, "gate_a_blocks": gate_a_blocks, "out_weight": out_weight, "ffn_gain": ffn_gain, "ffn_gate": ffn_gate, "ffn_up": ffn_up, "ffn_down": ffn_down, "cotangent": cotangent}


@jax.custom_vjp
def low(v):
    return lax.optimization_barrier(v.astype(jnp.bfloat16)).astype(jnp.float32)

@jax.custom_vjp
def low_back(v):
    return v

def low_keep(v):
    return (low(v), None)

def low_pass(kept, grad):
    return (grad,)

def back_keep(v):
    return (v, None)

def back_low(kept, grad):
    return (low(grad),)
low.defvjp(low_keep, low_pass)
low_back.defvjp(back_keep, back_low)

def matmul_high(left, right):
    return jnp.dot(left, right, precision=lax.Precision.HIGHEST, preferred_element_type=jnp.float32)

def scaled_norm(values, gain):
    return values * lax.rsqrt(lax.optimization_barrier(jnp.mean(values * values, axis=-1, keepdims=True)) + 1e-06) * gain

def gelu_tanh(values):
    return jax.nn.gelu(values, approximate=True)

def decay_gates(conv_out, pre_x, pre_a, bias_x, bias_a, decay_param, first):
    gate_x = jax.nn.sigmoid(pre_x + bias_x)
    gate_a = jax.nn.sigmoid(pre_a + bias_a)
    log_a = -8.0 * gate_a * jax.nn.softplus(decay_param)
    decay = jnp.exp(log_a)
    mult = jnp.sqrt(jnp.maximum(1.0 - decay * decay, 0.001))
    mult = jnp.where(first, jnp.ones_like(mult), mult)
    return (conv_out * gate_x * mult, decay)

def recurrence(decay, driven):

    def advance(state, pair):
        fresh = pair[0] * state + pair[1]
        return (fresh, fresh)
    _, states = lax.scan(advance, jnp.zeros((decay.shape[1],), decay.dtype), (decay, driven))
    return states

def forward(x_float, norm_gain, branch_weight, input_weight, channel_params, gate_x_blocks, gate_a_blocks, out_weight, ffn_gain, ffn_gate, ffn_up, ffn_down):
    n_one = low(scaled_norm(x_float, norm_gain))
    y_pre = low_back(matmul_high(n_one, branch_weight))
    gelu_y = gelu_tanh(y_pre)
    x_branch = low_back(low(matmul_high(n_one, input_weight)))
    padded = jnp.concatenate([jnp.zeros((3, W), x_branch.dtype), x_branch], axis=0)
    conv_sum = channel_params[4][None, :]
    for offset in range(4):
        conv_sum = conv_sum + channel_params[offset][None, :] * padded[3 - offset:3 - offset + TOKENS]
    conv_out = low(conv_sum)
    blocks = conv_out.reshape(TOKENS, H, B)
    pre_x = low_back(jnp.einsum('thi,hij->thj', blocks, gate_x_blocks, precision=lax.Precision.HIGHEST).reshape(TOKENS, W))
    pre_a = low_back(jnp.einsum('thi,hij->thj', blocks, gate_a_blocks, precision=lax.Precision.HIGHEST).reshape(TOKENS, W))
    first = jnp.arange(TOKENS)[:, None] == 0
    driven, decay = decay_gates(conv_out, pre_x, pre_a, channel_params[5], channel_params[6], channel_params[7], first)
    states = recurrence(decay, driven)
    branch_out = low(states * gelu_y)
    mixed = low_back(matmul_high(branch_out, out_weight))
    resid = x_float + mixed
    n_two = low(scaled_norm(resid, ffn_gain))
    gate_pre = low_back(matmul_high(n_two, ffn_gate))
    up_pre = low_back(matmul_high(n_two, ffn_up))
    hidden = low(gelu_tanh(gate_pre) * up_pre)
    return resid + low_back(matmul_high(hidden, ffn_down))

def reference(inputs, norm_gain, branch_weight, input_weight, channel_params, gate_x_blocks, gate_a_blocks, out_weight, ffn_gain, ffn_gate, ffn_up, ffn_down, cotangent):
    f32 = jnp.float32
    primals = (inputs.astype(f32), norm_gain.astype(f32), branch_weight.astype(f32), input_weight.astype(f32), channel_params.astype(f32), gate_x_blocks.astype(f32), gate_a_blocks.astype(f32), out_weight.astype(f32), ffn_gain.astype(f32), ffn_gate.astype(f32), ffn_up.astype(f32), ffn_down.astype(f32))
    result, pullback = jax.vjp(forward, *primals)
    grads = pullback(cotangent.astype(f32))
    return (result.astype(jnp.bfloat16), grads[0], grads[1], grads[2], grads[3], grads[4], grads[5], grads[6], grads[7], grads[8], grads[9], grads[10], grads[11])
```

```python
import jax
import jax.numpy as jnp
from jax import lax
from jax.sharding import PartitionSpec as P

F32 = jnp.float32
BF16 = jnp.bfloat16
INNER = 4


def shifted(value, axis, by):
    length = lax.axis_size(axis)
    pairs = [(i, i + by) for i in range(length) if 0 <= i + by < length]
    return lax.ppermute(value, axis, pairs)


def swap(value, axis, mask):
    return lax.ppermute(value, axis, [(i, i ^ mask) for i in range(lax.axis_size(axis))])


def pick(array, index, axis=0):
    return lax.dynamic_index_in_dim(array, index, axis, False)


def put(array, block, index, axis=0):
    return lax.dynamic_update_index_in_dim(array, block, index, axis)


def prefix(part, axis, combine, identity, reverse):
    count = lax.axis_size(axis)
    place = lax.axis_index(axis)
    ahead = count - 1 - place if reverse else place
    gathered = jax.tree.map(lambda a: lax.all_gather(a, axis), part)
    state = jax.tree.map(lambda a, e: jnp.zeros_like(a) + jnp.asarray(e, a.dtype), part, identity)

    def one(turn, state):
        source = count - 1 - turn if reverse else turn
        return combine(
            state, jax.tree.map(lambda a: lax.dynamic_index_in_dim(a, source, 0, False), gathered)
        )

    return lax.fori_loop(0, ahead, one, state)


def scaled_norm(values, gain):
    return values * lax.rsqrt(jnp.mean(values * values, axis=-1, keepdims=True) + 1e-06) * gain


def gelu_tanh(values):
    return jax.nn.gelu(values, approximate=True)


def decay_gates(conv_out, pre_x, pre_a, bias_x, bias_a, decay_param, first):
    gate_x = jax.nn.sigmoid(pre_x + bias_x)
    gate_a = jax.nn.sigmoid(pre_a + bias_a)
    log_a = -8.0 * gate_a * jax.nn.softplus(decay_param)
    decay = jnp.exp(log_a)
    mult = jnp.sqrt(jnp.maximum(1.0 - decay * decay, 0.001))
    mult = jnp.where(first, jnp.ones_like(mult), mult)
    return (conv_out * gate_x * mult, decay)


def combine(earlier, later):
    return (earlier[0] * later[0], later[0] * earlier[1] + later[1])


def outer_exchange(blocks):
    groups = blocks.shape[0]
    outer = lax.axis_index("seq") // INNER
    got = blocks
    own = pick(blocks, outer)
    received = []
    for step in range(1, groups):
        received.append(swap(pick(blocks, outer ^ step), "seq", step * INNER))
    got = put(jnp.zeros_like(blocks), own, outer)
    for step in range(1, groups):
        got = put(got, received[step - 1], outer ^ step)
    return got


def weights_in(pack):
    groups, kinds, rows, units = pack.shape
    column = outer_exchange(pack)
    inner = lax.axis_index("seq") % INNER
    half = rows // 2
    first, second = column[:, :, :half], column[:, :, half:]
    first_x = swap(first, "seq", 1)
    second_y = swap(second, "seq", 2)
    first_y, first_xy = (swap(v, "seq", 2) for v in (first, first_x))
    second_x, second_xy = (swap(v, "seq", 1) for v in (second, second_y))
    whole = jnp.zeros((kinds, groups, INNER, rows, units), pack.dtype)
    for mask, top, low in (
        (0, first, second),
        (1, first_x, second_x),
        (2, first_y, second_y),
        (3, first_xy, second_xy),
    ):
        place = inner ^ mask
        for block, start in ((top, 0), (low, half)):
            block = jnp.moveaxis(block, 0, 1)[:, :, None]
            whole = lax.dynamic_update_slice(whole, block, (0, 0, place, start, 0))
    return whole.reshape(kinds, groups * INNER * rows, units)


def grads_out(terms, rows):
    units = terms[0].shape[1]
    groups = terms[0].shape[0] // (INNER * rows)
    inner = lax.axis_index("seq") % INNER
    half = rows // 2
    parts = [t.reshape(groups, INNER, rows, units) for t in terms]

    def mine(place, start):
        return jnp.stack(
            [lax.dynamic_slice(t, (0, place, start, 0), (groups, 1, half, units))[:, 0] for t in parts],
            axis=1,
        )

    def reduce(start, near, far):
        low = lambda place: mine(place, start).astype(BF16)
        got_far = swap(low(inner ^ far), "seq", far)
        got_both = swap(low(inner ^ far ^ near), "seq", far)
        mid = (mine(inner ^ near, start) + got_both.astype(F32)).astype(BF16)
        got_near = swap(mid, "seq", near)
        return (mine(inner, start) + got_far.astype(F32) + got_near.astype(F32)).astype(BF16)

    summed = jnp.concatenate([reduce(0, 1, 2), reduce(half, 2, 1)], axis=2)
    got = outer_exchange(summed)
    return jnp.transpose(got, (1, 2, 0, 3)).reshape(3, rows, groups * units).astype(F32)


def tokens_in(values):
    rows, width = values.shape
    groups = lax.axis_size("seq") // INNER
    outer = lax.axis_index("seq") // INNER
    core = lax.axis_index("ch")
    half = rows // 2
    own = lax.dynamic_slice_in_dim(values, core * half, half, 0)
    got = put(jnp.zeros((groups, half, width), values.dtype), own, outer)
    for step in range(1, groups):
        got = put(got, swap(own, "seq", step * INNER), outer ^ step)
    other = swap(got, "ch", 1)
    first = jnp.where(core == 0, got, other)
    second = jnp.where(core == 0, other, got)
    return jnp.stack([first, second], axis=1).reshape(groups * rows, width)


def tokens_out(partial, rows):
    width = partial.shape[1]
    groups = lax.axis_size("seq") // INNER
    outer = lax.axis_index("seq") // INNER
    core = lax.axis_index("ch")
    half = rows // 2
    parts = partial.reshape(groups, 2, half, width)
    theirs = pick(parts, 1 - core, 1).astype(BF16)
    summed = (pick(parts, core, 1) + swap(theirs, "ch", 1).astype(F32)).astype(BF16)
    total = pick(summed, outer).astype(F32)
    for step in range(1, groups):
        total = total + swap(pick(summed, outer ^ step), "seq", step * INNER).astype(F32)
    other = swap(total, "ch", 1)
    return jnp.concatenate(
        [jnp.where(core == 0, total, other), jnp.where(core == 0, other, total)], axis=0
    )


def scatter(term):
    return lax.psum_scatter(term.astype(BF16), "seq", scatter_dimension=0, tiled=True).astype(F32)


def shards(
    inputs,
    norm_gain,
    branch_weight,
    input_weight,
    channel_params,
    gate_x_blocks,
    gate_a_blocks,
    out_weight,
    ffn_gain,
    ffn_gate,
    ffn_up,
    ffn_down,
    cotangent,
):
    f32 = F32
    bf16 = BF16
    tok_rows = inputs.shape[0]
    heads_here = gate_x_blocks.shape[0]
    block_size = gate_x_blocks.shape[2]
    width_here = heads_here * block_size
    depth = ffn_gate.shape[0]
    groups = lax.axis_size("seq") // INNER
    units = ffn_gate.shape[1] // groups
    first = jnp.logical_and(
        lax.axis_index("seq") == 0, lax.broadcasted_iota(jnp.int32, (tok_rows, 1), 0) == 0
    )
    x_float = inputs.astype(f32)
    n_one_f, norm_back_one = jax.vjp(scaled_norm, x_float, norm_gain)
    n_one = n_one_f.astype(bf16)

    full_branch = lax.all_gather(branch_weight, "seq", axis=0, tiled=True)
    full_input = lax.all_gather(input_weight, "seq", axis=0, tiled=True)
    full_out = lax.all_gather(out_weight.T, "seq", axis=0, tiled=True)
    full_gx = lax.all_gather(gate_x_blocks, "seq", axis=1, tiled=True)
    full_ga = lax.all_gather(gate_a_blocks, "seq", axis=1, tiled=True)

    pack = jnp.stack(
        [w.reshape(depth, groups, units).transpose(1, 0, 2) for w in (ffn_gate, ffn_up, ffn_down.T)],
        axis=1,
    )
    full_ffn = weights_in(pack)
    all_cot = tokens_in(cotangent)

    y_pre = jnp.dot(n_one, full_branch, preferred_element_type=f32)
    gelu_y, gelu_back_y = jax.vjp(gelu_tanh, y_pre)
    x_branch = jnp.dot(n_one, full_input, preferred_element_type=f32).astype(bf16)
    previous = shifted(x_branch[tok_rows - 3 :], "seq", 1)
    extended = jnp.concatenate([previous, x_branch], axis=0).astype(f32)
    conv_sum = channel_params[4][None, :]
    for offset in range(4):
        conv_sum = (
            conv_sum
            + channel_params[offset][None, :] * extended[3 - offset : 3 - offset + tok_rows]
        )
    conv_out = conv_sum.astype(bf16)
    conv_blocks = conv_out.reshape(tok_rows, heads_here, block_size)
    pre_x = jnp.einsum("thi,hij->thj", conv_blocks, full_gx, preferred_element_type=f32).reshape(
        tok_rows, width_here
    )
    pre_a = jnp.einsum("thi,hij->thj", conv_blocks, full_ga, preferred_element_type=f32).reshape(
        tok_rows, width_here
    )

    def gate_piece(conv_in, px_in, pa_in, bias_x, bias_a, decay_param):
        return decay_gates(conv_in, px_in, pa_in, bias_x, bias_a, decay_param, first)

    (driven, decay), gate_back = jax.vjp(
        gate_piece,
        conv_out.astype(f32),
        pre_x,
        pre_a,
        channel_params[5],
        channel_params[6],
        channel_params[7],
    )
    cum_decay, local_state = lax.associative_scan(combine, (decay, driven))
    identity = (jnp.ones((width_here,), f32), jnp.zeros((width_here,), f32))
    carry_decay, carry_state = prefix(
        (cum_decay[-1], local_state[-1]), "seq", combine, identity, False
    )
    states = local_state + cum_decay * carry_state[None, :]
    branch_out = (states * gelu_y).astype(bf16)
    mixed = lax.psum(jnp.einsum("tw,dw->td", branch_out, full_out, preferred_element_type=f32), "ch")
    resid = x_float + mixed
    n_two_f, norm_back_two = jax.vjp(scaled_norm, resid, ffn_gain)
    all_two = tokens_in(n_two_f.astype(bf16))
    gate_pre = jnp.dot(all_two, full_ffn[0], preferred_element_type=f32)
    up_pre = jnp.dot(all_two, full_ffn[1], preferred_element_type=f32)
    gate_act, gelu_back_gate = jax.vjp(gelu_tanh, gate_pre)
    hidden = (gate_act * up_pre).astype(bf16)
    ffn_term = jnp.einsum("tf,df->td", hidden, full_ffn[2], preferred_element_type=f32)
    block_out = (resid + tokens_out(ffn_term, tok_rows)).astype(bf16)

    d_hidden = jnp.einsum("td,df->tf", all_cot, full_ffn[2], preferred_element_type=f32)
    d_gate = gelu_back_gate(d_hidden * up_pre)[0].astype(bf16)
    d_up = (d_hidden * gate_act).astype(bf16)
    d_n_two = tokens_out(
        jnp.einsum("tf,df->td", d_gate, full_ffn[0], preferred_element_type=f32)
        + jnp.einsum("tf,df->td", d_up, full_ffn[1], preferred_element_type=f32),
        tok_rows,
    )
    d_gate_term = jnp.einsum("td,tf->df", all_two, d_gate, preferred_element_type=f32)
    d_up_term = jnp.einsum("td,tf->df", all_two, d_up, preferred_element_type=f32)
    d_down_term = jnp.einsum("td,tf->df", all_cot, hidden, preferred_element_type=f32)
    ffn_grads = grads_out([d_gate_term, d_up_term, d_down_term], depth)
    d_resid_norm, d_ffn_gain_term = norm_back_two(d_n_two)
    d_resid = cotangent.astype(f32) + d_resid_norm
    d_mixed = d_resid.astype(bf16)
    d_branch_out = jnp.einsum("td,dw->tw", d_mixed, full_out, preferred_element_type=f32)
    d_out_term = jnp.einsum("td,tw->dw", d_mixed, branch_out, preferred_element_type=f32)
    d_y = gelu_back_y(d_branch_out * states)[0].astype(bf16)
    direct_grad = d_branch_out * gelu_y
    shifted_decay = jnp.concatenate([decay[1:], jnp.ones((1, width_here), f32)], axis=0)
    cum_later, local_adj = lax.associative_scan(combine, (shifted_decay, direct_grad), reverse=True)
    _, carry_adj = prefix(
        (decay[0] * cum_later[0], decay[0] * local_adj[0]), "seq", combine, identity, True
    )
    adjoint = local_adj + cum_later * carry_adj[None, :]
    states_before = jnp.concatenate([carry_state[None, :], states[:-1]], axis=0)
    d_decay = adjoint * states_before
    d_conv_direct, d_pre_x, d_pre_a, d_bias_x, d_bias_a, d_decay_param = gate_back(
        (adjoint, d_decay)
    )
    d_px_low = d_pre_x.astype(bf16).reshape(tok_rows, heads_here, block_size)
    d_pa_low = d_pre_a.astype(bf16).reshape(tok_rows, heads_here, block_size)
    d_conv = d_conv_direct + (
        jnp.einsum("thj,hij->thi", d_px_low, full_gx, preferred_element_type=f32)
        + jnp.einsum("thj,hij->thi", d_pa_low, full_ga, preferred_element_type=f32)
    ).reshape(tok_rows, width_here)
    d_gx_term = jnp.einsum("thi,thj->hij", conv_blocks, d_px_low, preferred_element_type=f32)
    d_ga_term = jnp.einsum("thi,thj->hij", conv_blocks, d_pa_low, preferred_element_type=f32)
    following = shifted(d_conv[:3], "seq", -1)
    d_extended = jnp.concatenate([d_conv, following], axis=0)
    d_xb_sum = jnp.zeros((tok_rows, width_here), f32)
    tap_grads = []
    for offset in range(4):
        d_xb_sum = (
            d_xb_sum + channel_params[offset][None, :] * d_extended[offset : offset + tok_rows]
        )
        tap_grads.append(jnp.sum(d_conv * extended[3 - offset : 3 - offset + tok_rows], axis=0))
    d_xb = d_xb_sum.astype(bf16)
    d_channel_term = jnp.stack(
        tap_grads + [jnp.sum(d_conv, axis=0), d_bias_x, d_bias_a, d_decay_param], axis=0
    )
    d_n_one = lax.psum(
        (
            jnp.einsum("tw,dw->td", d_y, full_branch, preferred_element_type=f32)
            + jnp.einsum("tw,dw->td", d_xb, full_input, preferred_element_type=f32)
        ).astype(jnp.bfloat16),
        "ch",
    ).astype(jnp.float32)
    d_branch_term = jnp.einsum("td,tw->dw", n_one, d_y, preferred_element_type=f32)
    d_input_term = jnp.einsum("td,tw->dw", n_one, d_xb, preferred_element_type=f32)
    d_x_norm, d_norm_gain_term = norm_back_one(d_n_one)
    d_inputs = d_resid + d_x_norm
    d_norm_gain, d_ffn_gain, d_channel = lax.psum(
        (d_norm_gain_term, d_ffn_gain_term, d_channel_term), "seq"
    )
    return (
        block_out,
        d_inputs,
        d_norm_gain,
        scatter(d_branch_term),
        scatter(d_input_term),
        d_channel,
        lax.psum_scatter(d_gx_term, "seq", scatter_dimension=1, tiled=True),
        lax.psum_scatter(d_ga_term, "seq", scatter_dimension=1, tiled=True),
        scatter(d_out_term).T,
        d_ffn_gain,
        ffn_grads[0],
        ffn_grads[1],
        ffn_grads[2].T,
    )


def solution(mesh):
    placed = (
        P("seq", None),
        P(),
        P("seq", "ch"),
        P("seq", "ch"),
        P(None, "ch"),
        P("ch", "seq", None),
        P("ch", "seq", None),
        P("ch", "seq"),
        P(),
        P("seq", "ch"),
        P("seq", "ch"),
        P("ch", "seq"),
        P("seq", None),
    )
    return jax.shard_map(
        shards,
        mesh=mesh,
        in_specs=placed,
        out_specs=(
            P("seq", None),
            P("seq", None),
            P(),
            P("seq", "ch"),
            P("seq", "ch"),
            P(None, "ch"),
            P("ch", "seq", None),
            P("ch", "seq", None),
            P("ch", "seq"),
            P(),
            P("seq", "ch"),
            P("seq", "ch"),
            P("ch", "seq"),
        ),
        check_vma=False,
    )
```

```python
import functools

import jax
import jax.numpy as jnp
from jax import lax
from jax.experimental import pallas as pl
from jax.experimental.pallas import tpu as pltpu
from jax.sharding import PartitionSpec as P

F32 = jnp.float32
BF16 = jnp.bfloat16
INNER = 4
MESH = pl.DeviceIdType.MESH
VMEM = pl.BlockSpec(memory_space=pltpu.VMEM)
ANY = pl.BlockSpec(memory_space=pl.ANY)


def swap(value, axis, mask):
    return lax.ppermute(value, axis, [(i, i ^ mask) for i in range(lax.axis_size(axis))])


def pick(array, index, axis=0):
    return lax.dynamic_index_in_dim(array, index, axis, False)


def put(array, block, index, axis=0):
    return lax.dynamic_update_index_in_dim(array, block, index, axis)


def scaled_norm(values, gain):
    return values * lax.rsqrt(jnp.mean(values * values, axis=-1, keepdims=True) + 1e-06) * gain


def gelu_tanh(values):
    return jax.nn.gelu(values, approximate=True)


def whereabouts():
    me = lax.axis_index("seq")
    outer = me // INNER
    inner = me - outer * INNER
    y = inner // 2
    x = inner - 2 * y
    by_x = me + 1 - 2 * x
    by_y = me + 2 - 4 * y
    return me, outer, by_x, by_y, by_x + 2 - 4 * y


def when(condition, action):
    if condition is None:
        action()
    else:
        pl.when(condition)(action)


def both(one, other):
    if one is None or other is None:
        return one if other is None else other
    return jnp.logical_and(one, other)


def greet(peers):
    barrier = pltpu.get_barrier_semaphore()
    for condition, peer in peers:
        when(
            condition,
            lambda peer=peer: pl.semaphore_signal(
                barrier, inc=1, device_id={"seq": peer}, device_id_type=MESH
            ),
        )
    count = 0
    for condition, _ in peers:
        count = count + (1 if condition is None else condition.astype(jnp.int32))
    pl.semaphore_wait(barrier, count)


def greet_all(n, me):
    barrier = pltpu.get_barrier_semaphore()

    def hello(step, carry):
        pl.semaphore_signal(
            barrier, inc=1, device_id={"seq": lax.rem(me + step, n)}, device_id_type=MESH
        )
        return carry

    lax.fori_loop(1, n, hello, 0)
    pl.semaphore_wait(barrier, n - 1)


def remote(src, dst, send_sem, recv_sem, place):
    return pltpu.make_async_remote_copy(
        src_ref=src,
        dst_ref=dst,
        send_sem=send_sem,
        recv_sem=recv_sem,
        device_id={"seq": place},
        device_id_type=MESH,
    )


def params(collective_id, mib):
    return pltpu.CompilerParams(
        collective_id=collective_id, has_side_effects=True, vmem_limit_bytes=mib * 2**20
    )


def gather_body(n, w_ref, g_ref, wo_ref, go_ref, send_w, send_g, recv_w, recv_g, here):
    groups = n // INNER
    me, outer, by_x, by_y, by_xy = whereabouts()
    above, below = outer + 1 < groups, outer > 0
    greet([(below, me - INNER), (above, me + INNER), (None, by_x), (None, by_y)])
    half = w_ref.shape[2] // 2
    keep_w = pltpu.make_async_copy(w_ref, wo_ref.at[:, me], here.at[0])
    keep_g = pltpu.make_async_copy(g_ref, go_ref.at[me], here.at[1])
    keep_w.start()
    keep_g.start()
    sent = []

    def copies(h, source, kind, target, own):
        cols = pl.ds(h * half, half)
        w_dst = wo_ref.at[:, source, :, cols]
        g_dst = go_ref.at[source, :, cols]
        w_src = w_ref.at[:, :, cols] if own else w_dst
        g_src = g_ref.at[:, cols] if own else g_dst
        return (
            remote(w_src, w_dst, send_w.at[h, source, kind], recv_w.at[h, source], target),
            remote(g_src, g_dst, send_g.at[h, source, kind], recv_g.at[h, source], target),
        )

    def send(condition, *what):
        def go():
            for copy in copies(*what):
                copy.start()

        when(condition, go)
        sent.append((condition, what))

    def arrive(condition, h, source):
        def go():
            for copy in copies(h, source, 0, by_x, False):
                copy.wait_recv()

        when(condition, go)

    for step in range(groups):
        for h in range(2):
            flip_p, flip_q = (by_x, by_y) if h == 0 else (by_y, by_x)
            if step == 0:
                send(above, h, me, 0, me + INNER, True)
                send(below, h, me, 1, me - INNER, True)
                send(None, h, me, 2, flip_p, True)
                send(None, h, me, 3, flip_q, True)
                continue
            for source, there, onward, kind, to in (
                (me - step * INNER, outer >= step, above, 0, me + INNER),
                (me + step * INNER, outer + step < groups, below, 1, me - INNER),
            ):
                arrive(there, h, source)
                send(both(there, onward), h, source, kind, to, False)
                send(there, h, source, 2, flip_p, False)
                send(there, h, source, 3, flip_q, False)
        for h in range(2):
            flip_p, flip_q = (by_x, by_y) if h == 0 else (by_y, by_x)
            if step == 0:
                arrive(None, h, flip_p)
                send(None, h, flip_p, 3, flip_q, False)
                continue
            for source, there in (
                (flip_p - step * INNER, outer >= step),
                (flip_p + step * INNER, outer + step < groups),
            ):
                arrive(there, h, source)
                send(there, h, source, 3, flip_q, False)
    for place in range(groups):
        shift = (place - outer) * INNER
        for h in range(2):
            arrive(None, h, (by_y if h == 0 else by_x) + shift)
            arrive(None, h, by_xy + shift)
    for condition, what in sent:

        def finish(what=what):
            for copy in copies(*what):
                copy.wait_send()

        when(condition, finish)
    keep_w.wait()
    keep_g.wait()


def gather_mixer(weights, gates):
    n = lax.axis_size("seq")
    kinds, rows, width = weights.shape
    dma = pltpu.SemaphoreType.DMA
    return pl.pallas_call(
        functools.partial(gather_body, n),
        out_shape=(
            jax.ShapeDtypeStruct((kinds, n, rows, width), weights.dtype),
            jax.ShapeDtypeStruct((n,) + gates.shape, gates.dtype),
        ),
        in_specs=[ANY, ANY],
        out_specs=(ANY, ANY),
        scratch_shapes=[
            dma((2, n, 4)),
            dma((2, n, 4)),
            dma((2, n)),
            dma((2, n)),
            dma((2,)),
        ],
        compiler_params=params(1, 16),
        name="gather_mixer",
    )(weights, gates)


def scatter_body(
    n, one_ref, mixed_ref, dy_ref, dxb_ref, branch_ref, gate_ref, out_ref, made, got_q, got_p, got_z, *sems
):
    send_q, recv_q, send_p, recv_p, send_z, recv_z = sems
    groups = n // INNER
    me, outer, by_x, by_y, by_xy = whereabouts()
    rows = one_ref.shape[1]
    total, width = out_ref.shape
    half = width // 2

    def place_of(turn):
        return lax.rem(outer + 1 + turn, groups)

    def base_of(turn):
        return (place_of(turn) - outer) * INNER

    barrier = pltpu.get_barrier_semaphore()

    def hello(peer):
        pl.semaphore_signal(barrier, inc=1, device_id={"seq": peer}, device_id_type=MESH)

    hello(by_x)
    hello(by_y)

    def hello_outer(turn, carry):
        hello(me + base_of(turn))
        return carry

    lax.fori_loop(0, groups - 1, hello_outer, 0)
    pl.semaphore_wait(barrier, groups + 1)

    flips = ((by_x, by_y), (by_y, by_x))

    def cols(h):
        return pl.ds(h * half, half)

    def along_q(turn, h, other):
        source = (by_xy if other else flips[h][1]) + base_of(turn)
        return remote(
            made.at[source, :, cols(h)],
            got_q.at[h, turn, other],
            send_q.at[h, turn, other],
            recv_q.at[h, turn, other],
            flips[h][1],
        )

    def along_p(turn, h):
        return remote(
            made.at[flips[h][0] + base_of(turn), :, cols(h)],
            got_p.at[h, turn],
            send_p.at[h, turn],
            recv_p.at[h, turn],
            flips[h][0],
        )

    def along_z(turn, h):
        target = me + base_of(turn)
        return remote(
            made.at[target, :, cols(h)],
            got_z.at[h, turn],
            send_z.at[h, turn],
            recv_z.at[h, turn],
            target,
        )

    def make(block):
        left = one_ref[block]
        parts = [
            jnp.dot(left, dy_ref[...], preferred_element_type=F32),
            jnp.dot(left, dxb_ref[...], preferred_element_type=F32),
            jnp.dot(mixed_ref[block], branch_ref[...], preferred_element_type=F32),
        ]
        if rows % 16 == 0:
            for at, part in enumerate(parts):
                made[block, at * rows : (at + 1) * rows] = part.astype(BF16)
            made[block, 3 * rows :] = gate_ref[block]
        else:
            parts.append(gate_ref[block].astype(F32))
            made[block] = jnp.concatenate(parts, axis=0).astype(BF16)

    step = 32

    def add(block, h, ref, index):
        def one(at, carry):
            r = pl.ds(pl.multiple_of(at * step, step), step)
            made[block, r, cols(h)] = (
                made[block, r, cols(h)].astype(F32) + ref[index + (r,)].astype(F32)
            ).astype(BF16)
            return carry

        lax.fori_loop(0, total // step, one, 0)

    def turn_of(turn, carry):
        @pl.when(turn < groups)
        def _():
            base = base_of(turn)
            for h in range(2):
                make(flips[h][1] + base)
            make(by_xy + base)
            for h in range(2):
                for other in range(2):
                    along_q(turn, h, other).start()
            make(me + base)

        @pl.when(jnp.logical_and(turn >= 1, turn <= groups))
        def _():
            now = turn - 1
            base = base_of(now)
            for h in range(2):
                along_q(now, h, 1).wait_recv()
                add(flips[h][0] + base, h, got_q, (h, now, 1))
                along_p(now, h).start()
            for h in range(2):
                along_q(now, h, 0).wait_recv()
                add(me + base, h, got_q, (h, now, 0))

        @pl.when(turn >= 2)
        def _():
            now = turn - 2
            for h in range(2):
                along_p(now, h).wait_recv()
                add(me + base_of(now), h, got_p, (h, now))

                @pl.when(now < groups - 1)
                def _():
                    along_z(now, h).start()

        return carry

    lax.fori_loop(0, groups + 2, turn_of, 0)
    for h in range(2):

        def landed(turn, carry):
            along_z(turn, h).wait_recv()
            return carry

        lax.fori_loop(0, groups - 1, landed, 0)

        def finish(at, carry):
            r = pl.ds(pl.multiple_of(at * step, step), step)
            value = made[me, r, cols(h)].astype(F32)
            for turn in range(groups - 1):
                value = value + got_z[h, turn, r].astype(F32)
            out_ref[r, cols(h)] = value
            return carry

        lax.fori_loop(0, total // step, finish, 0)

    def clear(turn, carry):
        for h in range(2):
            along_q(turn, h, 0).wait_send()
            along_q(turn, h, 1).wait_send()
            along_p(turn, h).wait_send()

            @pl.when(turn < groups - 1)
            def _():
                along_z(turn, h).wait_send()

        return carry

    lax.fori_loop(0, groups, clear, 0)


def scatter_mixer(one, mixed, dy, dxb, branch, gates):
    n, rows, _ = one.shape
    groups = n // INNER
    width = dy.shape[1]
    total = 3 * rows + gates.shape[1]
    dma = pltpu.SemaphoreType.DMA
    return pl.pallas_call(
        functools.partial(scatter_body, n),
        out_shape=jax.ShapeDtypeStruct((total, width), F32),
        in_specs=[VMEM] * 6,
        out_specs=VMEM,
        scratch_shapes=[
            pltpu.VMEM((n, total, width), BF16),
            pltpu.VMEM((2, groups, 2, total, width // 2), BF16),
            pltpu.VMEM((2, groups, total, width // 2), BF16),
            pltpu.VMEM((2, groups, total, width // 2), BF16),
            dma((2, groups, 2)),
            dma((2, groups, 2)),
            dma((2, groups)),
            dma((2, groups)),
            dma((2, groups)),
            dma((2, groups)),
        ],
        compiler_params=params(2, 60),
        cost_estimate=pl.CostEstimate(
            flops=6 * 256 * 2560 * 1280, bytes_accessed=30 * 2**20, transcendentals=0
        ),
        name="scatter_mixer",
    )(one, mixed, dy, dxb, branch, gates)


def small_body(n, value_ref, out_ref, got, send_sem, recv_sem):
    me = lax.axis_index("seq")
    core = lax.axis_index("ch")
    masks = [1 << bit for bit in range(n.bit_length() - 1)]
    peers = [{"seq": me + mask * (1 - 2 * lax.rem(me // mask, 2))} for mask in masks]
    peers.append({"ch": 1 - core})
    barrier = pltpu.get_barrier_semaphore()
    for peer in peers:
        pl.semaphore_signal(barrier, inc=1, device_id=peer, device_id_type=MESH)
    pl.semaphore_wait(barrier, len(peers))
    out_ref[...] = value_ref[...]
    for turn, peer in enumerate(peers):
        copy = pltpu.make_async_remote_copy(
            src_ref=out_ref,
            dst_ref=got.at[turn],
            send_sem=send_sem.at[turn],
            recv_sem=recv_sem.at[turn],
            device_id=peer,
            device_id_type=MESH,
        )
        copy.start()
        copy.wait()
        if turn < len(masks):
            out_ref[...] = out_ref[...] + got[turn]
        else:
            out_ref[8:] = out_ref[8:] + got[turn, 8:]


def small_sums(value):
    n = lax.axis_size("seq")
    turns = n.bit_length()
    return pl.pallas_call(
        functools.partial(small_body, n),
        out_shape=jax.ShapeDtypeStruct(value.shape, F32),
        in_specs=[VMEM],
        out_specs=VMEM,
        scratch_shapes=[
            pltpu.VMEM((turns,) + value.shape, F32),
            pltpu.SemaphoreType.DMA((turns,)),
            pltpu.SemaphoreType.DMA((turns,)),
        ],
        compiler_params=params(3, 16),
        name="small_sums",
    )(value)


GELU_A = 0.7978845608028654
GELU_B = 0.044715


def gelu_parts(v):
    t = jnp.tanh(GELU_A * (v + GELU_B * v * v * v))
    value = 0.5 * v * (1.0 + t)
    slope = 0.5 * (1.0 + t) + 0.5 * v * (1.0 - t * t) * GELU_A * (1.0 + 3.0 * GELU_B * v * v)
    return value, slope


def gates_of(conv_low, gate_ref, par_ref, head, cols, first):
    pre_x = jnp.dot(conv_low, gate_ref[0, head], preferred_element_type=F32)
    pre_a = jnp.dot(conv_low, gate_ref[1, head], preferred_element_type=F32)
    gate_x = jax.nn.sigmoid(pre_x + par_ref[5:6, cols])
    gate_a = jax.nn.sigmoid(pre_a + par_ref[6:7, cols])
    decay = jnp.exp(-8.0 * gate_a * par_ref[8:9, cols])
    room = 1.0 - decay * decay
    mult = jnp.where(first, 1.0, jnp.sqrt(jnp.maximum(room, 0.001)))
    return gate_x, gate_a, decay, room, mult


def first_row(tokens):
    row = lax.broadcasted_iota(jnp.int32, (tokens, 1), 0)
    return jnp.logical_and(row == 0, lax.axis_index("seq") == 0)


def forward_body(
    n, xb_ref, yp_ref, gate_ref, par_ref, conv_ref, state_ref, branch_ref, edge_ref, wide, tail, fade, mine, theirs, *sems
):
    send_tail, recv_tail, send_tot, recv_tot = sems
    tokens, width = xb_ref.shape
    me = lax.axis_index("seq")
    size = gate_ref.shape[2]
    greet_all(n, me)
    tail_copy = remote(
        xb_ref.at[pl.ds(tokens - 16, 16)], tail, send_tail, recv_tail, lax.rem(me + 1, n)
    )
    pl.when(me + 1 < n)(tail_copy.start)
    wide[8:] = xb_ref[...].astype(F32)

    @pl.when(me > 0)
    def _():
        tail_copy.wait_recv()
        wide[:8] = tail[...].astype(F32)[8:]

    @pl.when(me == 0)
    def _():
        wide[:8] = jnp.zeros((8, width), F32)

    pl.when(me + 1 < n)(tail_copy.wait_send)
    edge_ref[:8] = wide[:8]
    first = first_row(tokens)
    for head in range(width // size):
        cols = slice(head * size, (head + 1) * size)
        conv = par_ref[4:5, cols]
        for tap in range(4):
            conv = conv + par_ref[tap : tap + 1, cols] * wide[8 - tap : 8 - tap + tokens, cols]
        conv_low = conv.astype(BF16)
        conv_ref[:, cols] = conv_low
        gate_x, _, decay, _, mult = gates_of(conv_low, gate_ref, par_ref, head, cols, first)
        fade[:, cols] = decay
        state_ref[:, cols] = conv_low.astype(F32) * gate_x * mult

    row = lax.broadcasted_iota(jnp.int32, (8, width), 0)

    def inside(at, carry):
        r = pl.ds(pl.multiple_of(at * 8, 8), 8)
        a, b = fade[r], state_ref[r]
        for by in (1, 2, 4):
            a_back = pltpu.roll(a, by, 0)
            b_back = pltpu.roll(b, by, 0)
            b = jnp.where(row >= by, a * b_back + b, b)
            a = jnp.where(row >= by, a * a_back, a)
        fade[r] = a
        state_ref[r] = b
        return a[7:8] * carry[0], a[7:8] * carry[1] + b[7:8]

    ones, zeros = jnp.ones((1, width), F32), jnp.zeros((1, width), F32)
    tot_a, tot_b = lax.fori_loop(0, tokens // 8, inside, (ones, zeros))
    mine[...] = jnp.where(row == 0, tot_a, tot_b)

    def told(place):
        return remote(mine, theirs.at[me], send_tot.at[place], recv_tot.at[me], place)

    def heard(place):
        return remote(mine, theirs.at[place], send_tot.at[place], recv_tot.at[place], place)

    def tell(place, carry):
        told(place).start()
        return carry

    lax.fori_loop(me + 1, n, tell, 0)

    def hear(place, state):
        heard(place).wait_recv()
        return theirs[place, 0:1] * state + theirs[place, 1:2]

    carry_in = lax.fori_loop(0, me, hear, zeros)
    edge_ref[8:] = jnp.broadcast_to(carry_in, (8, width))

    def finish(at, carry):
        r = pl.ds(pl.multiple_of(at * 16, 16), 16)
        a, b = fade[r], state_ref[r]
        top = b[:8] + a[:8] * carry
        low = b[8:] + a[8:] * top[7:8]
        states = jnp.concatenate([top, low], axis=0)
        state_ref[r] = states
        branch_ref[r] = (states * gelu_parts(yp_ref[r])[0]).astype(BF16)
        return low[7:8]

    lax.fori_loop(0, tokens // 16, finish, carry_in)

    def sent(place, carry):
        told(place).wait_send()
        return carry

    lax.fori_loop(me + 1, n, sent, 0)


def mixer_forward(x_branch, y_pre, gates, par):
    n = lax.axis_size("seq")
    tokens, width = x_branch.shape
    dma = pltpu.SemaphoreType.DMA
    return pl.pallas_call(
        functools.partial(forward_body, n),
        out_shape=(
            jax.ShapeDtypeStruct((tokens, width), BF16),
            jax.ShapeDtypeStruct((tokens, width), F32),
            jax.ShapeDtypeStruct((tokens, width), BF16),
            jax.ShapeDtypeStruct((16, width), F32),
        ),
        in_specs=[VMEM] * 4,
        out_specs=(VMEM,) * 4,
        scratch_shapes=[
            pltpu.VMEM((tokens + 8, width), F32),
            pltpu.VMEM((16, width), BF16),
            pltpu.VMEM((tokens, width), F32),
            pltpu.VMEM((8, width), F32),
            pltpu.VMEM((n, 8, width), F32),
            dma(()),
            dma(()),
            dma((n,)),
            dma((n,)),
        ],
        compiler_params=params(4, 40),
        name="mixer_forward",
    )(x_branch, y_pre, gates, par)


def backward_body(
    n,
    grad_ref,
    yp_ref,
    state_ref,
    edge_ref,
    conv_ref,
    xb_ref,
    gate_ref,
    par_ref,
    dy_ref,
    dxb_ref,
    dgate_ref,
    dpar_ref,
    fade,
    shift,
    adj,
    gate_x_s,
    gate_a_s,
    dconv,
    wide,
    mine,
    theirs,
    head_rows,
    *sems,
):
    send_rows, recv_rows, send_tot, recv_tot = sems
    tokens, width = xb_ref.shape
    me = lax.axis_index("seq")
    size = gate_ref.shape[2]
    greet_all(n, me)
    first = first_row(tokens)
    fade[tokens:] = jnp.ones((8, width), F32)
    for head in range(width // size):
        cols = slice(head * size, (head + 1) * size)
        gate_x, gate_a, decay, _, _ = gates_of(conv_ref[:, cols], gate_ref, par_ref, head, cols, first)
        gate_x_s[:, cols] = gate_x
        gate_a_s[:, cols] = gate_a
        fade[:tokens, cols] = decay
        value, slope = gelu_parts(yp_ref[:, cols])
        grad = grad_ref[:, cols]
        dy_ref[:, cols] = (grad * state_ref[:, cols] * slope).astype(BF16)
        adj[:, cols] = grad * value
        shift[:, cols] = fade[1 : tokens + 1, cols]

    row = lax.broadcasted_iota(jnp.int32, (8, width), 0)
    tiles = tokens // 8

    def inside(turn, carry):
        r = pl.ds(pl.multiple_of((tiles - 1 - turn) * 8, 8), 8)
        a, b = shift[r], adj[r]
        for by in (1, 2, 4):
            a_next = pltpu.roll(a, 8 - by, 0)
            b_next = pltpu.roll(b, 8 - by, 0)
            b = jnp.where(row < 8 - by, a * b_next + b, b)
            a = jnp.where(row < 8 - by, a * a_next, a)
        shift[r] = a
        adj[r] = b
        return a[0:1] * carry[0], a[0:1] * carry[1] + b[0:1]

    ones, zeros = jnp.ones((1, width), F32), jnp.zeros((1, width), F32)
    tot_a, tot_b = lax.fori_loop(0, tiles, inside, (ones, zeros))
    first_fade = fade[0:1]
    mine[...] = jnp.where(row == 0, first_fade * tot_a, first_fade * tot_b)

    def told(place):
        return remote(mine, theirs.at[me], send_tot.at[place], recv_tot.at[me], place)

    def heard(place):
        return remote(mine, theirs.at[place], send_tot.at[place], recv_tot.at[place], place)

    def tell(place, carry):
        told(place).start()
        return carry

    lax.fori_loop(0, me, tell, 0)

    def hear(turn, state):
        place = n - 1 - turn
        heard(place).wait_recv()
        return theirs[place, 0:1] * state + theirs[place, 1:2]

    carry_in = lax.fori_loop(0, n - 1 - me, hear, zeros)

    def finish(turn, carry):
        r = pl.ds(pl.multiple_of((tiles - 1 - turn) * 8, 8), 8)
        value = adj[r] + shift[r] * carry
        adj[r] = value
        return value[0:1]

    lax.fori_loop(0, tiles, finish, carry_in)

    wide[:8] = edge_ref[:8]
    wide[8:] = xb_ref[...].astype(F32)
    at_first = lax.broadcasted_iota(jnp.int32, (tokens, 1), 0) == 0
    for head in range(width // size):
        cols = slice(head * size, (head + 1) * size)
        conv_low = conv_ref[:, cols]
        conv = conv_low.astype(F32)
        gate_x, gate_a, decay = gate_x_s[:, cols], gate_a_s[:, cols], fade[:tokens, cols]
        room = 1.0 - decay * decay
        mult = jnp.where(first, 1.0, jnp.sqrt(jnp.maximum(room, 0.001)))
        back = adj[:, cols]
        before = jnp.where(at_first, edge_ref[8:9, cols], pltpu.roll(state_ref[:, cols], 1, 0))
        d_mult = back * conv * gate_x
        moves = jnp.logical_and(room > 0.001, jnp.logical_not(first))
        d_decay = back * before - jnp.where(moves, d_mult * decay / mult, 0.0)
        d_log = d_decay * decay
        d_pre_x = back * conv * mult * gate_x * (1.0 - gate_x)
        d_pre_a = d_log * (-8.0 * par_ref[8:9, cols]) * gate_a * (1.0 - gate_a)
        dpar_ref[5:6, cols] = jnp.sum(d_pre_x, axis=0, keepdims=True)
        dpar_ref[6:7, cols] = jnp.sum(d_pre_a, axis=0, keepdims=True)
        dpar_ref[7:8, cols] = (
            jnp.sum(d_log * (-8.0 * gate_a), axis=0, keepdims=True) * par_ref[9:10, cols]
        )
        low_x, low_a = d_pre_x.astype(BF16), d_pre_a.astype(BF16)
        flipped = (((1,), (1,)), ((), ()))
        d_conv = (
            back * gate_x * mult
            + lax.dot_general(low_x, gate_ref[0, head], flipped, preferred_element_type=F32)
            + lax.dot_general(low_a, gate_ref[1, head], flipped, preferred_element_type=F32)
        )
        dconv[:tokens, cols] = d_conv
        over_rows = (((0,), (0,)), ((), ()))
        dgate_ref[0, head] = lax.dot_general(
            conv_low, low_x, over_rows, preferred_element_type=F32
        ).astype(BF16)
        dgate_ref[1, head] = lax.dot_general(
            conv_low, low_a, over_rows, preferred_element_type=F32
        ).astype(BF16)
        dpar_ref[4:5, cols] = jnp.sum(d_conv, axis=0, keepdims=True)
        for tap in range(4):
            dpar_ref[tap : tap + 1, cols] = jnp.sum(
                d_conv * wide[8 - tap : 8 - tap + tokens, cols], axis=0, keepdims=True
            )

    rows_copy = remote(
        dconv.at[pl.ds(0, 8)], head_rows, send_rows, recv_rows, lax.rem(me + n - 1, n)
    )
    pl.when(me > 0)(rows_copy.start)

    @pl.when(me + 1 < n)
    def _():
        rows_copy.wait_recv()
        dconv[tokens:] = head_rows[...]

    @pl.when(me + 1 == n)
    def _():
        dconv[tokens:] = jnp.zeros((8, width), F32)

    for head in range(width // size):
        cols = slice(head * size, (head + 1) * size)
        total = par_ref[0:1, cols] * dconv[:tokens, cols]
        for tap in range(1, 4):
            total = total + par_ref[tap : tap + 1, cols] * dconv[tap : tap + tokens, cols]
        dxb_ref[:, cols] = total.astype(BF16)

    pl.when(me > 0)(rows_copy.wait_send)

    def sent(place, carry):
        told(place).wait_send()
        return carry

    lax.fori_loop(0, me, sent, 0)


def mixer_backward(grad, y_pre, states, edge, conv, x_branch, gates, par):
    n = lax.axis_size("seq")
    tokens, width = x_branch.shape
    dma = pltpu.SemaphoreType.DMA
    whole = pltpu.VMEM((tokens, width), F32)
    longer = pltpu.VMEM((tokens + 8, width), F32)
    return pl.pallas_call(
        functools.partial(backward_body, n),
        out_shape=(
            jax.ShapeDtypeStruct((tokens, width), BF16),
            jax.ShapeDtypeStruct((tokens, width), BF16),
            jax.ShapeDtypeStruct(gates.shape, BF16),
            jax.ShapeDtypeStruct((8, width), F32),
        ),
        in_specs=[VMEM] * 8,
        out_specs=(VMEM,) * 4,
        scratch_shapes=[
            longer,
            whole,
            whole,
            whole,
            whole,
            longer,
            longer,
            pltpu.VMEM((8, width), F32),
            pltpu.VMEM((n, 8, width), F32),
            pltpu.VMEM((8, width), F32),
            dma(()),
            dma(()),
            dma((n,)),
            dma((n,)),
        ],
        compiler_params=params(5, 48),
        name="mixer_backward",
    )(grad, y_pre, states, edge, conv, x_branch, gates, par)


def outer_exchange(blocks):
    groups = blocks.shape[0]
    outer = lax.axis_index("seq") // INNER
    got = blocks
    own = pick(blocks, outer)
    received = []
    for step in range(1, groups):
        received.append(swap(pick(blocks, outer ^ step), "seq", step * INNER))
    got = put(jnp.zeros_like(blocks), own, outer)
    for step in range(1, groups):
        got = put(got, received[step - 1], outer ^ step)
    return got


def weights_in(pack):
    groups, kinds, rows, units = pack.shape
    column = outer_exchange(pack)
    inner = lax.axis_index("seq") % INNER
    half = rows // 2
    first, second = column[:, :, :half], column[:, :, half:]
    first_x = swap(first, "seq", 1)
    second_y = swap(second, "seq", 2)
    first_y, first_xy = (swap(v, "seq", 2) for v in (first, first_x))
    second_x, second_xy = (swap(v, "seq", 1) for v in (second, second_y))
    whole = jnp.zeros((kinds, groups, INNER, rows, units), pack.dtype)
    for mask, top, low in (
        (0, first, second),
        (1, first_x, second_x),
        (2, first_y, second_y),
        (3, first_xy, second_xy),
    ):
        place = inner ^ mask
        for block, start in ((top, 0), (low, half)):
            block = jnp.moveaxis(block, 0, 1)[:, :, None]
            whole = lax.dynamic_update_slice(whole, block, (0, 0, place, start, 0))
    return whole.reshape(kinds, groups * INNER * rows, units)


def grads_out(terms, rows):
    units = terms[0].shape[1]
    groups = terms[0].shape[0] // (INNER * rows)
    inner = lax.axis_index("seq") % INNER
    half = rows // 2
    parts = [t.reshape(groups, INNER, rows, units) for t in terms]

    def mine(place, start):
        return jnp.stack(
            [lax.dynamic_slice(t, (0, place, start, 0), (groups, 1, half, units))[:, 0] for t in parts],
            axis=1,
        )

    def reduce(start, near, far):
        low = lambda place: mine(place, start).astype(BF16)
        got_far = swap(low(inner ^ far), "seq", far)
        got_both = swap(low(inner ^ far ^ near), "seq", far)
        mid = (mine(inner ^ near, start) + got_both.astype(F32)).astype(BF16)
        got_near = swap(mid, "seq", near)
        return (mine(inner, start) + got_far.astype(F32) + got_near.astype(F32)).astype(BF16)

    summed = jnp.concatenate([reduce(0, 1, 2), reduce(half, 2, 1)], axis=2)
    got = outer_exchange(summed)
    return jnp.transpose(got, (1, 2, 0, 3)).reshape(3, rows, groups * units).astype(F32)


def my_half(values):
    half = values.shape[0] // 2
    return lax.dynamic_slice_in_dim(values, lax.axis_index("ch") * half, half, 0)


def join(own):
    other = swap(own, "ch", 1)
    core = lax.axis_index("ch")
    return jnp.concatenate(
        [jnp.where(core == 0, own, other), jnp.where(core == 0, other, own)], axis=0
    )


def half_sum(partial):
    core = lax.axis_index("ch")
    parts = partial.reshape((2, partial.shape[0] // 2) + partial.shape[1:])
    theirs = swap(pick(parts, 1 - core), "ch", 1)
    return pick(parts, core).astype(F32) + theirs.astype(F32)


def tokens_in(own):
    half, width = own.shape
    groups = lax.axis_size("seq") // INNER
    outer = lax.axis_index("seq") // INNER
    core = lax.axis_index("ch")
    got = put(jnp.zeros((groups, half, width), own.dtype), own, outer)
    for step in range(1, groups):
        got = put(got, swap(own, "seq", step * INNER), outer ^ step)
    other = swap(got, "ch", 1)
    first = jnp.where(core == 0, got, other)
    second = jnp.where(core == 0, other, got)
    return jnp.stack([first, second], axis=1).reshape(groups * 2 * half, width)


def tokens_out(partial, half):
    width = partial.shape[1]
    groups = lax.axis_size("seq") // INNER
    outer = lax.axis_index("seq") // INNER
    core = lax.axis_index("ch")
    parts = partial.reshape(groups, 2, half, width)
    theirs = pick(parts, 1 - core, 1).astype(BF16)
    summed = (pick(parts, core, 1).astype(F32) + swap(theirs, "ch", 1).astype(F32)).astype(BF16)
    total = pick(summed, outer).astype(F32)
    for step in range(1, groups):
        total = total + swap(pick(summed, outer ^ step), "seq", step * INNER).astype(F32)
    return total


def gate_rows(blocks, n):
    _, heads, depth, size = blocks.shape
    part = depth // n
    rows = 2 * part
    split = blocks.reshape(2, heads, n, part, size).transpose(2, 0, 1, 3, 4)
    return split.reshape(n, 2, rows, heads * size // 2).transpose(0, 2, 1, 3).reshape(n, rows, heads * size)


def gate_blocks(rows, heads, size):
    n, count, width = rows.shape
    split = rows.reshape(n, count, 2, width // 2).transpose(0, 2, 1, 3)
    part = count * width // (2 * heads * size)
    return split.reshape(n, 2, heads, part, size).transpose(1, 2, 0, 3, 4).reshape(2, heads, n * part, size)


def shards(
    inputs,
    norm_gain,
    branch_weight,
    input_weight,
    channel_params,
    gate_x_blocks,
    gate_a_blocks,
    out_weight,
    ffn_gain,
    ffn_gate,
    ffn_up,
    ffn_down,
    cotangent,
):
    f32 = F32
    bf16 = BF16
    n = lax.axis_size("seq")
    tok_rows, model = inputs.shape
    half_rows = tok_rows // 2
    heads, part, size = gate_x_blocks.shape
    width = heads * size
    depth = ffn_gate.shape[0]
    groups = n // INNER
    units = ffn_gate.shape[1] // groups
    x_float = inputs.astype(f32)
    n_one = scaled_norm(x_float, norm_gain).astype(bf16)
    x_half = my_half(inputs).astype(f32)
    _, norm_back_one = jax.vjp(scaled_norm, x_half, norm_gain)

    mixer_pack = jnp.stack([branch_weight, input_weight, out_weight.T])
    gate_pack = gate_rows(jnp.stack([gate_x_blocks, gate_a_blocks]), 1)[0]
    full_mixer, full_gates = gather_mixer(mixer_pack, gate_pack)
    full_mixer = full_mixer.reshape(3, model, width)
    full_branch, full_input, full_out = full_mixer[0], full_mixer[1], full_mixer[2]
    gates = gate_blocks(full_gates, heads, size)
    par = jnp.concatenate(
        [
            channel_params,
            jax.nn.softplus(channel_params[7:8]),
            jax.nn.sigmoid(channel_params[7:8]),
            jnp.zeros((6, width), f32),
        ],
        axis=0,
    )

    pack = jnp.stack(
        [w.reshape(depth, groups, units).transpose(1, 0, 2) for w in (ffn_gate, ffn_up, ffn_down.T)],
        axis=1,
    )
    full_ffn = weights_in(pack)
    cot_half = my_half(cotangent)
    all_cot = tokens_in(cot_half)

    x_branch = jnp.dot(n_one, full_input, preferred_element_type=f32).astype(bf16)
    y_pre = jnp.dot(n_one, full_branch, preferred_element_type=f32)
    conv_out, states, branch_out, edge = mixer_forward(x_branch, y_pre, gates, par)
    mixed = half_sum(jnp.einsum("tw,dw->td", branch_out, full_out, preferred_element_type=f32))
    resid = x_half + mixed
    n_two_f, norm_back_two = jax.vjp(scaled_norm, resid, ffn_gain)
    all_two = tokens_in(n_two_f.astype(bf16))
    gate_pre = jnp.dot(all_two, full_ffn[0], preferred_element_type=f32)
    up_pre = jnp.dot(all_two, full_ffn[1], preferred_element_type=f32)
    gate_act, gelu_back_gate = jax.vjp(gelu_tanh, gate_pre)
    hidden = (gate_act * up_pre).astype(bf16)
    ffn_term = jnp.einsum("tf,df->td", hidden, full_ffn[2], preferred_element_type=f32)
    block_out = join((resid + tokens_out(ffn_term, half_rows)).astype(bf16))

    d_hidden = jnp.einsum("td,df->tf", all_cot, full_ffn[2], preferred_element_type=f32)
    d_gate = gelu_back_gate(d_hidden * up_pre)[0].astype(bf16)
    d_up = (d_hidden * gate_act).astype(bf16)
    d_n_two = tokens_out(
        jnp.einsum("tf,df->td", d_gate, full_ffn[0], preferred_element_type=f32)
        + jnp.einsum("tf,df->td", d_up, full_ffn[1], preferred_element_type=f32),
        half_rows,
    )
    d_gate_term = jnp.einsum("td,tf->df", all_two, d_gate, preferred_element_type=f32)
    d_up_term = jnp.einsum("td,tf->df", all_two, d_up, preferred_element_type=f32)
    d_down_term = jnp.einsum("td,tf->df", all_cot, hidden, preferred_element_type=f32)
    ffn_grads = grads_out([d_gate_term, d_up_term, d_down_term], depth)
    d_resid_norm, d_ffn_gain_term = norm_back_two(d_n_two)
    d_resid = cot_half.astype(f32) + d_resid_norm
    d_mixed = join(d_resid.astype(bf16))
    d_branch_out = jnp.einsum("td,dw->tw", d_mixed, full_out, preferred_element_type=f32)
    d_y, d_xb, d_gates, d_channel_term = mixer_backward(
        d_branch_out, y_pre, states, edge, conv_out, x_branch, gates, par
    )
    d_n_one = half_sum(
        (
            jnp.einsum("tw,dw->td", d_y, full_branch, preferred_element_type=f32)
            + jnp.einsum("tw,dw->td", d_xb, full_input, preferred_element_type=f32)
        ).astype(bf16)
    )
    d_x_norm, d_norm_gain_term = norm_back_one(d_n_one)
    d_inputs = join(d_resid + d_x_norm)
    small = small_sums(
        jnp.concatenate(
            [
                d_channel_term,
                d_norm_gain_term.reshape(-1, width),
                d_ffn_gain_term.reshape(-1, width),
                jnp.zeros((8 - 2 * (model // width), width), f32),
            ],
            axis=0,
        )
    )
    gain_rows = model // width
    scattered = scatter_mixer(
        n_one.T.reshape(n, depth, tok_rows),
        d_mixed.T.reshape(n, depth, tok_rows),
        d_y,
        d_xb,
        branch_out,
        gate_rows(d_gates, n),
    )
    d_gate_pair = gate_blocks(scattered[None, 3 * depth :], heads, size)
    return (
        block_out,
        d_inputs,
        small[8 : 8 + gain_rows].reshape(model),
        scattered[:depth],
        scattered[depth : 2 * depth],
        small[:8],
        d_gate_pair[0],
        d_gate_pair[1],
        scattered[2 * depth : 3 * depth].T,
        small[8 + gain_rows : 8 + 2 * gain_rows].reshape(model),
        ffn_grads[0],
        ffn_grads[1],
        ffn_grads[2].T,
    )


def solution(mesh):
    placed = (
        P("seq", None),
        P(),
        P("seq", "ch"),
        P("seq", "ch"),
        P(None, "ch"),
        P("ch", "seq", None),
        P("ch", "seq", None),
        P("ch", "seq"),
        P(),
        P("seq", "ch"),
        P("seq", "ch"),
        P("ch", "seq"),
        P("seq", None),
    )
    return jax.shard_map(
        shards,
        mesh=mesh,
        in_specs=placed,
        out_specs=(
            P("seq", None),
            P("seq", None),
            P(),
            P("seq", "ch"),
            P("seq", "ch"),
            P(None, "ch"),
            P("ch", "seq", None),
            P("ch", "seq", None),
            P("ch", "seq"),
            P(),
            P("seq", "ch"),
            P("seq", "ch"),
            P("ch", "seq"),
        ),
        check_vma=False,
    )
```

```python
import functools

import jax
import jax.numpy as jnp
from jax import lax
from jax.experimental import pallas as pl
from jax.experimental.pallas import tpu as pltpu
from jax.sharding import PartitionSpec as P

F32 = jnp.float32
BF16 = jnp.bfloat16
INNER = 4
MESH = pl.DeviceIdType.MESH
VMEM = pl.BlockSpec(memory_space=pltpu.VMEM)
ANY = pl.BlockSpec(memory_space=pl.ANY)


def swap(value, axis, mask):
    return lax.ppermute(value, axis, [(i, i ^ mask) for i in range(lax.axis_size(axis))])


def pick(array, index, axis=0):
    return lax.dynamic_index_in_dim(array, index, axis, False)


def put(array, block, index, axis=0):
    return lax.dynamic_update_index_in_dim(array, block, index, axis)


def scaled_norm(values, gain):
    return values * lax.rsqrt(jnp.mean(values * values, axis=-1, keepdims=True) + 1e-06) * gain


def gelu_tanh(values):
    return jax.nn.gelu(values, approximate=True)


def whereabouts():
    me = lax.axis_index("seq")
    outer = me // INNER
    inner = me - outer * INNER
    y = inner // 2
    x = inner - 2 * y
    by_x = me + 1 - 2 * x
    by_y = me + 2 - 4 * y
    return me, outer, by_x, by_y, by_x + 2 - 4 * y


def when(condition, action):
    if condition is None:
        action()
    else:
        pl.when(condition)(action)


def both(one, other):
    if one is None or other is None:
        return one if other is None else other
    return jnp.logical_and(one, other)


def greet(peers):
    barrier = pltpu.get_barrier_semaphore()
    for condition, peer in peers:
        when(
            condition,
            lambda peer=peer: pl.semaphore_signal(
                barrier, inc=1, device_id={"seq": peer}, device_id_type=MESH
            ),
        )
    count = 0
    for condition, _ in peers:
        count = count + (1 if condition is None else condition.astype(jnp.int32))
    pl.semaphore_wait(barrier, count)


def greet_all(n, me):
    barrier = pltpu.get_barrier_semaphore()

    def hello(step, carry):
        pl.semaphore_signal(
            barrier, inc=1, device_id={"seq": lax.rem(me + step, n)}, device_id_type=MESH
        )
        return carry

    lax.fori_loop(1, n, hello, 0)
    pl.semaphore_wait(barrier, n - 1)


def remote(src, dst, send_sem, recv_sem, place):
    return pltpu.make_async_remote_copy(
        src_ref=src,
        dst_ref=dst,
        send_sem=send_sem,
        recv_sem=recv_sem,
        device_id={"seq": place},
        device_id_type=MESH,
    )


def params(collective_id, mib):
    return pltpu.CompilerParams(
        collective_id=collective_id, has_side_effects=True, vmem_limit_bytes=mib * 2**20
    )


def gather_body(n, *refs):
    w_refs, g_ref, f_ref = refs[:3], refs[3], refs[4]
    wo_refs, go_ref, column_ref = refs[5:8], refs[8], refs[9]
    send_m, recv_m, send_f, recv_f, here = refs[10:]
    groups = n // INNER
    me, outer, by_x, by_y, by_xy = whereabouts()
    above, below = outer + 1 < groups, outer > 0
    barrier = pltpu.get_barrier_semaphore()

    def hello(peer):
        pl.semaphore_signal(barrier, inc=1, device_id={"seq": peer}, device_id_type=MESH)

    hello(by_x)
    hello(by_y)

    def column_peer(turn):
        return lax.rem(outer + turn, groups)

    def hello_column(turn, carry):
        hello(me + (column_peer(turn) - outer) * INNER)
        return carry

    lax.fori_loop(1, groups, hello_column, 0)
    pl.semaphore_wait(barrier, groups + 1)
    units = column_ref.shape[3]
    half = w_refs[0].shape[1] // 2

    def units_of(place):
        return pl.ds(pl.multiple_of(place * units, units), units)

    keep = [
        pltpu.make_async_copy(w_refs[kind], wo_refs[kind].at[me], here.at[kind])
        for kind in range(3)
    ]
    keep.append(pltpu.make_async_copy(g_ref, go_ref.at[me], here.at[3]))
    keep.append(
        pltpu.make_async_copy(
            f_ref.at[:, :, units_of(outer)], column_ref.at[:, outer], here.at[4]
        )
    )
    for copy in keep:
        copy.start()
    sent = []

    def copies(h, source, way, target, own):
        cols = pl.ds(h * half, half)
        pairs = [(w_refs[kind], wo_refs[kind].at[source]) for kind in range(3)]
        pairs.append((g_ref, go_ref.at[source]))
        return [
            remote(
                (given if own else dst).at[:, cols],
                dst.at[:, cols],
                send_m.at[kind, h, source, way],
                recv_m.at[kind, h, source],
                target,
            )
            for kind, (given, dst) in enumerate(pairs)
        ]

    def send(condition, *what):
        def go():
            for copy in copies(*what):
                copy.start()

        when(condition, go)
        sent.append((condition, what))

    def arrive(condition, h, source):
        def go():
            for copy in copies(h, source, 0, by_x, False):
                copy.wait_recv()

        when(condition, go)

    def exchange(turn, receive):
        place = lax.rem(outer + groups - turn, groups) if receive else column_peer(turn)
        target = me + (place - outer) * INNER
        return remote(
            f_ref.at[:, :, units_of(place)],
            column_ref.at[:, place if receive else outer],
            send_f.at[turn],
            recv_f.at[turn],
            target,
        )

    def each_turn(action):
        def one(turn, carry):
            action(turn)
            return carry

        lax.fori_loop(1, groups, one, 0)

    for step in range(groups):
        for h in range(2):
            flip_p, flip_q = (by_x, by_y) if h == 0 else (by_y, by_x)
            if step == 0:
                send(above, h, me, 0, me + INNER, True)
                send(below, h, me, 1, me - INNER, True)
                send(None, h, me, 2, flip_p, True)
                send(None, h, me, 3, flip_q, True)
                continue
            for source, there, onward, way, to in (
                (me - step * INNER, outer >= step, above, 0, me + INNER),
                (me + step * INNER, outer + step < groups, below, 1, me - INNER),
            ):
                arrive(there, h, source)
                send(both(there, onward), h, source, way, to, False)
                send(there, h, source, 2, flip_p, False)
                send(there, h, source, 3, flip_q, False)
        if step == groups - 1:
            each_turn(lambda turn: exchange(turn, False).start())
        for h in range(2):
            flip_p, flip_q = (by_x, by_y) if h == 0 else (by_y, by_x)
            if step == 0:
                arrive(None, h, flip_p)
                send(None, h, flip_p, 3, flip_q, False)
                continue
            for source, there in (
                (flip_p - step * INNER, outer >= step),
                (flip_p + step * INNER, outer + step < groups),
            ):
                arrive(there, h, source)
                send(there, h, source, 3, flip_q, False)
    for place in range(groups):
        shift = (place - outer) * INNER
        for h in range(2):
            arrive(None, h, (by_y if h == 0 else by_x) + shift)
            arrive(None, h, by_xy + shift)
    each_turn(lambda turn: exchange(turn, True).wait_recv())
    for condition, what in sent:

        def finish(what=what):
            for copy in copies(*what):
                copy.wait_send()

        when(condition, finish)
    each_turn(lambda turn: exchange(turn, False).wait_send())
    for copy in keep:
        copy.wait()


def gather_weights(weights, gates, ffn):
    n = lax.axis_size("seq")
    groups = n // INNER
    kinds, rows, padded = ffn.shape
    dma = pltpu.SemaphoreType.DMA
    made = [jax.ShapeDtypeStruct((n,) + w.shape, w.dtype) for w in (*weights, gates)]
    made.append(jax.ShapeDtypeStruct((kinds, groups, rows, padded // groups), ffn.dtype))
    return pl.pallas_call(
        functools.partial(gather_body, n),
        out_shape=tuple(made),
        in_specs=[ANY] * 5,
        out_specs=(ANY,) * 5,
        scratch_shapes=[
            dma((4, 2, n, 4)),
            dma((4, 2, n)),
            dma((groups,)),
            dma((groups,)),
            dma((5,)),
        ],
        compiler_params=params(1, 16),
        name="gather_weights",
    )(*weights, gates, ffn)


def tokens_body(n, *refs):
    own_refs, column_ref, near_ref = refs[:2], refs[2], refs[3]
    all_refs, w_refs = refs[4:6], refs[6:9]
    send_t, recv_z, recv_c, send_w, recv_w, here = refs[9:]
    groups = n // INNER
    half = groups // 2
    me, outer, by_x, by_y, by_xy = whereabouts()
    base = outer * INNER
    core = lax.axis_index("ch")
    above, below = outer + 1 < groups, outer > 0
    sibling = {"ch": 1 - core}
    barrier = pltpu.get_barrier_semaphore()

    def hello(peer):
        pl.semaphore_signal(barrier, inc=1, device_id=peer, device_id_type=MESH)

    hello({"seq": by_x})
    hello({"seq": by_y})
    hello(sibling)
    pl.when(above)(lambda: hello({"seq": me + INNER}))
    pl.when(below)(lambda: hello({"seq": me - INNER}))
    pl.semaphore_wait(barrier, 3 + above.astype(jnp.int32) + below.astype(jnp.int32))

    def token_copy(kind, source, way, own=False):
        dst = all_refs[kind].at[source, core]
        to = ({"seq": me + INNER}, {"seq": me - INNER}, sibling)[way]
        return pltpu.make_async_remote_copy(
            src_ref=own_refs[kind] if own else dst,
            dst_ref=dst,
            send_sem=send_t.at[kind, source, way],
            recv_sem=(recv_c if way == 2 else recv_z).at[kind, source],
            device_id=to,
            device_id_type=MESH,
        )

    def from_sibling(kind, source):
        dst = all_refs[kind].at[source, 1 - core]
        return pltpu.make_async_remote_copy(
            src_ref=own_refs[kind],
            dst_ref=dst,
            send_sem=send_t.at[kind, source, 2],
            recv_sem=recv_c.at[kind, source],
            device_id=sibling,
            device_id_type=MESH,
        )

    def part(h):
        return pl.ds(h * half, half)

    flips = ((by_x, by_y), (by_y, by_x))

    def weight_copy(kind, h, far, receive=False):
        source = flips[h][0] if far else me
        if receive:
            source = by_xy if far else flips[h][1]
        return remote(
            near_ref.at[h, kind] if far else column_ref.at[kind, part(h)],
            w_refs[kind].at[part(h), source - base],
            send_w.at[kind, h, far],
            recv_w.at[kind, h, far],
            flips[h][1],
        )

    keep = []
    for kind in range(2):
        keep.append(
            pltpu.make_async_copy(own_refs[kind], all_refs[kind].at[outer, core], here.at[kind])
        )
    for kind in range(3):
        keep.append(
            pltpu.make_async_copy(
                column_ref.at[kind], w_refs[kind].at[:, me - base], here.at[2 + kind]
            )
        )
        for h in range(2):
            keep.append(
                pltpu.make_async_copy(
                    near_ref.at[h, kind],
                    w_refs[kind].at[part(h), flips[h][0] - base],
                    here.at[5 + 2 * kind + h],
                )
            )
    every_w = [(kind, h, far) for kind in range(3) for h in range(2) for far in range(2)]

    for kind in range(2):
        pl.when(above)(token_copy(kind, outer, 0, True).start)
        pl.when(below)(token_copy(kind, outer, 1, True).start)
        token_copy(kind, outer, 2, True).start()
    for what in every_w:
        weight_copy(*what).start()
    for copy in keep:
        copy.start()
    for kind in range(2):
        for step in range(1, groups):
            for source, there, onward, way in (
                (outer - step, outer >= step, above, 0),
                (outer + step, outer + step < groups, below, 1),
            ):
                pl.when(there)(token_copy(kind, source, way).wait_recv)
                pl.when(both(there, onward))(token_copy(kind, source, way).start)
                pl.when(there)(token_copy(kind, source, 2).start)
    for kind in range(2):
        for source in range(groups):
            from_sibling(kind, source).wait_recv()
    for what in every_w:
        weight_copy(*what, receive=True).wait_recv()
    for kind in range(2):
        pl.when(above)(token_copy(kind, outer, 0, True).wait_send)
        pl.when(below)(token_copy(kind, outer, 1, True).wait_send)
        token_copy(kind, outer, 2, True).wait_send()
        for step in range(1, groups):
            for source, there, onward, way in (
                (outer - step, outer >= step, above, 0),
                (outer + step, outer + step < groups, below, 1),
            ):
                pl.when(both(there, onward))(token_copy(kind, source, way).wait_send)
                pl.when(there)(token_copy(kind, source, 2).wait_send)
    for what in every_w:
        weight_copy(*what).wait_send()
    for copy in keep:
        copy.wait()


def gather_tokens(tokens, cotangent, column, near):
    n = lax.axis_size("seq")
    groups = n // INNER
    kinds, _, rows, units = column.shape
    dma = pltpu.SemaphoreType.DMA
    wide = jax.ShapeDtypeStruct((groups, 2) + tokens.shape, tokens.dtype)
    weight = jax.ShapeDtypeStruct((groups, INNER, rows, units), column.dtype)
    return pl.pallas_call(
        functools.partial(tokens_body, n),
        out_shape=(wide, wide, weight, weight, weight),
        in_specs=[ANY] * 4,
        out_specs=(ANY,) * 5,
        scratch_shapes=[
            dma((2, groups, 3)),
            dma((2, groups)),
            dma((2, groups)),
            dma((kinds, 2, 2)),
            dma((kinds, 2, 2)),
            dma((11,)),
        ],
        compiler_params=params(6, 16),
        name="gather_tokens",
    )(tokens, cotangent, column, near)


def reduce_body(n, kinds, *refs):
    p_refs, t_refs = refs[:kinds], refs[kinds : kinds + 3]
    out_refs, far_ref = refs[kinds + 3 : 2 * kinds + 3], refs[2 * kinds + 3]
    summed, got, send_c, recv_c, send_z, recv_z, send_f, recv_f = refs[2 * kinds + 4 :]
    groups = n // INNER
    half = groups // 2
    me, outer, by_x, by_y, by_xy = whereabouts()
    base = outer * INNER
    core = lax.axis_index("ch")
    above, below = outer + 1 < groups, outer > 0
    sibling = {"ch": 1 - core}
    barrier = pltpu.get_barrier_semaphore()

    def hello(peer):
        pl.semaphore_signal(barrier, inc=1, device_id=peer, device_id_type=MESH)

    hello({"seq": by_x})
    hello({"seq": by_y})
    hello(sibling)
    pl.when(above)(lambda: hello({"seq": me + INNER}))
    pl.when(below)(lambda: hello({"seq": me - INNER}))
    pl.semaphore_wait(barrier, 3 + above.astype(jnp.int32) + below.astype(jnp.int32))
    flips = ((by_x, by_y), (by_y, by_x))

    def gradient_copy(kind, h, far):
        source = by_xy if far else flips[h][1]
        return remote(
            t_refs[kind].at[pl.ds(h * half, half), source - base],
            far_ref.at[h, far, kind],
            send_f.at[kind, h, far],
            recv_f.at[kind, h, far],
            flips[h][1],
        )

    def to_sibling(kind, place):
        return pltpu.make_async_remote_copy(
            src_ref=p_refs[kind].at[place, 1 - core],
            dst_ref=summed.at[kind, place],
            send_sem=send_c.at[kind, place],
            recv_sem=recv_c.at[kind, place],
            device_id=sibling,
            device_id_type=MESH,
        )

    def along(kind, place, up):
        last = place == (outer + 1 if up else outer - 1)
        slot = place if up else jnp.where(last, groups, place)
        return remote(
            summed.at[kind, place],
            got.at[kind, slot],
            send_z.at[kind, place],
            recv_z.at[kind, slot],
            me + (INNER if up else -INNER),
        )

    def landed(kind, slot):
        return remote(
            summed.at[kind, 0], got.at[kind, slot], send_z.at[kind, 0], recv_z.at[kind, slot], by_x
        )

    def each(limit, action):
        def one(turn, carry):
            action(turn)
            return carry

        lax.fori_loop(0, limit, one, 0)

    every_f = [(kind, h, far) for far in (1, 0) for kind in range(3) for h in range(2)]
    for kind in range(kinds):
        each(groups, lambda place, kind=kind: to_sibling(kind, place).start())
    for what in every_f:
        gradient_copy(*what).start()

    tall = summed.shape[2]
    chunk = 16

    def rows_of(at):
        return pl.ds(pl.multiple_of(at * chunk, chunk), chunk)

    def ready(kind, place, incoming):
        to_sibling(kind, place).wait_recv()

        def local(at):
            r = rows_of(at)
            summed[kind, place, r] = (
                summed[kind, place, r].astype(F32) + p_refs[kind][place, core, r].astype(F32)
            ).astype(BF16)

        def more(at):
            r = rows_of(at)
            summed[kind, place, r] = (
                summed[kind, place, r].astype(F32)
                + p_refs[kind][place, core, r].astype(F32)
                + got[kind, place, r].astype(F32)
            ).astype(BF16)

        @pl.when(incoming)
        def _():
            landed(kind, place).wait_recv()
            each(tall // chunk, more)

        @pl.when(jnp.logical_not(incoming))
        def _():
            each(tall // chunk, local)

    for kind in range(kinds):

        def climb(turn, kind=kind):
            place = groups - 1 - turn

            @pl.when(place > outer)
            def _():
                ready(kind, place, below)
                along(kind, place, True).start()

        def sink(turn, kind=kind):
            place = turn

            @pl.when(place < outer)
            def _():
                ready(kind, place, above)
                along(kind, place, False).start()

        def turns(turn):
            @pl.when(outer < half)
            def _():
                climb(turn)
                sink(turn)

            @pl.when(outer >= half)
            def _():
                sink(turn)
                climb(turn)

        each(groups - 1, turns)
    for kind in range(kinds):
        to_sibling(kind, outer).wait_recv()

        def own(at, kind=kind):
            r = rows_of(at)
            out_refs[kind][r] = summed[kind, outer, r].astype(F32) + p_refs[kind][
                outer, core, r
            ].astype(F32)

        each(tall // chunk, own)
        for there, slot in ((below, outer), (above, groups)):

            @pl.when(there)
            def _():
                landed(kind, slot).wait_recv()

                def plus(at):
                    r = rows_of(at)
                    out_refs[kind][r] = out_refs[kind][r] + got[kind, slot, r].astype(F32)

                each(tall // chunk, plus)

    for kind in range(kinds):

        def clear(place, kind=kind):
            to_sibling(kind, place).wait_send()

            @pl.when(place > outer)
            def _():
                along(kind, place, True).wait_send()

            @pl.when(place < outer)
            def _():
                along(kind, place, False).wait_send()

        each(groups, clear)
    for what in every_f:
        gradient_copy(*what).wait()


def reduce_tokens(partials, gradients):
    n = lax.axis_size("seq")
    groups = n // INNER
    kinds = len(partials)
    _, _, tall, width = partials[0].shape
    _, _, rows, units = gradients[0].shape
    dma = pltpu.SemaphoreType.DMA
    return pl.pallas_call(
        functools.partial(reduce_body, n, kinds),
        out_shape=(jax.ShapeDtypeStruct((tall, width), F32),) * kinds
        + (jax.ShapeDtypeStruct((2, 2, 3, groups // 2, rows, units), BF16),),
        in_specs=[VMEM] * kinds + [ANY] * 3,
        out_specs=(VMEM,) * kinds + (ANY,),
        scratch_shapes=[
            pltpu.VMEM((kinds, groups, tall, width), BF16),
            pltpu.VMEM((kinds, groups + 1, tall, width), BF16),
            dma((kinds, groups)),
            dma((kinds, groups)),
            dma((kinds, groups)),
            dma((kinds, groups + 1)),
            dma((3, 2, 2)),
            dma((3, 2, 2)),
        ],
        compiler_params=params(7, 60),
        name="reduce_tokens",
    )(*partials, *gradients)


def scatter_body(
    n,
    one_ref,
    mixed_ref,
    dy_ref,
    dxb_ref,
    branch_ref,
    gate_ref,
    small_ref,
    column_ref,
    out_ref,
    small_out,
    spread_ref,
    made,
    got_q,
    got_p,
    got_z,
    got_s,
    *sems,
):
    send_q, recv_q, send_p, recv_p, send_z, recv_z, send_s, recv_s, send_f, recv_f, here = sems
    groups = n // INNER
    me, outer, by_x, by_y, by_xy = whereabouts()
    rows = one_ref.shape[1]
    total, width = out_ref.shape
    half = width // 2

    def place_of(turn):
        return lax.rem(outer + 1 + turn, groups)

    def base_of(turn):
        return (place_of(turn) - outer) * INNER

    barrier = pltpu.get_barrier_semaphore()

    def hello(peer):
        pl.semaphore_signal(barrier, inc=1, device_id={"seq": peer}, device_id_type=MESH)

    hello(by_x)
    hello(by_y)

    def hello_outer(turn, carry):
        hello(me + base_of(turn))
        return carry

    lax.fori_loop(0, groups - 1, hello_outer, 0)
    core = lax.axis_index("ch")
    masks = [1 << bit for bit in range(n.bit_length() - 1)]
    pl.semaphore_signal(barrier, inc=1, device_id={"ch": 1 - core}, device_id_type=MESH)
    pl.semaphore_wait(barrier, groups + 2)

    flips = ((by_x, by_y), (by_y, by_x))
    units = column_ref.shape[3]

    def units_of(place):
        return pl.ds(pl.multiple_of(place * units, units), units)

    def exchange(turn, receive=False):
        place = lax.rem(outer + groups - 1 - turn, groups) if receive else place_of(turn)
        return remote(
            column_ref.at[:, place],
            spread_ref.at[:, :, units_of(place if receive else outer)],
            send_f.at[turn],
            recv_f.at[turn],
            me + (place - outer) * INNER,
        )

    def small(turn):
        place = me
        for at, mask in enumerate(masks):
            flipped = me + mask * (1 - 2 * lax.rem(me // mask, 2))
            place = jnp.where(turn == at, flipped, place)
        other = jnp.where(turn == len(masks), 1 - core, core)
        return pltpu.make_async_remote_copy(
            src_ref=small_out,
            dst_ref=got_s.at[turn],
            send_sem=send_s.at[turn],
            recv_sem=recv_s.at[turn],
            device_id=(place, other),
            device_id_type=MESH,
        )

    small_out[...] = small_ref[...]
    small_row = lax.broadcasted_iota(jnp.int32, small_ref.shape, 0)

    def cols(h):
        return pl.ds(h * half, half)

    def along_q(turn, h, other):
        source = (by_xy if other else flips[h][1]) + base_of(turn)
        return remote(
            made.at[source, :, cols(h)],
            got_q.at[h, turn, other],
            send_q.at[h, turn, other],
            recv_q.at[h, turn, other],
            flips[h][1],
        )

    def along_p(turn, h):
        return remote(
            made.at[flips[h][0] + base_of(turn), :, cols(h)],
            got_p.at[h, turn],
            send_p.at[h, turn],
            recv_p.at[h, turn],
            flips[h][0],
        )

    def along_z(turn, h):
        target = me + base_of(turn)
        return remote(
            made.at[target, :, cols(h)],
            got_z.at[h, turn],
            send_z.at[h, turn],
            recv_z.at[h, turn],
            target,
        )

    def make(block):
        left = one_ref[block]
        parts = [
            jnp.dot(left, dy_ref[...], preferred_element_type=F32),
            jnp.dot(left, dxb_ref[...], preferred_element_type=F32),
            jnp.dot(mixed_ref[block], branch_ref[...], preferred_element_type=F32),
        ]
        if rows % 16 == 0:
            for at, part in enumerate(parts):
                made[block, at * rows : (at + 1) * rows] = part.astype(BF16)
            made[block, 3 * rows :] = gate_ref[block]
        else:
            parts.append(gate_ref[block].astype(F32))
            made[block] = jnp.concatenate(parts, axis=0).astype(BF16)

    step = 32

    def add(block, h, ref, index):
        def one(at, carry):
            r = pl.ds(pl.multiple_of(at * step, step), step)
            made[block, r, cols(h)] = (
                made[block, r, cols(h)].astype(F32) + ref[index + (r,)].astype(F32)
            ).astype(BF16)
            return carry

        lax.fori_loop(0, total // step, one, 0)

    keep = pltpu.make_async_copy(
        column_ref.at[:, outer], spread_ref.at[:, :, units_of(outer)], here
    )
    keep.start()

    def turn_of(turn, carry):
        pl.when(turn <= len(masks))(lambda: small(turn).start())

        @pl.when(turn < groups)
        def _():
            base = base_of(turn)
            for h in range(2):
                make(flips[h][1] + base)
            make(by_xy + base)
            for h in range(2):
                for other in range(2):
                    along_q(turn, h, other).start()
            pl.when(turn < groups - 1)(lambda: exchange(turn).start())
            make(me + base)

        @pl.when(jnp.logical_and(turn >= 1, turn <= groups))
        def _():
            now = turn - 1
            base = base_of(now)
            for h in range(2):
                along_q(now, h, 1).wait_recv()
                add(flips[h][0] + base, h, got_q, (h, now, 1))
                along_p(now, h).start()
            for h in range(2):
                along_q(now, h, 0).wait_recv()
                add(me + base, h, got_q, (h, now, 0))

        @pl.when(turn >= 2)
        def _():
            now = turn - 2
            for h in range(2):
                along_p(now, h).wait_recv()
                add(me + base_of(now), h, got_p, (h, now))

                @pl.when(now < groups - 1)
                def _():
                    along_z(now, h).start()

        @pl.when(turn <= len(masks))
        def _():
            small(turn).wait()
            counts = jnp.logical_or(turn < len(masks), small_row >= 8)
            small_out[...] = small_out[...] + jnp.where(counts, got_s[turn], 0.0)

        return carry

    assert len(masks) < groups + 2
    lax.fori_loop(0, groups + 2, turn_of, 0)
    for h in range(2):

        def landed(turn, carry):
            along_z(turn, h).wait_recv()
            return carry

        lax.fori_loop(0, groups - 1, landed, 0)

        def finish(at, carry):
            r = pl.ds(pl.multiple_of(at * step, step), step)
            value = made[me, r, cols(h)].astype(F32)
            for turn in range(groups - 1):
                value = value + got_z[h, turn, r].astype(F32)
            out_ref[r, cols(h)] = value
            return carry

        lax.fori_loop(0, total // step, finish, 0)

    def clear(turn, carry):
        for h in range(2):
            along_q(turn, h, 0).wait_send()
            along_q(turn, h, 1).wait_send()
            along_p(turn, h).wait_send()

            @pl.when(turn < groups - 1)
            def _():
                along_z(turn, h).wait_send()

        @pl.when(turn < groups - 1)
        def _():
            exchange(turn, True).wait_recv()
            exchange(turn).wait_send()

        return carry

    lax.fori_loop(0, groups, clear, 0)
    keep.wait()


def scatter_mixer(one, mixed, dy, dxb, branch, gates, small, column):
    n, rows, _ = one.shape
    groups = n // INNER
    width = dy.shape[1]
    total = 3 * rows + gates.shape[1]
    kinds, _, _, units = column.shape
    turns = n.bit_length()
    dma = pltpu.SemaphoreType.DMA
    return pl.pallas_call(
        functools.partial(scatter_body, n),
        out_shape=(
            jax.ShapeDtypeStruct((total, width), F32),
            jax.ShapeDtypeStruct(small.shape, F32),
            jax.ShapeDtypeStruct((kinds, rows, groups * units), BF16),
        ),
        in_specs=[VMEM] * 7 + [ANY],
        out_specs=(VMEM, VMEM, ANY),
        scratch_shapes=[
            pltpu.VMEM((n, total, width), BF16),
            pltpu.VMEM((2, groups, 2, total, width // 2), BF16),
            pltpu.VMEM((2, groups, total, width // 2), BF16),
            pltpu.VMEM((2, groups, total, width // 2), BF16),
            pltpu.VMEM((turns,) + small.shape, F32),
            dma((2, groups, 2)),
            dma((2, groups, 2)),
            dma((2, groups)),
            dma((2, groups)),
            dma((2, groups)),
            dma((2, groups)),
            dma((turns,)),
            dma((turns,)),
            dma((groups,)),
            dma((groups,)),
            dma(()),
        ],
        compiler_params=params(2, 62),
        name="scatter_mixer",
    )(one, mixed, dy, dxb, branch, gates, small, column)


GELU_A = 0.7978845608028654
GELU_B = 0.044715


def gelu_parts(v):
    t = jnp.tanh(GELU_A * (v + GELU_B * v * v * v))
    value = 0.5 * v * (1.0 + t)
    slope = 0.5 * (1.0 + t) + 0.5 * v * (1.0 - t * t) * GELU_A * (1.0 + 3.0 * GELU_B * v * v)
    return value, slope


def gates_of(conv_low, gate_ref, par_ref, head, cols, first):
    pre_x = jnp.dot(conv_low, gate_ref[0, head], preferred_element_type=F32)
    pre_a = jnp.dot(conv_low, gate_ref[1, head], preferred_element_type=F32)
    gate_x = jax.nn.sigmoid(pre_x + par_ref[5:6, cols])
    gate_a = jax.nn.sigmoid(pre_a + par_ref[6:7, cols])
    decay = jnp.exp(-8.0 * gate_a * par_ref[8:9, cols])
    room = 1.0 - decay * decay
    mult = jnp.where(first, 1.0, jnp.sqrt(jnp.maximum(room, 0.001)))
    return gate_x, gate_a, decay, room, mult


def first_row(tokens):
    row = lax.broadcasted_iota(jnp.int32, (tokens, 1), 0)
    return jnp.logical_and(row == 0, lax.axis_index("seq") == 0)


def forward_body(
    n,
    xb_ref,
    yp_ref,
    gate_ref,
    par_ref,
    column_ref,
    conv_ref,
    state_ref,
    branch_ref,
    edge_ref,
    near_ref,
    wide,
    tail,
    fade,
    mine,
    theirs,
    *sems,
):
    send_tail, recv_tail, send_tot, recv_tot, send_f, recv_f = sems
    tokens, width = xb_ref.shape
    me = lax.axis_index("seq")
    size = gate_ref.shape[2]
    greet_all(n, me)
    tail_copy = remote(
        xb_ref.at[pl.ds(tokens - 16, 16)], tail, send_tail, recv_tail, lax.rem(me + 1, n)
    )
    pl.when(me + 1 < n)(tail_copy.start)
    _, _, by_x, by_y, _ = whereabouts()
    part = column_ref.shape[1] // 2
    hosted = [
        remote(
            column_ref.at[:, pl.ds(h * part, part)],
            near_ref.at[h],
            send_f.at[h],
            recv_f.at[h],
            (by_x, by_y)[h],
        )
        for h in range(2)
    ]
    wide[8:] = xb_ref[...].astype(F32)

    @pl.when(me > 0)
    def _():
        tail_copy.wait_recv()
        wide[:8] = tail[...].astype(F32)[8:]

    @pl.when(me == 0)
    def _():
        wide[:8] = jnp.zeros((8, width), F32)

    pl.when(me + 1 < n)(tail_copy.wait_send)
    for copy in hosted:
        copy.start()
    edge_ref[:8] = wide[:8]
    first = first_row(tokens)
    for head in range(width // size):
        cols = slice(head * size, (head + 1) * size)
        conv = par_ref[4:5, cols]
        for tap in range(4):
            conv = conv + par_ref[tap : tap + 1, cols] * wide[8 - tap : 8 - tap + tokens, cols]
        conv_low = conv.astype(BF16)
        conv_ref[:, cols] = conv_low
        gate_x, _, decay, _, mult = gates_of(conv_low, gate_ref, par_ref, head, cols, first)
        fade[:, cols] = decay
        state_ref[:, cols] = conv_low.astype(F32) * gate_x * mult

    row = lax.broadcasted_iota(jnp.int32, (8, width), 0)

    def inside(at, carry):
        r = pl.ds(pl.multiple_of(at * 8, 8), 8)
        a, b = fade[r], state_ref[r]
        for by in (1, 2, 4):
            a_back = pltpu.roll(a, by, 0)
            b_back = pltpu.roll(b, by, 0)
            b = jnp.where(row >= by, a * b_back + b, b)
            a = jnp.where(row >= by, a * a_back, a)
        fade[r] = a
        state_ref[r] = b
        return a[7:8] * carry[0], a[7:8] * carry[1] + b[7:8]

    ones, zeros = jnp.ones((1, width), F32), jnp.zeros((1, width), F32)
    tot_a, tot_b = lax.fori_loop(0, tokens // 8, inside, (ones, zeros))
    mine[...] = jnp.where(row == 0, tot_a, tot_b)

    def told(place):
        return remote(mine, theirs.at[me], send_tot.at[place], recv_tot.at[me], place)

    def heard(place):
        return remote(mine, theirs.at[place], send_tot.at[place], recv_tot.at[place], place)

    def tell(place, carry):
        told(place).start()
        return carry

    lax.fori_loop(me + 1, n, tell, 0)

    def hear(place, state):
        heard(place).wait_recv()
        return theirs[place, 0:1] * state + theirs[place, 1:2]

    carry_in = lax.fori_loop(0, me, hear, zeros)
    edge_ref[8:] = jnp.broadcast_to(carry_in, (8, width))

    def finish(at, carry):
        r = pl.ds(pl.multiple_of(at * 16, 16), 16)
        a, b = fade[r], state_ref[r]
        top = b[:8] + a[:8] * carry
        low = b[8:] + a[8:] * top[7:8]
        states = jnp.concatenate([top, low], axis=0)
        state_ref[r] = states
        branch_ref[r] = (states * gelu_parts(yp_ref[r])[0]).astype(BF16)
        return low[7:8]

    lax.fori_loop(0, tokens // 16, finish, carry_in)

    def sent(place, carry):
        told(place).wait_send()
        return carry

    lax.fori_loop(me + 1, n, sent, 0)
    for copy in hosted:
        copy.wait()


def mixer_forward(x_branch, y_pre, gates, par, column):
    n = lax.axis_size("seq")
    tokens, width = x_branch.shape
    kinds, groups, rows, units = column.shape
    dma = pltpu.SemaphoreType.DMA
    return pl.pallas_call(
        functools.partial(forward_body, n),
        out_shape=(
            jax.ShapeDtypeStruct((tokens, width), BF16),
            jax.ShapeDtypeStruct((tokens, width), F32),
            jax.ShapeDtypeStruct((tokens, width), BF16),
            jax.ShapeDtypeStruct((16, width), F32),
            jax.ShapeDtypeStruct((2, kinds, groups // 2, rows, units), column.dtype),
        ),
        in_specs=[VMEM] * 4 + [ANY],
        out_specs=(VMEM,) * 4 + (ANY,),
        scratch_shapes=[
            pltpu.VMEM((tokens + 8, width), F32),
            pltpu.VMEM((16, width), BF16),
            pltpu.VMEM((tokens, width), F32),
            pltpu.VMEM((8, width), F32),
            pltpu.VMEM((n, 8, width), F32),
            dma(()),
            dma(()),
            dma((n,)),
            dma((n,)),
            dma((2,)),
            dma((2,)),
        ],
        compiler_params=params(4, 40),
        name="mixer_forward",
    )(x_branch, y_pre, gates, par, column)


def backward_body(
    n,
    grad_ref,
    yp_ref,
    state_ref,
    edge_ref,
    conv_ref,
    xb_ref,
    gate_ref,
    par_ref,
    half_ref,
    dy_ref,
    dxb_ref,
    dgate_ref,
    dpar_ref,
    near_ref,
    fade,
    shift,
    adj,
    gate_x_s,
    gate_a_s,
    dconv,
    wide,
    mine,
    theirs,
    head_rows,
    *sems,
):
    send_rows, recv_rows, send_tot, recv_tot, send_f, recv_f = sems
    tokens, width = xb_ref.shape
    me = lax.axis_index("seq")
    size = gate_ref.shape[2]
    greet_all(n, me)
    _, _, by_x, by_y, _ = whereabouts()
    hosted = [
        remote(half_ref.at[h], near_ref.at[h], send_f.at[h], recv_f.at[h], (by_x, by_y)[h])
        for h in range(2)
    ]
    for copy in hosted:
        copy.start()
    first = first_row(tokens)
    fade[tokens:] = jnp.ones((8, width), F32)
    for head in range(width // size):
        cols = slice(head * size, (head + 1) * size)
        gate_x, gate_a, decay, _, _ = gates_of(conv_ref[:, cols], gate_ref, par_ref, head, cols, first)
        gate_x_s[:, cols] = gate_x
        gate_a_s[:, cols] = gate_a
        fade[:tokens, cols] = decay
        value, slope = gelu_parts(yp_ref[:, cols])
        grad = grad_ref[:, cols]
        dy_ref[:, cols] = (grad * state_ref[:, cols] * slope).astype(BF16)
        adj[:, cols] = grad * value
        shift[:, cols] = fade[1 : tokens + 1, cols]

    row = lax.broadcasted_iota(jnp.int32, (8, width), 0)
    tiles = tokens // 8

    def inside(turn, carry):
        r = pl.ds(pl.multiple_of((tiles - 1 - turn) * 8, 8), 8)
        a, b = shift[r], adj[r]
        for by in (1, 2, 4):
            a_next = pltpu.roll(a, 8 - by, 0)
            b_next = pltpu.roll(b, 8 - by, 0)
            b = jnp.where(row < 8 - by, a * b_next + b, b)
            a = jnp.where(row < 8 - by, a * a_next, a)
        shift[r] = a
        adj[r] = b
        return a[0:1] * carry[0], a[0:1] * carry[1] + b[0:1]

    ones, zeros = jnp.ones((1, width), F32), jnp.zeros((1, width), F32)
    tot_a, tot_b = lax.fori_loop(0, tiles, inside, (ones, zeros))
    first_fade = fade[0:1]
    mine[...] = jnp.where(row == 0, first_fade * tot_a, first_fade * tot_b)

    def told(place):
        return remote(mine, theirs.at[me], send_tot.at[place], recv_tot.at[me], place)

    def heard(place):
        return remote(mine, theirs.at[place], send_tot.at[place], recv_tot.at[place], place)

    def tell(place, carry):
        told(place).start()
        return carry

    lax.fori_loop(0, me, tell, 0)

    def hear(turn, state):
        place = n - 1 - turn
        heard(place).wait_recv()
        return theirs[place, 0:1] * state + theirs[place, 1:2]

    carry_in = lax.fori_loop(0, n - 1 - me, hear, zeros)

    def finish(turn, carry):
        r = pl.ds(pl.multiple_of((tiles - 1 - turn) * 8, 8), 8)
        value = adj[r] + shift[r] * carry
        adj[r] = value
        return value[0:1]

    lax.fori_loop(0, tiles, finish, carry_in)

    wide[:8] = edge_ref[:8]
    wide[8:] = xb_ref[...].astype(F32)
    at_first = lax.broadcasted_iota(jnp.int32, (tokens, 1), 0) == 0
    for head in range(width // size):
        cols = slice(head * size, (head + 1) * size)
        conv_low = conv_ref[:, cols]
        conv = conv_low.astype(F32)
        gate_x, gate_a, decay = gate_x_s[:, cols], gate_a_s[:, cols], fade[:tokens, cols]
        room = 1.0 - decay * decay
        mult = jnp.where(first, 1.0, jnp.sqrt(jnp.maximum(room, 0.001)))
        back = adj[:, cols]
        before = jnp.where(at_first, edge_ref[8:9, cols], pltpu.roll(state_ref[:, cols], 1, 0))
        d_mult = back * conv * gate_x
        moves = jnp.logical_and(room > 0.001, jnp.logical_not(first))
        d_decay = back * before - jnp.where(moves, d_mult * decay / mult, 0.0)
        d_log = d_decay * decay
        d_pre_x = back * conv * mult * gate_x * (1.0 - gate_x)
        d_pre_a = d_log * (-8.0 * par_ref[8:9, cols]) * gate_a * (1.0 - gate_a)
        dpar_ref[5:6, cols] = jnp.sum(d_pre_x, axis=0, keepdims=True)
        dpar_ref[6:7, cols] = jnp.sum(d_pre_a, axis=0, keepdims=True)
        dpar_ref[7:8, cols] = (
            jnp.sum(d_log * (-8.0 * gate_a), axis=0, keepdims=True) * par_ref[9:10, cols]
        )
        low_x, low_a = d_pre_x.astype(BF16), d_pre_a.astype(BF16)
        flipped = (((1,), (1,)), ((), ()))
        d_conv = (
            back * gate_x * mult
            + lax.dot_general(low_x, gate_ref[0, head], flipped, preferred_element_type=F32)
            + lax.dot_general(low_a, gate_ref[1, head], flipped, preferred_element_type=F32)
        )
        dconv[:tokens, cols] = d_conv
        over_rows = (((0,), (0,)), ((), ()))
        dgate_ref[0, head] = lax.dot_general(
            conv_low, low_x, over_rows, preferred_element_type=F32
        ).astype(BF16)
        dgate_ref[1, head] = lax.dot_general(
            conv_low, low_a, over_rows, preferred_element_type=F32
        ).astype(BF16)
        dpar_ref[4:5, cols] = jnp.sum(d_conv, axis=0, keepdims=True)
        for tap in range(4):
            dpar_ref[tap : tap + 1, cols] = jnp.sum(
                d_conv * wide[8 - tap : 8 - tap + tokens, cols], axis=0, keepdims=True
            )

    rows_copy = remote(
        dconv.at[pl.ds(0, 8)], head_rows, send_rows, recv_rows, lax.rem(me + n - 1, n)
    )
    pl.when(me > 0)(rows_copy.start)

    @pl.when(me + 1 < n)
    def _():
        rows_copy.wait_recv()
        dconv[tokens:] = head_rows[...]

    @pl.when(me + 1 == n)
    def _():
        dconv[tokens:] = jnp.zeros((8, width), F32)

    for head in range(width // size):
        cols = slice(head * size, (head + 1) * size)
        total = par_ref[0:1, cols] * dconv[:tokens, cols]
        for tap in range(1, 4):
            total = total + par_ref[tap : tap + 1, cols] * dconv[tap : tap + tokens, cols]
        dxb_ref[:, cols] = total.astype(BF16)

    pl.when(me > 0)(rows_copy.wait_send)

    def sent(place, carry):
        told(place).wait_send()
        return carry

    lax.fori_loop(0, me, sent, 0)
    for copy in hosted:
        copy.wait()


def mixer_backward(grad, y_pre, states, edge, conv, x_branch, gates, par, halves):
    n = lax.axis_size("seq")
    tokens, width = x_branch.shape
    dma = pltpu.SemaphoreType.DMA
    whole = pltpu.VMEM((tokens, width), F32)
    longer = pltpu.VMEM((tokens + 8, width), F32)
    return pl.pallas_call(
        functools.partial(backward_body, n),
        out_shape=(
            jax.ShapeDtypeStruct((tokens, width), BF16),
            jax.ShapeDtypeStruct((tokens, width), BF16),
            jax.ShapeDtypeStruct(gates.shape, BF16),
            jax.ShapeDtypeStruct((8, width), F32),
            jax.ShapeDtypeStruct(halves.shape, BF16),
        ),
        in_specs=[VMEM] * 8 + [ANY],
        out_specs=(VMEM,) * 4 + (ANY,),
        scratch_shapes=[
            longer,
            whole,
            whole,
            whole,
            whole,
            longer,
            longer,
            pltpu.VMEM((8, width), F32),
            pltpu.VMEM((n, 8, width), F32),
            pltpu.VMEM((8, width), F32),
            dma(()),
            dma(()),
            dma((n,)),
            dma((n,)),
            dma((2,)),
            dma((2,)),
        ],
        compiler_params=params(5, 48),
        name="mixer_backward",
    )(grad, y_pre, states, edge, conv, x_branch, gates, par, halves)


def my_half(values):
    half = values.shape[0] // 2
    return lax.dynamic_slice_in_dim(values, lax.axis_index("ch") * half, half, 0)


def join(own):
    other = swap(own, "ch", 1)
    core = lax.axis_index("ch")
    return jnp.concatenate(
        [jnp.where(core == 0, own, other), jnp.where(core == 0, other, own)], axis=0
    )


def half_sum(partial):
    core = lax.axis_index("ch")
    parts = partial.reshape((2, partial.shape[0] // 2) + partial.shape[1:])
    theirs = swap(pick(parts, 1 - core), "ch", 1)
    return pick(parts, core).astype(F32) + theirs.astype(F32)


def tokens_out(partial, half):
    width = partial.shape[1]
    groups = lax.axis_size("seq") // INNER
    outer = lax.axis_index("seq") // INNER
    core = lax.axis_index("ch")
    parts = partial.reshape(groups, 2, half, width)
    theirs = pick(parts, 1 - core, 1).astype(BF16)
    summed = (pick(parts, core, 1).astype(F32) + swap(theirs, "ch", 1).astype(F32)).astype(BF16)
    total = pick(summed, outer).astype(F32)
    for step in range(1, groups):
        total = total + swap(pick(summed, outer ^ step), "seq", step * INNER).astype(F32)
    return total


def gate_rows(blocks, n):
    _, heads, depth, size = blocks.shape
    part = depth // n
    rows = 2 * part
    split = blocks.reshape(2, heads, n, part, size).transpose(2, 0, 1, 3, 4)
    return split.reshape(n, 2, rows, heads * size // 2).transpose(0, 2, 1, 3).reshape(n, rows, heads * size)


def gate_blocks(rows, heads, size):
    n, count, width = rows.shape
    split = rows.reshape(n, count, 2, width // 2).transpose(0, 2, 1, 3)
    part = count * width // (2 * heads * size)
    return split.reshape(n, 2, heads, part, size).transpose(1, 2, 0, 3, 4).reshape(2, heads, n * part, size)


def shards(
    inputs,
    norm_gain,
    branch_weight,
    input_weight,
    channel_params,
    gate_x_blocks,
    gate_a_blocks,
    out_weight,
    ffn_gain,
    ffn_gate,
    ffn_up,
    ffn_down,
    cotangent,
):
    f32 = F32
    bf16 = BF16
    n = lax.axis_size("seq")
    tok_rows, model = inputs.shape
    half_rows = tok_rows // 2
    heads, part, size = gate_x_blocks.shape
    width = heads * size
    depth = ffn_gate.shape[0]
    groups = n // INNER
    hidden_units = ffn_gate.shape[1]
    units = -(-hidden_units // (groups * 128)) * 128
    x_float = inputs.astype(f32)
    n_one = scaled_norm(x_float, norm_gain).astype(bf16)
    x_half = my_half(inputs).astype(f32)
    _, norm_back_one = jax.vjp(scaled_norm, x_half, norm_gain)

    gate_pack = gate_rows(jnp.stack([gate_x_blocks, gate_a_blocks]), 1)[0]
    ffn_pack = jnp.pad(
        jnp.stack([ffn_gate, ffn_up, ffn_down.T]), ((0, 0), (0, 0), (0, groups * units - hidden_units))
    )
    *full_mixer, full_gates, column = gather_weights(
        [branch_weight, input_weight, out_weight.T], gate_pack, ffn_pack
    )
    full_branch, full_input, full_out = (w.reshape(model, width) for w in full_mixer)
    gates = gate_blocks(full_gates, heads, size)
    par = jnp.concatenate(
        [
            channel_params,
            jax.nn.softplus(channel_params[7:8]),
            jax.nn.sigmoid(channel_params[7:8]),
            jnp.zeros((6, width), f32),
        ],
        axis=0,
    )

    cot_half = my_half(cotangent)

    x_branch = jnp.dot(n_one, full_input, preferred_element_type=f32).astype(bf16)
    y_pre = jnp.dot(n_one, full_branch, preferred_element_type=f32)
    conv_out, states, branch_out, edge, near = mixer_forward(x_branch, y_pre, gates, par, column)
    mixed = half_sum(jnp.einsum("tw,dw->td", branch_out, full_out, preferred_element_type=f32))
    resid = x_half + mixed
    n_two_f, norm_back_two = jax.vjp(scaled_norm, resid, ffn_gain)
    all_two, all_cot, *full_ffn = gather_tokens(n_two_f.astype(bf16), cot_half, column, near)
    all_two, all_cot = (v.reshape(groups * tok_rows, model) for v in (all_two, all_cot))
    full_ffn = [w.reshape(model, units) for w in full_ffn]
    gate_pre = jnp.dot(all_two, full_ffn[0], preferred_element_type=f32)
    up_pre = jnp.dot(all_two, full_ffn[1], preferred_element_type=f32)
    gate_act, gelu_back_gate = jax.vjp(gelu_tanh, gate_pre)
    hidden = (gate_act * up_pre).astype(bf16)
    ffn_term = jnp.einsum("tf,df->td", hidden, full_ffn[2], preferred_element_type=f32).astype(bf16)
    d_hidden = jnp.einsum("td,df->tf", all_cot, full_ffn[2], preferred_element_type=f32)
    d_gate = gelu_back_gate(d_hidden * up_pre)[0].astype(bf16)
    d_up = (d_hidden * gate_act).astype(bf16)
    d_n_two = (
        jnp.einsum("tf,df->td", d_gate, full_ffn[0], preferred_element_type=f32)
        + jnp.einsum("tf,df->td", d_up, full_ffn[1], preferred_element_type=f32)
    ).astype(bf16)
    terms = [
        jnp.einsum("td,tf->df", left, right, preferred_element_type=f32)
        .astype(bf16)
        .reshape(groups, INNER, depth, units)
        for left, right in ((all_two, d_gate), (all_two, d_up), (all_cot, hidden))
    ]
    split = [v.reshape(groups, 2, half_rows, model) for v in (d_n_two, ffn_term)]
    if groups <= 4:
        d_n_two, ffn_out, far = reduce_tokens(split, terms)
    else:
        d_n_two, far = reduce_tokens(split[:1], terms)
        ffn_out = tokens_out(ffn_term, half_rows)
    block_out = join((resid + ffn_out).astype(bf16))
    inner = lax.axis_index("seq") % INNER
    by_half = [t.reshape(2, groups // 2, INNER, depth, units) for t in terms]

    def block_at(h, place):
        return jnp.stack([pick(t[h], place, 1) for t in by_half]).astype(f32)

    halves = jnp.stack(
        [(block_at(h, inner ^ (1, 2)[h]) + far[h, 1].astype(f32)).astype(bf16) for h in range(2)]
    )
    d_resid_norm, d_ffn_gain_term = norm_back_two(d_n_two)
    d_resid = cot_half.astype(f32) + d_resid_norm
    d_mixed = join(d_resid.astype(bf16))
    d_branch_out = jnp.einsum("td,dw->tw", d_mixed, full_out, preferred_element_type=f32)
    d_y, d_xb, d_gates, d_channel_term, near_back = mixer_backward(
        d_branch_out, y_pre, states, edge, conv_out, x_branch, gates, par, halves
    )
    column_back = jnp.concatenate(
        [
            (block_at(h, inner) + far[h, 0].astype(f32) + near_back[h].astype(f32)).astype(bf16)
            for h in range(2)
        ],
        axis=1,
    )
    d_n_one = half_sum(
        (
            jnp.einsum("tw,dw->td", d_y, full_branch, preferred_element_type=f32)
            + jnp.einsum("tw,dw->td", d_xb, full_input, preferred_element_type=f32)
        ).astype(bf16)
    )
    d_x_norm, d_norm_gain_term = norm_back_one(d_n_one)
    d_inputs = join(d_resid + d_x_norm)
    small_terms = jnp.concatenate(
        [
            d_channel_term,
            d_norm_gain_term.reshape(-1, width),
            d_ffn_gain_term.reshape(-1, width),
            jnp.zeros((8 - 2 * (model // width), width), f32),
        ],
        axis=0,
    )
    gain_rows = model // width
    scattered, small, spread = scatter_mixer(
        n_one.T.reshape(n, depth, tok_rows),
        d_mixed.T.reshape(n, depth, tok_rows),
        d_y,
        d_xb,
        branch_out,
        gate_rows(d_gates, n),
        small_terms,
        column_back,
    )
    ffn_grads = [spread[kind, :, :hidden_units].astype(f32) for kind in range(3)]
    d_gate_pair = gate_blocks(scattered[None, 3 * depth :], heads, size)
    return (
        block_out,
        d_inputs,
        small[8 : 8 + gain_rows].reshape(model),
        scattered[:depth],
        scattered[depth : 2 * depth],
        small[:8],
        d_gate_pair[0],
        d_gate_pair[1],
        scattered[2 * depth : 3 * depth].T,
        small[8 + gain_rows : 8 + 2 * gain_rows].reshape(model),
        ffn_grads[0],
        ffn_grads[1],
        ffn_grads[2].T,
    )


def solution(mesh):
    placed = (
        P("seq", None),
        P(),
        P("seq", "ch"),
        P("seq", "ch"),
        P(None, "ch"),
        P("ch", "seq", None),
        P("ch", "seq", None),
        P("ch", "seq"),
        P(),
        P("seq", "ch"),
        P("seq", "ch"),
        P("ch", "seq"),
        P("seq", None),
    )
    return jax.shard_map(
        shards,
        mesh=mesh,
        in_specs=placed,
        out_specs=(
            P("seq", None),
            P("seq", None),
            P(),
            P("seq", "ch"),
            P("seq", "ch"),
            P(None, "ch"),
            P("ch", "seq", None),
            P("ch", "seq", None),
            P("ch", "seq"),
            P(),
            P("seq", "ch"),
            P("seq", "ch"),
            P("ch", "seq"),
        ),
        check_vma=False,
    )
```

```python
import functools

import jax
import jax.numpy as jnp
from jax import lax
from jax.experimental import pallas as pl
from jax.experimental.pallas import tpu as pltpu
from jax.sharding import PartitionSpec as P

F32 = jnp.float32
BF16 = jnp.bfloat16
INNER = 4
MESH = pl.DeviceIdType.MESH
VMEM = pl.BlockSpec(memory_space=pltpu.VMEM)
ANY = pl.BlockSpec(memory_space=pl.ANY)
HBM = pl.BlockSpec(memory_space=pltpu.HBM)


def swap(value, axis, mask):
    return lax.ppermute(value, axis, [(i, i ^ mask) for i in range(lax.axis_size(axis))])


def pick(array, index, axis=0):
    return lax.dynamic_index_in_dim(array, index, axis, False)


def put(array, block, index, axis=0):
    return lax.dynamic_update_index_in_dim(array, block, index, axis)


def scaled_norm(values, gain):
    return values * lax.rsqrt(jnp.mean(values * values, axis=-1, keepdims=True) + 1e-06) * gain


def gelu_tanh(values):
    return jax.nn.gelu(values, approximate=True)


def whereabouts():
    me = lax.axis_index("seq")
    outer = me // INNER
    inner = me - outer * INNER
    y = inner // 2
    x = inner - 2 * y
    by_x = me + 1 - 2 * x
    by_y = me + 2 - 4 * y
    return me, outer, by_x, by_y, by_x + 2 - 4 * y


def when(condition, action):
    if condition is None:
        action()
    else:
        pl.when(condition)(action)


def both(one, other):
    if one is None or other is None:
        return one if other is None else other
    return jnp.logical_and(one, other)


def greet(peers):
    barrier = pltpu.get_barrier_semaphore()
    for condition, peer in peers:
        when(
            condition,
            lambda peer=peer: pl.semaphore_signal(
                barrier, inc=1, device_id={"seq": peer}, device_id_type=MESH
            ),
        )
    count = 0
    for condition, _ in peers:
        count = count + (1 if condition is None else condition.astype(jnp.int32))
    pl.semaphore_wait(barrier, count)


def greet_all(n, me, sibling=False):
    barrier = pltpu.get_barrier_semaphore()

    def hello(step, carry):
        pl.semaphore_signal(
            barrier, inc=1, device_id={"seq": lax.rem(me + step, n)}, device_id_type=MESH
        )
        return carry

    lax.fori_loop(1, n, hello, 0)
    if sibling:
        pl.semaphore_signal(
            barrier, inc=1, device_id={"ch": 1 - lax.axis_index("ch")}, device_id_type=MESH
        )
    pl.semaphore_wait(barrier, n if sibling else n - 1)


def remote(src, dst, send_sem, recv_sem, place):
    return pltpu.make_async_remote_copy(
        src_ref=src,
        dst_ref=dst,
        send_sem=send_sem,
        recv_sem=recv_sem,
        device_id={"seq": place},
        device_id_type=MESH,
    )


def params(collective_id, mib):
    return pltpu.CompilerParams(
        collective_id=collective_id, has_side_effects=True, vmem_limit_bytes=mib * 2**20
    )


def gather_body(n, *refs):
    w_refs, g_ref, f_ref = refs[:3], refs[3], refs[4]
    wo_refs, go_ref, column_ref = refs[5:8], refs[8], refs[9]
    send_m, recv_m, send_f, recv_f, here = refs[10:]
    groups = n // INNER
    me, outer, by_x, by_y, by_xy = whereabouts()
    above, below = outer + 1 < groups, outer > 0
    barrier = pltpu.get_barrier_semaphore()

    def hello(peer):
        pl.semaphore_signal(barrier, inc=1, device_id={"seq": peer}, device_id_type=MESH)

    hello(by_x)
    hello(by_y)

    def column_peer(turn):
        return lax.rem(outer + turn, groups)

    def hello_column(turn, carry):
        hello(me + (column_peer(turn) - outer) * INNER)
        return carry

    lax.fori_loop(1, groups, hello_column, 0)
    pl.semaphore_wait(barrier, groups + 1)
    units = column_ref.shape[3]
    half = w_refs[0].shape[1] // 2

    def units_of(place):
        return pl.ds(pl.multiple_of(place * units, units), units)

    keep = [
        pltpu.make_async_copy(w_refs[kind], wo_refs[kind].at[me], here.at[kind])
        for kind in range(3)
    ]
    keep.append(pltpu.make_async_copy(g_ref, go_ref.at[:, :, me], here.at[3]))
    keep.append(
        pltpu.make_async_copy(
            f_ref.at[:, :, units_of(outer)], column_ref.at[:, outer], here.at[4]
        )
    )
    for copy in keep:
        copy.start()
    sent = []

    def copies(h, source, way, target, own):
        cols = pl.ds(h * half, half)
        pairs = [
            (w_refs[kind].at[:, cols], wo_refs[kind].at[source, :, cols]) for kind in range(3)
        ]
        pairs.append((g_ref.at[h], go_ref.at[h, :, source]))
        return [
            remote(
                given if own else dst,
                dst,
                send_m.at[kind, h, source, way],
                recv_m.at[kind, h, source],
                target,
            )
            for kind, (given, dst) in enumerate(pairs)
        ]

    def send(condition, *what):
        def go():
            for copy in copies(*what):
                copy.start()

        when(condition, go)
        sent.append((condition, what))

    def arrive(condition, h, source):
        def go():
            for copy in copies(h, source, 0, by_x, False):
                copy.wait_recv()

        when(condition, go)

    def exchange(turn, receive):
        place = lax.rem(outer + groups - turn, groups) if receive else column_peer(turn)
        target = me + (place - outer) * INNER
        return remote(
            f_ref.at[:, :, units_of(place)],
            column_ref.at[:, place if receive else outer],
            send_f.at[turn],
            recv_f.at[turn],
            target,
        )

    def each_turn(action):
        def one(turn, carry):
            action(turn)
            return carry

        lax.fori_loop(1, groups, one, 0)

    for step in range(groups):
        for h in range(2):
            flip_p, flip_q = (by_x, by_y) if h == 0 else (by_y, by_x)
            if step == 0:
                send(above, h, me, 0, me + INNER, True)
                send(below, h, me, 1, me - INNER, True)
                send(None, h, me, 2, flip_p, True)
                send(None, h, me, 3, flip_q, True)
                continue
            for source, there, onward, way, to in (
                (me - step * INNER, outer >= step, above, 0, me + INNER),
                (me + step * INNER, outer + step < groups, below, 1, me - INNER),
            ):
                arrive(there, h, source)
                send(both(there, onward), h, source, way, to, False)
                send(there, h, source, 2, flip_p, False)
                send(there, h, source, 3, flip_q, False)
    each_turn(lambda turn: exchange(turn, False).start())
    for step in range(groups):
        for h in range(2):
            flip_p, flip_q = (by_x, by_y) if h == 0 else (by_y, by_x)
            if step == 0:
                arrive(None, h, flip_p)
                send(None, h, flip_p, 3, flip_q, False)
                continue
            for source, there in (
                (flip_p - step * INNER, outer >= step),
                (flip_p + step * INNER, outer + step < groups),
            ):
                arrive(there, h, source)
                send(there, h, source, 3, flip_q, False)
    for place in range(groups):
        shift = (place - outer) * INNER
        for h in range(2):
            arrive(None, h, (by_y if h == 0 else by_x) + shift)
            arrive(None, h, by_xy + shift)
    each_turn(lambda turn: exchange(turn, True).wait_recv())
    for condition, what in sent:

        def finish(what=what):
            for copy in copies(*what):
                copy.wait_send()

        when(condition, finish)
    each_turn(lambda turn: exchange(turn, False).wait_send())
    for copy in keep:
        copy.wait()


def gather_weights(weights, gates, ffn):
    n = lax.axis_size("seq")
    groups = n // INNER
    kinds, rows, padded = ffn.shape
    dma = pltpu.SemaphoreType.DMA
    made = [jax.ShapeDtypeStruct((n,) + w.shape, w.dtype) for w in weights]
    made.append(jax.ShapeDtypeStruct(gates.shape[:2] + (n,) + gates.shape[2:], gates.dtype))
    made.append(jax.ShapeDtypeStruct((kinds, groups, rows, padded // groups), ffn.dtype))
    return pl.pallas_call(
        functools.partial(gather_body, n),
        out_shape=tuple(made),
        in_specs=[ANY] * 5,
        out_specs=(ANY,) * 5,
        scratch_shapes=[
            dma((4, 2, n, 4)),
            dma((4, 2, n)),
            dma((groups,)),
            dma((groups,)),
            dma((5,)),
        ],
        compiler_params=params(1, 16),
        name="gather_weights",
    )(*weights, gates, ffn)


class Chain:
    def __init__(self, n, own, whole, send, recv_z, recv_c):
        me = lax.axis_index("seq")
        self.groups = n // INNER
        self.outer = outer = me // INNER
        self.core = lax.axis_index("ch")
        self.above, self.below = outer + 1 < self.groups, outer > 0
        self.sibling = {"ch": 1 - self.core}
        self.to = ({"seq": me + INNER}, {"seq": me - INNER}, self.sibling)
        self.own, self.whole = own, whole
        self.send, self.recv_z, self.recv_c = send, recv_z, recv_c

    def copy(self, source, way, own=False):
        dst = self.whole.at[source, self.core]
        return pltpu.make_async_remote_copy(
            src_ref=self.own if own else dst,
            dst_ref=dst,
            send_sem=self.send.at[source, way],
            recv_sem=(self.recv_c if way == 2 else self.recv_z).at[source],
            device_id=self.to[way],
            device_id_type=MESH,
        )

    def from_sibling(self, source):
        return pltpu.make_async_remote_copy(
            src_ref=self.own,
            dst_ref=self.whole.at[source, 1 - self.core],
            send_sem=self.send.at[source, 2],
            recv_sem=self.recv_c.at[source],
            device_id=self.sibling,
            device_id_type=MESH,
        )

    def keep(self, sem):
        return pltpu.make_async_copy(self.own, self.whole.at[self.outer, self.core], sem)

    def ways(self, step):
        return (
            (self.outer - step, self.outer >= step, self.above, 0),
            (self.outer + step, self.outer + step < self.groups, self.below, 1),
        )

    def start(self):
        pl.when(self.above)(self.copy(self.outer, 0, True).start)
        pl.when(self.below)(self.copy(self.outer, 1, True).start)
        self.copy(self.outer, 2, True).start()

    def step(self, step):
        for source, there, onward, way in self.ways(step):
            pl.when(there)(self.copy(source, way).wait_recv)
            pl.when(both(there, onward))(self.copy(source, way).start)
            pl.when(there)(self.copy(source, 2).start)

    def finish(self):
        for source in range(self.groups):
            self.from_sibling(source).wait_recv()
        pl.when(self.above)(self.copy(self.outer, 0, True).wait_send)
        pl.when(self.below)(self.copy(self.outer, 1, True).wait_send)
        self.copy(self.outer, 2, True).wait_send()
        for step in range(1, self.groups):
            for source, there, onward, way in self.ways(step):
                pl.when(both(there, onward))(self.copy(source, way).wait_send)
                pl.when(there)(self.copy(source, 2).wait_send)


def chain_semaphores(groups):
    dma = pltpu.SemaphoreType.DMA
    return [dma((groups, 3)), dma((groups,)), dma((groups,))]


def tokens_body(n, *refs):
    own_ref, column_ref, near_ref = refs[:3]
    all_ref, w_refs = refs[3], refs[4:7]
    send_t, recv_z, recv_c, send_w, recv_w, here = refs[7:]
    groups = n // INNER
    half = groups // 2
    me, outer, by_x, by_y, by_xy = whereabouts()
    base = outer * INNER
    core = lax.axis_index("ch")
    above, below = outer + 1 < groups, outer > 0
    sibling = {"ch": 1 - core}
    barrier = pltpu.get_barrier_semaphore()

    def hello(peer):
        pl.semaphore_signal(barrier, inc=1, device_id=peer, device_id_type=MESH)

    hello({"seq": by_x})
    hello({"seq": by_y})
    hello(sibling)
    pl.when(above)(lambda: hello({"seq": me + INNER}))
    pl.when(below)(lambda: hello({"seq": me - INNER}))
    pl.semaphore_wait(barrier, 3 + above.astype(jnp.int32) + below.astype(jnp.int32))

    chain = Chain(n, own_ref, all_ref, send_t, recv_z, recv_c)

    def part(h):
        return pl.ds(h * half, half)

    flips = ((by_x, by_y), (by_y, by_x))

    def weight_copy(kind, h, far, receive=False):
        source = flips[h][0] if far else me
        if receive:
            source = by_xy if far else flips[h][1]
        return remote(
            near_ref.at[h, kind] if far else column_ref.at[kind, part(h)],
            w_refs[kind].at[part(h), source - base],
            send_w.at[kind, h, far],
            recv_w.at[kind, h, far],
            flips[h][1],
        )

    keep = [chain.keep(here.at[0])]
    for kind in range(3):
        keep.append(
            pltpu.make_async_copy(
                column_ref.at[kind], w_refs[kind].at[:, me - base], here.at[1 + kind]
            )
        )
        for h in range(2):
            keep.append(
                pltpu.make_async_copy(
                    near_ref.at[h, kind],
                    w_refs[kind].at[part(h), flips[h][0] - base],
                    here.at[4 + 2 * kind + h],
                )
            )
    every_w = [(kind, h, far) for kind in range(3) for h in range(2) for far in range(2)]

    chain.start()
    for what in every_w:
        weight_copy(*what).start()
    for copy in keep:
        copy.start()
    for step in range(1, groups):
        chain.step(step)
    for what in every_w:
        weight_copy(*what, receive=True).wait_recv()
    chain.finish()
    for what in every_w:
        weight_copy(*what).wait_send()
    for copy in keep:
        copy.wait()


def gather_tokens(tokens, column, near):
    n = lax.axis_size("seq")
    groups = n // INNER
    kinds, _, rows, units = column.shape
    dma = pltpu.SemaphoreType.DMA
    wide = jax.ShapeDtypeStruct((groups, 2) + tokens.shape, tokens.dtype)
    weight = jax.ShapeDtypeStruct((groups, INNER, rows, units), column.dtype)
    return pl.pallas_call(
        functools.partial(tokens_body, n),
        out_shape=(wide, weight, weight, weight),
        in_specs=[ANY] * 3,
        out_specs=(ANY,) * 4,
        scratch_shapes=chain_semaphores(groups)
        + [dma((kinds, 2, 2)), dma((kinds, 2, 2)), dma((10,))],
        compiler_params=params(6, 16),
        name="gather_tokens",
    )(tokens, column, near)


def reduce_body(n, kinds, *refs):
    p_refs, t_refs = refs[:kinds], refs[kinds : kinds + 3]
    out_refs, far_ref = refs[kinds + 3 : 2 * kinds + 3], refs[2 * kinds + 3]
    summed, got, send_c, recv_c, send_z, recv_z, send_f, recv_f = refs[2 * kinds + 4 :]
    groups = n // INNER
    half = groups // 2
    me, outer, by_x, by_y, by_xy = whereabouts()
    base = outer * INNER
    core = lax.axis_index("ch")
    above, below = outer + 1 < groups, outer > 0
    sibling = {"ch": 1 - core}
    barrier = pltpu.get_barrier_semaphore()

    def hello(peer):
        pl.semaphore_signal(barrier, inc=1, device_id=peer, device_id_type=MESH)

    hello({"seq": by_x})
    hello({"seq": by_y})
    hello(sibling)
    pl.when(above)(lambda: hello({"seq": me + INNER}))
    pl.when(below)(lambda: hello({"seq": me - INNER}))
    pl.semaphore_wait(barrier, 3 + above.astype(jnp.int32) + below.astype(jnp.int32))
    flips = ((by_x, by_y), (by_y, by_x))

    def gradient_copy(kind, h, far):
        source = by_xy if far else flips[h][1]
        return remote(
            t_refs[kind].at[pl.ds(h * half, half), source - base],
            far_ref.at[h, far, kind],
            send_f.at[kind, h, far],
            recv_f.at[kind, h, far],
            flips[h][1],
        )

    def to_sibling(kind, place):
        return pltpu.make_async_remote_copy(
            src_ref=p_refs[kind].at[place, 1 - core],
            dst_ref=summed.at[kind, place],
            send_sem=send_c.at[kind, place],
            recv_sem=recv_c.at[kind, place],
            device_id=sibling,
            device_id_type=MESH,
        )

    def along(kind, place, up):
        last = place == (outer + 1 if up else outer - 1)
        slot = place if up else jnp.where(last, groups, place)
        return remote(
            summed.at[kind, place],
            got.at[kind, slot],
            send_z.at[kind, place],
            recv_z.at[kind, slot],
            me + (INNER if up else -INNER),
        )

    def landed(kind, slot):
        return remote(
            summed.at[kind, 0], got.at[kind, slot], send_z.at[kind, 0], recv_z.at[kind, slot], by_x
        )

    def each(limit, action):
        def one(turn, carry):
            action(turn)
            return carry

        lax.fori_loop(0, limit, one, 0)

    every_f = [(kind, h, far) for far in (1, 0) for kind in range(3) for h in range(2)]
    for kind in range(kinds):
        each(groups, lambda place, kind=kind: to_sibling(kind, place).start())
    for what in every_f:
        gradient_copy(*what).start()

    tall = summed.shape[2]
    chunk = 16

    def rows_of(at):
        return pl.ds(pl.multiple_of(at * chunk, chunk), chunk)

    def ready(kind, place, incoming):
        to_sibling(kind, place).wait_recv()

        def local(at):
            r = rows_of(at)
            summed[kind, place, r] = (
                summed[kind, place, r].astype(F32) + p_refs[kind][place, core, r].astype(F32)
            ).astype(BF16)

        def more(at):
            r = rows_of(at)
            summed[kind, place, r] = (
                summed[kind, place, r].astype(F32)
                + p_refs[kind][place, core, r].astype(F32)
                + got[kind, place, r].astype(F32)
            ).astype(BF16)

        @pl.when(incoming)
        def _():
            landed(kind, place).wait_recv()
            each(tall // chunk, more)

        @pl.when(jnp.logical_not(incoming))
        def _():
            each(tall // chunk, local)

    for kind in range(kinds):

        def climb(turn, kind=kind):
            place = groups - 1 - turn

            @pl.when(place > outer)
            def _():
                ready(kind, place, below)
                along(kind, place, True).start()

        def sink(turn, kind=kind):
            place = turn

            @pl.when(place < outer)
            def _():
                ready(kind, place, above)
                along(kind, place, False).start()

        def turns(turn):
            @pl.when(outer < half)
            def _():
                climb(turn)
                sink(turn)

            @pl.when(outer >= half)
            def _():
                sink(turn)
                climb(turn)

        each(groups - 1, turns)
    for kind in range(kinds):
        to_sibling(kind, outer).wait_recv()

        def own(at, kind=kind):
            r = rows_of(at)
            out_refs[kind][r] = summed[kind, outer, r].astype(F32) + p_refs[kind][
                outer, core, r
            ].astype(F32)

        each(tall // chunk, own)
        for there, slot in ((below, outer), (above, groups)):

            @pl.when(there)
            def _():
                landed(kind, slot).wait_recv()

                def plus(at):
                    r = rows_of(at)
                    out_refs[kind][r] = out_refs[kind][r] + got[kind, slot, r].astype(F32)

                each(tall // chunk, plus)

    for kind in range(kinds):

        def clear(place, kind=kind):
            to_sibling(kind, place).wait_send()

            @pl.when(place > outer)
            def _():
                along(kind, place, True).wait_send()

            @pl.when(place < outer)
            def _():
                along(kind, place, False).wait_send()

        each(groups, clear)
    for what in every_f:
        gradient_copy(*what).wait()


def reduce_tokens(partials, gradients):
    n = lax.axis_size("seq")
    groups = n // INNER
    kinds = len(partials)
    _, _, tall, width = partials[0].shape
    _, _, rows, units = gradients[0].shape
    dma = pltpu.SemaphoreType.DMA
    return pl.pallas_call(
        functools.partial(reduce_body, n, kinds),
        out_shape=(jax.ShapeDtypeStruct((tall, width), F32),) * kinds
        + (jax.ShapeDtypeStruct((2, 2, 3, groups // 2, rows, units), BF16),),
        in_specs=[VMEM] * kinds + [ANY] * 3,
        out_specs=(VMEM,) * kinds + (ANY,),
        scratch_shapes=[
            pltpu.VMEM((kinds, groups, tall, width), BF16),
            pltpu.VMEM((kinds, groups + 1, tall, width), BF16),
            dma((kinds, groups)),
            dma((kinds, groups)),
            dma((kinds, groups)),
            dma((kinds, groups + 1)),
            dma((3, 2, 2)),
            dma((3, 2, 2)),
        ],
        compiler_params=params(7, 60),
        name="reduce_tokens",
    )(*partials, *gradients)


def scatter_body(
    n,
    one_ref,
    mixed_ref,
    dy_ref,
    dxb_ref,
    branch_ref,
    gate_ref,
    dpar_ref,
    gain_one_ref,
    gain_two_ref,
    column_ref,
    out_ref,
    small_out,
    spread_ref,
    made,
    got_q,
    got_p,
    got_z,
    got_s,
    *sems,
):
    send_q, recv_q, send_p, recv_p, send_z, recv_z, send_s, recv_s, send_f, recv_f, here = sems
    groups = n // INNER
    me, outer, by_x, by_y, by_xy = whereabouts()
    rows = one_ref.shape[1]
    part_rows = gate_ref.shape[2]
    total, width = out_ref.shape
    half = width // 2

    def place_of(turn):
        return lax.rem(outer + 1 + turn, groups)

    def base_of(turn):
        return (place_of(turn) - outer) * INNER

    barrier = pltpu.get_barrier_semaphore()

    def hello(peer):
        pl.semaphore_signal(barrier, inc=1, device_id={"seq": peer}, device_id_type=MESH)

    hello(by_x)
    hello(by_y)

    def hello_outer(turn, carry):
        hello(me + base_of(turn))
        return carry

    lax.fori_loop(0, groups - 1, hello_outer, 0)
    core = lax.axis_index("ch")
    masks = [1 << bit for bit in range(n.bit_length() - 1)]
    pl.semaphore_signal(barrier, inc=1, device_id={"ch": 1 - core}, device_id_type=MESH)
    pl.semaphore_wait(barrier, groups + 2)

    flips = ((by_x, by_y), (by_y, by_x))
    units = column_ref.shape[3]

    def units_of(place):
        return pl.ds(pl.multiple_of(place * units, units), units)

    def exchange(turn, receive=False):
        place = lax.rem(outer + groups - 1 - turn, groups) if receive else place_of(turn)
        return remote(
            column_ref.at[:, place],
            spread_ref.at[:, :, units_of(place if receive else outer)],
            send_f.at[turn],
            recv_f.at[turn],
            me + (place - outer) * INNER,
        )

    def small(turn):
        place = me
        for at, mask in enumerate(masks):
            flipped = me + mask * (1 - 2 * lax.rem(me // mask, 2))
            place = jnp.where(turn == at, flipped, place)
        other = jnp.where(turn == len(masks), 1 - core, core)
        return pltpu.make_async_remote_copy(
            src_ref=small_out,
            dst_ref=got_s.at[turn],
            send_sem=send_s.at[turn],
            recv_sem=recv_s.at[turn],
            device_id=(place, other),
            device_id_type=MESH,
        )

    small_out[:8] = dpar_ref[...]
    small_out[8:] = jnp.zeros((8, width), F32)
    at = 8
    for gain_ref in (gain_one_ref, gain_two_ref):
        for start in range(0, gain_ref.shape[1], width):
            small_out[at : at + 1] = gain_ref[:, start : start + width]
            at += 1
    small_row = lax.broadcasted_iota(jnp.int32, small_out.shape, 0)

    def cols(h):
        return pl.ds(h * half, half)

    def along_q(turn, h, other):
        source = (by_xy if other else flips[h][1]) + base_of(turn)
        return remote(
            made.at[source, :, cols(h)],
            got_q.at[h, turn, other],
            send_q.at[h, turn, other],
            recv_q.at[h, turn, other],
            flips[h][1],
        )

    def along_p(turn, h):
        return remote(
            made.at[flips[h][0] + base_of(turn), :, cols(h)],
            got_p.at[h, turn],
            send_p.at[h, turn],
            recv_p.at[h, turn],
            flips[h][0],
        )

    def along_z(turn, h):
        target = me + base_of(turn)
        return remote(
            made.at[target, :, cols(h)],
            got_z.at[h, turn],
            send_z.at[h, turn],
            recv_z.at[h, turn],
            target,
        )

    def make(block):
        left = one_ref[block]
        parts = [
            jnp.dot(left, dy_ref[...], preferred_element_type=F32),
            jnp.dot(left, dxb_ref[...], preferred_element_type=F32),
            jnp.dot(mixed_ref[block], branch_ref[...], preferred_element_type=F32),
        ]
        if rows % 16 == 0:
            for at, part in enumerate(parts):
                made[block, at * rows : (at + 1) * rows] = part.astype(BF16)
            for gate in range(2):
                at = 3 * rows + gate * part_rows
                made[block, at : at + part_rows] = gate_ref[block, gate]
        else:
            parts.extend(gate_ref[block, gate].astype(F32) for gate in range(2))
            made[block] = jnp.concatenate(parts, axis=0).astype(BF16)

    step = 32

    def add(block, h, ref, index):
        def one(at, carry):
            r = pl.ds(pl.multiple_of(at * step, step), step)
            made[block, r, cols(h)] = (
                made[block, r, cols(h)].astype(F32) + ref[index + (r,)].astype(F32)
            ).astype(BF16)
            return carry

        lax.fori_loop(0, total // step, one, 0)

    keep = pltpu.make_async_copy(
        column_ref.at[:, outer], spread_ref.at[:, :, units_of(outer)], here
    )
    keep.start()

    def turn_of(turn, carry):
        pl.when(turn <= len(masks))(lambda: small(turn).start())

        @pl.when(turn < groups)
        def _():
            base = base_of(turn)
            for h in range(2):
                make(flips[h][1] + base)
            make(by_xy + base)
            for h in range(2):
                for other in range(2):
                    along_q(turn, h, other).start()
            pl.when(turn < groups - 1)(lambda: exchange(turn).start())
            make(me + base)

        @pl.when(jnp.logical_and(turn >= 1, turn <= groups))
        def _():
            now = turn - 1
            base = base_of(now)
            for h in range(2):
                along_q(now, h, 1).wait_recv()
                add(flips[h][0] + base, h, got_q, (h, now, 1))
                along_p(now, h).start()
            for h in range(2):
                along_q(now, h, 0).wait_recv()
                add(me + base, h, got_q, (h, now, 0))

        @pl.when(turn >= 2)
        def _():
            now = turn - 2
            for h in range(2):
                along_p(now, h).wait_recv()
                add(me + base_of(now), h, got_p, (h, now))

                @pl.when(now < groups - 1)
                def _():
                    along_z(now, h).start()

        @pl.when(turn <= len(masks))
        def _():
            small(turn).wait()
            counts = jnp.logical_or(turn < len(masks), small_row >= 8)
            small_out[...] = small_out[...] + jnp.where(counts, got_s[turn], 0.0)

        return carry

    assert len(masks) < groups + 2
    lax.fori_loop(0, groups + 2, turn_of, 0)
    for h in range(2):

        def landed(turn, carry):
            along_z(turn, h).wait_recv()
            return carry

        lax.fori_loop(0, groups - 1, landed, 0)

        def finish(at, carry):
            r = pl.ds(pl.multiple_of(at * step, step), step)
            value = made[me, r, cols(h)].astype(F32)
            for turn in range(groups - 1):
                value = value + got_z[h, turn, r].astype(F32)
            out_ref[r, cols(h)] = value
            return carry

        lax.fori_loop(0, total // step, finish, 0)

    def clear(turn, carry):
        for h in range(2):
            along_q(turn, h, 0).wait_send()
            along_q(turn, h, 1).wait_send()
            along_p(turn, h).wait_send()

            @pl.when(turn < groups - 1)
            def _():
                along_z(turn, h).wait_send()

        @pl.when(turn < groups - 1)
        def _():
            exchange(turn, True).wait_recv()
            exchange(turn).wait_send()

        return carry

    lax.fori_loop(0, groups, clear, 0)
    keep.wait()


def scatter_mixer(one, mixed, dy, dxb, branch, gates, dpar, gain_one, gain_two, column):
    n, rows, _ = one.shape
    groups = n // INNER
    width = dy.shape[1]
    total = 3 * rows + 2 * gates.shape[2]
    kinds, _, _, units = column.shape
    turns = n.bit_length()
    dma = pltpu.SemaphoreType.DMA
    return pl.pallas_call(
        functools.partial(scatter_body, n),
        out_shape=(
            jax.ShapeDtypeStruct((total, width), F32),
            jax.ShapeDtypeStruct((16, width), F32),
            jax.ShapeDtypeStruct((kinds, rows, groups * units), BF16),
        ),
        in_specs=[VMEM] * 9 + [ANY],
        out_specs=(VMEM, VMEM, ANY),
        scratch_shapes=[
            pltpu.VMEM((n, total, width), BF16),
            pltpu.VMEM((2, groups, 2, total, width // 2), BF16),
            pltpu.VMEM((2, groups, total, width // 2), BF16),
            pltpu.VMEM((2, groups, total, width // 2), BF16),
            pltpu.VMEM((turns, 16, width), F32),
            dma((2, groups, 2)),
            dma((2, groups, 2)),
            dma((2, groups)),
            dma((2, groups)),
            dma((2, groups)),
            dma((2, groups)),
            dma((turns,)),
            dma((turns,)),
            dma((groups,)),
            dma((groups,)),
            dma(()),
        ],
        compiler_params=params(2, 62),
        name="scatter_mixer",
    )(one, mixed, dy, dxb, branch, gates, dpar, gain_one, gain_two, column)


GELU_A = 0.7978845608028654
GELU_B = 0.044715


def gelu_parts(v):
    t = jnp.tanh(GELU_A * (v + GELU_B * v * v * v))
    value = 0.5 * v * (1.0 + t)
    slope = 0.5 * (1.0 + t) + 0.5 * v * (1.0 - t * t) * GELU_A * (1.0 + 3.0 * GELU_B * v * v)
    return value, slope


def gates_of(conv_low, gate_ref, par_ref, head, cols, first):
    pre_x = jnp.dot(conv_low, gate_ref[0, head], preferred_element_type=F32)
    pre_a = jnp.dot(conv_low, gate_ref[1, head], preferred_element_type=F32)
    gate_x = jax.nn.sigmoid(pre_x + par_ref[5:6, cols])
    gate_a = jax.nn.sigmoid(pre_a + par_ref[6:7, cols])
    decay = jnp.exp(-8.0 * gate_a * par_ref[8:9, cols])
    room = 1.0 - decay * decay
    mult = jnp.where(first, 1.0, jnp.sqrt(jnp.maximum(room, 0.001)))
    return gate_x, gate_a, decay, room, mult


FLIPPED = (((1,), (1,)), ((), ()))


def first_row(tokens):
    row = lax.broadcasted_iota(jnp.int32, (tokens, 1), 0)
    return jnp.logical_and(row == 0, lax.axis_index("seq") == 0)


def forward_body(
    n,
    one_ref,
    w_in_ref,
    w_branch_ref,
    w_out_ref,
    gate_ref,
    par_ref,
    x_ref,
    gain_ref,
    column_ref,
    cot_ref,
    xb_ref,
    yp_ref,
    conv_ref,
    state_ref,
    branch_ref,
    edge_ref,
    resid_ref,
    two_ref,
    near_ref,
    cots_ref,
    w_in,
    w_branch,
    w_out,
    mixed,
    mixed_got,
    wide,
    tail,
    fade,
    mine,
    theirs,
    *sems,
):
    send_tail, recv_tail, send_tot, recv_tot, send_f, recv_f, here, send_m, recv_m, loaded = sems[:10]
    tokens, width = xb_ref.shape
    model = one_ref.shape[1]
    me = lax.axis_index("seq")
    size = gate_ref.shape[2]
    loads = [
        pltpu.make_async_copy(src, dst, loaded.at[at])
        for at, (src, dst) in enumerate(
            ((w_in_ref, w_in), (w_branch_ref, w_branch), (w_out_ref, w_out))
        )
    ]
    for load in loads:
        load.start()
    greet_all(n, me, True)
    tail_copy = remote(
        xb_ref.at[pl.ds(tokens - 16, 16)], tail, send_tail, recv_tail, lax.rem(me + 1, n)
    )
    _, _, by_x, by_y, _ = whereabouts()
    part = column_ref.shape[1] // 2
    kinds = column_ref.shape[0]
    hosted = [
        [
            remote(
                column_ref.at[kind, pl.ds(h * part, part)],
                near_ref.at[h, kind],
                send_f.at[kind, h],
                recv_f.at[kind, h],
                (by_x, by_y)[h],
            )
            for h in range(2)
        ]
        for kind in range(kinds)
    ]
    chain = Chain(n, cot_ref, cots_ref, *sems[10:])
    keep = chain.keep(here)

    def host(kind):
        for copy in hosted[kind]:
            copy.start()

    host(0)
    chain.start()
    keep.start()
    loads[0].wait()
    for start in range(0, width, size):
        cols = slice(start, start + size)
        xb_ref[:, cols] = jnp.dot(
            one_ref[...], w_in[:, cols], preferred_element_type=F32
        ).astype(BF16)
    pl.when(me + 1 < n)(tail_copy.start)
    wide[8:] = xb_ref[...].astype(F32)
    loads[1].wait()
    for start in range(0, width, size):
        cols = slice(start, start + size)
        yp_ref[:, cols] = jnp.dot(one_ref[...], w_branch[:, cols], preferred_element_type=F32)

    @pl.when(me > 0)
    def _():
        tail_copy.wait_recv()
        wide[:8] = tail[...].astype(F32)[8:]

    @pl.when(me == 0)
    def _():
        wide[:8] = jnp.zeros((8, width), F32)

    pl.when(me + 1 < n)(tail_copy.wait_send)
    edge_ref[:8] = wide[:8]
    first = first_row(tokens)
    for head in range(width // size):
        cols = slice(head * size, (head + 1) * size)
        conv = par_ref[4:5, cols]
        for tap in range(4):
            conv = conv + par_ref[tap : tap + 1, cols] * wide[8 - tap : 8 - tap + tokens, cols]
        conv_low = conv.astype(BF16)
        conv_ref[:, cols] = conv_low
        gate_x, _, decay, _, mult = gates_of(conv_low, gate_ref, par_ref, head, cols, first)
        fade[:, cols] = decay
        state_ref[:, cols] = conv_low.astype(F32) * gate_x * mult

    row = lax.broadcasted_iota(jnp.int32, (8, width), 0)

    def inside(at, carry):
        r = pl.ds(pl.multiple_of(at * 8, 8), 8)
        a, b = fade[r], state_ref[r]
        for by in (1, 2, 4):
            a_back = pltpu.roll(a, by, 0)
            b_back = pltpu.roll(b, by, 0)
            b = jnp.where(row >= by, a * b_back + b, b)
            a = jnp.where(row >= by, a * a_back, a)
        fade[r] = a
        state_ref[r] = b
        return a[7:8] * carry[0], a[7:8] * carry[1] + b[7:8]

    ones, zeros = jnp.ones((1, width), F32), jnp.zeros((1, width), F32)
    tot_a, tot_b = lax.fori_loop(0, tokens // 8, inside, (ones, zeros))
    mine[0:1] = tot_a
    mine[1:2] = tot_b

    def told(place):
        return remote(mine, theirs.at[me], send_tot.at[place], recv_tot.at[me], place)

    def heard(place):
        return remote(mine, theirs.at[place], send_tot.at[place], recv_tot.at[place], place)

    def tell(place, carry):
        told(place).start()
        return carry

    lax.fori_loop(me + 1, n, tell, 0)
    host(1)

    def hear(place, state):
        heard(place).wait_recv()
        return theirs[place, 0:1] * state + theirs[place, 1:2]

    carry_in = lax.fori_loop(0, me, hear, zeros)
    edge_ref[8:] = jnp.broadcast_to(carry_in, (8, width))
    for kind in range(2, kinds):
        host(kind)
    chain.step(1)

    def finish(at, carry):
        r = pl.ds(pl.multiple_of(at * 16, 16), 16)
        a, b = fade[r], state_ref[r]
        top = b[:8] + a[:8] * carry
        low = b[8:] + a[8:] * top[7:8]
        states = jnp.concatenate([top, low], axis=0)
        state_ref[r] = states
        branch_ref[r] = (states * gelu_parts(yp_ref[r])[0]).astype(BF16)
        return low[7:8]

    lax.fori_loop(0, tokens // 16, finish, carry_in)

    def sent(place, carry):
        told(place).wait_send()
        return carry

    lax.fori_loop(me + 1, n, sent, 0)
    loads[2].wait()
    core = lax.axis_index("ch")
    half = tokens // 2
    for start in range(0, model, size):
        cols = slice(start, start + size)
        part = lax.dot_general(branch_ref[...], w_out[cols], FLIPPED, preferred_element_type=F32)
        mixed[0, :, cols] = part[:half]
        mixed[1, :, cols] = part[half:]
    exchange = pltpu.make_async_remote_copy(
        src_ref=mixed.at[1 - core],
        dst_ref=mixed_got,
        send_sem=send_m,
        recv_sem=recv_m,
        device_id={"ch": 1 - core},
        device_id_type=MESH,
    )
    exchange.start()
    exchange.wait_recv()

    def norm(at, carry):
        r = pl.ds(pl.multiple_of(at * 16, 16), 16)
        resid = x_ref[r].astype(F32) + (mixed[core, r] + mixed_got[r])
        resid_ref[r] = resid
        scale = lax.rsqrt(jnp.mean(resid * resid, axis=-1, keepdims=True) + 1e-06)
        two_ref[r] = (resid * scale * gain_ref[...]).astype(BF16)
        return carry

    lax.fori_loop(0, half // 16, norm, 0)
    exchange.wait_send()
    for step in range(2, n // INNER):
        chain.step(step)
    for pair in hosted:
        for copy in pair:
            copy.wait()
    chain.finish()
    keep.wait()


def mixer_forward(one, weights, gates, par, x_half, gain, column, cotangent):
    n = lax.axis_size("seq")
    tokens, model = one.shape
    width = par.shape[1]
    half = tokens // 2
    kinds, groups, rows, units = column.shape
    dma = pltpu.SemaphoreType.DMA
    whole = jax.ShapeDtypeStruct((tokens, width), F32)
    low = jax.ShapeDtypeStruct((tokens, width), BF16)
    return pl.pallas_call(
        functools.partial(forward_body, n),
        out_shape=(
            low,
            whole,
            low,
            whole,
            low,
            jax.ShapeDtypeStruct((16, width), F32),
            jax.ShapeDtypeStruct((half, model), F32),
            jax.ShapeDtypeStruct((half, model), BF16),
            jax.ShapeDtypeStruct((2, kinds, groups // 2, rows, units), column.dtype),
            jax.ShapeDtypeStruct((groups, 2) + cotangent.shape, cotangent.dtype),
        ),
        in_specs=[VMEM] + [HBM] * 3 + [VMEM] * 4 + [HBM, HBM],
        out_specs=(VMEM,) * 8 + (ANY, ANY),
        scratch_shapes=[
            pltpu.VMEM((model, width), BF16),
            pltpu.VMEM((model, width), BF16),
            pltpu.VMEM((model, width), BF16),
            pltpu.VMEM((2, half, model), F32),
            pltpu.VMEM((half, model), F32),
            pltpu.VMEM((tokens + 8, width), F32),
            pltpu.VMEM((16, width), BF16),
            pltpu.VMEM((tokens, width), F32),
            pltpu.VMEM((2, width), F32),
            pltpu.VMEM((n, 2, width), F32),
            dma(()),
            dma(()),
            dma((n,)),
            dma((n,)),
            dma((kinds, 2)),
            dma((kinds, 2)),
            dma(()),
            dma(()),
            dma(()),
            dma((3,)),
            *chain_semaphores(groups),
        ],
        compiler_params=params(4, 60),
        name="mixer_forward",
    )(one, *weights, gates, par, x_half, gain, column, cotangent)


def backward_body(
    n,
    mixed_ref,
    w_in_ref,
    w_branch_ref,
    w_out_ref,
    x_ref,
    gain_ref,
    resid_ref,
    yp_ref,
    state_ref,
    edge_ref,
    conv_ref,
    xb_ref,
    gate_ref,
    par_ref,
    half_ref,
    dy_ref,
    dxb_ref,
    dgate_ref,
    dpar_ref,
    dx_ref,
    dgain_ref,
    near_ref,
    w_in,
    w_branch,
    w_out,
    d_one,
    d_one_got,
    fade,
    shift,
    adj,
    gate_x_s,
    gate_a_s,
    dconv,
    wide,
    mine,
    theirs,
    head_rows,
    *sems,
):
    send_rows, recv_rows, send_tot, recv_tot, send_f, recv_f, send_m, recv_m, loaded = sems
    tokens, width = xb_ref.shape
    model = gain_ref.shape[1]
    me = lax.axis_index("seq")
    size = gate_ref.shape[2]
    loads = [
        pltpu.make_async_copy(src, dst, loaded.at[at])
        for at, (src, dst) in enumerate(
            ((w_out_ref, w_out), (w_in_ref, w_in), (w_branch_ref, w_branch))
        )
    ]
    for load in loads:
        load.start()
    greet_all(n, me, True)
    _, _, by_x, by_y, _ = whereabouts()
    hosted = [
        remote(half_ref.at[h], near_ref.at[h], send_f.at[h], recv_f.at[h], (by_x, by_y)[h])
        for h in range(2)
    ]
    for copy in hosted:
        copy.start()
    first = first_row(tokens)
    fade[tokens:] = jnp.ones((8, width), F32)
    loads[0].wait()
    for head in range(width // size):
        cols = slice(head * size, (head + 1) * size)
        gate_x, gate_a, decay, _, _ = gates_of(conv_ref[:, cols], gate_ref, par_ref, head, cols, first)
        gate_x_s[:, cols] = gate_x
        gate_a_s[:, cols] = gate_a
        fade[:tokens, cols] = decay
        value, slope = gelu_parts(yp_ref[:, cols])
        grad = jnp.dot(mixed_ref[...], w_out[:, cols], preferred_element_type=F32)
        dy_ref[:, cols] = (grad * state_ref[:, cols] * slope).astype(BF16)
        adj[:, cols] = grad * value
        shift[:, cols] = fade[1 : tokens + 1, cols]

    row = lax.broadcasted_iota(jnp.int32, (8, width), 0)
    tiles = tokens // 8

    def inside(turn, carry):
        r = pl.ds(pl.multiple_of((tiles - 1 - turn) * 8, 8), 8)
        a, b = shift[r], adj[r]
        for by in (1, 2, 4):
            a_next = pltpu.roll(a, 8 - by, 0)
            b_next = pltpu.roll(b, 8 - by, 0)
            b = jnp.where(row < 8 - by, a * b_next + b, b)
            a = jnp.where(row < 8 - by, a * a_next, a)
        shift[r] = a
        adj[r] = b
        return a[0:1] * carry[0], a[0:1] * carry[1] + b[0:1]

    ones, zeros = jnp.ones((1, width), F32), jnp.zeros((1, width), F32)
    tot_a, tot_b = lax.fori_loop(0, tiles, inside, (ones, zeros))
    first_fade = fade[0:1]
    mine[0:1] = first_fade * tot_a
    mine[1:2] = first_fade * tot_b

    def told(place):
        return remote(mine, theirs.at[me], send_tot.at[place], recv_tot.at[me], place)

    def heard(place):
        return remote(mine, theirs.at[place], send_tot.at[place], recv_tot.at[place], place)

    def tell(place, carry):
        told(place).start()
        return carry

    lax.fori_loop(0, me, tell, 0)

    def hear(turn, state):
        place = n - 1 - turn
        heard(place).wait_recv()
        return theirs[place, 0:1] * state + theirs[place, 1:2]

    carry_in = lax.fori_loop(0, n - 1 - me, hear, zeros)

    def finish(turn, carry):
        r = pl.ds(pl.multiple_of((tiles - 1 - turn) * 8, 8), 8)
        value = adj[r] + shift[r] * carry
        adj[r] = value
        return value[0:1]

    lax.fori_loop(0, tiles, finish, carry_in)

    wide[:8] = edge_ref[:8]
    wide[8:] = xb_ref[...].astype(F32)
    at_first = lax.broadcasted_iota(jnp.int32, (tokens, 1), 0) == 0
    for head in range(width // size):
        cols = slice(head * size, (head + 1) * size)
        conv_low = conv_ref[:, cols]
        conv = conv_low.astype(F32)
        gate_x, gate_a, decay = gate_x_s[:, cols], gate_a_s[:, cols], fade[:tokens, cols]
        room = 1.0 - decay * decay
        mult = jnp.where(first, 1.0, jnp.sqrt(jnp.maximum(room, 0.001)))
        back = adj[:, cols]
        before = jnp.where(at_first, edge_ref[8:9, cols], pltpu.roll(state_ref[:, cols], 1, 0))
        d_mult = back * conv * gate_x
        moves = jnp.logical_and(room > 0.001, jnp.logical_not(first))
        d_decay = back * before - jnp.where(moves, d_mult * decay / mult, 0.0)
        d_log = d_decay * decay
        d_pre_x = back * conv * mult * gate_x * (1.0 - gate_x)
        d_pre_a = d_log * (-8.0 * par_ref[8:9, cols]) * gate_a * (1.0 - gate_a)
        dpar_ref[5:6, cols] = jnp.sum(d_pre_x, axis=0, keepdims=True)
        dpar_ref[6:7, cols] = jnp.sum(d_pre_a, axis=0, keepdims=True)
        dpar_ref[7:8, cols] = (
            jnp.sum(d_log * (-8.0 * gate_a), axis=0, keepdims=True) * par_ref[9:10, cols]
        )
        low_x, low_a = d_pre_x.astype(BF16), d_pre_a.astype(BF16)
        d_conv = (
            back * gate_x * mult
            + lax.dot_general(low_x, gate_ref[0, head], FLIPPED, preferred_element_type=F32)
            + lax.dot_general(low_a, gate_ref[1, head], FLIPPED, preferred_element_type=F32)
        )
        dconv[:tokens, cols] = d_conv
        over_rows = (((0,), (0,)), ((), ()))
        for gate, low in enumerate((low_x, low_a)):
            d_gate = lax.dot_general(conv_low, low, over_rows, preferred_element_type=F32)
            dgate_ref[:, gate, :, cols] = d_gate.astype(BF16).reshape(n, size // n, size)
        dpar_ref[4:5, cols] = jnp.sum(d_conv, axis=0, keepdims=True)
        for tap in range(4):
            dpar_ref[tap : tap + 1, cols] = jnp.sum(
                d_conv * wide[8 - tap : 8 - tap + tokens, cols], axis=0, keepdims=True
            )

    rows_copy = remote(
        dconv.at[pl.ds(0, 8)], head_rows, send_rows, recv_rows, lax.rem(me + n - 1, n)
    )
    pl.when(me > 0)(rows_copy.start)

    @pl.when(me + 1 < n)
    def _():
        rows_copy.wait_recv()
        dconv[tokens:] = head_rows[...]

    @pl.when(me + 1 == n)
    def _():
        dconv[tokens:] = jnp.zeros((8, width), F32)

    for head in range(width // size):
        cols = slice(head * size, (head + 1) * size)
        total = par_ref[0:1, cols] * dconv[:tokens, cols]
        for tap in range(1, 4):
            total = total + par_ref[tap : tap + 1, cols] * dconv[tap : tap + tokens, cols]
        dxb_ref[:, cols] = total.astype(BF16)

    pl.when(me > 0)(rows_copy.wait_send)

    def sent(place, carry):
        told(place).wait_send()
        return carry

    lax.fori_loop(0, me, sent, 0)
    core = lax.axis_index("ch")
    half = tokens // 2
    loads[1].wait()
    loads[2].wait()
    for start in range(0, model, size):
        cols = slice(start, start + size)
        part = (
            lax.dot_general(dy_ref[...], w_branch[cols], FLIPPED, preferred_element_type=F32)
            + lax.dot_general(dxb_ref[...], w_in[cols], FLIPPED, preferred_element_type=F32)
        ).astype(BF16)
        d_one[0, :, cols] = part[:half]
        d_one[1, :, cols] = part[half:]
    exchange = pltpu.make_async_remote_copy(
        src_ref=d_one.at[1 - core],
        dst_ref=d_one_got,
        send_sem=send_m,
        recv_sem=recv_m,
        device_id={"ch": 1 - core},
        device_id_type=MESH,
    )
    exchange.start()
    exchange.wait_recv()

    def norm(at, total):
        r = pl.ds(pl.multiple_of(at * 16, 16), 16)
        x = x_ref[r].astype(F32)
        scale = lax.rsqrt(jnp.mean(x * x, axis=-1, keepdims=True) + 1e-06)
        grad = d_one[core, r].astype(F32) + d_one_got[r].astype(F32)
        back = grad * gain_ref[...]
        shrink = scale * scale * scale * jnp.mean(x * back, axis=-1, keepdims=True)
        dx_ref[r] = resid_ref[r] + (scale * back - x * shrink)
        return total + jnp.sum(grad * (x * scale), axis=0, keepdims=True)

    dgain_ref[...] = lax.fori_loop(0, half // 16, norm, jnp.zeros((1, model), F32))
    exchange.wait_send()
    for copy in hosted:
        copy.wait()


def mixer_backward(
    mixed, weights, x_half, gain, d_resid, y_pre, states, edge, conv, x_branch, gates, par, halves
):
    n = lax.axis_size("seq")
    tokens, width = x_branch.shape
    model = mixed.shape[1]
    size = gates.shape[2]
    half = tokens // 2
    dma = pltpu.SemaphoreType.DMA
    whole = pltpu.VMEM((tokens, width), F32)
    longer = pltpu.VMEM((tokens + 8, width), F32)
    weight = pltpu.VMEM((model, width), BF16)
    return pl.pallas_call(
        functools.partial(backward_body, n),
        out_shape=(
            jax.ShapeDtypeStruct((tokens, width), BF16),
            jax.ShapeDtypeStruct((tokens, width), BF16),
            jax.ShapeDtypeStruct((n, 2, size // n, width), BF16),
            jax.ShapeDtypeStruct((8, width), F32),
            jax.ShapeDtypeStruct((half, model), F32),
            jax.ShapeDtypeStruct((1, model), F32),
            jax.ShapeDtypeStruct(halves.shape, BF16),
        ),
        in_specs=[VMEM] + [HBM] * 3 + [VMEM] * 10 + [HBM],
        out_specs=(VMEM,) * 6 + (ANY,),
        scratch_shapes=[
            weight,
            weight,
            weight,
            pltpu.VMEM((2, half, model), BF16),
            pltpu.VMEM((half, model), BF16),
            longer,
            whole,
            whole,
            whole,
            whole,
            longer,
            longer,
            pltpu.VMEM((2, width), F32),
            pltpu.VMEM((n, 2, width), F32),
            pltpu.VMEM((8, width), F32),
            dma(()),
            dma(()),
            dma((n,)),
            dma((n,)),
            dma((2,)),
            dma((2,)),
            dma(()),
            dma(()),
            dma((3,)),
        ],
        compiler_params=params(5, 60),
        name="mixer_backward",
    )(mixed, *weights, x_half, gain, d_resid, y_pre, states, edge, conv, x_branch, gates, par, halves)


def ffn_body(n, *refs):
    own_ref, column_ref, near_ref, cots_ref, resid_ref, gain_ref = refs[:6]
    block_ref, d_resid_ref, mixed_ref, d_gain_ref, halves_ref, mine_ref, far_ref = refs[6:13]
    tokens, cots, w, hidden, box, sib, got, d_hidden, stage, turned = refs[13:23]
    send_t, recv_z, recv_c, send_w, recv_w, keep_w, keep_c, keep_t = refs[23:31]
    send_c, recv_s, send_z, recv_r, send_f, recv_f, send_m, recv_m, move, out_sem = refs[31:]
    groups = n // INNER
    half = groups // 2
    me, outer, by_x, by_y, by_xy = whereabouts()
    base = outer * INNER
    core = lax.axis_index("ch")
    above, below = outer + 1 < groups, outer > 0
    sibling = {"ch": 1 - core}
    barrier = pltpu.get_barrier_semaphore()

    def hello(peer):
        pl.semaphore_signal(barrier, inc=1, device_id=peer, device_id_type=MESH)

    hello({"seq": by_x})
    hello({"seq": by_y})
    hello(sibling)
    pl.when(above)(lambda: hello({"seq": me + INNER}))
    pl.when(below)(lambda: hello({"seq": me - INNER}))
    pl.semaphore_wait(barrier, 3 + above.astype(jnp.int32) + below.astype(jnp.int32))
    flips = ((by_x, by_y), (by_y, by_x))
    rows, units = w.shape[3], w.shape[4]
    tall, model = own_ref.shape
    count = 2 * tall
    deep = INNER * rows
    tile = 256

    def part(h):
        return pl.ds(h * half, half)


    chain = Chain(n, own_ref, tokens, send_t, recv_z, recv_c)

    def weight_copy(kind, h, far, receive=False):
        source = flips[h][0] if far else me
        if receive:
            source = by_xy if far else flips[h][1]
        return remote(
            near_ref.at[h, kind] if far else column_ref.at[kind, part(h)],
            w.at[kind, part(h), source - base],
            send_w.at[kind, h, far],
            recv_w.at[kind, h, far],
            flips[h][1],
        )

    keep = [
        [
            pltpu.make_async_copy(
                column_ref.at[kind], w.at[kind, :, me - base], keep_w.at[kind, 0]
            ),
            *(
                pltpu.make_async_copy(
                    near_ref.at[h, kind],
                    w.at[kind, part(h), flips[h][0] - base],
                    keep_w.at[kind, 1 + h],
                )
                for h in range(2)
            ),
        ]
        for kind in range(3)
    ]
    every = [(h, far) for far in range(2) for h in range(2)]
    load_c = pltpu.make_async_copy(cots_ref, cots, keep_c)
    own = chain.keep(keep_t)
    chain.start()
    for kind in (2, 0, 1):
        for h, far in every:
            weight_copy(kind, h, far).start()
    load_c.start()
    own.start()
    for kind in (2, 0, 1):
        for copy in keep[kind]:
            copy.start()
    for step in range(1, groups):
        chain.step(step)
    chain.finish()
    own.wait()
    load_c.wait()

    def weights_landed(kind):
        for h, far in every:
            weight_copy(kind, h, far, True).wait_recv()
        for copy in keep[kind]:
            copy.wait()

    def columns(kind, at):
        return w[kind, :, :, :, at : at + tile].reshape(model, tile)

    def token_rows(place):
        return pl.ds(pl.multiple_of(place * count, count), count)

    def each(limit, action):
        def one(turn, carry):
            action(turn)
            return carry

        lax.fori_loop(0, limit, one, 0)

    weights_landed(2)

    def back_hidden(place):
        left = cots[place].reshape(count, model)
        for at in range(0, units, tile):
            d_hidden[token_rows(place), at : at + tile] = jnp.dot(
                left, columns(2, at), preferred_element_type=F32
            )

    each(groups, back_hidden)
    weights_landed(0)
    weights_landed(1)

    def middle(place):
        left = tokens[place].reshape(count, model)
        r = token_rows(place)
        for at in range(0, units, tile):
            c = slice(at, at + tile)
            gate = jnp.dot(left, columns(0, at), preferred_element_type=F32)
            up = jnp.dot(left, columns(1, at), preferred_element_type=F32)
            value, slope = gelu_parts(gate)
            back = d_hidden[r, c]
            hidden[0, r, c] = (value * up).astype(BF16)
            hidden[1, r, c] = (back * up * slope).astype(BF16)
            hidden[2, r, c] = (back * value).astype(BF16)

    each(groups, middle)
    for kind in range(3):
        for h, far in every:
            weight_copy(kind, h, far).wait_send()


    def partial(kind, place):
        r = token_rows(place)
        for at in range(groups):
            pairs = ((1, 0), (2, 1)) if kind == 0 else ((0, 2),)
            value = 0.0
            for left, right in pairs:
                value = value + lax.dot_general(
                    hidden[left, r],
                    w[right, at].reshape(deep, units),
                    FLIPPED,
                    preferred_element_type=F32,
                )
            value = value.astype(BF16)
            box[place, 0, :, at * deep : (at + 1) * deep] = value[:tall]
            box[place, 1, :, at * deep : (at + 1) * deep] = value[tall:]
        to_sibling(kind, place).start()

    def to_sibling(kind, place):
        return pltpu.make_async_remote_copy(
            src_ref=box.at[place, 1 - core],
            dst_ref=sib.at[kind, place],
            send_sem=send_c.at[kind, place],
            recv_sem=recv_s.at[kind, place],
            device_id=sibling,
            device_id_type=MESH,
        )

    def along(kind, place, up):
        last = place == (outer + 1 if up else outer - 1)
        slot = place if up else jnp.where(last, groups, place)
        return remote(
            box.at[place, core],
            got.at[kind, slot],
            send_z.at[kind, place],
            recv_r.at[kind, slot],
            me + (INNER if up else -INNER),
        )

    def landed(kind, slot):
        return remote(
            box.at[0, core], got.at[kind, slot], send_z.at[kind, 0], recv_r.at[kind, slot], by_x
        )

    chunk = 16

    def rows_of(at):
        return pl.ds(pl.multiple_of(at * chunk, chunk), chunk)

    def ready(kind, place, incoming):
        to_sibling(kind, place).wait_recv()

        def add(at, with_got):
            r = rows_of(at)
            value = box[place, core, r].astype(F32) + sib[kind, place, r].astype(F32)
            if with_got:
                value = value + got[kind, place, r].astype(F32)
            box[place, core, r] = value.astype(BF16)

        @pl.when(incoming)
        def _():
            landed(kind, place).wait_recv()
            each(tall // chunk, lambda at: add(at, True))

        @pl.when(jnp.logical_not(incoming))
        def _():
            each(tall // chunk, lambda at: add(at, False))

    def climb(kind, turn):
        place = groups - 1 - turn

        @pl.when(place > outer)
        def _():
            ready(kind, place, below)
            along(kind, place, True).start()

    def sink(kind, turn):
        @pl.when(turn < outer)
        def _():
            ready(kind, turn, above)
            along(kind, turn, False).start()

    def pass_on(kind):
        def turns(turn):
            @pl.when(outer < half)
            def _():
                climb(kind, turn)
                sink(kind, turn)

            @pl.when(outer >= half)
            def _():
                sink(kind, turn)
                climb(kind, turn)

        each(groups - 1, turns)

    def totals(kind, use):
        to_sibling(kind, outer).wait_recv()
        for condition, slots in (
            (jnp.logical_and(below, above), (outer, groups)),
            (jnp.logical_and(below, jnp.logical_not(above)), (outer,)),
            (jnp.logical_and(jnp.logical_not(below), above), (groups,)),
        ):

            @pl.when(condition)
            def _(slots=slots):
                for slot in slots:
                    landed(kind, slot).wait_recv()

                def one(at):
                    r = rows_of(at)
                    value = box[outer, core, r].astype(F32) + sib[kind, outer, r].astype(F32)
                    for slot in slots:
                        value = value + got[kind, slot, r].astype(F32)
                    use(r, value)

                each(tall // chunk, one)

    def clear(kind):
        def one(place):
            to_sibling(kind, place).wait_send()

            @pl.when(place > outer)
            def _():
                along(kind, place, True).wait_send()

            @pl.when(place < outer)
            def _():
                along(kind, place, False).wait_send()

        each(groups, one)


    def gradient_copy(kind, h, far):
        source = by_xy if far else flips[h][1]
        return remote(
            w.at[kind, part(h), source - base],
            far_ref.at[h, far, kind],
            send_f.at[kind, h, far],
            recv_f.at[kind, h, far],
            flips[h][1],
        )

    def gradients(kinds, source):
        for h in range(2):
            for at in range(h * half, (h + 1) * half):
                left = source[:, :, :, at * deep : (at + 1) * deep].reshape(groups * count, deep)
                turned[...] = left.T
                for kind, right in kinds:
                    for start in range(0, units, tile):
                        c = slice(start, start + tile)
                        w[kind, at, :, :, c] = (
                            jnp.dot(
                                turned[...], hidden[right, :, c], preferred_element_type=F32
                            )
                            .astype(BF16)
                            .reshape(INNER, rows, tile)
                        )
            for kind, _ in kinds:
                for far in (1, 0):
                    gradient_copy(kind, h, far).start()

    def collect(kind, h, far):
        inner = (flips[h][0] if far else me) - base
        gradient_copy(kind, h, far).wait_recv()
        load = pltpu.make_async_copy(far_ref.at[h, far, kind], stage, move)
        load.start()
        load.wait()
        for place in range(half):
            at = h * half + place

            def one(turn, place=place, at=at):
                r = rows_of(turn)
                w[kind, at, inner, r] = (
                    w[kind, at, inner, r].astype(F32) + stage[place, r].astype(F32)
                ).astype(BF16)

            each(rows // chunk, one)
        out_copy(kind, h, far).start()

    def out_copy(kind, h, far):
        inner = (flips[h][0] if far else me) - base
        return pltpu.make_async_copy(
            w.at[kind, part(h), inner],
            (halves_ref if far else mine_ref).at[h, kind],
            out_sem.at[kind, h, far],
        )

    def in_order(action):
        @pl.when(outer < half)
        def _():
            for turn in range(half):
                action(groups - 1 - turn)
                action(turn)

        @pl.when(outer >= half)
        def _():
            for turn in range(half):
                action(turn)
                action(groups - 1 - turn)

    in_order(lambda place: partial(0, place))
    gradients(((0, 1), (1, 2)), tokens)
    pass_on(0)
    d_gain_ref[...] = jnp.zeros((1, model), F32)

    def norm(r, grad):
        resid = resid_ref[r]
        scale = lax.rsqrt(jnp.mean(resid * resid, axis=-1, keepdims=True) + 1e-06)
        back = grad * gain_ref[...]
        shrink = scale * scale * scale * jnp.mean(resid * back, axis=-1, keepdims=True)
        value = cots[outer, core, r].astype(F32) + (scale * back - resid * shrink)
        d_resid_ref[r] = value
        mixed_ref[core, r] = value.astype(BF16)
        d_gain_ref[...] = d_gain_ref[...] + jnp.sum(grad * (resid * scale), axis=0, keepdims=True)

    totals(0, norm)
    share = pltpu.make_async_remote_copy(
        src_ref=mixed_ref.at[core],
        dst_ref=mixed_ref.at[core],
        send_sem=send_m,
        recv_sem=recv_m,
        device_id=sibling,
        device_id_type=MESH,
    )
    share.start()
    clear(0)
    in_order(lambda place: partial(1, place))
    gradients(((2, 0),), cots)
    pass_on(1)
    for far in (1, 0):
        for kind in range(2):
            for h in range(2):
                collect(kind, h, far)

    def finish(r, value):
        block_ref[r] = (resid_ref[r] + value).astype(BF16)

    totals(1, finish)
    clear(1)
    for far in (1, 0):
        for h in range(2):
            collect(2, h, far)
    pltpu.make_async_remote_copy(
        src_ref=mixed_ref.at[core],
        dst_ref=mixed_ref.at[1 - core],
        send_sem=send_m,
        recv_sem=recv_m,
        device_id=sibling,
        device_id_type=MESH,
    ).wait_recv()
    share.wait_send()
    for kind in range(3):
        for h, far in every:
            gradient_copy(kind, h, far).wait_send()
            out_copy(kind, h, far).wait()


def feed_forward(own, column, near, cots, resid, gain):
    n = lax.axis_size("seq")
    groups = n // INNER
    tall, model = own.shape
    kinds, _, rows, units = column.shape
    half = groups // 2
    dma = pltpu.SemaphoreType.DMA
    part = jax.ShapeDtypeStruct((2, kinds, half, rows, units), BF16)
    return pl.pallas_call(
        functools.partial(ffn_body, n),
        out_shape=(
            jax.ShapeDtypeStruct((tall, model), BF16),
            jax.ShapeDtypeStruct((tall, model), F32),
            jax.ShapeDtypeStruct((2, tall, model), BF16),
            jax.ShapeDtypeStruct((1, model), F32),
            part,
            part,
            jax.ShapeDtypeStruct((2, 2, kinds, half, rows, units), BF16),
        ),
        in_specs=[HBM] * 4 + [VMEM] * 2,
        out_specs=(VMEM,) * 4 + (HBM,) * 3,
        scratch_shapes=[
            pltpu.VMEM((groups, 2, tall, model), BF16),
            pltpu.VMEM((groups, 2, tall, model), BF16),
            pltpu.VMEM((kinds, groups, INNER, rows, units), BF16),
            pltpu.VMEM((3, groups * 2 * tall, units), BF16),
            pltpu.VMEM((groups, 2, tall, model), BF16),
            pltpu.VMEM((2, groups, tall, model), BF16),
            pltpu.VMEM((2, groups + 1, tall, model), BF16),
            pltpu.VMEM((groups * 2 * tall, units), F32),
            pltpu.VMEM((half, rows, units), BF16),
            pltpu.VMEM((INNER * rows, groups * 2 * tall), BF16),
            *chain_semaphores(groups),
            dma((kinds, 2, 2)),
            dma((kinds, 2, 2)),
            dma((kinds, 3)),
            dma(()),
            dma(()),
            dma((2, groups)),
            dma((2, groups)),
            dma((2, groups)),
            dma((2, groups + 1)),
            dma((kinds, 2, 2)),
            dma((kinds, 2, 2)),
            dma(()),
            dma(()),
            dma(()),
            dma((kinds, 2, 2)),
        ],
        compiler_params=params(8, 63),
        name="feed_forward",
    )(own, column, near, cots, resid, gain)


def my_half(values):
    half = values.shape[0] // 2
    return lax.dynamic_slice_in_dim(values, lax.axis_index("ch") * half, half, 0)


def join(own):
    other = swap(own, "ch", 1)
    core = lax.axis_index("ch")
    return jnp.concatenate(
        [jnp.where(core == 0, own, other), jnp.where(core == 0, other, own)], axis=0
    )


def tokens_out(partial, half):
    width = partial.shape[1]
    groups = lax.axis_size("seq") // INNER
    outer = lax.axis_index("seq") // INNER
    core = lax.axis_index("ch")
    parts = partial.reshape(groups, 2, half, width)
    theirs = pick(parts, 1 - core, 1).astype(BF16)
    summed = (pick(parts, core, 1).astype(F32) + swap(theirs, "ch", 1).astype(F32)).astype(BF16)
    total = pick(summed, outer).astype(F32)
    for step in range(1, groups):
        total = total + swap(pick(summed, outer ^ step), "seq", step * INNER).astype(F32)
    return total


def feed_forward_parts(n_two, column, near, all_cot, resid, ffn_gain, cot_half):
    f32, bf16 = F32, BF16
    _, groups, depth, units = column.shape
    half_rows, model = n_two.shape
    tok_rows = 2 * half_rows
    _, norm_back_two = jax.vjp(scaled_norm, resid, ffn_gain)
    all_two, *full_ffn = gather_tokens(n_two, column, near)
    all_two, all_cot = (v.reshape(groups * tok_rows, model) for v in (all_two, all_cot))
    full_ffn = [w.reshape(model, units) for w in full_ffn]
    gate_pre = jnp.dot(all_two, full_ffn[0], preferred_element_type=f32)
    up_pre = jnp.dot(all_two, full_ffn[1], preferred_element_type=f32)
    gate_act, gelu_back_gate = jax.vjp(gelu_tanh, gate_pre)
    hidden = (gate_act * up_pre).astype(bf16)
    ffn_term = jnp.einsum("tf,df->td", hidden, full_ffn[2], preferred_element_type=f32).astype(bf16)
    d_hidden = jnp.einsum("td,df->tf", all_cot, full_ffn[2], preferred_element_type=f32)
    d_gate = gelu_back_gate(d_hidden * up_pre)[0].astype(bf16)
    d_up = (d_hidden * gate_act).astype(bf16)
    d_n_two = (
        jnp.einsum("tf,df->td", d_gate, full_ffn[0], preferred_element_type=f32)
        + jnp.einsum("tf,df->td", d_up, full_ffn[1], preferred_element_type=f32)
    ).astype(bf16)
    terms = [
        jnp.einsum("td,tf->df", left, right, preferred_element_type=f32)
        .astype(bf16)
        .reshape(groups, INNER, depth, units)
        for left, right in ((all_two, d_gate), (all_two, d_up), (all_cot, hidden))
    ]
    split = [v.reshape(groups, 2, half_rows, model) for v in (d_n_two, ffn_term)]
    if groups <= 4:
        d_n_two, ffn_out, far = reduce_tokens(split, terms)
    else:
        d_n_two, far = reduce_tokens(split[:1], terms)
        ffn_out = tokens_out(ffn_term, half_rows)
    block_half = (resid + ffn_out).astype(bf16)
    inner = lax.axis_index("seq") % INNER
    by_half = [t.reshape(2, groups // 2, INNER, depth, units) for t in terms]

    def block_at(h, place):
        return jnp.stack([pick(t[h], place, 1) for t in by_half]).astype(f32)

    mine = jnp.stack(
        [(block_at(h, inner) + far[h, 0].astype(f32)).astype(bf16) for h in range(2)]
    )
    halves = jnp.stack(
        [(block_at(h, inner ^ (1, 2)[h]) + far[h, 1].astype(f32)).astype(bf16) for h in range(2)]
    )
    d_resid_norm, d_ffn_gain_term = norm_back_two(d_n_two)
    d_resid = cot_half.astype(f32) + d_resid_norm
    d_mixed = join(d_resid.astype(bf16))
    return block_half, d_resid, d_mixed, d_ffn_gain_term.reshape(1, model), halves, mine


def shards(
    inputs,
    norm_gain,
    branch_weight,
    input_weight,
    channel_params,
    gate_x_blocks,
    gate_a_blocks,
    out_weight,
    ffn_gain,
    ffn_gate,
    ffn_up,
    ffn_down,
    cotangent,
):
    f32 = F32
    bf16 = BF16
    n = lax.axis_size("seq")
    tok_rows, model = inputs.shape
    half_rows = tok_rows // 2
    heads, part, size = gate_x_blocks.shape
    width = heads * size
    depth = ffn_gate.shape[0]
    groups = n // INNER
    hidden_units = ffn_gate.shape[1]
    units = -(-hidden_units // (groups * 128)) * 128
    x_float = inputs.astype(f32)
    n_one = scaled_norm(x_float, norm_gain).astype(bf16)
    x_half = my_half(inputs)

    gate_pack = jnp.stack([gate_x_blocks, gate_a_blocks])
    ffn_pack = jnp.pad(
        jnp.stack([ffn_gate, ffn_up, ffn_down.T]), ((0, 0), (0, 0), (0, groups * units - hidden_units))
    )
    *full_mixer, full_gates, column = gather_weights(
        [input_weight, branch_weight, out_weight.T], gate_pack, ffn_pack
    )
    full_mixer = [w.reshape(model, width) for w in full_mixer]
    gates = full_gates.reshape(2, heads, size, size)
    par = jnp.concatenate(
        [
            channel_params,
            jax.nn.softplus(channel_params[7:8]),
            jax.nn.sigmoid(channel_params[7:8]),
            jnp.zeros((6, width), f32),
        ],
        axis=0,
    )

    cot_half = my_half(cotangent)

    x_branch, y_pre, conv_out, states, branch_out, edge, resid, n_two, near, all_cot = mixer_forward(
        n_one,
        full_mixer,
        gates,
        par,
        x_half,
        ffn_gain.reshape(1, model),
        column,
        cot_half,
    )
    if groups <= 4 and depth % 16 == 0:
        block_half, d_resid, d_mixed, d_ffn_gain_term, halves, mine, _ = feed_forward(
            n_two, column, near, all_cot, resid, ffn_gain.reshape(1, model)
        )
        d_mixed = d_mixed.reshape(tok_rows, model)
    else:
        block_half, d_resid, d_mixed, d_ffn_gain_term, halves, mine = feed_forward_parts(
            n_two, column, near, all_cot, resid, ffn_gain, cot_half
        )
    block_out = join(block_half)
    d_y, d_xb, d_gates, d_par, d_inputs, d_norm_gain_term, near_back = mixer_backward(
        d_mixed,
        full_mixer,
        x_half,
        norm_gain.reshape(1, model),
        d_resid,
        y_pre,
        states,
        edge,
        conv_out,
        x_branch,
        gates,
        par,
        halves,
    )
    column_back = jnp.concatenate(
        [
            (mine[h].astype(f32) + near_back[h].astype(f32)).astype(bf16) for h in range(2)
        ],
        axis=1,
    )
    d_inputs = join(d_inputs)
    gain_rows = model // width
    scattered, small, spread = scatter_mixer(
        n_one.T.reshape(n, depth, tok_rows),
        d_mixed.T.reshape(n, depth, tok_rows),
        d_y,
        d_xb,
        branch_out,
        d_gates,
        d_par,
        d_norm_gain_term,
        d_ffn_gain_term,
        column_back,
    )
    ffn_grads = [spread[kind, :, :hidden_units].astype(f32) for kind in range(3)]
    d_gate_pair = scattered[3 * depth :].reshape(2, part, heads, size).transpose(0, 2, 1, 3)
    return (
        block_out,
        d_inputs,
        small[8 : 8 + gain_rows].reshape(model),
        scattered[:depth],
        scattered[depth : 2 * depth],
        small[:8],
        d_gate_pair[0],
        d_gate_pair[1],
        scattered[2 * depth : 3 * depth].T,
        small[8 + gain_rows : 8 + 2 * gain_rows].reshape(model),
        ffn_grads[0],
        ffn_grads[1],
        ffn_grads[2].T,
    )


def solution(mesh):
    placed = (
        P("seq", None),
        P(),
        P("seq", "ch"),
        P("seq", "ch"),
        P(None, "ch"),
        P("ch", "seq", None),
        P("ch", "seq", None),
        P("ch", "seq"),
        P(),
        P("seq", "ch"),
        P("seq", "ch"),
        P("ch", "seq"),
        P("seq", None),
    )
    return jax.shard_map(
        shards,
        mesh=mesh,
        in_specs=placed,
        out_specs=(
            P("seq", None),
            P("seq", None),
            P(),
            P("seq", "ch"),
            P("seq", "ch"),
            P(None, "ch"),
            P("ch", "seq", None),
            P("ch", "seq", None),
            P("ch", "seq"),
            P(),
            P("seq", "ch"),
            P("seq", "ch"),
            P("ch", "seq"),
        ),
        check_vma=False,
    )
```

```python
import functools

import jax
import jax.numpy as jnp
from jax import lax
from jax.experimental import pallas as pl
from jax.experimental.pallas import tpu as pltpu
from jax.sharding import PartitionSpec as P

F32 = jnp.float32
BF16 = jnp.bfloat16
INNER = 4
MESH = pl.DeviceIdType.MESH
VMEM = pl.BlockSpec(memory_space=pltpu.VMEM)
ANY = pl.BlockSpec(memory_space=pl.ANY)
HBM = pl.BlockSpec(memory_space=pltpu.HBM)


def swap(value, axis, mask):
    return lax.ppermute(value, axis, [(i, i ^ mask) for i in range(lax.axis_size(axis))])


def pick(array, index, axis=0):
    return lax.dynamic_index_in_dim(array, index, axis, False)


def put(array, block, index, axis=0):
    return lax.dynamic_update_index_in_dim(array, block, index, axis)


def scaled_norm(values, gain):
    return values * lax.rsqrt(jnp.mean(values * values, axis=-1, keepdims=True) + 1e-06) * gain


def gelu_tanh(values):
    return jax.nn.gelu(values, approximate=True)


def whereabouts():
    me = lax.axis_index("seq")
    outer = me // INNER
    inner = me - outer * INNER
    y = inner // 2
    x = inner - 2 * y
    by_x = me + 1 - 2 * x
    by_y = me + 2 - 4 * y
    return me, outer, by_x, by_y, by_x + 2 - 4 * y


def when(condition, action):
    if condition is None:
        action()
    else:
        pl.when(condition)(action)


def both(one, other):
    if one is None or other is None:
        return one if other is None else other
    return jnp.logical_and(one, other)


def greet(peers):
    barrier = pltpu.get_barrier_semaphore()
    for condition, peer in peers:
        when(
            condition,
            lambda peer=peer: pl.semaphore_signal(
                barrier, inc=1, device_id={"seq": peer}, device_id_type=MESH
            ),
        )
    count = 0
    for condition, _ in peers:
        count = count + (1 if condition is None else condition.astype(jnp.int32))
    pl.semaphore_wait(barrier, count)


def greet_all(n, me, sibling=False):
    barrier = pltpu.get_barrier_semaphore()

    def hello(step, carry):
        pl.semaphore_signal(
            barrier, inc=1, device_id={"seq": lax.rem(me + step, n)}, device_id_type=MESH
        )
        return carry

    lax.fori_loop(1, n, hello, 0)
    if sibling:
        pl.semaphore_signal(
            barrier, inc=1, device_id={"ch": 1 - lax.axis_index("ch")}, device_id_type=MESH
        )
    pl.semaphore_wait(barrier, n if sibling else n - 1)


def remote(src, dst, send_sem, recv_sem, place):
    return pltpu.make_async_remote_copy(
        src_ref=src,
        dst_ref=dst,
        send_sem=send_sem,
        recv_sem=recv_sem,
        device_id={"seq": place},
        device_id_type=MESH,
    )


def params(collective_id, mib):
    return pltpu.CompilerParams(
        collective_id=collective_id, has_side_effects=True, vmem_limit_bytes=mib * 2**20
    )


def gather_body(n, *refs):
    w_refs, g_ref, f_ref = refs[:3], refs[3], refs[4]
    wo_refs, go_ref, column_ref = refs[5:8], refs[8], refs[9]
    send_m, recv_m, send_f, recv_f, here = refs[10:]
    groups = n // INNER
    me, outer, by_x, by_y, by_xy = whereabouts()
    above, below = outer + 1 < groups, outer > 0
    barrier = pltpu.get_barrier_semaphore()

    def hello(peer):
        pl.semaphore_signal(barrier, inc=1, device_id={"seq": peer}, device_id_type=MESH)

    hello(by_x)
    hello(by_y)

    def column_peer(turn):
        return lax.rem(outer + turn, groups)

    def hello_column(turn, carry):
        hello(me + (column_peer(turn) - outer) * INNER)
        return carry

    lax.fori_loop(1, groups, hello_column, 0)
    pl.semaphore_wait(barrier, groups + 1)
    units = column_ref.shape[3]
    half = w_refs[0].shape[1] // 2

    def units_of(place):
        return pl.ds(pl.multiple_of(place * units, units), units)

    keep = [
        pltpu.make_async_copy(w_refs[kind], wo_refs[kind].at[me], here.at[kind])
        for kind in range(3)
    ]
    keep.append(pltpu.make_async_copy(g_ref, go_ref.at[:, :, me], here.at[3]))
    keep.append(
        pltpu.make_async_copy(
            f_ref.at[:, :, units_of(outer)], column_ref.at[:, outer], here.at[4]
        )
    )
    for copy in keep:
        copy.start()
    sent = []

    def copies(h, source, way, target, own):
        cols = pl.ds(h * half, half)
        pairs = [
            (w_refs[kind].at[:, cols], wo_refs[kind].at[source, :, cols]) for kind in range(3)
        ]
        pairs.append((g_ref.at[h], go_ref.at[h, :, source]))
        return [
            remote(
                given if own else dst,
                dst,
                send_m.at[kind, h, source, way],
                recv_m.at[kind, h, source],
                target,
            )
            for kind, (given, dst) in enumerate(pairs)
        ]

    def send(condition, *what):
        def go():
            for copy in copies(*what):
                copy.start()

        when(condition, go)
        sent.append((condition, what))

    def arrive(condition, h, source):
        def go():
            for copy in copies(h, source, 0, by_x, False):
                copy.wait_recv()

        when(condition, go)

    def exchange(turn, receive):
        place = lax.rem(outer + groups - turn, groups) if receive else column_peer(turn)
        target = me + (place - outer) * INNER
        return remote(
            f_ref.at[:, :, units_of(place)],
            column_ref.at[:, place if receive else outer],
            send_f.at[turn],
            recv_f.at[turn],
            target,
        )

    def each_turn(action):
        def one(turn, carry):
            action(turn)
            return carry

        lax.fori_loop(1, groups, one, 0)

    for step in range(groups):
        for h in range(2):
            flip_p, flip_q = (by_x, by_y) if h == 0 else (by_y, by_x)
            if step == 0:
                send(above, h, me, 0, me + INNER, True)
                send(below, h, me, 1, me - INNER, True)
                send(None, h, me, 2, flip_p, True)
                send(None, h, me, 3, flip_q, True)
                continue
            for source, there, onward, way, to in (
                (me - step * INNER, outer >= step, above, 0, me + INNER),
                (me + step * INNER, outer + step < groups, below, 1, me - INNER),
            ):
                arrive(there, h, source)
                send(both(there, onward), h, source, way, to, False)
                send(there, h, source, 2, flip_p, False)
                send(there, h, source, 3, flip_q, False)
    each_turn(lambda turn: exchange(turn, False).start())
    for step in range(groups):
        for h in range(2):
            flip_p, flip_q = (by_x, by_y) if h == 0 else (by_y, by_x)
            if step == 0:
                arrive(None, h, flip_p)
                send(None, h, flip_p, 3, flip_q, False)
                continue
            for source, there in (
                (flip_p - step * INNER, outer >= step),
                (flip_p + step * INNER, outer + step < groups),
            ):
                arrive(there, h, source)
                send(there, h, source, 3, flip_q, False)
    for place in range(groups):
        shift = (place - outer) * INNER
        for h in range(2):
            arrive(None, h, (by_y if h == 0 else by_x) + shift)
            arrive(None, h, by_xy + shift)
    each_turn(lambda turn: exchange(turn, True).wait_recv())
    for condition, what in sent:

        def finish(what=what):
            for copy in copies(*what):
                copy.wait_send()

        when(condition, finish)
    each_turn(lambda turn: exchange(turn, False).wait_send())
    for copy in keep:
        copy.wait()


def gather_weights(weights, gates, ffn):
    n = lax.axis_size("seq")
    groups = n // INNER
    kinds, rows, padded = ffn.shape
    dma = pltpu.SemaphoreType.DMA
    made = [jax.ShapeDtypeStruct((n,) + w.shape, w.dtype) for w in weights]
    made.append(jax.ShapeDtypeStruct(gates.shape[:2] + (n,) + gates.shape[2:], gates.dtype))
    made.append(jax.ShapeDtypeStruct((kinds, groups, rows, padded // groups), ffn.dtype))
    return pl.pallas_call(
        functools.partial(gather_body, n),
        out_shape=tuple(made),
        in_specs=[HBM] * 5,
        out_specs=(HBM,) * 5,
        scratch_shapes=[
            dma((4, 2, n, 4)),
            dma((4, 2, n)),
            dma((groups,)),
            dma((groups,)),
            dma((5,)),
        ],
        compiler_params=params(1, 16),
        name="gather_weights",
    )(*weights, gates, ffn)


def far_first(groups, outer, turn):
    def order(at):
        alone = groups - 1 - 2 * at
        later = turn - alone
        step = later // 2
        return jnp.where(
            turn < alone, groups - 1 - turn, jnp.where(later - 2 * step == 0, step, 2 * at - step)
        )

    return jnp.where(
        outer < groups // 2, order(outer), groups - 1 - order(groups - 1 - outer)
    )


class Chain:
    def __init__(self, n, own, whole, send, recv_z, recv_c):
        me = lax.axis_index("seq")
        self.groups = n // INNER
        self.outer = outer = me // INNER
        self.core = lax.axis_index("ch")
        self.above, self.below = outer + 1 < self.groups, outer > 0
        self.sibling = {"ch": 1 - self.core}
        self.to = ({"seq": me + INNER}, {"seq": me - INNER}, self.sibling)
        self.own, self.whole = own, whole
        self.send, self.recv_z, self.recv_c = send, recv_z, recv_c

    def copy(self, source, way, own=False):
        dst = self.whole.at[source, self.core]
        return pltpu.make_async_remote_copy(
            src_ref=self.own if own else dst,
            dst_ref=dst,
            send_sem=self.send.at[source, way],
            recv_sem=(self.recv_c if way == 2 else self.recv_z).at[source],
            device_id=self.to[way],
            device_id_type=MESH,
        )

    def from_sibling(self, source):
        return pltpu.make_async_remote_copy(
            src_ref=self.own,
            dst_ref=self.whole.at[source, 1 - self.core],
            send_sem=self.send.at[source, 2],
            recv_sem=self.recv_c.at[source],
            device_id=self.sibling,
            device_id_type=MESH,
        )

    def keep(self, sem):
        return pltpu.make_async_copy(self.own, self.whole.at[self.outer, self.core], sem)

    def ways(self, step):
        return (
            (self.outer - step, self.outer >= step, self.above, 0),
            (self.outer + step, self.outer + step < self.groups, self.below, 1),
        )

    def start(self):
        pl.when(self.above)(self.copy(self.outer, 0, True).start)
        pl.when(self.below)(self.copy(self.outer, 1, True).start)
        self.copy(self.outer, 2, True).start()

    def step(self, step):
        for source, there, onward, way in self.ways(step):
            pl.when(there)(self.copy(source, way).wait_recv)
            pl.when(both(there, onward))(self.copy(source, way).start)
            pl.when(there)(self.copy(source, 2).start)

    def finish(self):
        for source in range(self.groups):
            self.from_sibling(source).wait_recv()
        pl.when(self.above)(self.copy(self.outer, 0, True).wait_send)
        pl.when(self.below)(self.copy(self.outer, 1, True).wait_send)
        self.copy(self.outer, 2, True).wait_send()
        for step in range(1, self.groups):
            for source, there, onward, way in self.ways(step):
                pl.when(both(there, onward))(self.copy(source, way).wait_send)
                pl.when(there)(self.copy(source, 2).wait_send)


def chain_semaphores(groups):
    dma = pltpu.SemaphoreType.DMA
    return [dma((groups, 3)), dma((groups,)), dma((groups,))]


def tokens_body(n, *refs):
    own_ref, column_ref, near_ref = refs[:3]
    all_ref, w_refs = refs[3], refs[4:7]
    send_t, recv_z, recv_c, send_w, recv_w, here = refs[7:]
    groups = n // INNER
    half = groups // 2
    me, outer, by_x, by_y, by_xy = whereabouts()
    base = outer * INNER
    core = lax.axis_index("ch")
    above, below = outer + 1 < groups, outer > 0
    sibling = {"ch": 1 - core}
    barrier = pltpu.get_barrier_semaphore()

    def hello(peer):
        pl.semaphore_signal(barrier, inc=1, device_id=peer, device_id_type=MESH)

    hello({"seq": by_x})
    hello({"seq": by_y})
    hello(sibling)
    pl.when(above)(lambda: hello({"seq": me + INNER}))
    pl.when(below)(lambda: hello({"seq": me - INNER}))
    pl.semaphore_wait(barrier, 3 + above.astype(jnp.int32) + below.astype(jnp.int32))

    chain = Chain(n, own_ref, all_ref, send_t, recv_z, recv_c)

    def part(h):
        return pl.ds(h * half, half)

    flips = ((by_x, by_y), (by_y, by_x))

    def weight_copy(kind, h, far, receive=False):
        source = flips[h][0] if far else me
        if receive:
            source = by_xy if far else flips[h][1]
        return remote(
            near_ref.at[h, kind] if far else column_ref.at[kind, part(h)],
            w_refs[kind].at[part(h), source - base],
            send_w.at[kind, h, far],
            recv_w.at[kind, h, far],
            flips[h][1],
        )

    keep = [chain.keep(here.at[0])]
    for kind in range(3):
        keep.append(
            pltpu.make_async_copy(
                column_ref.at[kind], w_refs[kind].at[:, me - base], here.at[1 + kind]
            )
        )
        for h in range(2):
            keep.append(
                pltpu.make_async_copy(
                    near_ref.at[h, kind],
                    w_refs[kind].at[part(h), flips[h][0] - base],
                    here.at[4 + 2 * kind + h],
                )
            )
    every_w = [(kind, h, far) for kind in range(3) for h in range(2) for far in range(2)]

    chain.start()
    for what in every_w:
        weight_copy(*what).start()
    for copy in keep:
        copy.start()
    for step in range(1, groups):
        chain.step(step)
    for what in every_w:
        weight_copy(*what, receive=True).wait_recv()
    chain.finish()
    for what in every_w:
        weight_copy(*what).wait_send()
    for copy in keep:
        copy.wait()


def gather_tokens(tokens, column, near):
    n = lax.axis_size("seq")
    groups = n // INNER
    kinds, _, rows, units = column.shape
    dma = pltpu.SemaphoreType.DMA
    wide = jax.ShapeDtypeStruct((groups, 2) + tokens.shape, tokens.dtype)
    weight = jax.ShapeDtypeStruct((groups, INNER, rows, units), column.dtype)
    return pl.pallas_call(
        functools.partial(tokens_body, n),
        out_shape=(wide, weight, weight, weight),
        in_specs=[ANY] * 3,
        out_specs=(ANY,) * 4,
        scratch_shapes=chain_semaphores(groups)
        + [dma((kinds, 2, 2)), dma((kinds, 2, 2)), dma((10,))],
        compiler_params=params(6, 16),
        name="gather_tokens",
    )(tokens, column, near)


def reduce_body(n, kinds, *refs):
    p_refs, t_refs = refs[:kinds], refs[kinds : kinds + 3]
    out_refs, far_ref = refs[kinds + 3 : 2 * kinds + 3], refs[2 * kinds + 3]
    summed, got, send_c, recv_c, send_z, recv_z, send_f, recv_f = refs[2 * kinds + 4 :]
    groups = n // INNER
    half = groups // 2
    me, outer, by_x, by_y, by_xy = whereabouts()
    base = outer * INNER
    core = lax.axis_index("ch")
    above, below = outer + 1 < groups, outer > 0
    sibling = {"ch": 1 - core}
    barrier = pltpu.get_barrier_semaphore()

    def hello(peer):
        pl.semaphore_signal(barrier, inc=1, device_id=peer, device_id_type=MESH)

    hello({"seq": by_x})
    hello({"seq": by_y})
    hello(sibling)
    pl.when(above)(lambda: hello({"seq": me + INNER}))
    pl.when(below)(lambda: hello({"seq": me - INNER}))
    pl.semaphore_wait(barrier, 3 + above.astype(jnp.int32) + below.astype(jnp.int32))
    flips = ((by_x, by_y), (by_y, by_x))

    def gradient_copy(kind, h, far):
        source = by_xy if far else flips[h][1]
        return remote(
            t_refs[kind].at[pl.ds(h * half, half), source - base],
            far_ref.at[h, far, kind],
            send_f.at[kind, h, far],
            recv_f.at[kind, h, far],
            flips[h][1],
        )

    def to_sibling(kind, place):
        return pltpu.make_async_remote_copy(
            src_ref=p_refs[kind].at[place, 1 - core],
            dst_ref=summed.at[kind, place],
            send_sem=send_c.at[kind, place],
            recv_sem=recv_c.at[kind, place],
            device_id=sibling,
            device_id_type=MESH,
        )

    def along(kind, place, up):
        last = place == (outer + 1 if up else outer - 1)
        slot = place if up else jnp.where(last, groups, place)
        return remote(
            summed.at[kind, place],
            got.at[kind, slot],
            send_z.at[kind, place],
            recv_z.at[kind, slot],
            me + (INNER if up else -INNER),
        )

    def landed(kind, slot):
        return remote(
            summed.at[kind, 0], got.at[kind, slot], send_z.at[kind, 0], recv_z.at[kind, slot], by_x
        )

    def each(limit, action):
        def one(turn, carry):
            action(turn)
            return carry

        lax.fori_loop(0, limit, one, 0)

    every_f = [(kind, h, far) for far in (1, 0) for kind in range(3) for h in range(2)]
    for kind in range(kinds):
        each(groups, lambda place, kind=kind: to_sibling(kind, place).start())
    for what in every_f:
        gradient_copy(*what).start()

    tall = summed.shape[2]
    chunk = 16

    def rows_of(at):
        return pl.ds(pl.multiple_of(at * chunk, chunk), chunk)

    def ready(kind, place, incoming):
        to_sibling(kind, place).wait_recv()

        def local(at):
            r = rows_of(at)
            summed[kind, place, r] = (
                summed[kind, place, r].astype(F32) + p_refs[kind][place, core, r].astype(F32)
            ).astype(BF16)

        def more(at):
            r = rows_of(at)
            summed[kind, place, r] = (
                summed[kind, place, r].astype(F32)
                + p_refs[kind][place, core, r].astype(F32)
                + got[kind, place, r].astype(F32)
            ).astype(BF16)

        @pl.when(incoming)
        def _():
            landed(kind, place).wait_recv()
            each(tall // chunk, more)

        @pl.when(jnp.logical_not(incoming))
        def _():
            each(tall // chunk, local)

    for kind in range(kinds):

        def climb(turn, kind=kind):
            place = groups - 1 - turn

            @pl.when(place > outer)
            def _():
                ready(kind, place, below)
                along(kind, place, True).start()

        def sink(turn, kind=kind):
            place = turn

            @pl.when(place < outer)
            def _():
                ready(kind, place, above)
                along(kind, place, False).start()

        def turns(turn):
            @pl.when(outer < half)
            def _():
                climb(turn)
                sink(turn)

            @pl.when(outer >= half)
            def _():
                sink(turn)
                climb(turn)

        each(groups - 1, turns)
    for kind in range(kinds):
        to_sibling(kind, outer).wait_recv()

        def own(at, kind=kind):
            r = rows_of(at)
            out_refs[kind][r] = summed[kind, outer, r].astype(F32) + p_refs[kind][
                outer, core, r
            ].astype(F32)

        each(tall // chunk, own)
        for there, slot in ((below, outer), (above, groups)):

            @pl.when(there)
            def _():
                landed(kind, slot).wait_recv()

                def plus(at):
                    r = rows_of(at)
                    out_refs[kind][r] = out_refs[kind][r] + got[kind, slot, r].astype(F32)

                each(tall // chunk, plus)

    for kind in range(kinds):

        def clear(place, kind=kind):
            to_sibling(kind, place).wait_send()

            @pl.when(place > outer)
            def _():
                along(kind, place, True).wait_send()

            @pl.when(place < outer)
            def _():
                along(kind, place, False).wait_send()

        each(groups, clear)
    for what in every_f:
        gradient_copy(*what).wait()


def reduce_tokens(partials, gradients):
    n = lax.axis_size("seq")
    groups = n // INNER
    kinds = len(partials)
    _, _, tall, width = partials[0].shape
    _, _, rows, units = gradients[0].shape
    dma = pltpu.SemaphoreType.DMA
    return pl.pallas_call(
        functools.partial(reduce_body, n, kinds),
        out_shape=(jax.ShapeDtypeStruct((tall, width), F32),) * kinds
        + (jax.ShapeDtypeStruct((2, 2, 3, groups // 2, rows, units), BF16),),
        in_specs=[VMEM] * kinds + [ANY] * 3,
        out_specs=(VMEM,) * kinds + (ANY,),
        scratch_shapes=[
            pltpu.VMEM((kinds, groups, tall, width), BF16),
            pltpu.VMEM((kinds, groups + 1, tall, width), BF16),
            dma((kinds, groups)),
            dma((kinds, groups)),
            dma((kinds, groups)),
            dma((kinds, groups + 1)),
            dma((3, 2, 2)),
            dma((3, 2, 2)),
        ],
        compiler_params=params(7, 60),
        name="reduce_tokens",
    )(*partials, *gradients)


def scatter_body(
    n,
    one_ref,
    mixed_ref,
    dy_ref,
    dxb_ref,
    branch_ref,
    gate_ref,
    dpar_ref,
    gain_one_ref,
    gain_two_ref,
    column_ref,
    out_ref,
    small_out,
    spread_ref,
    made,
    got_q,
    got_p,
    got_z,
    got_s,
    *sems,
):
    send_q, recv_q, send_p, recv_p, send_z, recv_z, send_s, recv_s, send_f, recv_f, here = sems
    groups = n // INNER
    me, outer, by_x, by_y, by_xy = whereabouts()
    rows = one_ref.shape[1]
    part_rows = gate_ref.shape[2]
    total, width = out_ref.shape
    half = width // 2

    def place_of(turn):
        return far_first(groups, outer, turn)

    def base_of(turn):
        return (place_of(turn) - outer) * INNER

    barrier = pltpu.get_barrier_semaphore()

    def hello(peer):
        pl.semaphore_signal(barrier, inc=1, device_id={"seq": peer}, device_id_type=MESH)

    hello(by_x)
    hello(by_y)

    def hello_outer(turn, carry):
        hello(me + base_of(turn))
        return carry

    lax.fori_loop(0, groups - 1, hello_outer, 0)
    core = lax.axis_index("ch")
    masks = [1 << bit for bit in range(n.bit_length() - 1)]
    pl.semaphore_signal(barrier, inc=1, device_id={"ch": 1 - core}, device_id_type=MESH)
    pl.semaphore_wait(barrier, groups + 2)

    flips = ((by_x, by_y), (by_y, by_x))
    units = column_ref.shape[3]

    def units_of(place):
        return pl.ds(pl.multiple_of(place * units, units), units)

    def exchange(turn, receive=False):
        place = lax.rem(outer + (groups - 1 - turn if receive else turn + 1), groups)
        return remote(
            column_ref.at[:, place],
            spread_ref.at[:, :, units_of(place if receive else outer)],
            send_f.at[turn],
            recv_f.at[turn],
            me + (place - outer) * INNER,
        )

    def small(turn):
        place = me
        for at, mask in enumerate(masks):
            flipped = me + mask * (1 - 2 * lax.rem(me // mask, 2))
            place = jnp.where(turn == at, flipped, place)
        other = jnp.where(turn == len(masks), 1 - core, core)
        return pltpu.make_async_remote_copy(
            src_ref=small_out,
            dst_ref=got_s.at[turn],
            send_sem=send_s.at[turn],
            recv_sem=recv_s.at[turn],
            device_id=(place, other),
            device_id_type=MESH,
        )

    small_out[:8] = dpar_ref[...]
    small_out[8:] = jnp.zeros((8, width), F32)
    at = 8
    for gain_ref in (gain_one_ref, gain_two_ref):
        for start in range(0, gain_ref.shape[1], width):
            small_out[at : at + 1] = gain_ref[:, start : start + width]
            at += 1
    small_row = lax.broadcasted_iota(jnp.int32, small_out.shape, 0)

    def cols(h):
        return pl.ds(h * half, half)

    def along_q(turn, h, other):
        source = (by_xy if other else flips[h][1]) + base_of(turn)
        return remote(
            made.at[source, :, cols(h)],
            got_q.at[h, turn, other],
            send_q.at[h, turn, other],
            recv_q.at[h, turn, other],
            flips[h][1],
        )

    def along_p(turn, h):
        return remote(
            made.at[flips[h][0] + base_of(turn), :, cols(h)],
            got_p.at[h, turn],
            send_p.at[h, turn],
            recv_p.at[h, turn],
            flips[h][0],
        )

    def along_z(turn, h):
        place = place_of(turn)
        up = place > outer
        onto = jnp.where(up, outer + 1, outer - 1)
        slot = jnp.where(jnp.logical_and(place == onto, jnp.logical_not(up)), groups, place)
        return remote(
            made.at[me + base_of(turn), :, cols(h)],
            got_z.at[h, slot],
            send_z.at[h, turn],
            recv_z.at[h, slot],
            me + (onto - outer) * INNER,
        )

    def landed(slot, h):
        return remote(
            made.at[me, :, cols(h)], got_z.at[h, slot], send_z.at[h, 0], recv_z.at[h, slot], by_x
        )

    def has_incoming(turn):
        return jnp.where(place_of(turn) > outer, outer > 0, outer < groups - 1)

    def pass_on(turn):
        incoming = has_incoming(turn)
        for h in range(2):

            @pl.when(incoming)
            def _():
                landed(place_of(turn), h).wait_recv()
                add(me + base_of(turn), h, got_z, (h, place_of(turn)))

            along_z(turn, h).start()

    def make(block):
        left = one_ref[block]
        parts = [
            jnp.dot(left, dy_ref[...], preferred_element_type=F32),
            jnp.dot(left, dxb_ref[...], preferred_element_type=F32),
            jnp.dot(mixed_ref[block], branch_ref[...], preferred_element_type=F32),
        ]
        if rows % 16 == 0:
            for at, part in enumerate(parts):
                made[block, at * rows : (at + 1) * rows] = part.astype(BF16)
            for gate in range(2):
                at = 3 * rows + gate * part_rows
                made[block, at : at + part_rows] = gate_ref[block, gate]
        else:
            parts.extend(gate_ref[block, gate].astype(F32) for gate in range(2))
            made[block] = jnp.concatenate(parts, axis=0).astype(BF16)

    step = 32

    def add(block, h, ref, index):
        def one(at, carry):
            r = pl.ds(pl.multiple_of(at * step, step), step)
            made[block, r, cols(h)] = (
                made[block, r, cols(h)].astype(F32) + ref[index + (r,)].astype(F32)
            ).astype(BF16)
            return carry

        lax.fori_loop(0, total // step, one, 0)

    keep = pltpu.make_async_copy(
        column_ref.at[:, outer], spread_ref.at[:, :, units_of(outer)], here
    )
    keep.start()

    def begin(turn, other):
        base = base_of(turn)
        if other:
            make(by_xy + base)
        else:
            for h in range(2):
                make(flips[h][1] + base)
        for h in range(2):
            along_q(turn, h, other).start()

    begin(0, 1)
    begin(0, 0)
    make(me + base_of(0))

    def turn_of(turn, carry):
        pl.when(turn <= len(masks))(lambda: small(turn).start())
        pl.when(turn < groups - 1)(lambda: exchange(turn).start())

        @pl.when(turn < groups)
        def _():
            base = base_of(turn)
            for h in range(2):
                along_q(turn, h, 1).wait_recv()
                add(flips[h][0] + base, h, got_q, (h, turn, 1))
                along_p(turn, h).start()
            pl.when(turn < groups - 1)(lambda: begin(turn + 1, 1))
            for h in range(2):
                along_q(turn, h, 0).wait_recv()
                add(me + base, h, got_q, (h, turn, 0))

            @pl.when(turn < groups - 1)
            def _():
                begin(turn + 1, 0)
                make(me + base_of(turn + 1))

            for h in range(2):
                along_p(turn, h).wait_recv()
                add(me + base, h, got_p, (h, turn))

            @pl.when(jnp.logical_and(turn < groups - 1, jnp.logical_not(has_incoming(turn))))
            def _():
                pass_on(turn)

            @pl.when(jnp.logical_and(turn >= 1, turn < groups - 1))
            def _():
                pl.when(has_incoming(turn - 1))(lambda: pass_on(turn - 1))

            @pl.when(jnp.logical_and(turn == groups - 2, has_incoming(turn)))
            def _():
                pass_on(turn)

        @pl.when(turn <= len(masks))
        def _():
            small(turn).wait()
            counts = jnp.logical_or(turn < len(masks), small_row >= 8)
            small_out[...] = small_out[...] + jnp.where(counts, got_s[turn], 0.0)

        return carry

    assert len(masks) < groups + 2
    lax.fori_loop(0, groups + 2, turn_of, 0)
    for condition, slots in (
        (jnp.logical_and(outer > 0, outer < groups - 1), (outer, groups)),
        (outer == groups - 1, (outer,)),
        (outer == 0, (groups,)),
    ):

        @pl.when(condition)
        def _(slots=slots):
            for h in range(2):
                for slot in slots:
                    landed(slot, h).wait_recv()

                def finish(at, carry):
                    r = pl.ds(pl.multiple_of(at * step, step), step)
                    value = made[me, r, cols(h)].astype(F32)
                    for slot in slots:
                        value = value + got_z[h, slot, r].astype(F32)
                    out_ref[r, cols(h)] = value
                    return carry

                lax.fori_loop(0, total // step, finish, 0)

    def clear(turn, carry):
        for h in range(2):
            along_q(turn, h, 0).wait_send()
            along_q(turn, h, 1).wait_send()
            along_p(turn, h).wait_send()

            @pl.when(turn < groups - 1)
            def _():
                along_z(turn, h).wait_send()

        @pl.when(turn < groups - 1)
        def _():
            exchange(turn, True).wait_recv()
            exchange(turn).wait_send()

        return carry

    lax.fori_loop(0, groups, clear, 0)
    keep.wait()


def scatter_mixer(one, mixed, dy, dxb, branch, gates, dpar, gain_one, gain_two, column):
    n, rows, _ = one.shape
    groups = n // INNER
    width = dy.shape[1]
    total = 3 * rows + 2 * gates.shape[2]
    kinds, _, _, units = column.shape
    turns = n.bit_length()
    dma = pltpu.SemaphoreType.DMA
    return pl.pallas_call(
        functools.partial(scatter_body, n),
        out_shape=(
            jax.ShapeDtypeStruct((total, width), F32),
            jax.ShapeDtypeStruct((16, width), F32),
            jax.ShapeDtypeStruct((kinds, rows, groups * units), BF16),
        ),
        in_specs=[VMEM] * 9 + [ANY],
        out_specs=(VMEM, VMEM, ANY),
        scratch_shapes=[
            pltpu.VMEM((n, total, width), BF16),
            pltpu.VMEM((2, groups, 2, total, width // 2), BF16),
            pltpu.VMEM((2, groups, total, width // 2), BF16),
            pltpu.VMEM((2, groups + 1, total, width // 2), BF16),
            pltpu.VMEM((turns, 16, width), F32),
            dma((2, groups, 2)),
            dma((2, groups, 2)),
            dma((2, groups)),
            dma((2, groups)),
            dma((2, groups)),
            dma((2, groups + 1)),
            dma((turns,)),
            dma((turns,)),
            dma((groups,)),
            dma((groups,)),
            dma(()),
        ],
        compiler_params=params(2, 62),
        name="scatter_mixer",
    )(one, mixed, dy, dxb, branch, gates, dpar, gain_one, gain_two, column)


GELU_A = 0.7978845608028654
GELU_B = 0.044715


def gelu_parts(v):
    t = jnp.tanh(GELU_A * (v + GELU_B * v * v * v))
    value = 0.5 * v * (1.0 + t)
    slope = 0.5 * (1.0 + t) + 0.5 * v * (1.0 - t * t) * GELU_A * (1.0 + 3.0 * GELU_B * v * v)
    return value, slope


def gates_of(conv_low, gate_ref, par_ref, head, cols, first):
    pre_x = jnp.dot(conv_low, gate_ref[0, head], preferred_element_type=F32)
    pre_a = jnp.dot(conv_low, gate_ref[1, head], preferred_element_type=F32)
    gate_x = jax.nn.sigmoid(pre_x + par_ref[5:6, cols])
    gate_a = jax.nn.sigmoid(pre_a + par_ref[6:7, cols])
    decay = jnp.exp(-8.0 * gate_a * par_ref[8:9, cols])
    room = 1.0 - decay * decay
    mult = jnp.where(first, 1.0, jnp.sqrt(jnp.maximum(room, 0.001)))
    return gate_x, gate_a, decay, room, mult


FLIPPED = (((1,), (1,)), ((), ()))


def first_row(tokens):
    row = lax.broadcasted_iota(jnp.int32, (tokens, 1), 0)
    return jnp.logical_and(row == 0, lax.axis_index("seq") == 0)


def forward_body(
    n,
    one_ref,
    w_in_ref,
    w_branch_ref,
    w_out_ref,
    gate_ref,
    par_ref,
    x_ref,
    gain_ref,
    column_ref,
    xb_ref,
    yp_ref,
    conv_ref,
    state_ref,
    branch_ref,
    edge_ref,
    resid_ref,
    two_ref,
    near_ref,
    w_in,
    w_branch,
    w_out,
    mixed,
    mixed_got,
    wide,
    tail,
    fade,
    mine,
    theirs,
    *sems,
):
    send_tail, recv_tail, send_tot, recv_tot, send_f, recv_f, send_m, recv_m, loaded = sems
    tokens, width = xb_ref.shape
    model = one_ref.shape[1]
    me = lax.axis_index("seq")
    size = gate_ref.shape[2]
    loads = [
        pltpu.make_async_copy(src, dst, loaded.at[at])
        for at, (src, dst) in enumerate(
            ((w_in_ref, w_in), (w_branch_ref, w_branch), (w_out_ref, w_out))
        )
    ]
    for load in loads:
        load.start()
    greet_all(n, me, True)
    tail_copy = remote(
        xb_ref.at[pl.ds(tokens - 16, 16)], tail, send_tail, recv_tail, lax.rem(me + 1, n)
    )
    _, _, by_x, by_y, _ = whereabouts()
    part = column_ref.shape[1] // 2
    kinds = column_ref.shape[0]
    hosted = [
        [
            remote(
                column_ref.at[kind, pl.ds(h * part, part)],
                near_ref.at[h, kind],
                send_f.at[kind, h],
                recv_f.at[kind, h],
                (by_x, by_y)[h],
            )
            for h in range(2)
        ]
        for kind in range(kinds)
    ]

    def host(kind):
        for copy in hosted[kind]:
            copy.start()

    loads[0].wait()
    for start in range(0, width, size):
        cols = slice(start, start + size)
        xb_ref[:, cols] = jnp.dot(
            one_ref[...], w_in[:, cols], preferred_element_type=F32
        ).astype(BF16)
    pl.when(me + 1 < n)(tail_copy.start)
    host(0)
    wide[8:] = xb_ref[...].astype(F32)
    loads[1].wait()
    for start in range(0, width, size):
        cols = slice(start, start + size)
        yp_ref[:, cols] = jnp.dot(one_ref[...], w_branch[:, cols], preferred_element_type=F32)

    @pl.when(me > 0)
    def _():
        tail_copy.wait_recv()
        wide[:8] = tail[...].astype(F32)[8:]

    @pl.when(me == 0)
    def _():
        wide[:8] = jnp.zeros((8, width), F32)

    pl.when(me + 1 < n)(tail_copy.wait_send)
    edge_ref[:8] = wide[:8]
    first = first_row(tokens)
    for head in range(width // size):
        cols = slice(head * size, (head + 1) * size)
        conv = par_ref[4:5, cols]
        for tap in range(4):
            conv = conv + par_ref[tap : tap + 1, cols] * wide[8 - tap : 8 - tap + tokens, cols]
        conv_low = conv.astype(BF16)
        conv_ref[:, cols] = conv_low
        gate_x, _, decay, _, mult = gates_of(conv_low, gate_ref, par_ref, head, cols, first)
        fade[:, cols] = decay
        state_ref[:, cols] = conv_low.astype(F32) * gate_x * mult

    row = lax.broadcasted_iota(jnp.int32, (8, width), 0)

    def inside(at, carry):
        r = pl.ds(pl.multiple_of(at * 8, 8), 8)
        a, b = fade[r], state_ref[r]
        for by in (1, 2, 4):
            a_back = pltpu.roll(a, by, 0)
            b_back = pltpu.roll(b, by, 0)
            b = jnp.where(row >= by, a * b_back + b, b)
            a = jnp.where(row >= by, a * a_back, a)
        fade[r] = a
        state_ref[r] = b
        return a[7:8] * carry[0], a[7:8] * carry[1] + b[7:8]

    ones, zeros = jnp.ones((1, width), F32), jnp.zeros((1, width), F32)
    tot_a, tot_b = lax.fori_loop(0, tokens // 8, inside, (ones, zeros))
    mine[0:1] = tot_a
    mine[1:2] = tot_b

    def told(place):
        return remote(mine, theirs.at[me], send_tot.at[place], recv_tot.at[me], place)

    def heard(place):
        return remote(mine, theirs.at[place], send_tot.at[place], recv_tot.at[place], place)

    def tell(place, carry):
        told(place).start()
        return carry

    lax.fori_loop(me + 1, n, tell, 0)
    for kind in range(1, kinds):
        host(kind)

    def hear(place, state):
        heard(place).wait_recv()
        return theirs[place, 0:1] * state + theirs[place, 1:2]

    carry_in = lax.fori_loop(0, me, hear, zeros)
    edge_ref[8:] = jnp.broadcast_to(carry_in, (8, width))

    def finish(at, carry):
        r = pl.ds(pl.multiple_of(at * 16, 16), 16)
        a, b = fade[r], state_ref[r]
        top = b[:8] + a[:8] * carry
        low = b[8:] + a[8:] * top[7:8]
        states = jnp.concatenate([top, low], axis=0)
        state_ref[r] = states
        branch_ref[r] = (states * gelu_parts(yp_ref[r])[0]).astype(BF16)
        return low[7:8]

    lax.fori_loop(0, tokens // 16, finish, carry_in)

    def sent(place, carry):
        told(place).wait_send()
        return carry

    lax.fori_loop(me + 1, n, sent, 0)
    loads[2].wait()
    core = lax.axis_index("ch")
    half = tokens // 2
    for start in range(0, model, size):
        cols = slice(start, start + size)
        part = lax.dot_general(branch_ref[...], w_out[cols], FLIPPED, preferred_element_type=F32)
        mixed[0, :, cols] = part[:half]
        mixed[1, :, cols] = part[half:]
    exchange = pltpu.make_async_remote_copy(
        src_ref=mixed.at[1 - core],
        dst_ref=mixed_got,
        send_sem=send_m,
        recv_sem=recv_m,
        device_id={"ch": 1 - core},
        device_id_type=MESH,
    )
    exchange.start()
    exchange.wait_recv()

    def norm(at, carry):
        r = pl.ds(pl.multiple_of(at * 16, 16), 16)
        resid = x_ref[r].astype(F32) + (mixed[core, r] + mixed_got[r])
        resid_ref[r] = resid
        scale = lax.rsqrt(jnp.mean(resid * resid, axis=-1, keepdims=True) + 1e-06)
        two_ref[r] = (resid * scale * gain_ref[...]).astype(BF16)
        return carry

    lax.fori_loop(0, half // 16, norm, 0)
    exchange.wait_send()
    for pair in hosted:
        for copy in pair:
            copy.wait()


def mixer_forward(one, weights, gates, par, x_half, gain, column):
    n = lax.axis_size("seq")
    tokens, model = one.shape
    width = par.shape[1]
    half = tokens // 2
    kinds, groups, rows, units = column.shape
    dma = pltpu.SemaphoreType.DMA
    whole = jax.ShapeDtypeStruct((tokens, width), F32)
    low = jax.ShapeDtypeStruct((tokens, width), BF16)
    return pl.pallas_call(
        functools.partial(forward_body, n),
        out_shape=(
            low,
            whole,
            low,
            whole,
            low,
            jax.ShapeDtypeStruct((16, width), F32),
            jax.ShapeDtypeStruct((half, model), F32),
            jax.ShapeDtypeStruct((half, model), BF16),
            jax.ShapeDtypeStruct((2, kinds, groups // 2, rows, units), column.dtype),
        ),
        in_specs=[VMEM] + [HBM] * 3 + [VMEM] * 4 + [HBM],
        out_specs=(VMEM,) * 8 + (HBM,),
        scratch_shapes=[
            pltpu.VMEM((model, width), BF16),
            pltpu.VMEM((model, width), BF16),
            pltpu.VMEM((model, width), BF16),
            pltpu.VMEM((2, half, model), F32),
            pltpu.VMEM((half, model), F32),
            pltpu.VMEM((tokens + 8, width), F32),
            pltpu.VMEM((16, width), BF16),
            pltpu.VMEM((tokens, width), F32),
            pltpu.VMEM((2, width), F32),
            pltpu.VMEM((n, 2, width), F32),
            dma(()),
            dma(()),
            dma((n,)),
            dma((n,)),
            dma((kinds, 2)),
            dma((kinds, 2)),
            dma(()),
            dma(()),
            dma((3,)),
        ],
        compiler_params=params(4, 60),
        name="mixer_forward",
    )(one, *weights, gates, par, x_half, gain, column)


def backward_body(
    n,
    mixed_ref,
    w_in_ref,
    w_branch_ref,
    w_out_ref,
    x_ref,
    gain_ref,
    resid_ref,
    yp_ref,
    state_ref,
    edge_ref,
    conv_ref,
    xb_ref,
    gate_ref,
    par_ref,
    half_ref,
    dy_ref,
    dxb_ref,
    dgate_ref,
    dpar_ref,
    dx_ref,
    dgain_ref,
    near_ref,
    w_in,
    w_branch,
    w_out,
    d_one,
    d_one_got,
    fade,
    shift,
    adj,
    gate_x_s,
    gate_a_s,
    dconv,
    wide,
    mine,
    theirs,
    head_rows,
    *sems,
):
    send_rows, recv_rows, send_tot, recv_tot, send_f, recv_f, send_m, recv_m, send_x, recv_x, loaded = sems
    tokens, width = xb_ref.shape
    model = gain_ref.shape[1]
    me = lax.axis_index("seq")
    size = gate_ref.shape[2]
    loads = [
        pltpu.make_async_copy(src, dst, loaded.at[at])
        for at, (src, dst) in enumerate(
            ((w_out_ref, w_out), (w_in_ref, w_in), (w_branch_ref, w_branch))
        )
    ]
    for load in loads:
        load.start()
    greet_all(n, me, True)
    _, _, by_x, by_y, _ = whereabouts()
    kinds = half_ref.shape[1]
    hosted = [
        [
            remote(
                half_ref.at[h, kind],
                near_ref.at[h, kind],
                send_f.at[kind, h],
                recv_f.at[kind, h],
                (by_x, by_y)[h],
            )
            for h in range(2)
        ]
        for kind in range(kinds)
    ]

    def host(kind):
        for copy in hosted[kind]:
            copy.start()

    host(0)
    first = first_row(tokens)
    fade[tokens:] = jnp.ones((8, width), F32)
    loads[0].wait()
    for head in range(width // size):
        cols = slice(head * size, (head + 1) * size)
        gate_x, gate_a, decay, _, _ = gates_of(conv_ref[:, cols], gate_ref, par_ref, head, cols, first)
        gate_x_s[:, cols] = gate_x
        gate_a_s[:, cols] = gate_a
        fade[:tokens, cols] = decay
        value, slope = gelu_parts(yp_ref[:, cols])
        grad = jnp.dot(mixed_ref[...], w_out[:, cols], preferred_element_type=F32)
        dy_ref[:, cols] = (grad * state_ref[:, cols] * slope).astype(BF16)
        adj[:, cols] = grad * value
        shift[:, cols] = fade[1 : tokens + 1, cols]

    row = lax.broadcasted_iota(jnp.int32, (8, width), 0)
    tiles = tokens // 8

    def inside(turn, carry):
        r = pl.ds(pl.multiple_of((tiles - 1 - turn) * 8, 8), 8)
        a, b = shift[r], adj[r]
        for by in (1, 2, 4):
            a_next = pltpu.roll(a, 8 - by, 0)
            b_next = pltpu.roll(b, 8 - by, 0)
            b = jnp.where(row < 8 - by, a * b_next + b, b)
            a = jnp.where(row < 8 - by, a * a_next, a)
        shift[r] = a
        adj[r] = b
        return a[0:1] * carry[0], a[0:1] * carry[1] + b[0:1]

    ones, zeros = jnp.ones((1, width), F32), jnp.zeros((1, width), F32)
    tot_a, tot_b = lax.fori_loop(0, tiles, inside, (ones, zeros))
    first_fade = fade[0:1]
    mine[0:1] = first_fade * tot_a
    mine[1:2] = first_fade * tot_b

    def told(place):
        return remote(mine, theirs.at[me], send_tot.at[place], recv_tot.at[me], place)

    def heard(place):
        return remote(mine, theirs.at[place], send_tot.at[place], recv_tot.at[place], place)

    def tell(place, carry):
        told(place).start()
        return carry

    lax.fori_loop(0, me, tell, 0)
    host(1)

    def hear(turn, state):
        place = n - 1 - turn
        heard(place).wait_recv()
        return theirs[place, 0:1] * state + theirs[place, 1:2]

    carry_in = lax.fori_loop(0, n - 1 - me, hear, zeros)

    def finish(turn, carry):
        r = pl.ds(pl.multiple_of((tiles - 1 - turn) * 8, 8), 8)
        value = adj[r] + shift[r] * carry
        adj[r] = value
        return value[0:1]

    lax.fori_loop(0, tiles, finish, carry_in)

    wide[:8] = edge_ref[:8]
    wide[8:] = xb_ref[...].astype(F32)
    at_first = lax.broadcasted_iota(jnp.int32, (tokens, 1), 0) == 0
    for head in range(width // size):
        cols = slice(head * size, (head + 1) * size)
        conv_low = conv_ref[:, cols]
        conv = conv_low.astype(F32)
        gate_x, gate_a, decay = gate_x_s[:, cols], gate_a_s[:, cols], fade[:tokens, cols]
        room = 1.0 - decay * decay
        mult = jnp.where(first, 1.0, jnp.sqrt(jnp.maximum(room, 0.001)))
        back = adj[:, cols]
        before = jnp.where(at_first, edge_ref[8:9, cols], pltpu.roll(state_ref[:, cols], 1, 0))
        d_mult = back * conv * gate_x
        moves = jnp.logical_and(room > 0.001, jnp.logical_not(first))
        d_decay = back * before - jnp.where(moves, d_mult * decay / mult, 0.0)
        d_log = d_decay * decay
        d_pre_x = back * conv * mult * gate_x * (1.0 - gate_x)
        d_pre_a = d_log * (-8.0 * par_ref[8:9, cols]) * gate_a * (1.0 - gate_a)
        dpar_ref[5:6, cols] = jnp.sum(d_pre_x, axis=0, keepdims=True)
        dpar_ref[6:7, cols] = jnp.sum(d_pre_a, axis=0, keepdims=True)
        dpar_ref[7:8, cols] = (
            jnp.sum(d_log * (-8.0 * gate_a), axis=0, keepdims=True) * par_ref[9:10, cols]
        )
        low_x, low_a = d_pre_x.astype(BF16), d_pre_a.astype(BF16)
        d_conv = (
            back * gate_x * mult
            + lax.dot_general(low_x, gate_ref[0, head], FLIPPED, preferred_element_type=F32)
            + lax.dot_general(low_a, gate_ref[1, head], FLIPPED, preferred_element_type=F32)
        )
        dconv[:tokens, cols] = d_conv
        over_rows = (((0,), (0,)), ((), ()))
        for gate, low in enumerate((low_x, low_a)):
            d_gate = lax.dot_general(conv_low, low, over_rows, preferred_element_type=F32)
            dgate_ref[:, gate, :, cols] = d_gate.astype(BF16).reshape(n, size // n, size)
        dpar_ref[4:5, cols] = jnp.sum(d_conv, axis=0, keepdims=True)
        for tap in range(4):
            dpar_ref[tap : tap + 1, cols] = jnp.sum(
                d_conv * wide[8 - tap : 8 - tap + tokens, cols], axis=0, keepdims=True
            )

    rows_copy = remote(
        dconv.at[pl.ds(0, 8)], head_rows, send_rows, recv_rows, lax.rem(me + n - 1, n)
    )
    pl.when(me > 0)(rows_copy.start)
    for kind in range(2, kinds):
        host(kind)

    @pl.when(me + 1 < n)
    def _():
        rows_copy.wait_recv()
        dconv[tokens:] = head_rows[...]

    @pl.when(me + 1 == n)
    def _():
        dconv[tokens:] = jnp.zeros((8, width), F32)

    for head in range(width // size):
        cols = slice(head * size, (head + 1) * size)
        total = par_ref[0:1, cols] * dconv[:tokens, cols]
        for tap in range(1, 4):
            total = total + par_ref[tap : tap + 1, cols] * dconv[tap : tap + tokens, cols]
        dxb_ref[:, cols] = total.astype(BF16)

    pl.when(me > 0)(rows_copy.wait_send)

    def sent(place, carry):
        told(place).wait_send()
        return carry

    lax.fori_loop(0, me, sent, 0)
    core = lax.axis_index("ch")
    half = tokens // 2
    loads[1].wait()
    loads[2].wait()
    for start in range(0, model, size):
        cols = slice(start, start + size)
        part = (
            lax.dot_general(dy_ref[...], w_branch[cols], FLIPPED, preferred_element_type=F32)
            + lax.dot_general(dxb_ref[...], w_in[cols], FLIPPED, preferred_element_type=F32)
        ).astype(BF16)
        d_one[0, :, cols] = part[:half]
        d_one[1, :, cols] = part[half:]
    exchange = pltpu.make_async_remote_copy(
        src_ref=d_one.at[1 - core],
        dst_ref=d_one_got,
        send_sem=send_m,
        recv_sem=recv_m,
        device_id={"ch": 1 - core},
        device_id_type=MESH,
    )
    exchange.start()
    exchange.wait_recv()

    def norm(at, total):
        r = pl.ds(pl.multiple_of(at * 16, 16), 16)
        x = x_ref[r].astype(F32)
        scale = lax.rsqrt(jnp.mean(x * x, axis=-1, keepdims=True) + 1e-06)
        grad = d_one[core, r].astype(F32) + d_one_got[r].astype(F32)
        back = grad * gain_ref[...]
        shrink = scale * scale * scale * jnp.mean(x * back, axis=-1, keepdims=True)
        dx_ref[core, r] = resid_ref[r] + (scale * back - x * shrink)
        return total + jnp.sum(grad * (x * scale), axis=0, keepdims=True)

    dgain_ref[...] = lax.fori_loop(0, half // 16, norm, jnp.zeros((1, model), F32))
    share = pltpu.make_async_remote_copy(
        src_ref=dx_ref.at[core],
        dst_ref=dx_ref.at[core],
        send_sem=send_x,
        recv_sem=recv_x,
        device_id={"ch": 1 - core},
        device_id_type=MESH,
    )
    share.start()
    exchange.wait_send()
    for pair in hosted:
        for copy in pair:
            copy.wait()
    pltpu.make_async_remote_copy(
        src_ref=dx_ref.at[core],
        dst_ref=dx_ref.at[1 - core],
        send_sem=send_x,
        recv_sem=recv_x,
        device_id={"ch": 1 - core},
        device_id_type=MESH,
    ).wait_recv()
    share.wait_send()


def mixer_backward(
    mixed, weights, x_half, gain, d_resid, y_pre, states, edge, conv, x_branch, gates, par, halves
):
    n = lax.axis_size("seq")
    tokens, width = x_branch.shape
    model = mixed.shape[1]
    size = gates.shape[2]
    half = tokens // 2
    dma = pltpu.SemaphoreType.DMA
    whole = pltpu.VMEM((tokens, width), F32)
    longer = pltpu.VMEM((tokens + 8, width), F32)
    weight = pltpu.VMEM((model, width), BF16)
    return pl.pallas_call(
        functools.partial(backward_body, n),
        out_shape=(
            jax.ShapeDtypeStruct((tokens, width), BF16),
            jax.ShapeDtypeStruct((tokens, width), BF16),
            jax.ShapeDtypeStruct((n, 2, size // n, width), BF16),
            jax.ShapeDtypeStruct((8, width), F32),
            jax.ShapeDtypeStruct((2, half, model), F32),
            jax.ShapeDtypeStruct((1, model), F32),
            jax.ShapeDtypeStruct(halves.shape, BF16),
        ),
        in_specs=[VMEM] + [HBM] * 3 + [VMEM] * 10 + [HBM],
        out_specs=(VMEM,) * 6 + (HBM,),
        scratch_shapes=[
            weight,
            weight,
            weight,
            pltpu.VMEM((2, half, model), BF16),
            pltpu.VMEM((half, model), BF16),
            longer,
            whole,
            whole,
            whole,
            whole,
            longer,
            longer,
            pltpu.VMEM((2, width), F32),
            pltpu.VMEM((n, 2, width), F32),
            pltpu.VMEM((8, width), F32),
            dma(()),
            dma(()),
            dma((n,)),
            dma((n,)),
            dma((halves.shape[1], 2)),
            dma((halves.shape[1], 2)),
            dma(()),
            dma(()),
            dma(()),
            dma(()),
            dma((3,)),
        ],
        compiler_params=params(5, 60),
        name="mixer_backward",
    )(mixed, *weights, x_half, gain, d_resid, y_pre, states, edge, conv, x_branch, gates, par, halves)


def ffn_body(n, *refs):
    own_ref, cot_ref, column_ref, near_ref, resid_ref, gain_ref = refs[:6]
    block_ref, d_resid_ref, mixed_ref, d_gain_ref, halves_ref, mine_ref, far_ref = refs[6:13]
    tokens, cots, w, hidden, box, sib, got, d_hidden, stage, turned = refs[13:23]
    token_sems, cot_sems = refs[23:26], refs[26:29]
    send_w, recv_w, keep_w, keep_c, keep_t = refs[29:34]
    send_c, recv_s, send_z, recv_r, send_f, recv_f, send_m, recv_m, move, out_sem = refs[34:]
    groups = n // INNER
    half = groups // 2
    me, outer, by_x, by_y, by_xy = whereabouts()
    base = outer * INNER
    core = lax.axis_index("ch")
    above, below = outer + 1 < groups, outer > 0
    sibling = {"ch": 1 - core}
    barrier = pltpu.get_barrier_semaphore()

    def hello(peer):
        pl.semaphore_signal(barrier, inc=1, device_id=peer, device_id_type=MESH)

    hello({"seq": by_x})
    hello({"seq": by_y})
    hello(sibling)
    pl.when(above)(lambda: hello({"seq": me + INNER}))
    pl.when(below)(lambda: hello({"seq": me - INNER}))
    pl.semaphore_wait(barrier, 3 + above.astype(jnp.int32) + below.astype(jnp.int32))
    flips = ((by_x, by_y), (by_y, by_x))
    rows, units = w.shape[3], w.shape[4]
    tall, model = own_ref.shape
    count = 2 * tall
    deep = INNER * rows
    tile = 256

    def part(h):
        return pl.ds(h * half, half)


    chain_t = Chain(n, own_ref, tokens, *token_sems)
    chain_c = Chain(n, cot_ref, cots, *cot_sems)

    def weight_copy(kind, h, far, receive=False):
        source = flips[h][0] if far else me
        if receive:
            source = by_xy if far else flips[h][1]
        return remote(
            near_ref.at[h, kind] if far else column_ref.at[kind, part(h)],
            w.at[kind, part(h), source - base],
            send_w.at[kind, h, far],
            recv_w.at[kind, h, far],
            flips[h][1],
        )

    keep = [
        [
            pltpu.make_async_copy(
                column_ref.at[kind], w.at[kind, :, me - base], keep_w.at[kind, 0]
            ),
            *(
                pltpu.make_async_copy(
                    near_ref.at[h, kind],
                    w.at[kind, part(h), flips[h][0] - base],
                    keep_w.at[kind, 1 + h],
                )
                for h in range(2)
            ),
        ]
        for kind in range(3)
    ]
    every = [(h, far) for far in range(2) for h in range(2)]
    own_t, own_c = chain_t.keep(keep_t), chain_c.keep(keep_c)
    chain_c.start()
    for kind in (2, 0, 1):
        for h, far in every:
            weight_copy(kind, h, far).start()
    own_c.start()
    own_t.start()
    for kind in (2, 0, 1):
        for copy in keep[kind]:
            copy.start()
    for step in range(1, groups - 1):
        chain_c.step(step)
    chain_t.start()
    chain_c.step(groups - 1)
    chain_c.finish()
    own_c.wait()

    def weights_landed(kind):
        for h, far in every:
            weight_copy(kind, h, far, True).wait_recv()
        for copy in keep[kind]:
            copy.wait()

    def columns(kind, at):
        return w[kind, :, :, :, at : at + tile].reshape(model, tile)

    def token_rows(place):
        return pl.ds(pl.multiple_of(place * count, count), count)

    def each(limit, action):
        def one(turn, carry):
            action(turn)
            return carry

        lax.fori_loop(0, limit, one, 0)

    weights_landed(2)

    def back_hidden(place):
        left = cots[place].reshape(count, model)
        for at in range(0, units, tile):
            d_hidden[token_rows(place), at : at + tile] = jnp.dot(
                left, columns(2, at), preferred_element_type=F32
            )

    each(groups, back_hidden)
    for step in range(1, groups):
        chain_t.step(step)
    chain_t.finish()
    own_t.wait()
    weights_landed(0)
    weights_landed(1)

    def middle(place):
        left = tokens[place].reshape(count, model)
        r = token_rows(place)
        for at in range(0, units, tile):
            c = slice(at, at + tile)
            gate = jnp.dot(left, columns(0, at), preferred_element_type=F32)
            up = jnp.dot(left, columns(1, at), preferred_element_type=F32)
            value, slope = gelu_parts(gate)
            back = d_hidden[r, c]
            hidden[0, r, c] = (value * up).astype(BF16)
            hidden[1, r, c] = (back * up * slope).astype(BF16)
            hidden[2, r, c] = (back * value).astype(BF16)

    each(groups, middle)
    for kind in range(3):
        for h, far in every:
            weight_copy(kind, h, far).wait_send()


    boxes = (box, tokens)

    def partial(kind, place):
        r = token_rows(place)
        for at in range(groups):
            pairs = ((1, 0), (2, 1)) if kind == 0 else ((0, 2),)
            value = 0.0
            for left, right in pairs:
                value = value + lax.dot_general(
                    hidden[left, r],
                    w[right, at].reshape(deep, units),
                    FLIPPED,
                    preferred_element_type=F32,
                )
            value = value.astype(BF16)
            boxes[kind][place, 0, :, at * deep : (at + 1) * deep] = value[:tall]
            boxes[kind][place, 1, :, at * deep : (at + 1) * deep] = value[tall:]
        to_sibling(kind, place).start()

    def to_sibling(kind, place):
        return pltpu.make_async_remote_copy(
            src_ref=boxes[kind].at[place, 1 - core],
            dst_ref=sib.at[kind, place],
            send_sem=send_c.at[kind, place],
            recv_sem=recv_s.at[kind, place],
            device_id=sibling,
            device_id_type=MESH,
        )

    def along(kind, place, up):
        last = place == (outer + 1 if up else outer - 1)
        slot = place if up else jnp.where(last, groups, place)
        return remote(
            boxes[kind].at[place, core],
            got.at[kind, slot],
            send_z.at[kind, place],
            recv_r.at[kind, slot],
            me + (INNER if up else -INNER),
        )

    def landed(kind, slot):
        return remote(
            box.at[0, core], got.at[kind, slot], send_z.at[kind, 0], recv_r.at[kind, slot], by_x
        )

    chunk = 16

    def rows_of(at):
        return pl.ds(pl.multiple_of(at * chunk, chunk), chunk)

    def ready(kind, place, incoming):
        to_sibling(kind, place).wait_recv()

        def add(at, with_got):
            r = rows_of(at)
            value = boxes[kind][place, core, r].astype(F32) + sib[kind, place, r].astype(F32)
            if with_got:
                value = value + got[kind, place, r].astype(F32)
            boxes[kind][place, core, r] = value.astype(BF16)

        @pl.when(incoming)
        def _():
            landed(kind, place).wait_recv()
            each(tall // chunk, lambda at: add(at, True))

        @pl.when(jnp.logical_not(incoming))
        def _():
            each(tall // chunk, lambda at: add(at, False))

    def pass_on(kind, turn):
        ups = groups - 1 - outer
        upper = jnp.where(outer < half, turn < ups, turn >= outer)
        later = jnp.where(outer < half, turn, turn - outer)
        earlier = jnp.where(outer < half, turn - ups, turn)

        @pl.when(upper)
        def _():
            place = groups - 1 - later
            ready(kind, place, below)
            along(kind, place, True).start()

        @pl.when(jnp.logical_not(upper))
        def _():
            ready(kind, earlier, above)
            along(kind, earlier, False).start()

    at_end = jnp.logical_or(outer == 0, outer == groups - 1)

    def partials(kind):
        def one(turn):
            partial(kind, far_first(groups, outer, turn))

            @pl.when(jnp.logical_and(at_end, turn >= 1))
            def _():
                pass_on(kind, turn - 1)

        each(groups, one)

    def between(kind, turns):
        @pl.when(jnp.logical_not(at_end))
        def _():
            for turn in turns:
                pass_on(kind, turn)

    def totals(kind, use):
        to_sibling(kind, outer).wait_recv()
        for condition, slots in (
            (jnp.logical_and(below, above), (outer, groups)),
            (jnp.logical_and(below, jnp.logical_not(above)), (outer,)),
            (jnp.logical_and(jnp.logical_not(below), above), (groups,)),
        ):

            @pl.when(condition)
            def _(slots=slots):
                for slot in slots:
                    landed(kind, slot).wait_recv()

                def one(at):
                    r = rows_of(at)
                    value = boxes[kind][outer, core, r].astype(F32) + sib[kind, outer, r].astype(F32)
                    for slot in slots:
                        value = value + got[kind, slot, r].astype(F32)
                    use(r, value)

                each(tall // chunk, one)

    def clear(kind):
        def one(place):
            to_sibling(kind, place).wait_send()

            @pl.when(place > outer)
            def _():
                along(kind, place, True).wait_send()

            @pl.when(place < outer)
            def _():
                along(kind, place, False).wait_send()

        each(groups, one)


    def gradient_copy(kind, h, far):
        source = by_xy if far else flips[h][1]
        return remote(
            w.at[kind, part(h), source - base],
            far_ref.at[h, far, kind],
            send_f.at[kind, h, far],
            recv_f.at[kind, h, far],
            flips[h][1],
        )

    def gradients(kinds, source, h):
        for at in range(h * half, (h + 1) * half):
            left = source[:, :, :, at * deep : (at + 1) * deep].reshape(groups * count, deep)
            turned[...] = left.T
            for kind, right in kinds:
                for start in range(0, units, tile):
                    c = slice(start, start + tile)
                    w[kind, at, :, :, c] = (
                        jnp.dot(turned[...], hidden[right, :, c], preferred_element_type=F32)
                        .astype(BF16)
                        .reshape(INNER, rows, tile)
                    )
        for kind, _ in kinds:
            for far in (1, 0):
                gradient_copy(kind, h, far).start()

    def collect(kind, h, far):
        inner = (flips[h][0] if far else me) - base
        gradient_copy(kind, h, far).wait_recv()
        load = pltpu.make_async_copy(far_ref.at[h, far, kind], stage, move)
        load.start()
        load.wait()
        for place in range(half):
            at = h * half + place

            def one(turn, place=place, at=at):
                r = rows_of(turn)
                w[kind, at, inner, r] = (
                    w[kind, at, inner, r].astype(F32) + stage[place, r].astype(F32)
                ).astype(BF16)

            each(rows // chunk, one)
        out_copy(kind, h, far).start()

    def out_copy(kind, h, far):
        inner = (flips[h][0] if far else me) - base
        return pltpu.make_async_copy(
            w.at[kind, part(h), inner],
            (halves_ref if far else mine_ref).at[h, kind],
            out_sem.at[kind, h, far],
        )

    first, second = range(groups // 2), range(groups // 2, groups - 1)
    pair = ((0, 1), (1, 2))
    partials(0)
    gradients(pair, tokens, 0)
    between(0, first[:1])
    gradients(pair, tokens, 1)
    between(0, first[1:])
    between(0, second)
    partials(1)
    gradients(((2, 0),), cots, 0)
    between(1, first[:1])
    gradients(((2, 0),), cots, 1)
    between(1, first[1:])
    d_gain_ref[...] = jnp.zeros((1, model), F32)

    def norm(r, grad):
        resid = resid_ref[r]
        scale = lax.rsqrt(jnp.mean(resid * resid, axis=-1, keepdims=True) + 1e-06)
        back = grad * gain_ref[...]
        shrink = scale * scale * scale * jnp.mean(resid * back, axis=-1, keepdims=True)
        value = cots[outer, core, r].astype(F32) + (scale * back - resid * shrink)
        d_resid_ref[r] = value
        mixed_ref[core, r] = value.astype(BF16)
        d_gain_ref[...] = d_gain_ref[...] + jnp.sum(grad * (resid * scale), axis=0, keepdims=True)

    totals(0, norm)

    def shared(ref, at, part):
        return pltpu.make_async_remote_copy(
            src_ref=ref.at[core],
            dst_ref=ref.at[part],
            send_sem=send_m.at[at],
            recv_sem=recv_m.at[at],
            device_id=sibling,
            device_id_type=MESH,
        )

    share = shared(mixed_ref, 0, core)
    share.start()
    between(1, second)
    for far in (1, 0):
        for h in range(2):
            for kind in range(2):
                collect(kind, h, far)

    def finish(r, value):
        block_ref[core, r] = (resid_ref[r] + value).astype(BF16)

    totals(1, finish)
    show = shared(block_ref, 1, core)
    show.start()
    clear(0)
    clear(1)
    for far in (1, 0):
        for h in range(2):
            collect(2, h, far)
    shared(mixed_ref, 0, 1 - core).wait_recv()
    shared(block_ref, 1, 1 - core).wait_recv()
    share.wait_send()
    show.wait_send()
    for kind in range(3):
        for h, far in every:
            gradient_copy(kind, h, far).wait_send()
            out_copy(kind, h, far).wait()


def feed_forward(own, cotangent, column, near, resid, gain):
    n = lax.axis_size("seq")
    groups = n // INNER
    tall, model = own.shape
    kinds, _, rows, units = column.shape
    half = groups // 2
    dma = pltpu.SemaphoreType.DMA
    part = jax.ShapeDtypeStruct((2, kinds, half, rows, units), BF16)
    return pl.pallas_call(
        functools.partial(ffn_body, n),
        out_shape=(
            jax.ShapeDtypeStruct((2, tall, model), BF16),
            jax.ShapeDtypeStruct((tall, model), F32),
            jax.ShapeDtypeStruct((2, tall, model), BF16),
            jax.ShapeDtypeStruct((1, model), F32),
            part,
            part,
            jax.ShapeDtypeStruct((2, 2, kinds, half, rows, units), BF16),
        ),
        in_specs=[HBM] * 4 + [VMEM] * 2,
        out_specs=(VMEM,) * 4 + (HBM,) * 3,
        scratch_shapes=[
            pltpu.VMEM((groups, 2, tall, model), BF16),
            pltpu.VMEM((groups, 2, tall, model), BF16),
            pltpu.VMEM((kinds, groups, INNER, rows, units), BF16),
            pltpu.VMEM((3, groups * 2 * tall, units), BF16),
            pltpu.VMEM((groups, 2, tall, model), BF16),
            pltpu.VMEM((2, groups, tall, model), BF16),
            pltpu.VMEM((2, groups + 1, tall, model), BF16),
            pltpu.VMEM((groups * 2 * tall, units), F32),
            pltpu.VMEM((half, rows, units), BF16),
            pltpu.VMEM((INNER * rows, groups * 2 * tall), BF16),
            *chain_semaphores(groups),
            *chain_semaphores(groups),
            dma((kinds, 2, 2)),
            dma((kinds, 2, 2)),
            dma((kinds, 3)),
            dma(()),
            dma(()),
            dma((2, groups)),
            dma((2, groups)),
            dma((2, groups)),
            dma((2, groups + 1)),
            dma((kinds, 2, 2)),
            dma((kinds, 2, 2)),
            dma((2,)),
            dma((2,)),
            dma(()),
            dma((kinds, 2, 2)),
        ],
        compiler_params=params(8, 63),
        name="feed_forward",
    )(own, cotangent, column, near, resid, gain)


def my_half(values):
    half = values.shape[0] // 2
    return lax.dynamic_slice_in_dim(values, lax.axis_index("ch") * half, half, 0)


def join(own):
    other = swap(own, "ch", 1)
    core = lax.axis_index("ch")
    return jnp.concatenate(
        [jnp.where(core == 0, own, other), jnp.where(core == 0, other, own)], axis=0
    )


def tokens_in(own):
    groups = lax.axis_size("seq") // INNER
    outer = lax.axis_index("seq") // INNER
    got = put(jnp.zeros((groups,) + own.shape, own.dtype), own, outer)
    for step in range(1, groups):
        got = put(got, swap(own, "seq", step * INNER), outer ^ step)
    other = swap(got, "ch", 1)
    first = lax.axis_index("ch") == 0
    return jnp.stack([jnp.where(first, got, other), jnp.where(first, other, got)], axis=1)


def tokens_out(partial, half):
    width = partial.shape[1]
    groups = lax.axis_size("seq") // INNER
    outer = lax.axis_index("seq") // INNER
    core = lax.axis_index("ch")
    parts = partial.reshape(groups, 2, half, width)
    theirs = pick(parts, 1 - core, 1).astype(BF16)
    summed = (pick(parts, core, 1).astype(F32) + swap(theirs, "ch", 1).astype(F32)).astype(BF16)
    total = pick(summed, outer).astype(F32)
    for step in range(1, groups):
        total = total + swap(pick(summed, outer ^ step), "seq", step * INNER).astype(F32)
    return total


def feed_forward_parts(n_two, cot_half, column, near, resid, ffn_gain):
    f32, bf16 = F32, BF16
    _, groups, depth, units = column.shape
    half_rows, model = n_two.shape
    tok_rows = 2 * half_rows
    _, norm_back_two = jax.vjp(scaled_norm, resid, ffn_gain)
    all_two, *full_ffn = gather_tokens(n_two, column, near)
    all_cot = tokens_in(cot_half)
    all_two, all_cot = (v.reshape(groups * tok_rows, model) for v in (all_two, all_cot))
    full_ffn = [w.reshape(model, units) for w in full_ffn]
    gate_pre = jnp.dot(all_two, full_ffn[0], preferred_element_type=f32)
    up_pre = jnp.dot(all_two, full_ffn[1], preferred_element_type=f32)
    gate_act, gelu_back_gate = jax.vjp(gelu_tanh, gate_pre)
    hidden = (gate_act * up_pre).astype(bf16)
    ffn_term = jnp.einsum("tf,df->td", hidden, full_ffn[2], preferred_element_type=f32).astype(bf16)
    d_hidden = jnp.einsum("td,df->tf", all_cot, full_ffn[2], preferred_element_type=f32)
    d_gate = gelu_back_gate(d_hidden * up_pre)[0].astype(bf16)
    d_up = (d_hidden * gate_act).astype(bf16)
    d_n_two = (
        jnp.einsum("tf,df->td", d_gate, full_ffn[0], preferred_element_type=f32)
        + jnp.einsum("tf,df->td", d_up, full_ffn[1], preferred_element_type=f32)
    ).astype(bf16)
    terms = [
        jnp.einsum("td,tf->df", left, right, preferred_element_type=f32)
        .astype(bf16)
        .reshape(groups, INNER, depth, units)
        for left, right in ((all_two, d_gate), (all_two, d_up), (all_cot, hidden))
    ]
    split = [v.reshape(groups, 2, half_rows, model) for v in (d_n_two, ffn_term)]
    if groups <= 4:
        d_n_two, ffn_out, far = reduce_tokens(split, terms)
    else:
        d_n_two, far = reduce_tokens(split[:1], terms)
        ffn_out = tokens_out(ffn_term, half_rows)
    block_out = join((resid + ffn_out).astype(bf16))
    inner = lax.axis_index("seq") % INNER
    by_half = [t.reshape(2, groups // 2, INNER, depth, units) for t in terms]

    def block_at(h, place):
        return jnp.stack([pick(t[h], place, 1) for t in by_half]).astype(f32)

    mine = jnp.stack(
        [(block_at(h, inner) + far[h, 0].astype(f32)).astype(bf16) for h in range(2)]
    )
    halves = jnp.stack(
        [(block_at(h, inner ^ (1, 2)[h]) + far[h, 1].astype(f32)).astype(bf16) for h in range(2)]
    )
    d_resid_norm, d_ffn_gain_term = norm_back_two(d_n_two)
    d_resid = cot_half.astype(f32) + d_resid_norm
    d_mixed = join(d_resid.astype(bf16))
    return block_out, d_resid, d_mixed, d_ffn_gain_term.reshape(1, model), halves, mine


def shards(
    inputs,
    norm_gain,
    branch_weight,
    input_weight,
    channel_params,
    gate_x_blocks,
    gate_a_blocks,
    out_weight,
    ffn_gain,
    ffn_gate,
    ffn_up,
    ffn_down,
    cotangent,
):
    f32 = F32
    bf16 = BF16
    n = lax.axis_size("seq")
    tok_rows, model = inputs.shape
    half_rows = tok_rows // 2
    heads, part, size = gate_x_blocks.shape
    width = heads * size
    depth = ffn_gate.shape[0]
    groups = n // INNER
    hidden_units = ffn_gate.shape[1]
    units = -(-hidden_units // (groups * 128)) * 128
    x_float = inputs.astype(f32)
    n_one = scaled_norm(x_float, norm_gain).astype(bf16)
    x_half = my_half(inputs)

    gate_pack = jnp.stack([gate_x_blocks, gate_a_blocks])
    ffn_pack = jnp.pad(
        jnp.stack([ffn_gate, ffn_up, ffn_down.T]), ((0, 0), (0, 0), (0, groups * units - hidden_units))
    )
    *full_mixer, full_gates, column = gather_weights(
        [input_weight, branch_weight, out_weight.T], gate_pack, ffn_pack
    )
    full_mixer = [w.reshape(model, width) for w in full_mixer]
    gates = full_gates.reshape(2, heads, size, size)
    par = jnp.concatenate(
        [
            channel_params,
            jax.nn.softplus(channel_params[7:8]),
            jax.nn.sigmoid(channel_params[7:8]),
            jnp.zeros((6, width), f32),
        ],
        axis=0,
    )

    cot_half = my_half(cotangent)

    x_branch, y_pre, conv_out, states, branch_out, edge, resid, n_two, near = mixer_forward(
        n_one,
        full_mixer,
        gates,
        par,
        x_half,
        ffn_gain.reshape(1, model),
        column,
    )
    if groups <= 4 and depth % 16 == 0:
        block_out, d_resid, d_mixed, d_ffn_gain_term, halves, mine, _ = feed_forward(
            n_two, cot_half, column, near, resid, ffn_gain.reshape(1, model)
        )
        block_out = block_out.reshape(tok_rows, model)
        d_mixed = d_mixed.reshape(tok_rows, model)
    else:
        block_out, d_resid, d_mixed, d_ffn_gain_term, halves, mine = feed_forward_parts(
            n_two, cot_half, column, near, resid, ffn_gain
        )
    d_y, d_xb, d_gates, d_par, d_inputs, d_norm_gain_term, near_back = mixer_backward(
        d_mixed,
        full_mixer,
        x_half,
        norm_gain.reshape(1, model),
        d_resid,
        y_pre,
        states,
        edge,
        conv_out,
        x_branch,
        gates,
        par,
        halves,
    )
    column_back = jnp.concatenate(
        [
            (mine[h].astype(f32) + near_back[h].astype(f32)).astype(bf16) for h in range(2)
        ],
        axis=1,
    )
    d_inputs = d_inputs.reshape(tok_rows, model)
    gain_rows = model // width
    scattered, small, spread = scatter_mixer(
        n_one.T.reshape(n, depth, tok_rows),
        d_mixed.T.reshape(n, depth, tok_rows),
        d_y,
        d_xb,
        branch_out,
        d_gates,
        d_par,
        d_norm_gain_term,
        d_ffn_gain_term,
        column_back,
    )
    ffn_grads = [spread[kind, :, :hidden_units].astype(f32) for kind in range(3)]
    d_gate_pair = scattered[3 * depth :].reshape(2, part, heads, size).transpose(0, 2, 1, 3)
    return (
        block_out,
        d_inputs,
        small[8 : 8 + gain_rows].reshape(model),
        scattered[:depth],
        scattered[depth : 2 * depth],
        small[:8],
        d_gate_pair[0],
        d_gate_pair[1],
        scattered[2 * depth : 3 * depth].T,
        small[8 + gain_rows : 8 + 2 * gain_rows].reshape(model),
        ffn_grads[0],
        ffn_grads[1],
        ffn_grads[2].T,
    )


def solution(mesh):
    placed = (
        P("seq", None),
        P(),
        P("seq", "ch"),
        P("seq", "ch"),
        P(None, "ch"),
        P("ch", "seq", None),
        P("ch", "seq", None),
        P("ch", "seq"),
        P(),
        P("seq", "ch"),
        P("seq", "ch"),
        P("ch", "seq"),
        P("seq", None),
    )
    return jax.shard_map(
        shards,
        mesh=mesh,
        in_specs=placed,
        out_specs=(
            P("seq", None),
            P("seq", None),
            P(),
            P("seq", "ch"),
            P("seq", "ch"),
            P(None, "ch"),
            P("ch", "seq", None),
            P("ch", "seq", None),
            P("ch", "seq"),
            P(),
            P("seq", "ch"),
            P("seq", "ch"),
            P("ch", "seq"),
        ),
        check_vma=False,
    )
```

```python
import functools

import jax
import jax.numpy as jnp
from jax import lax
from jax.experimental import pallas as pl
from jax.experimental.pallas import tpu as pltpu
from jax.sharding import PartitionSpec as P

F32 = jnp.float32
BF16 = jnp.bfloat16
INNER = 4
MESH = pl.DeviceIdType.MESH
VMEM = pl.BlockSpec(memory_space=pltpu.VMEM)
ANY = pl.BlockSpec(memory_space=pl.ANY)
HBM = pl.BlockSpec(memory_space=pltpu.HBM)


def swap(value, axis, mask):
    return lax.ppermute(value, axis, [(i, i ^ mask) for i in range(lax.axis_size(axis))])


def pick(array, index, axis=0):
    return lax.dynamic_index_in_dim(array, index, axis, False)


def put(array, block, index, axis=0):
    return lax.dynamic_update_index_in_dim(array, block, index, axis)


def scaled_norm(values, gain):
    return values * lax.rsqrt(jnp.mean(values * values, axis=-1, keepdims=True) + 1e-06) * gain


def gelu_tanh(values):
    return jax.nn.gelu(values, approximate=True)


def whereabouts():
    me = lax.axis_index("seq")
    outer = me // INNER
    inner = me - outer * INNER
    y = inner // 2
    x = inner - 2 * y
    by_x = me + 1 - 2 * x
    by_y = me + 2 - 4 * y
    return me, outer, by_x, by_y, by_x + 2 - 4 * y


def when(condition, action):
    if condition is None:
        action()
    else:
        pl.when(condition)(action)


def both(one, other):
    if one is None or other is None:
        return one if other is None else other
    return jnp.logical_and(one, other)


def greet(peers):
    barrier = pltpu.get_barrier_semaphore()
    for condition, peer in peers:
        when(
            condition,
            lambda peer=peer: pl.semaphore_signal(
                barrier, inc=1, device_id={"seq": peer}, device_id_type=MESH
            ),
        )
    count = 0
    for condition, _ in peers:
        count = count + (1 if condition is None else condition.astype(jnp.int32))
    pl.semaphore_wait(barrier, count)


def greet_all(n, me, sibling=False):
    barrier = pltpu.get_barrier_semaphore()

    def hello(step, carry):
        pl.semaphore_signal(
            barrier, inc=1, device_id={"seq": lax.rem(me + step, n)}, device_id_type=MESH
        )
        return carry

    lax.fori_loop(1, n, hello, 0)
    if sibling:
        pl.semaphore_signal(
            barrier, inc=1, device_id={"ch": 1 - lax.axis_index("ch")}, device_id_type=MESH
        )
    pl.semaphore_wait(barrier, n if sibling else n - 1)


def remote(src, dst, send_sem, recv_sem, place):
    return pltpu.make_async_remote_copy(
        src_ref=src,
        dst_ref=dst,
        send_sem=send_sem,
        recv_sem=recv_sem,
        device_id={"seq": place},
        device_id_type=MESH,
    )


def params(collective_id, mib):
    return pltpu.CompilerParams(
        collective_id=collective_id, has_side_effects=True, vmem_limit_bytes=mib * 2**20
    )


def gather_body(n, *refs):
    w_refs, g_refs, f_refs, x_ref, gain_ref = refs[:3], refs[3:5], refs[5:8], refs[8], refs[9]
    wo_refs, go_ref, column_ref, one_ref, turned_ref, last_ref = refs[10:13], *refs[13:18]
    send_m, recv_m, send_f, recv_f, here, send_l, recv_l = refs[18:]
    groups = n // INNER
    me, outer, by_x, by_y, by_xy = whereabouts()
    above, below = outer + 1 < groups, outer > 0
    barrier = pltpu.get_barrier_semaphore()

    def hello(peer):
        pl.semaphore_signal(barrier, inc=1, device_id={"seq": peer}, device_id_type=MESH)

    hello(by_x)
    hello(by_y)

    def column_peer(turn):
        return lax.rem(outer + turn, groups)

    def hello_column(turn, carry):
        hello(me + (column_peer(turn) - outer) * INNER)
        return carry

    lax.fori_loop(1, groups, hello_column, 0)
    pl.when(me + 1 < n)(lambda: hello(me + 1))
    pl.when(me > 0)(lambda: hello(me - 1))
    neighbours = (me + 1 < n).astype(jnp.int32) + (me > 0).astype(jnp.int32)
    pl.semaphore_wait(barrier, groups + 1 + neighbours)
    units = Units(f_refs[0].shape[1], groups, lax.axis_index("ch"))
    half = w_refs[0].shape[1] // 2

    keep = [
        pltpu.make_async_copy(w_refs[kind], wo_refs[kind].at[me], here.at[kind])
        for kind in range(3)
    ]
    for gate in range(2):
        keep.append(pltpu.make_async_copy(g_refs[gate], go_ref.at[gate, :, me], here.at[3 + gate]))
    for kind in range(3):
        keep.append(
            Sized(
                units,
                outer,
                lambda width, kind=kind: pltpu.make_async_copy(
                    f_refs[kind].at[:, units.columns(outer, width)],
                    column_ref.at[kind, outer, :, pl.ds(0, width)],
                    here.at[5 + kind],
                ),
            )
        )
    for copy in keep:
        copy.start()
    sent = []

    def copies(h, source, way, target, own):
        cols = pl.ds(h * half, half)
        pairs = [
            (w_refs[kind].at[:, cols], wo_refs[kind].at[source, :, cols]) for kind in range(3)
        ]
        pairs.append((g_refs[h], go_ref.at[h, :, source]))
        return [
            remote(
                given if own else dst,
                dst,
                send_m.at[kind, h, source, way],
                recv_m.at[kind, h, source],
                target,
            )
            for kind, (given, dst) in enumerate(pairs)
        ]

    def send(condition, *what):
        def go():
            for copy in copies(*what):
                copy.start()

        when(condition, go)
        sent.append((condition, what))

    def arrive(condition, h, source):
        def go():
            for copy in copies(h, source, 0, by_x, False):
                copy.wait_recv()

        when(condition, go)

    def exchange(turn, receive):
        place = lax.rem(outer + groups - turn, groups) if receive else column_peer(turn)
        owner = outer if receive else place
        return [
            Sized(
                units,
                owner,
                lambda width, kind=kind: remote(
                    f_refs[kind].at[:, units.columns(owner, width)],
                    column_ref.at[kind, place if receive else outer, :, pl.ds(0, width)],
                    send_f.at[kind, turn],
                    recv_f.at[kind, turn],
                    me + (place - outer) * INNER,
                ),
            )
            for kind in range(3)
        ]

    def each_turn(action):
        def one(turn, carry):
            action(turn)
            return carry

        lax.fori_loop(1, groups, one, 0)

    tokens, model = x_ref.shape
    tall = last_ref.shape[0]
    last_copy = remote(one_ref.at[pl.ds(tokens - tall, tall)], last_ref, send_l, recv_l, me + 1)

    def norm(at, carry):
        r = pl.ds(pl.multiple_of(at * 16, 16), 16)
        x = x_ref[r].astype(F32)
        scale = lax.rsqrt(jnp.mean(x * x, axis=-1, keepdims=True) + 1e-06)
        one_ref[r] = (x * scale * gain_ref[...]).astype(BF16)
        return carry

    def norm_all():
        lax.fori_loop(0, tokens // 16, norm, 0)
        pl.when(me + 1 < n)(last_copy.start)
        for start in range(0, model, 256):
            cols = slice(start, start + 256)
            turned_ref[cols] = one_ref[:, cols].T

        @pl.when(me == 0)
        def _():
            last_ref[...] = jnp.zeros(last_ref.shape, BF16)

    for step in range(groups):
        if step == 1:
            norm_all()
        for h in range(2):
            flip_p, flip_q = (by_x, by_y) if h == 0 else (by_y, by_x)
            if step == 0:
                send(above, h, me, 0, me + INNER, True)
                send(below, h, me, 1, me - INNER, True)
                send(None, h, me, 2, flip_p, True)
                send(None, h, me, 3, flip_q, True)
                continue
            for source, there, onward, way, to in (
                (me - step * INNER, outer >= step, above, 0, me + INNER),
                (me + step * INNER, outer + step < groups, below, 1, me - INNER),
            ):
                arrive(there, h, source)
                send(both(there, onward), h, source, way, to, False)
                send(there, h, source, 2, flip_p, False)
                send(there, h, source, 3, flip_q, False)
    each_turn(lambda turn: [copy.start() for copy in exchange(turn, False)])
    for step in range(groups):
        for h in range(2):
            flip_p, flip_q = (by_x, by_y) if h == 0 else (by_y, by_x)
            if step == 0:
                arrive(None, h, flip_p)
                send(None, h, flip_p, 3, flip_q, False)
                continue
            for source, there in (
                (flip_p - step * INNER, outer >= step),
                (flip_p + step * INNER, outer + step < groups),
            ):
                arrive(there, h, source)
                send(there, h, source, 3, flip_q, False)
    for place in range(groups):
        shift = (place - outer) * INNER
        for h in range(2):
            arrive(None, h, (by_y if h == 0 else by_x) + shift)
            arrive(None, h, by_xy + shift)
    each_turn(lambda turn: [copy.wait_recv() for copy in exchange(turn, True)])
    for condition, what in sent:

        def finish(what=what):
            for copy in copies(*what):
                copy.wait_send()

        when(condition, finish)
    each_turn(lambda turn: [copy.wait_send() for copy in exchange(turn, False)])
    for copy in keep:
        copy.wait()
    pl.when(me > 0)(last_copy.wait_recv)
    pl.when(me + 1 < n)(last_copy.wait_send)


def gather_weights(weights, gates, ffn, x, gain):
    n = lax.axis_size("seq")
    groups = n // INNER
    rows, hidden_units = ffn[0].shape
    most = Units(hidden_units, groups, 0).most
    dma = pltpu.SemaphoreType.DMA
    made = [jax.ShapeDtypeStruct((n,) + w.shape, w.dtype) for w in weights]
    heads, part, size = gates[0].shape
    made.append(jax.ShapeDtypeStruct((2, heads, n, part, size), BF16))
    made.append(jax.ShapeDtypeStruct((3, groups, rows, most), BF16))
    made.append(jax.ShapeDtypeStruct(x.shape, BF16))
    made.append(jax.ShapeDtypeStruct(x.shape[::-1], BF16))
    made.append(jax.ShapeDtypeStruct((16, x.shape[1]), BF16))
    return pl.pallas_call(
        functools.partial(gather_body, n),
        out_shape=tuple(made),
        in_specs=[HBM] * 8 + [VMEM] * 2,
        out_specs=(HBM,) * 5 + (VMEM,) * 3,
        scratch_shapes=[
            dma((4, 2, n, 4)),
            dma((4, 2, n)),
            dma((3, groups)),
            dma((3, groups)),
            dma((8,)),
            dma(()),
            dma(()),
        ],
        compiler_params=params(1, 60),
        name="gather_weights",
    )(*weights, *gates, *ffn, x, gain)


LANES = 128


class Units:
    def __init__(self, total, groups, core):
        self.tiles, self.groups, self.core = total // LANES, groups, core
        self.most = -(-self.tiles // groups) * LANES
        self.even = self.tiles % groups == 0

    def start(self, place):
        up = (1 - self.core) * (self.groups - 1)
        return (place * self.tiles + up) // self.groups

    def full(self, place):
        return (self.start(place + 1) - self.start(place)) * LANES == self.most

    def width(self, place):
        return (self.start(place + 1) - self.start(place)) * LANES

    def columns(self, place, width):
        return pl.ds(pl.multiple_of(self.start(place) * LANES, LANES), width)


class Sized:
    def __init__(self, units, place, make):
        self.units, self.place, self.make = units, place, make

    def each(self, action):
        most = self.units.most
        if self.units.even:
            action(self.make(most))
            return
        full = self.units.full(self.place)
        pl.when(full)(lambda: action(self.make(most)))
        pl.when(jnp.logical_not(full))(lambda: action(self.make(most - LANES)))

    def start(self):
        self.each(lambda copy: copy.start())

    def wait(self):
        self.each(lambda copy: copy.wait())

    def wait_send(self):
        self.each(lambda copy: copy.wait_send())

    def wait_recv(self):
        self.each(lambda copy: copy.wait_recv())


def far_first(groups, outer, turn):
    def order(at):
        alone = groups - 1 - 2 * at
        later = turn - alone
        step = later // 2
        return jnp.where(
            turn < alone, groups - 1 - turn, jnp.where(later - 2 * step == 0, step, 2 * at - step)
        )

    return jnp.where(
        outer < groups // 2, order(outer), groups - 1 - order(groups - 1 - outer)
    )


class Chain:
    def __init__(self, n, own, whole, send, recv_z, recv_c):
        me = lax.axis_index("seq")
        self.groups = n // INNER
        self.outer = outer = me // INNER
        self.core = lax.axis_index("ch")
        self.above, self.below = outer + 1 < self.groups, outer > 0
        self.sibling = {"ch": 1 - self.core}
        self.to = ({"seq": me + INNER}, {"seq": me - INNER}, self.sibling)
        self.own, self.whole = own, whole
        self.send, self.recv_z, self.recv_c = send, recv_z, recv_c

    def copy(self, source, way, own=False):
        dst = self.whole.at[source, self.core]
        return pltpu.make_async_remote_copy(
            src_ref=self.own if own else dst,
            dst_ref=dst,
            send_sem=self.send.at[source, way],
            recv_sem=(self.recv_c if way == 2 else self.recv_z).at[source],
            device_id=self.to[way],
            device_id_type=MESH,
        )

    def from_sibling(self, source):
        return pltpu.make_async_remote_copy(
            src_ref=self.own,
            dst_ref=self.whole.at[source, 1 - self.core],
            send_sem=self.send.at[source, 2],
            recv_sem=self.recv_c.at[source],
            device_id=self.sibling,
            device_id_type=MESH,
        )

    def keep(self, sem):
        return pltpu.make_async_copy(self.own, self.whole.at[self.outer, self.core], sem)

    def ways(self, step):
        return (
            (self.outer - step, self.outer >= step, self.above, 0),
            (self.outer + step, self.outer + step < self.groups, self.below, 1),
        )

    def start(self):
        pl.when(self.above)(self.copy(self.outer, 0, True).start)
        pl.when(self.below)(self.copy(self.outer, 1, True).start)
        self.copy(self.outer, 2, True).start()

    def step(self, step):
        for source, there, onward, way in self.ways(step):
            pl.when(there)(self.copy(source, way).wait_recv)
            pl.when(both(there, onward))(self.copy(source, way).start)
            pl.when(there)(self.copy(source, 2).start)

    def finish(self):
        for source in range(self.groups):
            self.from_sibling(source).wait_recv()
        pl.when(self.above)(self.copy(self.outer, 0, True).wait_send)
        pl.when(self.below)(self.copy(self.outer, 1, True).wait_send)
        self.copy(self.outer, 2, True).wait_send()
        for step in range(1, self.groups):
            for source, there, onward, way in self.ways(step):
                pl.when(both(there, onward))(self.copy(source, way).wait_send)
                pl.when(there)(self.copy(source, 2).wait_send)


def chain_semaphores(groups):
    dma = pltpu.SemaphoreType.DMA
    return [dma((groups, 3)), dma((groups,)), dma((groups,))]


def tokens_body(n, *refs):
    own_ref, column_ref, near_ref = refs[:3]
    all_ref, w_refs = refs[3], refs[4:7]
    send_t, recv_z, recv_c, send_w, recv_w, here = refs[7:]
    groups = n // INNER
    half = groups // 2
    me, outer, by_x, by_y, by_xy = whereabouts()
    base = outer * INNER
    core = lax.axis_index("ch")
    above, below = outer + 1 < groups, outer > 0
    sibling = {"ch": 1 - core}
    barrier = pltpu.get_barrier_semaphore()

    def hello(peer):
        pl.semaphore_signal(barrier, inc=1, device_id=peer, device_id_type=MESH)

    hello({"seq": by_x})
    hello({"seq": by_y})
    hello(sibling)
    pl.when(above)(lambda: hello({"seq": me + INNER}))
    pl.when(below)(lambda: hello({"seq": me - INNER}))
    pl.semaphore_wait(barrier, 3 + above.astype(jnp.int32) + below.astype(jnp.int32))

    chain = Chain(n, own_ref, all_ref, send_t, recv_z, recv_c)

    def part(h):
        return pl.ds(h * half, half)

    flips = ((by_x, by_y), (by_y, by_x))

    def weight_copy(kind, h, far, receive=False):
        source = flips[h][0] if far else me
        if receive:
            source = by_xy if far else flips[h][1]
        return remote(
            near_ref.at[h, kind] if far else column_ref.at[kind, part(h)],
            w_refs[kind].at[part(h), source - base],
            send_w.at[kind, h, far],
            recv_w.at[kind, h, far],
            flips[h][1],
        )

    keep = [chain.keep(here.at[0])]
    for kind in range(3):
        keep.append(
            pltpu.make_async_copy(
                column_ref.at[kind], w_refs[kind].at[:, me - base], here.at[1 + kind]
            )
        )
        for h in range(2):
            keep.append(
                pltpu.make_async_copy(
                    near_ref.at[h, kind],
                    w_refs[kind].at[part(h), flips[h][0] - base],
                    here.at[4 + 2 * kind + h],
                )
            )
    every_w = [(kind, h, far) for kind in range(3) for h in range(2) for far in range(2)]

    chain.start()
    for what in every_w:
        weight_copy(*what).start()
    for copy in keep:
        copy.start()
    for step in range(1, groups):
        chain.step(step)
    for what in every_w:
        weight_copy(*what, receive=True).wait_recv()
    chain.finish()
    for what in every_w:
        weight_copy(*what).wait_send()
    for copy in keep:
        copy.wait()


def gather_tokens(tokens, column, near):
    n = lax.axis_size("seq")
    groups = n // INNER
    kinds, _, rows, units = column.shape
    dma = pltpu.SemaphoreType.DMA
    wide = jax.ShapeDtypeStruct((groups, 2) + tokens.shape, tokens.dtype)
    weight = jax.ShapeDtypeStruct((groups, INNER, rows, units), column.dtype)
    return pl.pallas_call(
        functools.partial(tokens_body, n),
        out_shape=(wide, weight, weight, weight),
        in_specs=[ANY] * 3,
        out_specs=(ANY,) * 4,
        scratch_shapes=chain_semaphores(groups)
        + [dma((kinds, 2, 2)), dma((kinds, 2, 2)), dma((10,))],
        compiler_params=params(6, 16),
        name="gather_tokens",
    )(tokens, column, near)


def reduce_body(n, kinds, *refs):
    p_refs, t_refs = refs[:kinds], refs[kinds : kinds + 3]
    out_refs, far_ref = refs[kinds + 3 : 2 * kinds + 3], refs[2 * kinds + 3]
    summed, got, send_c, recv_c, send_z, recv_z, send_f, recv_f = refs[2 * kinds + 4 :]
    groups = n // INNER
    half = groups // 2
    me, outer, by_x, by_y, by_xy = whereabouts()
    base = outer * INNER
    core = lax.axis_index("ch")
    above, below = outer + 1 < groups, outer > 0
    sibling = {"ch": 1 - core}
    barrier = pltpu.get_barrier_semaphore()

    def hello(peer):
        pl.semaphore_signal(barrier, inc=1, device_id=peer, device_id_type=MESH)

    hello({"seq": by_x})
    hello({"seq": by_y})
    hello(sibling)
    pl.when(above)(lambda: hello({"seq": me + INNER}))
    pl.when(below)(lambda: hello({"seq": me - INNER}))
    pl.semaphore_wait(barrier, 3 + above.astype(jnp.int32) + below.astype(jnp.int32))
    flips = ((by_x, by_y), (by_y, by_x))

    def gradient_copy(kind, h, far):
        source = by_xy if far else flips[h][1]
        return remote(
            t_refs[kind].at[pl.ds(h * half, half), source - base],
            far_ref.at[h, far, kind],
            send_f.at[kind, h, far],
            recv_f.at[kind, h, far],
            flips[h][1],
        )

    def to_sibling(kind, place):
        return pltpu.make_async_remote_copy(
            src_ref=p_refs[kind].at[place, 1 - core],
            dst_ref=summed.at[kind, place],
            send_sem=send_c.at[kind, place],
            recv_sem=recv_c.at[kind, place],
            device_id=sibling,
            device_id_type=MESH,
        )

    def along(kind, place, up):
        last = place == (outer + 1 if up else outer - 1)
        slot = place if up else jnp.where(last, groups, place)
        return remote(
            summed.at[kind, place],
            got.at[kind, slot],
            send_z.at[kind, place],
            recv_z.at[kind, slot],
            me + (INNER if up else -INNER),
        )

    def landed(kind, slot):
        return remote(
            summed.at[kind, 0], got.at[kind, slot], send_z.at[kind, 0], recv_z.at[kind, slot], by_x
        )

    def each(limit, action):
        def one(turn, carry):
            action(turn)
            return carry

        lax.fori_loop(0, limit, one, 0)

    every_f = [(kind, h, far) for far in (1, 0) for kind in range(3) for h in range(2)]
    for kind in range(kinds):
        each(groups, lambda place, kind=kind: to_sibling(kind, place).start())
    for what in every_f:
        gradient_copy(*what).start()

    tall = summed.shape[2]
    chunk = 16

    def rows_of(at):
        return pl.ds(pl.multiple_of(at * chunk, chunk), chunk)

    def ready(kind, place, incoming):
        to_sibling(kind, place).wait_recv()

        def local(at):
            r = rows_of(at)
            summed[kind, place, r] = (
                summed[kind, place, r].astype(F32) + p_refs[kind][place, core, r].astype(F32)
            ).astype(BF16)

        def more(at):
            r = rows_of(at)
            summed[kind, place, r] = (
                summed[kind, place, r].astype(F32)
                + p_refs[kind][place, core, r].astype(F32)
                + got[kind, place, r].astype(F32)
            ).astype(BF16)

        @pl.when(incoming)
        def _():
            landed(kind, place).wait_recv()
            each(tall // chunk, more)

        @pl.when(jnp.logical_not(incoming))
        def _():
            each(tall // chunk, local)

    for kind in range(kinds):

        def climb(turn, kind=kind):
            place = groups - 1 - turn

            @pl.when(place > outer)
            def _():
                ready(kind, place, below)
                along(kind, place, True).start()

        def sink(turn, kind=kind):
            place = turn

            @pl.when(place < outer)
            def _():
                ready(kind, place, above)
                along(kind, place, False).start()

        def turns(turn):
            @pl.when(outer < half)
            def _():
                climb(turn)
                sink(turn)

            @pl.when(outer >= half)
            def _():
                sink(turn)
                climb(turn)

        each(groups - 1, turns)
    for kind in range(kinds):
        to_sibling(kind, outer).wait_recv()

        def own(at, kind=kind):
            r = rows_of(at)
            out_refs[kind][r] = summed[kind, outer, r].astype(F32) + p_refs[kind][
                outer, core, r
            ].astype(F32)

        each(tall // chunk, own)
        for there, slot in ((below, outer), (above, groups)):

            @pl.when(there)
            def _():
                landed(kind, slot).wait_recv()

                def plus(at):
                    r = rows_of(at)
                    out_refs[kind][r] = out_refs[kind][r] + got[kind, slot, r].astype(F32)

                each(tall // chunk, plus)

    for kind in range(kinds):

        def clear(place, kind=kind):
            to_sibling(kind, place).wait_send()

            @pl.when(place > outer)
            def _():
                along(kind, place, True).wait_send()

            @pl.when(place < outer)
            def _():
                along(kind, place, False).wait_send()

        each(groups, clear)
    for what in every_f:
        gradient_copy(*what).wait()


def reduce_tokens(partials, gradients):
    n = lax.axis_size("seq")
    groups = n // INNER
    kinds = len(partials)
    _, _, tall, width = partials[0].shape
    _, _, rows, units = gradients[0].shape
    dma = pltpu.SemaphoreType.DMA
    return pl.pallas_call(
        functools.partial(reduce_body, n, kinds),
        out_shape=(jax.ShapeDtypeStruct((tall, width), F32),) * kinds
        + (jax.ShapeDtypeStruct((2, 2, 3, groups // 2, rows, units), BF16),),
        in_specs=[VMEM] * kinds + [ANY] * 3,
        out_specs=(VMEM,) * kinds + (ANY,),
        scratch_shapes=[
            pltpu.VMEM((kinds, groups, tall, width), BF16),
            pltpu.VMEM((kinds, groups + 1, tall, width), BF16),
            dma((kinds, groups)),
            dma((kinds, groups)),
            dma((kinds, groups)),
            dma((kinds, groups + 1)),
            dma((3, 2, 2)),
            dma((3, 2, 2)),
        ],
        compiler_params=params(7, 60),
        name="reduce_tokens",
    )(*partials, *gradients)


def scatter_body(
    n,
    one_ref,
    mixed_ref,
    dy_ref,
    dxb_ref,
    branch_ref,
    gate_ref,
    dpar_ref,
    gain_one_ref,
    gain_two_ref,
    column_ref,
    out_ref,
    small_out,
    spread_ref,
    made,
    got_q,
    got_p,
    got_z,
    got_s,
    *sems,
):
    send_q, recv_q, send_p, recv_p, send_z, recv_z, send_s, recv_s, send_f, recv_f, here = sems
    groups = n // INNER
    me, outer, by_x, by_y, by_xy = whereabouts()
    rows = one_ref.shape[1]
    part_rows = gate_ref.shape[2]
    total, width = out_ref.shape
    half = width // 2

    def place_of(turn):
        return far_first(groups, outer, turn)

    def base_of(turn):
        return (place_of(turn) - outer) * INNER

    barrier = pltpu.get_barrier_semaphore()

    def hello(peer):
        pl.semaphore_signal(barrier, inc=1, device_id={"seq": peer}, device_id_type=MESH)

    hello(by_x)
    hello(by_y)

    def hello_outer(turn, carry):
        hello(me + base_of(turn))
        return carry

    lax.fori_loop(0, groups - 1, hello_outer, 0)
    core = lax.axis_index("ch")
    masks = [1 << bit for bit in range(n.bit_length() - 1)]
    pl.semaphore_signal(barrier, inc=1, device_id={"ch": 1 - core}, device_id_type=MESH)
    pl.semaphore_wait(barrier, groups + 2)

    flips = ((by_x, by_y), (by_y, by_x))
    units = Units(spread_ref.shape[2], groups, core)

    def exchange(turn, receive=False):
        place = lax.rem(outer + (groups - 1 - turn if receive else turn + 1), groups)
        owner = place if receive else outer
        return Sized(
            units,
            owner,
            lambda width: remote(
                column_ref.at[:, place, :, pl.ds(0, width)],
                spread_ref.at[:, :, units.columns(owner, width)],
                send_f.at[turn],
                recv_f.at[turn],
                me + (place - outer) * INNER,
            ),
        )

    def small(turn):
        place = me
        for at, mask in enumerate(masks):
            flipped = me + mask * (1 - 2 * lax.rem(me // mask, 2))
            place = jnp.where(turn == at, flipped, place)
        other = jnp.where(turn == len(masks), 1 - core, core)
        return pltpu.make_async_remote_copy(
            src_ref=small_out,
            dst_ref=got_s.at[turn],
            send_sem=send_s.at[turn],
            recv_sem=recv_s.at[turn],
            device_id=(place, other),
            device_id_type=MESH,
        )

    small_out[:8] = dpar_ref[...]
    small_out[8:] = jnp.zeros((8, width), F32)
    at = 8
    for gain_ref in (gain_one_ref, gain_two_ref):
        for start in range(0, gain_ref.shape[1], width):
            small_out[at : at + 1] = gain_ref[:, start : start + width]
            at += 1
    small_row = lax.broadcasted_iota(jnp.int32, small_out.shape, 0)

    def cols(h):
        return pl.ds(h * half, half)

    def along_q(turn, h, other):
        source = (by_xy if other else flips[h][1]) + base_of(turn)
        return remote(
            made.at[source, :, cols(h)],
            got_q.at[h, turn, other],
            send_q.at[h, turn, other],
            recv_q.at[h, turn, other],
            flips[h][1],
        )

    def along_p(turn, h):
        return remote(
            made.at[flips[h][0] + base_of(turn), :, cols(h)],
            got_p.at[h, turn],
            send_p.at[h, turn],
            recv_p.at[h, turn],
            flips[h][0],
        )

    def along_z(turn, h):
        place = place_of(turn)
        up = place > outer
        onto = jnp.where(up, outer + 1, outer - 1)
        slot = jnp.where(jnp.logical_and(place == onto, jnp.logical_not(up)), groups, place)
        return remote(
            made.at[me + base_of(turn), :, cols(h)],
            got_z.at[h, slot],
            send_z.at[h, turn],
            recv_z.at[h, slot],
            me + (onto - outer) * INNER,
        )

    def landed(slot, h):
        return remote(
            made.at[me, :, cols(h)], got_z.at[h, slot], send_z.at[h, 0], recv_z.at[h, slot], by_x
        )

    def has_incoming(turn):
        return jnp.where(place_of(turn) > outer, outer > 0, outer < groups - 1)

    def pass_on(turn):
        incoming = has_incoming(turn)
        for h in range(2):

            @pl.when(incoming)
            def _():
                landed(place_of(turn), h).wait_recv()
                add(me + base_of(turn), h, got_z, (h, place_of(turn)))

            along_z(turn, h).start()

    def make(block):
        left = one_ref[block]
        parts = [
            jnp.dot(left, dy_ref[...], preferred_element_type=F32),
            jnp.dot(left, dxb_ref[...], preferred_element_type=F32),
            jnp.dot(mixed_ref[block], branch_ref[...], preferred_element_type=F32),
        ]
        if rows % 16 == 0:
            for at, part in enumerate(parts):
                made[block, at * rows : (at + 1) * rows] = part.astype(BF16)
            for gate in range(2):
                at = 3 * rows + gate * part_rows
                made[block, at : at + part_rows] = gate_ref[block, gate]
        else:
            parts.extend(gate_ref[block, gate].astype(F32) for gate in range(2))
            made[block] = jnp.concatenate(parts, axis=0).astype(BF16)

    step = 32

    def add(block, h, ref, index):
        def one(at, carry):
            r = pl.ds(pl.multiple_of(at * step, step), step)
            made[block, r, cols(h)] = (
                made[block, r, cols(h)].astype(F32) + ref[index + (r,)].astype(F32)
            ).astype(BF16)
            return carry

        lax.fori_loop(0, total // step, one, 0)

    keep = Sized(
        units,
        outer,
        lambda width: pltpu.make_async_copy(
            column_ref.at[:, outer, :, pl.ds(0, width)],
            spread_ref.at[:, :, units.columns(outer, width)],
            here,
        ),
    )
    keep.start()

    def begin(turn, other):
        base = base_of(turn)
        if other:
            make(by_xy + base)
        else:
            for h in range(2):
                make(flips[h][1] + base)
        for h in range(2):
            along_q(turn, h, other).start()

    begin(0, 1)
    begin(0, 0)
    make(me + base_of(0))

    def turn_of(turn, carry):
        pl.when(turn <= len(masks))(lambda: small(turn).start())
        pl.when(turn < groups - 1)(lambda: exchange(turn).start())

        @pl.when(turn < groups)
        def _():
            base = base_of(turn)
            for h in range(2):
                along_q(turn, h, 1).wait_recv()
                add(flips[h][0] + base, h, got_q, (h, turn, 1))
                along_p(turn, h).start()
            pl.when(turn < groups - 1)(lambda: begin(turn + 1, 1))
            for h in range(2):
                along_q(turn, h, 0).wait_recv()
                add(me + base, h, got_q, (h, turn, 0))

            @pl.when(turn < groups - 1)
            def _():
                begin(turn + 1, 0)
                make(me + base_of(turn + 1))

            for h in range(2):
                along_p(turn, h).wait_recv()
                add(me + base, h, got_p, (h, turn))

            @pl.when(jnp.logical_and(turn < groups - 1, jnp.logical_not(has_incoming(turn))))
            def _():
                pass_on(turn)

            @pl.when(jnp.logical_and(turn >= 1, turn < groups - 1))
            def _():
                pl.when(has_incoming(turn - 1))(lambda: pass_on(turn - 1))

            @pl.when(jnp.logical_and(turn == groups - 2, has_incoming(turn)))
            def _():
                pass_on(turn)

        @pl.when(turn <= len(masks))
        def _():
            small(turn).wait()
            counts = jnp.logical_or(turn < len(masks), small_row >= 8)
            small_out[...] = small_out[...] + jnp.where(counts, got_s[turn], 0.0)

        return carry

    assert len(masks) < groups + 2
    lax.fori_loop(0, groups + 2, turn_of, 0)
    for condition, slots in (
        (jnp.logical_and(outer > 0, outer < groups - 1), (outer, groups)),
        (outer == groups - 1, (outer,)),
        (outer == 0, (groups,)),
    ):

        @pl.when(condition)
        def _(slots=slots):
            for h in range(2):
                for slot in slots:
                    landed(slot, h).wait_recv()

                def finish(at, carry):
                    r = pl.ds(pl.multiple_of(at * step, step), step)
                    value = made[me, r, cols(h)].astype(F32)
                    for slot in slots:
                        value = value + got_z[h, slot, r].astype(F32)
                    out_ref[r, cols(h)] = value
                    return carry

                lax.fori_loop(0, total // step, finish, 0)

    def clear(turn, carry):
        for h in range(2):
            along_q(turn, h, 0).wait_send()
            along_q(turn, h, 1).wait_send()
            along_p(turn, h).wait_send()

            @pl.when(turn < groups - 1)
            def _():
                along_z(turn, h).wait_send()

        @pl.when(turn < groups - 1)
        def _():
            exchange(turn, True).wait_recv()
            exchange(turn).wait_send()

        return carry

    lax.fori_loop(0, groups, clear, 0)
    keep.wait()


def scatter_mixer(one, mixed, dy, dxb, branch, gates, dpar, gain_one, gain_two, column, hidden_units):
    n, rows, _ = one.shape
    groups = n // INNER
    width = dy.shape[1]
    total = 3 * rows + 2 * gates.shape[2]
    kinds = column.shape[0]
    turns = n.bit_length()
    dma = pltpu.SemaphoreType.DMA
    return pl.pallas_call(
        functools.partial(scatter_body, n),
        out_shape=(
            jax.ShapeDtypeStruct((total, width), F32),
            jax.ShapeDtypeStruct((16, width), F32),
            jax.ShapeDtypeStruct((kinds, rows, hidden_units), BF16),
        ),
        in_specs=[VMEM] * 9 + [ANY],
        out_specs=(VMEM, VMEM, ANY),
        scratch_shapes=[
            pltpu.VMEM((n, total, width), BF16),
            pltpu.VMEM((2, groups, 2, total, width // 2), BF16),
            pltpu.VMEM((2, groups, total, width // 2), BF16),
            pltpu.VMEM((2, groups + 1, total, width // 2), BF16),
            pltpu.VMEM((turns, 16, width), F32),
            dma((2, groups, 2)),
            dma((2, groups, 2)),
            dma((2, groups)),
            dma((2, groups)),
            dma((2, groups)),
            dma((2, groups + 1)),
            dma((turns,)),
            dma((turns,)),
            dma((groups,)),
            dma((groups,)),
            dma(()),
        ],
        compiler_params=params(2, 62),
        name="scatter_mixer",
    )(one, mixed, dy, dxb, branch, gates, dpar, gain_one, gain_two, column)


GELU_A = 0.7978845608028654
GELU_B = 0.044715


def gelu_parts(v):
    t = jnp.tanh(GELU_A * (v + GELU_B * v * v * v))
    value = 0.5 * v * (1.0 + t)
    slope = 0.5 * (1.0 + t) + 0.5 * v * (1.0 - t * t) * GELU_A * (1.0 + 3.0 * GELU_B * v * v)
    return value, slope


def gates_of(conv_low, gate_ref, par_ref, head, cols, first):
    pre_x = jnp.dot(conv_low, gate_ref[0, head], preferred_element_type=F32)
    pre_a = jnp.dot(conv_low, gate_ref[1, head], preferred_element_type=F32)
    gate_x = jax.nn.sigmoid(pre_x + par_ref[5:6, cols])
    gate_a = jax.nn.sigmoid(pre_a + par_ref[6:7, cols])
    decay = jnp.exp(-8.0 * gate_a * par_ref[8:9, cols])
    room = 1.0 - decay * decay
    mult = jnp.where(first, 1.0, jnp.sqrt(jnp.maximum(room, 0.001)))
    return gate_x, gate_a, decay, room, mult


FLIPPED = (((1,), (1,)), ((), ()))


def first_row(tokens):
    row = lax.broadcasted_iota(jnp.int32, (tokens, 1), 0)
    return jnp.logical_and(row == 0, lax.axis_index("seq") == 0)


def forward_body(
    n,
    hidden_units,
    one_ref,
    last_ref,
    w_in_ref,
    w_branch_ref,
    w_out_ref,
    gate_ref,
    par_ref,
    x_ref,
    gain_ref,
    column_ref,
    xb_ref,
    yp_ref,
    conv_ref,
    state_ref,
    branch_ref,
    edge_ref,
    resid_ref,
    two_ref,
    near_ref,
    w_in,
    w_branch,
    w_out,
    mixed,
    mixed_got,
    wide,
    fade,
    mine,
    theirs,
    *sems,
):
    send_tot, recv_tot, send_f, recv_f, send_m, recv_m, loaded = sems
    tokens, width = xb_ref.shape
    model = one_ref.shape[1]
    me = lax.axis_index("seq")
    size = gate_ref.shape[2]
    loads = [
        pltpu.make_async_copy(src, dst, loaded.at[at])
        for at, (src, dst) in enumerate(
            ((w_in_ref, w_in), (w_branch_ref, w_branch), (w_out_ref, w_out))
        )
    ]
    for load in loads:
        load.start()
    greet_all(n, me, True)
    _, _, by_x, by_y, _ = whereabouts()
    part = column_ref.shape[1] // 2
    kinds = column_ref.shape[0]
    units = Units(hidden_units, n // INNER, lax.axis_index("ch"))
    outer = me // INNER
    hosted = [
        [
            Sized(
                units,
                outer,
                lambda width, kind=kind, h=h, part=part: remote(
                    column_ref.at[kind, pl.ds(h * part, part), :, pl.ds(0, width)],
                    near_ref.at[h, kind, :, :, pl.ds(0, width)],
                    send_f.at[kind, h],
                    recv_f.at[kind, h],
                    (by_x, by_y)[h],
                ),
            )
            for h in range(2)
        ]
        for kind in range(kinds)
    ]

    def host(pieces):
        for pair in pieces:
            for copy in pair:
                copy.start()

    host(hosted[:1])
    loads[0].wait()
    for start in range(0, width, size):
        cols = slice(start, start + size)
        low = jnp.dot(one_ref[...], w_in[:, cols], preferred_element_type=F32).astype(BF16)
        xb_ref[:, cols] = low
        wide[8:, cols] = low.astype(F32)
        low = jnp.dot(last_ref[...], w_in[:, cols], preferred_element_type=F32).astype(BF16)
        wide[:8, cols] = low.astype(F32)[8:]
    loads[1].wait()
    for start in range(0, width, size):
        cols = slice(start, start + size)
        yp_ref[:, cols] = jnp.dot(one_ref[...], w_branch[:, cols], preferred_element_type=F32)

    edge_ref[:8] = wide[:8]
    first = first_row(tokens)
    for head in range(width // size):
        cols = slice(head * size, (head + 1) * size)
        conv = par_ref[4:5, cols]
        for tap in range(4):
            conv = conv + par_ref[tap : tap + 1, cols] * wide[8 - tap : 8 - tap + tokens, cols]
        conv_low = conv.astype(BF16)
        conv_ref[:, cols] = conv_low
        gate_x, _, decay, _, mult = gates_of(conv_low, gate_ref, par_ref, head, cols, first)
        fade[:, cols] = decay
        state_ref[:, cols] = conv_low.astype(F32) * gate_x * mult

    row = lax.broadcasted_iota(jnp.int32, (8, width), 0)

    def inside(at, carry):
        r = pl.ds(pl.multiple_of(at * 8, 8), 8)
        a, b = fade[r], state_ref[r]
        for by in (1, 2, 4):
            a_back = pltpu.roll(a, by, 0)
            b_back = pltpu.roll(b, by, 0)
            b = jnp.where(row >= by, a * b_back + b, b)
            a = jnp.where(row >= by, a * a_back, a)
        fade[r] = a
        state_ref[r] = b
        return a[7:8] * carry[0], a[7:8] * carry[1] + b[7:8]

    ones, zeros = jnp.ones((1, width), F32), jnp.zeros((1, width), F32)
    tot_a, tot_b = lax.fori_loop(0, tokens // 8, inside, (ones, zeros))
    mine[0:1] = tot_a
    mine[1:2] = tot_b

    def told(place):
        return remote(mine, theirs.at[me], send_tot.at[place], recv_tot.at[me], place)

    def heard(place):
        return remote(mine, theirs.at[place], send_tot.at[place], recv_tot.at[place], place)

    def tell(place, carry):
        told(place).start()
        return carry

    lax.fori_loop(me + 1, n, tell, 0)
    host(hosted[1:])

    def hear(place, state):
        heard(place).wait_recv()
        return theirs[place, 0:1] * state + theirs[place, 1:2]

    carry_in = lax.fori_loop(0, me, hear, zeros)
    edge_ref[8:] = jnp.broadcast_to(carry_in, (8, width))

    def finish(at, carry):
        r = pl.ds(pl.multiple_of(at * 16, 16), 16)
        a, b = fade[r], state_ref[r]
        top = b[:8] + a[:8] * carry
        low = b[8:] + a[8:] * top[7:8]
        states = jnp.concatenate([top, low], axis=0)
        state_ref[r] = states
        branch_ref[r] = (states * gelu_parts(yp_ref[r])[0]).astype(BF16)
        return low[7:8]

    lax.fori_loop(0, tokens // 16, finish, carry_in)

    def sent(place, carry):
        told(place).wait_send()
        return carry

    lax.fori_loop(me + 1, n, sent, 0)
    loads[2].wait()
    core = lax.axis_index("ch")
    half = tokens // 2
    for start in range(0, model, size):
        cols = slice(start, start + size)
        part = lax.dot_general(branch_ref[...], w_out[cols], FLIPPED, preferred_element_type=F32)
        mixed[0, :, cols] = part[:half]
        mixed[1, :, cols] = part[half:]
    exchange = pltpu.make_async_remote_copy(
        src_ref=mixed.at[1 - core],
        dst_ref=mixed_got,
        send_sem=send_m,
        recv_sem=recv_m,
        device_id={"ch": 1 - core},
        device_id_type=MESH,
    )
    exchange.start()
    exchange.wait_recv()

    def norm(at, carry):
        r = pl.ds(pl.multiple_of(at * 16, 16), 16)
        resid = x_ref[r].astype(F32) + (mixed[core, r] + mixed_got[r])
        resid_ref[r] = resid
        scale = lax.rsqrt(jnp.mean(resid * resid, axis=-1, keepdims=True) + 1e-06)
        two_ref[r] = (resid * scale * gain_ref[...]).astype(BF16)
        return carry

    lax.fori_loop(0, half // 16, norm, 0)
    exchange.wait_send()
    for pair in hosted:
        for copy in pair:
            copy.wait()


def mixer_forward(one, last, weights, gates, par, x_half, gain, column, hidden_units):
    n = lax.axis_size("seq")
    tokens, model = one.shape
    width = par.shape[1]
    half = tokens // 2
    kinds, groups, rows, units = column.shape
    dma = pltpu.SemaphoreType.DMA
    whole = jax.ShapeDtypeStruct((tokens, width), F32)
    low = jax.ShapeDtypeStruct((tokens, width), BF16)
    return pl.pallas_call(
        functools.partial(forward_body, n, hidden_units),
        out_shape=(
            low,
            whole,
            low,
            whole,
            low,
            jax.ShapeDtypeStruct((16, width), F32),
            jax.ShapeDtypeStruct((half, model), F32),
            jax.ShapeDtypeStruct((half, model), BF16),
            jax.ShapeDtypeStruct((2, kinds, groups // 2, rows, units), column.dtype),
        ),
        in_specs=[VMEM] * 2 + [HBM] * 3 + [VMEM] * 4 + [HBM],
        out_specs=(VMEM,) * 8 + (HBM,),
        scratch_shapes=[
            pltpu.VMEM((model, width), BF16),
            pltpu.VMEM((model, width), BF16),
            pltpu.VMEM((model, width), BF16),
            pltpu.VMEM((2, half, model), F32),
            pltpu.VMEM((half, model), F32),
            pltpu.VMEM((tokens + 8, width), F32),
            pltpu.VMEM((tokens, width), F32),
            pltpu.VMEM((2, width), F32),
            pltpu.VMEM((n, 2, width), F32),
            dma((n,)),
            dma((n,)),
            dma((kinds, 2)),
            dma((kinds, 2)),
            dma(()),
            dma(()),
            dma((3,)),
        ],
        compiler_params=params(4, 60),
        name="mixer_forward",
    )(one, last, *weights, gates, par, x_half, gain, column)


def backward_body(
    n,
    hidden_units,
    mixed_ref,
    w_in_ref,
    w_branch_ref,
    w_out_ref,
    x_ref,
    gain_ref,
    resid_ref,
    yp_ref,
    state_ref,
    edge_ref,
    conv_ref,
    xb_ref,
    gate_ref,
    par_ref,
    half_ref,
    own_ref,
    dy_ref,
    dxb_ref,
    dgate_ref,
    dpar_ref,
    dx_ref,
    dgain_ref,
    column_ref,
    near_ref,
    own,
    w_in,
    w_branch,
    w_out,
    d_one,
    d_one_got,
    d_one_part,
    fade,
    shift,
    adj,
    gate_x_s,
    gate_a_s,
    dconv,
    wide,
    mine,
    theirs,
    head_rows,
    *sems,
):
    send_rows, recv_rows, send_tot, recv_tot, send_f, recv_f, send_m, recv_m, send_x, recv_x, loaded, own_sem, out_sem = sems
    tokens, width = xb_ref.shape
    model = gain_ref.shape[1]
    me = lax.axis_index("seq")
    size = gate_ref.shape[2]
    loads = [
        pltpu.make_async_copy(src, dst, loaded.at[at])
        for at, (src, dst) in enumerate(
            ((w_out_ref, w_out), (w_in_ref, w_in), (w_branch_ref, w_branch))
        )
    ]
    for load in loads:
        load.start()
    greet_all(n, me, True)
    _, _, by_x, by_y, _ = whereabouts()
    kinds, pieces = half_ref.shape[1:3]
    units = Units(hidden_units, n // INNER, lax.axis_index("ch"))
    outer = me // INNER
    hosted = [
        [
            Sized(
                units,
                outer,
                lambda width, kind=kind, at=at, h=h: remote(
                    half_ref.at[h, kind, at, :, pl.ds(0, width)],
                    near_ref.at[h, kind, at, :, pl.ds(0, width)],
                    send_f.at[kind, at, h],
                    recv_f.at[kind, at, h],
                    (by_x, by_y)[h],
                ),
            )
            for h in range(2)
        ]
        for kind in range(kinds)
        for at in range(pieces)
    ]

    def host(some):
        for pair in some:
            for copy in pair:
                copy.start()

    host(hosted[:2])
    own_load = pltpu.make_async_copy(own_ref, own, own_sem)
    own_load.start()
    first = first_row(tokens)
    fade[tokens:] = jnp.ones((8, width), F32)
    loads[0].wait()
    for head in range(width // size):
        cols = slice(head * size, (head + 1) * size)
        gate_x, gate_a, decay, _, _ = gates_of(conv_ref[:, cols], gate_ref, par_ref, head, cols, first)
        gate_x_s[:, cols] = gate_x
        gate_a_s[:, cols] = gate_a
        fade[:tokens, cols] = decay
        value, slope = gelu_parts(yp_ref[:, cols])
        grad = jnp.dot(mixed_ref[...], w_out[:, cols], preferred_element_type=F32)
        dy_ref[:, cols] = (grad * state_ref[:, cols] * slope).astype(BF16)
        adj[:, cols] = grad * value
        shift[:, cols] = fade[1 : tokens + 1, cols]

    row = lax.broadcasted_iota(jnp.int32, (8, width), 0)
    tiles = tokens // 8

    def inside(turn, carry):
        r = pl.ds(pl.multiple_of((tiles - 1 - turn) * 8, 8), 8)
        a, b = shift[r], adj[r]
        for by in (1, 2, 4):
            a_next = pltpu.roll(a, 8 - by, 0)
            b_next = pltpu.roll(b, 8 - by, 0)
            b = jnp.where(row < 8 - by, a * b_next + b, b)
            a = jnp.where(row < 8 - by, a * a_next, a)
        shift[r] = a
        adj[r] = b
        return a[0:1] * carry[0], a[0:1] * carry[1] + b[0:1]

    ones, zeros = jnp.ones((1, width), F32), jnp.zeros((1, width), F32)
    tot_a, tot_b = lax.fori_loop(0, tiles, inside, (ones, zeros))
    first_fade = fade[0:1]
    mine[0:1] = first_fade * tot_a
    mine[1:2] = first_fade * tot_b

    def told(place):
        return remote(mine, theirs.at[me], send_tot.at[place], recv_tot.at[me], place)

    def heard(place):
        return remote(mine, theirs.at[place], send_tot.at[place], recv_tot.at[place], place)

    def tell(place, carry):
        told(place).start()
        return carry

    lax.fori_loop(0, me, tell, 0)
    host(hosted[2:3])

    def hear(turn, state):
        place = n - 1 - turn
        heard(place).wait_recv()
        return theirs[place, 0:1] * state + theirs[place, 1:2]

    carry_in = lax.fori_loop(0, n - 1 - me, hear, zeros)

    def finish(turn, carry):
        r = pl.ds(pl.multiple_of((tiles - 1 - turn) * 8, 8), 8)
        value = adj[r] + shift[r] * carry
        adj[r] = value
        return value[0:1]

    lax.fori_loop(0, tiles, finish, carry_in)

    wide[:8] = edge_ref[:8]
    wide[8:] = xb_ref[...].astype(F32)
    at_first = lax.broadcasted_iota(jnp.int32, (tokens, 1), 0) == 0
    for head in range(width // size):
        cols = slice(head * size, (head + 1) * size)
        conv_low = conv_ref[:, cols]
        conv = conv_low.astype(F32)
        gate_x, gate_a, decay = gate_x_s[:, cols], gate_a_s[:, cols], fade[:tokens, cols]
        room = 1.0 - decay * decay
        mult = jnp.where(first, 1.0, jnp.sqrt(jnp.maximum(room, 0.001)))
        back = adj[:, cols]
        before = jnp.where(at_first, edge_ref[8:9, cols], pltpu.roll(state_ref[:, cols], 1, 0))
        d_mult = back * conv * gate_x
        moves = jnp.logical_and(room > 0.001, jnp.logical_not(first))
        d_decay = back * before - jnp.where(moves, d_mult * decay / mult, 0.0)
        d_log = d_decay * decay
        d_pre_x = back * conv * mult * gate_x * (1.0 - gate_x)
        d_pre_a = d_log * (-8.0 * par_ref[8:9, cols]) * gate_a * (1.0 - gate_a)
        dpar_ref[5:6, cols] = jnp.sum(d_pre_x, axis=0, keepdims=True)
        dpar_ref[6:7, cols] = jnp.sum(d_pre_a, axis=0, keepdims=True)
        dpar_ref[7:8, cols] = (
            jnp.sum(d_log * (-8.0 * gate_a), axis=0, keepdims=True) * par_ref[9:10, cols]
        )
        low_x, low_a = d_pre_x.astype(BF16), d_pre_a.astype(BF16)
        d_conv = (
            back * gate_x * mult
            + lax.dot_general(low_x, gate_ref[0, head], FLIPPED, preferred_element_type=F32)
            + lax.dot_general(low_a, gate_ref[1, head], FLIPPED, preferred_element_type=F32)
        )
        dconv[:tokens, cols] = d_conv
        over_rows = (((0,), (0,)), ((), ()))
        for gate, low in enumerate((low_x, low_a)):
            d_gate = lax.dot_general(conv_low, low, over_rows, preferred_element_type=F32)
            dgate_ref[:, gate, :, cols] = d_gate.astype(BF16).reshape(n, size // n, size)
        dpar_ref[4:5, cols] = jnp.sum(d_conv, axis=0, keepdims=True)
        for tap in range(4):
            dpar_ref[tap : tap + 1, cols] = jnp.sum(
                d_conv * wide[8 - tap : 8 - tap + tokens, cols], axis=0, keepdims=True
            )

    rows_copy = remote(
        dconv.at[pl.ds(0, 8)], head_rows, send_rows, recv_rows, lax.rem(me + n - 1, n)
    )
    pl.when(me > 0)(rows_copy.start)
    host(hosted[3:])
    loads[2].wait()
    for start in range(0, model, size):
        cols = slice(start, start + size)
        d_one_part[:, cols] = lax.dot_general(
            dy_ref[...], w_branch[cols], FLIPPED, preferred_element_type=F32
        )

    @pl.when(me + 1 < n)
    def _():
        rows_copy.wait_recv()
        dconv[tokens:] = head_rows[...]

    @pl.when(me + 1 == n)
    def _():
        dconv[tokens:] = jnp.zeros((8, width), F32)

    for head in range(width // size):
        cols = slice(head * size, (head + 1) * size)
        total = par_ref[0:1, cols] * dconv[:tokens, cols]
        for tap in range(1, 4):
            total = total + par_ref[tap : tap + 1, cols] * dconv[tap : tap + tokens, cols]
        dxb_ref[:, cols] = total.astype(BF16)

    pl.when(me > 0)(rows_copy.wait_send)

    def sent(place, carry):
        told(place).wait_send()
        return carry

    lax.fori_loop(0, me, sent, 0)
    core = lax.axis_index("ch")
    half = tokens // 2
    loads[1].wait()
    for start in range(0, model, size):
        cols = slice(start, start + size)
        part = (
            d_one_part[:, cols]
            + lax.dot_general(dxb_ref[...], w_in[cols], FLIPPED, preferred_element_type=F32)
        ).astype(BF16)
        d_one[0, :, cols] = part[:half]
        d_one[1, :, cols] = part[half:]
    exchange = pltpu.make_async_remote_copy(
        src_ref=d_one.at[1 - core],
        dst_ref=d_one_got,
        send_sem=send_m,
        recv_sem=recv_m,
        device_id={"ch": 1 - core},
        device_id_type=MESH,
    )
    exchange.start()
    exchange.wait_recv()

    def norm(at, total):
        r = pl.ds(pl.multiple_of(at * 16, 16), 16)
        x = x_ref[r].astype(F32)
        scale = lax.rsqrt(jnp.mean(x * x, axis=-1, keepdims=True) + 1e-06)
        grad = d_one[core, r].astype(F32) + d_one_got[r].astype(F32)
        back = grad * gain_ref[...]
        shrink = scale * scale * scale * jnp.mean(x * back, axis=-1, keepdims=True)
        dx_ref[core, r] = resid_ref[r] + (scale * back - x * shrink)
        return total + jnp.sum(grad * (x * scale), axis=0, keepdims=True)

    dgain_ref[...] = lax.fori_loop(0, half // 16, norm, jnp.zeros((1, model), F32))
    share = pltpu.make_async_remote_copy(
        src_ref=dx_ref.at[core],
        dst_ref=dx_ref.at[core],
        send_sem=send_x,
        recv_sem=recv_x,
        device_id={"ch": 1 - core},
        device_id_type=MESH,
    )
    share.start()
    exchange.wait_send()
    own_load.wait()
    part, rows = own.shape[2:4]
    chunk = 16 if rows % 16 == 0 else rows
    outs = []
    for kind in range(kinds):
        for h in range(2):
            for place in range(part):
                hosted[kind * part + place][h].wait()

                def add(at, carry, kind=kind, h=h, place=place):
                    r = pl.ds(pl.multiple_of(at * chunk, chunk), chunk)
                    own[h, kind, place, r] = (
                        own[h, kind, place, r].astype(F32) + near_ref[h, kind, place, r].astype(F32)
                    ).astype(BF16)
                    return carry

                lax.fori_loop(0, rows // chunk, add, 0)
            outs.append(
                pltpu.make_async_copy(
                    own.at[h, kind],
                    column_ref.at[kind, pl.ds(h * part, part)],
                    out_sem.at[kind, h],
                )
            )
            outs[-1].start()
    for copy in outs:
        copy.wait()
    pltpu.make_async_remote_copy(
        src_ref=dx_ref.at[core],
        dst_ref=dx_ref.at[1 - core],
        send_sem=send_x,
        recv_sem=recv_x,
        device_id={"ch": 1 - core},
        device_id_type=MESH,
    ).wait_recv()
    share.wait_send()


def mixer_backward(
    mixed, weights, x_half, gain, d_resid, y_pre, states, edge, conv, x_branch, gates, par, halves, own, hidden_units
):
    n = lax.axis_size("seq")
    tokens, width = x_branch.shape
    model = mixed.shape[1]
    size = gates.shape[2]
    half = tokens // 2
    _, kinds, part, rows, units = halves.shape
    dma = pltpu.SemaphoreType.DMA
    whole = pltpu.VMEM((tokens, width), F32)
    longer = pltpu.VMEM((tokens + 8, width), F32)
    weight = pltpu.VMEM((model, width), BF16)
    return pl.pallas_call(
        functools.partial(backward_body, n, hidden_units),
        out_shape=(
            jax.ShapeDtypeStruct((tokens, width), BF16),
            jax.ShapeDtypeStruct((tokens, width), BF16),
            jax.ShapeDtypeStruct((n, 2, size // n, width), BF16),
            jax.ShapeDtypeStruct((8, width), F32),
            jax.ShapeDtypeStruct((2, half, model), F32),
            jax.ShapeDtypeStruct((1, model), F32),
            jax.ShapeDtypeStruct((kinds, 2 * part, rows, units), BF16),
        ),
        in_specs=[VMEM] + [HBM] * 3 + [VMEM] * 10 + [HBM, HBM],
        out_specs=(VMEM,) * 6 + (HBM,),
        scratch_shapes=[
            pltpu.VMEM(halves.shape, BF16),
            pltpu.VMEM(halves.shape, BF16),
            weight,
            weight,
            weight,
            pltpu.VMEM((2, half, model), BF16),
            pltpu.VMEM((half, model), BF16),
            pltpu.VMEM((tokens, model), F32),
            longer,
            whole,
            whole,
            whole,
            whole,
            longer,
            longer,
            pltpu.VMEM((2, width), F32),
            pltpu.VMEM((n, 2, width), F32),
            pltpu.VMEM((8, width), F32),
            dma(()),
            dma(()),
            dma((n,)),
            dma((n,)),
            dma((kinds, part, 2)),
            dma((kinds, part, 2)),
            dma(()),
            dma(()),
            dma(()),
            dma(()),
            dma((3,)),
            dma(()),
            dma((kinds, 2)),
        ],
        compiler_params=params(5, 60),
        name="mixer_backward",
    )(mixed, *weights, x_half, gain, d_resid, y_pre, states, edge, conv, x_branch, gates, par, halves, own)


def ffn_body(n, hidden_units, *refs):
    own_ref, cot_ref, column_ref, near_ref, resid_ref, gain_ref = refs[:6]
    block_ref, d_resid_ref, mixed_ref, d_gain_ref, turned_ref = refs[6:11]
    halves_ref, mine_ref, far_ref = refs[11:14]
    tokens, cots, w, extra, hidden, box, sib, got, stage, turned, my_cot = refs[14:25]
    token_sems, cot_sems = refs[25:28], refs[28:31]
    send_w, recv_w, keep_w, keep_c, keep_t, keep_m = refs[31:37]
    send_c, recv_s, send_z, recv_r, send_f, recv_f, send_m, recv_m, move, out_sem = refs[37:]
    groups = n // INNER
    half = groups // 2
    me, outer, by_x, by_y, by_xy = whereabouts()
    base = outer * INNER
    core = lax.axis_index("ch")
    above, below = outer + 1 < groups, outer > 0
    sibling = {"ch": 1 - core}
    barrier = pltpu.get_barrier_semaphore()

    def hello(peer):
        pl.semaphore_signal(barrier, inc=1, device_id=peer, device_id_type=MESH)

    hello({"seq": by_x})
    hello({"seq": by_y})
    hello(sibling)
    pl.when(above)(lambda: hello({"seq": me + INNER}))
    pl.when(below)(lambda: hello({"seq": me - INNER}))
    pl.semaphore_wait(barrier, 3 + above.astype(jnp.int32) + below.astype(jnp.int32))
    flips = ((by_x, by_y), (by_y, by_x))
    rows, units = w.shape[3], w.shape[4]
    split = Units(hidden_units, groups, core)
    tall, model = own_ref.shape
    count = 2 * tall
    deep = INNER * rows
    tile = 256

    def part(h):
        return pl.ds(h * half, half)


    chain_t = Chain(n, own_ref, tokens, *token_sems)
    chain_c = Chain(n, cot_ref, cots, *cot_sems)

    def weight_copy(kind, h, far, receive=False):
        source = flips[h][0] if far else me
        if receive:
            source = by_xy if far else flips[h][1]
        src = near_ref.at[h, kind] if far else column_ref.at[kind, part(h)]
        return Sized(
            split,
            outer,
            lambda width: remote(
                src.at[:, :, pl.ds(0, width)],
                w.at[kind, part(h), source - base, :, pl.ds(0, width)],
                send_w.at[kind, h, far],
                recv_w.at[kind, h, far],
                flips[h][1],
            ),
        )

    keep = [
        [
            pltpu.make_async_copy(
                column_ref.at[kind], w.at[kind, :, me - base], keep_w.at[kind, 0]
            ),
            *(
                pltpu.make_async_copy(
                    near_ref.at[h, kind],
                    w.at[kind, part(h), flips[h][0] - base],
                    keep_w.at[kind, 1 + h],
                )
                for h in range(2)
            ),
        ]
        for kind in range(3)
    ]
    every = [(h, far) for far in range(2) for h in range(2)]
    own_t, own_c = chain_t.keep(keep_t), chain_c.keep(keep_c)
    load_m = pltpu.make_async_copy(cot_ref, my_cot, keep_m)
    chain_t.start()
    for kind in range(3):
        for h, far in every:
            weight_copy(kind, h, far).start()
    own_t.start()
    own_c.start()
    load_m.start()
    for kind in range(3):
        for copy in keep[kind]:
            copy.start()
    for step in range(1, groups - 1):
        chain_t.step(step)
    chain_c.start()
    chain_t.step(groups - 1)
    chain_t.finish()
    own_t.wait()

    def weights_landed(kind):
        for h, far in every:
            weight_copy(kind, h, far, True).wait_recv()
        for copy in keep[kind]:
            copy.wait()
        if not split.even:

            @pl.when(jnp.logical_not(split.full(outer)))
            def _():
                rest = jnp.zeros((groups, INNER, rows, LANES), BF16)
                w[kind, :, :, :, units - LANES :] = rest

    def columns(kind, at):
        return w[kind, :, :, :, at : at + tile].reshape(model, tile)

    def token_rows(place):
        return pl.ds(pl.multiple_of(place * count, count), count)

    def each(limit, action):
        def one(turn, carry):
            action(turn)
            return carry

        lax.fori_loop(0, limit, one, 0)

    weights_landed(0)
    weights_landed(1)
    chain_c.step(1)

    def middle(place):
        left = tokens[place].reshape(count, model)
        r = token_rows(place)
        for at in range(0, units, tile):
            c = slice(at, at + tile)
            gate = jnp.dot(left, columns(0, at), preferred_element_type=F32)
            up = jnp.dot(left, columns(1, at), preferred_element_type=F32)
            value, slope = gelu_parts(gate)
            hidden[0, r, c] = (value * up).astype(BF16)
            hidden[1, r, c] = (up * slope).astype(BF16)
            hidden[2, r, c] = value.astype(BF16)

    each(groups, middle)
    for step in range(2, groups):
        chain_c.step(step)
    chain_c.finish()
    own_c.wait()
    weights_landed(2)
    for kind in range(3):
        for h, far in every:
            weight_copy(kind, h, far).wait_send()

    def back_hidden(place):
        left = cots[place].reshape(count, model)
        r = token_rows(place)
        for at in range(0, units, tile):
            c = slice(at, at + tile)
            back = jnp.dot(left, columns(2, at), preferred_element_type=F32)
            for kind in (1, 2):
                hidden[kind, r, c] = (back * hidden[kind, r, c].astype(F32)).astype(BF16)


    boxes = (cots, box)

    def partial(kind, place):
        r = token_rows(place)
        for at in range(groups):
            pairs = ((1, 0), (2, 1)) if kind == 0 else ((0, 2),)
            value = 0.0
            for left, right in pairs:
                value = value + lax.dot_general(
                    hidden[left, r],
                    w[right, at].reshape(deep, units),
                    FLIPPED,
                    preferred_element_type=F32,
                )
            value = value.astype(BF16)
            boxes[kind][place, 0, :, at * deep : (at + 1) * deep] = value[:tall]
            boxes[kind][place, 1, :, at * deep : (at + 1) * deep] = value[tall:]
        to_sibling(kind, place).start()

    def to_sibling(kind, place):
        return pltpu.make_async_remote_copy(
            src_ref=boxes[kind].at[place, 1 - core],
            dst_ref=sib.at[kind, place],
            send_sem=send_c.at[kind, place],
            recv_sem=recv_s.at[kind, place],
            device_id=sibling,
            device_id_type=MESH,
        )

    def along(kind, place, up):
        last = place == (outer + 1 if up else outer - 1)
        slot = place if up else jnp.where(last, groups, place)
        return remote(
            boxes[kind].at[place, core],
            got.at[kind, slot],
            send_z.at[kind, place],
            recv_r.at[kind, slot],
            me + (INNER if up else -INNER),
        )

    def landed(kind, slot):
        return remote(
            box.at[0, core], got.at[kind, slot], send_z.at[kind, 0], recv_r.at[kind, slot], by_x
        )

    chunk = 16

    def rows_of(at):
        return pl.ds(pl.multiple_of(at * chunk, chunk), chunk)

    def ready(kind, place, incoming):
        to_sibling(kind, place).wait_recv()

        def add(at, with_got):
            r = rows_of(at)
            value = boxes[kind][place, core, r].astype(F32) + sib[kind, place, r].astype(F32)
            if with_got:
                value = value + got[kind, place, r].astype(F32)
            boxes[kind][place, core, r] = value.astype(BF16)

        @pl.when(incoming)
        def _():
            landed(kind, place).wait_recv()
            each(tall // chunk, lambda at: add(at, True))

        @pl.when(jnp.logical_not(incoming))
        def _():
            each(tall // chunk, lambda at: add(at, False))

    def pass_on(kind, turn):
        ups = groups - 1 - outer
        upper = jnp.where(outer < half, turn < ups, turn >= outer)
        later = jnp.where(outer < half, turn, turn - outer)
        earlier = jnp.where(outer < half, turn - ups, turn)

        @pl.when(upper)
        def _():
            place = groups - 1 - later
            ready(kind, place, below)
            along(kind, place, True).start()

        @pl.when(jnp.logical_not(upper))
        def _():
            ready(kind, earlier, above)
            along(kind, earlier, False).start()

    at_end = jnp.logical_or(outer == 0, outer == groups - 1)

    def partials(kind, start, stop):
        def one(turn, carry):
            partial(kind, far_first(groups, outer, turn))

            @pl.when(jnp.logical_and(at_end, turn >= 1))
            def _():
                pass_on(kind, turn - 1)

            return carry

        lax.fori_loop(start, stop, one, 0)

    def between(kind, turns):
        @pl.when(jnp.logical_not(at_end))
        def _():
            for turn in turns:
                pass_on(kind, turn)

    def totals(kind, use):
        to_sibling(kind, outer).wait_recv()
        for condition, slots in (
            (jnp.logical_and(below, above), (outer, groups)),
            (jnp.logical_and(below, jnp.logical_not(above)), (outer,)),
            (jnp.logical_and(jnp.logical_not(below), above), (groups,)),
        ):

            @pl.when(condition)
            def _(slots=slots):
                for slot in slots:
                    landed(kind, slot).wait_recv()

                def one(at):
                    r = rows_of(at)
                    value = boxes[kind][outer, core, r].astype(F32) + sib[kind, outer, r].astype(F32)
                    for slot in slots:
                        value = value + got[kind, slot, r].astype(F32)
                    use(r, value)

                each(tall // chunk, one)

    def clear(kind):
        def one(place):
            to_sibling(kind, place).wait_send()

            @pl.when(place > outer)
            def _():
                along(kind, place, True).wait_send()

            @pl.when(place < outer)
            def _():
                along(kind, place, False).wait_send()

        each(groups, one)


    made = (w.at[0], w.at[1], extra)

    def gradient_copy(kind, h, far):
        source = by_xy if far else flips[h][1]
        return Sized(
            split,
            outer,
            lambda width: remote(
                made[kind].at[part(h), source - base, :, pl.ds(0, width)],
                far_ref.at[h, far, kind, :, :, pl.ds(0, width)],
                send_f.at[kind, h, far],
                recv_f.at[kind, h, far],
                flips[h][1],
            ),
        )

    def gradients(kinds, source, h):
        for at in range(h * half, (h + 1) * half):
            left = source[:, :, :, at * deep : (at + 1) * deep].reshape(groups * count, deep)
            turned[...] = left.T
            for kind, right in kinds:
                for start in range(0, units, tile):
                    c = slice(start, start + tile)
                    made[kind][at, :, :, c] = (
                        jnp.dot(turned[...], hidden[right, :, c], preferred_element_type=F32)
                        .astype(BF16)
                        .reshape(INNER, rows, tile)
                    )
        for kind, _ in kinds:
            for far in (1, 0):
                gradient_copy(kind, h, far).start()

    def collect(kind, h, far):
        inner = (flips[h][0] if far else me) - base
        gradient_copy(kind, h, far).wait_recv()
        load = pltpu.make_async_copy(far_ref.at[h, far, kind], stage, move)
        load.start()
        load.wait()
        for place in range(half):
            at = h * half + place

            def one(turn, place=place, at=at):
                r = rows_of(turn)
                made[kind][at, inner, r] = (
                    made[kind][at, inner, r].astype(F32) + stage[place, r].astype(F32)
                ).astype(BF16)

            each(rows // chunk, one)
        out_copy(kind, h, far).start()

    def out_copy(kind, h, far):
        inner = (flips[h][0] if far else me) - base
        return pltpu.make_async_copy(
            made[kind].at[part(h), inner],
            (halves_ref if far else mine_ref).at[h, kind],
            out_sem.at[kind, h, far],
        )

    partials(1, 0, 2)
    gradients(((2, 0),), cots, 0)
    partials(1, 2, groups)
    gradients(((2, 0),), cots, 1)
    each(groups, back_hidden)
    load_m.wait()
    partials(0, 0, groups)
    gradients(((0, 1),), tokens, 0)
    between(1, range(1))
    gradients(((0, 1),), tokens, 1)
    between(1, range(1, groups // 2))
    between(0, range(1))
    gradients(((1, 2),), tokens, 0)
    between(1, range(groups // 2, groups - 1))
    between(0, range(1, groups // 2))
    gradients(((1, 2),), tokens, 1)
    between(0, range(groups // 2, groups - 1))

    def shared(ref, at, part):
        return pltpu.make_async_remote_copy(
            src_ref=ref.at[core],
            dst_ref=ref.at[part],
            send_sem=send_m.at[at],
            recv_sem=recv_m.at[at],
            device_id=sibling,
            device_id_type=MESH,
        )

    def finish(r, value):
        block_ref[core, r] = (resid_ref[r] + value).astype(BF16)

    d_gain_ref[...] = jnp.zeros((1, model), F32)

    def norm(r, grad):
        resid = resid_ref[r]
        scale = lax.rsqrt(jnp.mean(resid * resid, axis=-1, keepdims=True) + 1e-06)
        back = grad * gain_ref[...]
        shrink = scale * scale * scale * jnp.mean(resid * back, axis=-1, keepdims=True)
        value = my_cot[r].astype(F32) + (scale * back - resid * shrink)
        d_resid_ref[r] = value
        mixed_ref[core, r] = value.astype(BF16)
        d_gain_ref[...] = d_gain_ref[...] + jnp.sum(grad * (resid * scale), axis=0, keepdims=True)

    for far in (1, 0):
        for h in range(2):
            collect(2, h, far)
    totals(1, finish)
    show = shared(block_ref, 1, core)
    show.start()
    for far in (1, 0):
        for h in range(2):
            collect(0, h, far)
    totals(0, norm)
    share = shared(mixed_ref, 0, core)
    share.start()
    shared(mixed_ref, 0, 1 - core).wait_recv()
    for start in range(0, model, tile):
        c = slice(start, start + tile)
        turned_ref[c, :tall] = mixed_ref[0, :, c].T
        turned_ref[c, tall:] = mixed_ref[1, :, c].T
    for far in (1, 0):
        for h in range(2):
            collect(1, h, far)
    clear(0)
    clear(1)
    shared(block_ref, 1, 1 - core).wait_recv()
    share.wait_send()
    show.wait_send()
    for kind in range(3):
        for h, far in every:
            gradient_copy(kind, h, far).wait_send()
            out_copy(kind, h, far).wait()


def feed_forward(own, cotangent, column, near, resid, gain, hidden_units):
    n = lax.axis_size("seq")
    groups = n // INNER
    tall, model = own.shape
    kinds, _, rows, units = column.shape
    half = groups // 2
    dma = pltpu.SemaphoreType.DMA
    part = jax.ShapeDtypeStruct((2, kinds, half, rows, units), BF16)
    return pl.pallas_call(
        functools.partial(ffn_body, n, hidden_units),
        out_shape=(
            jax.ShapeDtypeStruct((2, tall, model), BF16),
            jax.ShapeDtypeStruct((tall, model), F32),
            jax.ShapeDtypeStruct((2, tall, model), BF16),
            jax.ShapeDtypeStruct((1, model), F32),
            jax.ShapeDtypeStruct((model, 2 * tall), BF16),
            part,
            part,
            jax.ShapeDtypeStruct((2, 2, kinds, half, rows, units), BF16),
        ),
        in_specs=[HBM] * 4 + [VMEM] * 2,
        out_specs=(VMEM,) * 5 + (HBM,) * 3,
        scratch_shapes=[
            pltpu.VMEM((groups, 2, tall, model), BF16),
            pltpu.VMEM((groups, 2, tall, model), BF16),
            pltpu.VMEM((kinds, groups, INNER, rows, units), BF16),
            pltpu.VMEM((groups, INNER, rows, units), BF16),
            pltpu.VMEM((3, groups * 2 * tall, units), BF16),
            pltpu.VMEM((groups, 2, tall, model), BF16),
            pltpu.VMEM((2, groups, tall, model), BF16),
            pltpu.VMEM((2, groups + 1, tall, model), BF16),
            pltpu.VMEM((half, rows, units), BF16),
            pltpu.VMEM((INNER * rows, groups * 2 * tall), BF16),
            pltpu.VMEM((tall, model), BF16),
            *chain_semaphores(groups),
            *chain_semaphores(groups),
            dma((kinds, 2, 2)),
            dma((kinds, 2, 2)),
            dma((kinds, 3)),
            dma(()),
            dma(()),
            dma(()),
            dma((2, groups)),
            dma((2, groups)),
            dma((2, groups)),
            dma((2, groups + 1)),
            dma((kinds, 2, 2)),
            dma((kinds, 2, 2)),
            dma((2,)),
            dma((2,)),
            dma(()),
            dma((kinds, 2, 2)),
        ],
        compiler_params=params(8, 63),
        name="feed_forward",
    )(own, cotangent, column, near, resid, gain)


def my_half(values):
    half = values.shape[0] // 2
    return lax.dynamic_slice_in_dim(values, lax.axis_index("ch") * half, half, 0)


def join(own):
    other = swap(own, "ch", 1)
    core = lax.axis_index("ch")
    return jnp.concatenate(
        [jnp.where(core == 0, own, other), jnp.where(core == 0, other, own)], axis=0
    )


def tokens_in(own):
    groups = lax.axis_size("seq") // INNER
    outer = lax.axis_index("seq") // INNER
    got = put(jnp.zeros((groups,) + own.shape, own.dtype), own, outer)
    for step in range(1, groups):
        got = put(got, swap(own, "seq", step * INNER), outer ^ step)
    other = swap(got, "ch", 1)
    first = lax.axis_index("ch") == 0
    return jnp.stack([jnp.where(first, got, other), jnp.where(first, other, got)], axis=1)


def tokens_out(partial, half):
    width = partial.shape[1]
    groups = lax.axis_size("seq") // INNER
    outer = lax.axis_index("seq") // INNER
    core = lax.axis_index("ch")
    parts = partial.reshape(groups, 2, half, width)
    theirs = pick(parts, 1 - core, 1).astype(BF16)
    summed = (pick(parts, core, 1).astype(F32) + swap(theirs, "ch", 1).astype(F32)).astype(BF16)
    total = pick(summed, outer).astype(F32)
    for step in range(1, groups):
        total = total + swap(pick(summed, outer ^ step), "seq", step * INNER).astype(F32)
    return total


def feed_forward_parts(n_two, cot_half, column, near, resid, ffn_gain, hidden_units):
    f32, bf16 = F32, BF16
    _, groups, depth, units = column.shape
    half_rows, model = n_two.shape
    tok_rows = 2 * half_rows
    _, norm_back_two = jax.vjp(scaled_norm, resid, ffn_gain)
    all_two, *full_ffn = gather_tokens(n_two, column, near)
    all_cot = tokens_in(cot_half)
    all_two, all_cot = (v.reshape(groups * tok_rows, model) for v in (all_two, all_cot))
    own = Units(hidden_units, groups, lax.axis_index("ch")).width(lax.axis_index("seq") // INNER)
    valid = lax.broadcasted_iota(jnp.int32, (1, units), 1) < own
    full_ffn = [jnp.where(valid, w.reshape(model, units), 0) for w in full_ffn]
    gate_pre = jnp.dot(all_two, full_ffn[0], preferred_element_type=f32)
    up_pre = jnp.dot(all_two, full_ffn[1], preferred_element_type=f32)
    gate_act, gelu_back_gate = jax.vjp(gelu_tanh, gate_pre)
    hidden = (gate_act * up_pre).astype(bf16)
    ffn_term = jnp.einsum("tf,df->td", hidden, full_ffn[2], preferred_element_type=f32).astype(bf16)
    d_hidden = jnp.einsum("td,df->tf", all_cot, full_ffn[2], preferred_element_type=f32)
    d_gate = gelu_back_gate(d_hidden * up_pre)[0].astype(bf16)
    d_up = (d_hidden * gate_act).astype(bf16)
    d_n_two = (
        jnp.einsum("tf,df->td", d_gate, full_ffn[0], preferred_element_type=f32)
        + jnp.einsum("tf,df->td", d_up, full_ffn[1], preferred_element_type=f32)
    ).astype(bf16)
    terms = [
        jnp.einsum("td,tf->df", left, right, preferred_element_type=f32)
        .astype(bf16)
        .reshape(groups, INNER, depth, units)
        for left, right in ((all_two, d_gate), (all_two, d_up), (all_cot, hidden))
    ]
    split = [v.reshape(groups, 2, half_rows, model) for v in (d_n_two, ffn_term)]
    if groups <= 4:
        d_n_two, ffn_out, far = reduce_tokens(split, terms)
    else:
        d_n_two, far = reduce_tokens(split[:1], terms)
        ffn_out = tokens_out(ffn_term, half_rows)
    block_out = join((resid + ffn_out).astype(bf16))
    inner = lax.axis_index("seq") % INNER
    by_half = [t.reshape(2, groups // 2, INNER, depth, units) for t in terms]

    def block_at(h, place):
        return jnp.stack([pick(t[h], place, 1) for t in by_half]).astype(f32)

    mine = jnp.stack(
        [(block_at(h, inner) + far[h, 0].astype(f32)).astype(bf16) for h in range(2)]
    )
    halves = jnp.stack(
        [(block_at(h, inner ^ (1, 2)[h]) + far[h, 1].astype(f32)).astype(bf16) for h in range(2)]
    )
    d_resid_norm, d_ffn_gain_term = norm_back_two(d_n_two)
    d_resid = cot_half.astype(f32) + d_resid_norm
    d_mixed = join(d_resid.astype(bf16))
    return block_out, d_resid, d_mixed, d_ffn_gain_term.reshape(1, model), halves, mine


def shards(
    inputs,
    norm_gain,
    branch_weight,
    input_weight,
    channel_params,
    gate_x_blocks,
    gate_a_blocks,
    out_weight,
    ffn_gain,
    ffn_gate,
    ffn_up,
    ffn_down,
    cotangent,
):
    f32 = F32
    bf16 = BF16
    n = lax.axis_size("seq")
    tok_rows, model = inputs.shape
    half_rows = tok_rows // 2
    heads, part, size = gate_x_blocks.shape
    width = heads * size
    depth = ffn_gate.shape[0]
    groups = n // INNER
    hidden_units = ffn_gate.shape[1]
    x_half = my_half(inputs)
    *full_mixer, full_gates, column, n_one, n_one_turned, last_rows = gather_weights(
        [input_weight, branch_weight, out_weight.T],
        [gate_x_blocks, gate_a_blocks],
        [ffn_gate, ffn_up, ffn_down.T],
        inputs,
        norm_gain.reshape(1, model),
    )
    full_mixer = [w.reshape(model, width) for w in full_mixer]
    gates = full_gates.reshape(2, heads, size, size)
    par = jnp.concatenate(
        [
            channel_params,
            jax.nn.softplus(channel_params[7:8]),
            jax.nn.sigmoid(channel_params[7:8]),
            jnp.zeros((6, width), f32),
        ],
        axis=0,
    )

    cot_half = my_half(cotangent)

    x_branch, y_pre, conv_out, states, branch_out, edge, resid, n_two, near = mixer_forward(
        n_one,
        last_rows,
        full_mixer,
        gates,
        par,
        x_half,
        ffn_gain.reshape(1, model),
        column,
        hidden_units,
    )
    if groups <= 4 and depth % 16 == 0:
        block_out, d_resid, d_mixed, d_ffn_gain_term, d_mixed_turned, halves, mine, _ = feed_forward(
            n_two, cot_half, column, near, resid, ffn_gain.reshape(1, model), hidden_units
        )
        block_out = block_out.reshape(tok_rows, model)
        d_mixed = d_mixed.reshape(tok_rows, model)
    else:
        block_out, d_resid, d_mixed, d_ffn_gain_term, halves, mine = feed_forward_parts(
            n_two, cot_half, column, near, resid, ffn_gain, hidden_units
        )
        d_mixed_turned = d_mixed.T
    d_y, d_xb, d_gates, d_par, d_inputs, d_norm_gain_term, column_back = mixer_backward(
        d_mixed,
        full_mixer,
        x_half,
        norm_gain.reshape(1, model),
        d_resid,
        y_pre,
        states,
        edge,
        conv_out,
        x_branch,
        gates,
        par,
        halves,
        mine,
        hidden_units,
    )
    d_inputs = d_inputs.reshape(tok_rows, model)
    gain_rows = model // width
    scattered, small, spread = scatter_mixer(
        n_one_turned.reshape(n, depth, tok_rows),
        d_mixed_turned.reshape(n, depth, tok_rows),
        d_y,
        d_xb,
        branch_out,
        d_gates,
        d_par,
        d_norm_gain_term,
        d_ffn_gain_term,
        column_back,
        hidden_units,
    )
    ffn_grads = [spread[kind].astype(f32) for kind in range(3)]
    d_gate_pair = scattered[3 * depth :].reshape(2, part, heads, size).transpose(0, 2, 1, 3)
    return (
        block_out,
        d_inputs,
        small[8 : 8 + gain_rows].reshape(model),
        scattered[:depth],
        scattered[depth : 2 * depth],
        small[:8],
        d_gate_pair[0],
        d_gate_pair[1],
        scattered[2 * depth : 3 * depth].T,
        small[8 + gain_rows : 8 + 2 * gain_rows].reshape(model),
        ffn_grads[0],
        ffn_grads[1],
        ffn_grads[2].T,
    )


def solution(mesh):
    placed = (
        P("seq", None),
        P(),
        P("seq", "ch"),
        P("seq", "ch"),
        P(None, "ch"),
        P("ch", "seq", None),
        P("ch", "seq", None),
        P("ch", "seq"),
        P(),
        P("seq", "ch"),
        P("seq", "ch"),
        P("ch", "seq"),
        P("seq", None),
    )
    return jax.shard_map(
        shards,
        mesh=mesh,
        in_specs=placed,
        out_specs=(
            P("seq", None),
            P("seq", None),
            P(),
            P("seq", "ch"),
            P("seq", "ch"),
            P(None, "ch"),
            P("ch", "seq", None),
            P("ch", "seq", None),
            P("ch", "seq"),
            P(),
            P("seq", "ch"),
            P("seq", "ch"),
            P("ch", "seq"),
        ),
        check_vma=False,
    )
```

```python
import functools

import jax
import jax.numpy as jnp
from jax import lax
from jax.experimental import pallas as pl
from jax.experimental.pallas import tpu as pltpu
from jax.sharding import PartitionSpec as P

F32 = jnp.float32
BF16 = jnp.bfloat16
INNER = 4
MESH = pl.DeviceIdType.MESH
VMEM = pl.BlockSpec(memory_space=pltpu.VMEM)
ANY = pl.BlockSpec(memory_space=pl.ANY)
HBM = pl.BlockSpec(memory_space=pltpu.HBM)


def swap(value, axis, mask):
    return lax.ppermute(value, axis, [(i, i ^ mask) for i in range(lax.axis_size(axis))])


def pick(array, index, axis=0):
    return lax.dynamic_index_in_dim(array, index, axis, False)


def scaled_norm(values, gain):
    return values * lax.rsqrt(jnp.mean(values * values, axis=-1, keepdims=True) + 1e-06) * gain


def gelu_tanh(values):
    return jax.nn.gelu(values, approximate=True)


def whereabouts():
    me = lax.axis_index("seq")
    outer = me // INNER
    inner = me - outer * INNER
    y = inner // 2
    x = inner - 2 * y
    by_x = me + 1 - 2 * x
    by_y = me + 2 - 4 * y
    return me, outer, by_x, by_y, by_x + 2 - 4 * y


def when(condition, action):
    if condition is None:
        action()
    else:
        pl.when(condition)(action)


def both(one, other):
    if one is None or other is None:
        return one if other is None else other
    return jnp.logical_and(one, other)


def greet(peers):
    barrier = pltpu.get_barrier_semaphore()
    for condition, peer in peers:
        when(
            condition,
            lambda peer=peer: pl.semaphore_signal(
                barrier, inc=1, device_id={"seq": peer}, device_id_type=MESH
            ),
        )
    count = 0
    for condition, _ in peers:
        count = count + (1 if condition is None else condition.astype(jnp.int32))
    pl.semaphore_wait(barrier, count)


def greet_all(n, me, sibling=False):
    barrier = pltpu.get_barrier_semaphore()

    def hello(step, carry):
        pl.semaphore_signal(
            barrier, inc=1, device_id={"seq": lax.rem(me + step, n)}, device_id_type=MESH
        )
        return carry

    lax.fori_loop(1, n, hello, 0)
    if sibling:
        pl.semaphore_signal(
            barrier, inc=1, device_id={"ch": 1 - lax.axis_index("ch")}, device_id_type=MESH
        )
    pl.semaphore_wait(barrier, n if sibling else n - 1)


def remote(src, dst, send_sem, recv_sem, place):
    return pltpu.make_async_remote_copy(
        src_ref=src,
        dst_ref=dst,
        send_sem=send_sem,
        recv_sem=recv_sem,
        device_id={"seq": place},
        device_id_type=MESH,
    )


def params(collective_id, mib):
    return pltpu.CompilerParams(
        collective_id=collective_id, has_side_effects=True, vmem_limit_bytes=mib * 2**20
    )


def gather_begin(n, refs, greeted):
    w_refs, g_refs, f_refs, x_ref, gain_ref = refs[:3], refs[3:5], refs[5:8], refs[8], refs[9]
    wo_refs, go_ref, column_ref, one_ref, turned_ref, last_ref = refs[10:13], *refs[13:18]
    send_m, recv_m, send_f, recv_f, here, send_l, recv_l = refs[18:]
    groups = n // INNER
    me, outer, by_x, by_y, by_xy = whereabouts()
    above, below = outer + 1 < groups, outer > 0
    def column_peer(turn):
        return lax.rem(outer + turn, groups)

    if not greeted:
        barrier = pltpu.get_barrier_semaphore()

        def hello(peer):
            pl.semaphore_signal(barrier, inc=1, device_id={"seq": peer}, device_id_type=MESH)

        hello(by_x)
        hello(by_y)

        def hello_column(turn, carry):
            hello(me + (column_peer(turn) - outer) * INNER)
            return carry

        lax.fori_loop(1, groups, hello_column, 0)
        pl.when(me + 1 < n)(lambda: hello(me + 1))
        pl.when(me > 0)(lambda: hello(me - 1))
        neighbours = (me + 1 < n).astype(jnp.int32) + (me > 0).astype(jnp.int32)
        pl.semaphore_wait(barrier, groups + 1 + neighbours)
    units = Units(f_refs[0].shape[1], groups, lax.axis_index("ch"))
    half = w_refs[0].shape[1] // 2

    keep = [
        pltpu.make_async_copy(w_refs[kind], wo_refs[kind].at[me], here.at[kind])
        for kind in range(3)
    ]
    for gate in range(2):
        keep.append(pltpu.make_async_copy(g_refs[gate], go_ref.at[gate, :, me], here.at[3 + gate]))
    for kind in range(3):
        keep.append(
            Sized(
                units,
                outer,
                lambda width, kind=kind: pltpu.make_async_copy(
                    f_refs[kind].at[:, units.columns(outer, width)],
                    column_ref.at[kind, outer, :, pl.ds(0, width)],
                    here.at[5 + kind],
                ),
            )
        )
    for copy in keep:
        copy.start()
    sent = []

    def copies(h, source, way, target, own, kinds=range(4)):
        cols = pl.ds(h * half, half)
        pairs = [
            (w_refs[kind].at[:, cols], wo_refs[kind].at[source, :, cols]) for kind in range(3)
        ]
        pairs.append((g_refs[h], go_ref.at[h, :, source]))
        return [
            remote(
                given if own else dst,
                dst,
                send_m.at[kind, h, source, way],
                recv_m.at[kind, h, source],
                target,
            )
            for kind, (given, dst) in enumerate(pairs)
            if kind in kinds
        ]

    def send(condition, *what):
        def go():
            for copy in copies(*what):
                copy.start()

        when(condition, go)
        sent.append((condition, what))

    def arrive(condition, h, source, kinds=range(4)):
        def go():
            for copy in copies(h, source, 0, by_x, False, kinds):
                copy.wait_recv()

        when(condition, go)

    def exchange(turn, receive):
        place = lax.rem(outer + groups - turn, groups) if receive else column_peer(turn)
        owner = outer if receive else place
        return [
            Sized(
                units,
                owner,
                lambda width, kind=kind: remote(
                    f_refs[kind].at[:, units.columns(owner, width)],
                    column_ref.at[kind, place if receive else outer, :, pl.ds(0, width)],
                    send_f.at[kind, turn],
                    recv_f.at[kind, turn],
                    me + (place - outer) * INNER,
                ),
            )
            for kind in range(3)
        ]

    def each_turn(action):
        def one(turn, carry):
            action(turn)
            return carry

        lax.fori_loop(1, groups, one, 0)

    tokens, model = x_ref.shape
    tall = last_ref.shape[0]
    last_copy = remote(one_ref.at[pl.ds(tokens - tall, tall)], last_ref, send_l, recv_l, me + 1)

    def norm(at, carry):
        r = pl.ds(pl.multiple_of(at * 16, 16), 16)
        x = x_ref[r].astype(F32)
        scale = lax.rsqrt(jnp.mean(x * x, axis=-1, keepdims=True) + 1e-06)
        one_ref[r] = (x * scale * gain_ref[...]).astype(BF16)
        return carry

    def norm_all():
        lax.fori_loop(0, tokens // 16, norm, 0)
        pl.when(me + 1 < n)(last_copy.start)
        for start in range(0, model, 256):
            cols = slice(start, start + 256)
            turned_ref[cols] = one_ref[:, cols].T

        @pl.when(me == 0)
        def _():
            last_ref[...] = jnp.zeros(last_ref.shape, BF16)

    for step in range(groups):
        if step == 1:
            norm_all()
        for h in range(2):
            flip_p, flip_q = (by_x, by_y) if h == 0 else (by_y, by_x)
            if step == 0:
                send(above, h, me, 0, me + INNER, True)
                send(below, h, me, 1, me - INNER, True)
                send(None, h, me, 2, flip_p, True)
                send(None, h, me, 3, flip_q, True)
                continue
            for source, there, onward, way, to in (
                (me - step * INNER, outer >= step, above, 0, me + INNER),
                (me + step * INNER, outer + step < groups, below, 1, me - INNER),
            ):
                arrive(there, h, source)
                send(both(there, onward), h, source, way, to, False)
                send(there, h, source, 2, flip_p, False)
                send(there, h, source, 3, flip_q, False)
    each_turn(lambda turn: [copy.start() for copy in exchange(turn, False)])
    for step in range(groups):
        for h in range(2):
            flip_p, flip_q = (by_x, by_y) if h == 0 else (by_y, by_x)
            if step == 0:
                arrive(None, h, flip_p)
                send(None, h, flip_p, 3, flip_q, False)
                continue
            for source, there in (
                (flip_p - step * INNER, outer >= step),
                (flip_p + step * INNER, outer + step < groups),
            ):
                arrive(there, h, source)
                send(there, h, source, 3, flip_q, False)

    def last(kind):
        for place in range(groups):
            shift = (place - outer) * INNER
            for h in range(2):
                arrive(None, h, (by_y if h == 0 else by_x) + shift, (kind,))
                arrive(None, h, by_xy + shift, (kind,))
        for copy in keep[kind : kind + 1] if kind < 3 else keep[3:5]:
            copy.wait()

    def columns():
        each_turn(lambda turn: [copy.wait_recv() for copy in exchange(turn, True)])
        for copy in keep[5:]:
            copy.wait()

    def rows_before():
        pl.when(me > 0)(last_copy.wait_recv)

    def finish():
        for condition, what in sent:

            def done(what=what):
                for copy in copies(*what):
                    copy.wait_send()

            when(condition, done)
        each_turn(lambda turn: [copy.wait_send() for copy in exchange(turn, False)])
        pl.when(me + 1 < n)(last_copy.wait_send)

    return last, columns, rows_before, finish


def gather_body(n, *refs):
    last, columns, rows_before, finish = gather_begin(n, refs, False)
    for kind in range(4):
        last(kind)
    columns()
    rows_before()
    finish()


def gather_weights(weights, gates, ffn, x, gain):
    n = lax.axis_size("seq")
    groups = n // INNER
    rows, hidden_units = ffn[0].shape
    most = Units(hidden_units, groups, 0).most
    dma = pltpu.SemaphoreType.DMA
    made = [jax.ShapeDtypeStruct((n,) + w.shape, w.dtype) for w in weights]
    heads, part, size = gates[0].shape
    made.append(jax.ShapeDtypeStruct((2, heads, n, part, size), BF16))
    made.append(jax.ShapeDtypeStruct((3, groups, rows, most), BF16))
    made.append(jax.ShapeDtypeStruct(x.shape, BF16))
    made.append(jax.ShapeDtypeStruct(x.shape[::-1], BF16))
    made.append(jax.ShapeDtypeStruct((16, x.shape[1]), BF16))
    return pl.pallas_call(
        functools.partial(gather_body, n),
        out_shape=tuple(made),
        in_specs=[HBM] * 8 + [VMEM] * 2,
        out_specs=(HBM,) * 5 + (VMEM,) * 3,
        scratch_shapes=[
            dma((4, 2, n, 4)),
            dma((4, 2, n)),
            dma((3, groups)),
            dma((3, groups)),
            dma((8,)),
            dma(()),
            dma(()),
        ],
        compiler_params=params(1, 60),
        name="gather_weights",
    )(*weights, *gates, *ffn, x, gain)


LANES = 128


class Units:
    def __init__(self, total, groups, core):
        self.tiles, self.groups, self.core = total // LANES, groups, core
        self.most = -(-self.tiles // groups) * LANES
        self.even = self.tiles % groups == 0

    def start(self, place):
        up = (1 - self.core) * (self.groups - 1)
        return (place * self.tiles + up) // self.groups

    def full(self, place):
        return (self.start(place + 1) - self.start(place)) * LANES == self.most

    def width(self, place):
        return (self.start(place + 1) - self.start(place)) * LANES

    def columns(self, place, width):
        return pl.ds(pl.multiple_of(self.start(place) * LANES, LANES), width)


class Sized:
    def __init__(self, units, place, make):
        self.units, self.place, self.make = units, place, make

    def each(self, action):
        most = self.units.most
        if self.units.even:
            action(self.make(most))
            return
        full = self.units.full(self.place)
        pl.when(full)(lambda: action(self.make(most)))
        pl.when(jnp.logical_not(full))(lambda: action(self.make(most - LANES)))

    def start(self):
        self.each(lambda copy: copy.start())

    def wait(self):
        self.each(lambda copy: copy.wait())

    def wait_send(self):
        self.each(lambda copy: copy.wait_send())

    def wait_recv(self):
        self.each(lambda copy: copy.wait_recv())


def far_first(groups, outer, turn):
    def order(at):
        alone = groups - 1 - 2 * at
        later = turn - alone
        step = later // 2
        return jnp.where(
            turn < alone, groups - 1 - turn, jnp.where(later - 2 * step == 0, step, 2 * at - step)
        )

    return jnp.where(
        outer < groups // 2, order(outer), groups - 1 - order(groups - 1 - outer)
    )


class Chain:
    def __init__(self, n, own, whole, send, recv_z, recv_c):
        me = lax.axis_index("seq")
        self.groups = n // INNER
        self.outer = outer = me // INNER
        self.core = lax.axis_index("ch")
        self.above, self.below = outer + 1 < self.groups, outer > 0
        self.sibling = {"ch": 1 - self.core}
        self.to = ({"seq": me + INNER}, {"seq": me - INNER}, self.sibling)
        self.own, self.whole = own, whole
        self.send, self.recv_z, self.recv_c = send, recv_z, recv_c

    def copy(self, source, way, own=False):
        dst = self.whole.at[source, self.core]
        return pltpu.make_async_remote_copy(
            src_ref=self.own if own else dst,
            dst_ref=dst,
            send_sem=self.send.at[source, way],
            recv_sem=(self.recv_c if way == 2 else self.recv_z).at[source],
            device_id=self.to[way],
            device_id_type=MESH,
        )

    def from_sibling(self, source):
        return pltpu.make_async_remote_copy(
            src_ref=self.own,
            dst_ref=self.whole.at[source, 1 - self.core],
            send_sem=self.send.at[source, 2],
            recv_sem=self.recv_c.at[source],
            device_id=self.sibling,
            device_id_type=MESH,
        )

    def keep(self, sem):
        return pltpu.make_async_copy(self.own, self.whole.at[self.outer, self.core], sem)

    def ways(self, step):
        return (
            (self.outer - step, self.outer >= step, self.above, 0),
            (self.outer + step, self.outer + step < self.groups, self.below, 1),
        )

    def start(self):
        pl.when(self.above)(self.copy(self.outer, 0, True).start)
        pl.when(self.below)(self.copy(self.outer, 1, True).start)
        self.copy(self.outer, 2, True).start()

    def step(self, step):
        for source, there, onward, way in self.ways(step):
            pl.when(there)(self.copy(source, way).wait_recv)
            pl.when(both(there, onward))(self.copy(source, way).start)
            pl.when(there)(self.copy(source, 2).start)

    def finish(self):
        for source in range(self.groups):
            self.from_sibling(source).wait_recv()
        pl.when(self.above)(self.copy(self.outer, 0, True).wait_send)
        pl.when(self.below)(self.copy(self.outer, 1, True).wait_send)
        self.copy(self.outer, 2, True).wait_send()
        for step in range(1, self.groups):
            for source, there, onward, way in self.ways(step):
                pl.when(both(there, onward))(self.copy(source, way).wait_send)
                pl.when(there)(self.copy(source, 2).wait_send)


def chain_semaphores(groups):
    dma = pltpu.SemaphoreType.DMA
    return [dma((groups, 3)), dma((groups,)), dma((groups,))]


def tokens_body(n, *refs):
    own_ref, column_ref, near_ref = refs[:3]
    all_ref, w_refs = refs[3], refs[4:7]
    send_t, recv_z, recv_c, send_w, recv_w, here = refs[7:]
    groups = n // INNER
    half = groups // 2
    me, outer, by_x, by_y, by_xy = whereabouts()
    base = outer * INNER
    core = lax.axis_index("ch")
    above, below = outer + 1 < groups, outer > 0
    sibling = {"ch": 1 - core}
    barrier = pltpu.get_barrier_semaphore()

    def hello(peer):
        pl.semaphore_signal(barrier, inc=1, device_id=peer, device_id_type=MESH)

    hello({"seq": by_x})
    hello({"seq": by_y})
    hello(sibling)
    pl.when(above)(lambda: hello({"seq": me + INNER}))
    pl.when(below)(lambda: hello({"seq": me - INNER}))
    pl.semaphore_wait(barrier, 3 + above.astype(jnp.int32) + below.astype(jnp.int32))

    chain = Chain(n, own_ref, all_ref, send_t, recv_z, recv_c)

    def part(h):
        return pl.ds(h * half, half)

    flips = ((by_x, by_y), (by_y, by_x))

    def weight_copy(kind, h, far, receive=False):
        source = flips[h][0] if far else me
        if receive:
            source = by_xy if far else flips[h][1]
        return remote(
            near_ref.at[h, kind] if far else column_ref.at[kind, part(h)],
            w_refs[kind].at[part(h), source - base],
            send_w.at[kind, h, far],
            recv_w.at[kind, h, far],
            flips[h][1],
        )

    keep = [chain.keep(here.at[0])]
    for kind in range(3):
        keep.append(
            pltpu.make_async_copy(
                column_ref.at[kind], w_refs[kind].at[:, me - base], here.at[1 + kind]
            )
        )
        for h in range(2):
            keep.append(
                pltpu.make_async_copy(
                    near_ref.at[h, kind],
                    w_refs[kind].at[part(h), flips[h][0] - base],
                    here.at[4 + 2 * kind + h],
                )
            )
    every_w = [(kind, h, far) for kind in range(3) for h in range(2) for far in range(2)]

    chain.start()
    for what in every_w:
        weight_copy(*what).start()
    for copy in keep:
        copy.start()
    for step in range(1, groups):
        chain.step(step)
    for what in every_w:
        weight_copy(*what, receive=True).wait_recv()
    chain.finish()
    for what in every_w:
        weight_copy(*what).wait_send()
    for copy in keep:
        copy.wait()


def gather_tokens(tokens, column, near):
    n = lax.axis_size("seq")
    groups = n // INNER
    kinds, _, rows, units = column.shape
    dma = pltpu.SemaphoreType.DMA
    wide = jax.ShapeDtypeStruct((groups, 2) + tokens.shape, tokens.dtype)
    weight = jax.ShapeDtypeStruct((groups, INNER, rows, units), column.dtype)
    return pl.pallas_call(
        functools.partial(tokens_body, n),
        out_shape=(wide, weight, weight, weight),
        in_specs=[ANY] * 3,
        out_specs=(ANY,) * 4,
        scratch_shapes=chain_semaphores(groups)
        + [dma((kinds, 2, 2)), dma((kinds, 2, 2)), dma((10,))],
        compiler_params=params(6, 16),
        name="gather_tokens",
    )(tokens, column, near)


def reduce_body(n, kinds, *refs):
    p_refs, t_refs = refs[:kinds], refs[kinds : kinds + 3]
    out_refs, far_ref = refs[kinds + 3 : 2 * kinds + 3], refs[2 * kinds + 3]
    summed, got, send_c, recv_c, send_z, recv_z, send_f, recv_f = refs[2 * kinds + 4 :]
    groups = n // INNER
    half = groups // 2
    me, outer, by_x, by_y, by_xy = whereabouts()
    base = outer * INNER
    core = lax.axis_index("ch")
    above, below = outer + 1 < groups, outer > 0
    sibling = {"ch": 1 - core}
    barrier = pltpu.get_barrier_semaphore()

    def hello(peer):
        pl.semaphore_signal(barrier, inc=1, device_id=peer, device_id_type=MESH)

    hello({"seq": by_x})
    hello({"seq": by_y})
    hello(sibling)
    pl.when(above)(lambda: hello({"seq": me + INNER}))
    pl.when(below)(lambda: hello({"seq": me - INNER}))
    pl.semaphore_wait(barrier, 3 + above.astype(jnp.int32) + below.astype(jnp.int32))
    flips = ((by_x, by_y), (by_y, by_x))

    def gradient_copy(kind, h, far):
        source = by_xy if far else flips[h][1]
        return remote(
            t_refs[kind].at[pl.ds(h * half, half), source - base],
            far_ref.at[h, far, kind],
            send_f.at[kind, h, far],
            recv_f.at[kind, h, far],
            flips[h][1],
        )

    def to_sibling(kind, place):
        return pltpu.make_async_remote_copy(
            src_ref=p_refs[kind].at[place, 1 - core],
            dst_ref=summed.at[kind, place],
            send_sem=send_c.at[kind, place],
            recv_sem=recv_c.at[kind, place],
            device_id=sibling,
            device_id_type=MESH,
        )

    def along(kind, place, up):
        last = place == (outer + 1 if up else outer - 1)
        slot = place if up else jnp.where(last, groups, place)
        return remote(
            summed.at[kind, place],
            got.at[kind, slot],
            send_z.at[kind, place],
            recv_z.at[kind, slot],
            me + (INNER if up else -INNER),
        )

    def landed(kind, slot):
        return remote(
            summed.at[kind, 0], got.at[kind, slot], send_z.at[kind, 0], recv_z.at[kind, slot], by_x
        )

    def each(limit, action):
        def one(turn, carry):
            action(turn)
            return carry

        lax.fori_loop(0, limit, one, 0)

    every_f = [(kind, h, far) for far in (1, 0) for kind in range(3) for h in range(2)]
    for kind in range(kinds):
        each(groups, lambda place, kind=kind: to_sibling(kind, place).start())
    for what in every_f:
        gradient_copy(*what).start()

    tall = summed.shape[2]
    chunk = 16

    def rows_of(at):
        return pl.ds(pl.multiple_of(at * chunk, chunk), chunk)

    def ready(kind, place, incoming):
        to_sibling(kind, place).wait_recv()

        def local(at):
            r = rows_of(at)
            summed[kind, place, r] = (
                summed[kind, place, r].astype(F32) + p_refs[kind][place, core, r].astype(F32)
            ).astype(BF16)

        def more(at):
            r = rows_of(at)
            summed[kind, place, r] = (
                summed[kind, place, r].astype(F32)
                + p_refs[kind][place, core, r].astype(F32)
                + got[kind, place, r].astype(F32)
            ).astype(BF16)

        @pl.when(incoming)
        def _():
            landed(kind, place).wait_recv()
            each(tall // chunk, more)

        @pl.when(jnp.logical_not(incoming))
        def _():
            each(tall // chunk, local)

    for kind in range(kinds):

        def climb(turn, kind=kind):
            place = groups - 1 - turn

            @pl.when(place > outer)
            def _():
                ready(kind, place, below)
                along(kind, place, True).start()

        def sink(turn, kind=kind):
            place = turn

            @pl.when(place < outer)
            def _():
                ready(kind, place, above)
                along(kind, place, False).start()

        def turns(turn):
            @pl.when(outer < half)
            def _():
                climb(turn)
                sink(turn)

            @pl.when(outer >= half)
            def _():
                sink(turn)
                climb(turn)

        each(groups - 1, turns)
    for kind in range(kinds):
        to_sibling(kind, outer).wait_recv()

        def own(at, kind=kind):
            r = rows_of(at)
            out_refs[kind][r] = summed[kind, outer, r].astype(F32) + p_refs[kind][
                outer, core, r
            ].astype(F32)

        each(tall // chunk, own)
        for there, slot in ((below, outer), (above, groups)):

            @pl.when(there)
            def _():
                landed(kind, slot).wait_recv()

                def plus(at):
                    r = rows_of(at)
                    out_refs[kind][r] = out_refs[kind][r] + got[kind, slot, r].astype(F32)

                each(tall // chunk, plus)

    for kind in range(kinds):

        def clear(place, kind=kind):
            to_sibling(kind, place).wait_send()

            @pl.when(place > outer)
            def _():
                along(kind, place, True).wait_send()

            @pl.when(place < outer)
            def _():
                along(kind, place, False).wait_send()

        each(groups, clear)
    for what in every_f:
        gradient_copy(*what).wait()


def reduce_tokens(partials, gradients):
    n = lax.axis_size("seq")
    groups = n // INNER
    kinds = len(partials)
    _, _, tall, width = partials[0].shape
    _, _, rows, units = gradients[0].shape
    dma = pltpu.SemaphoreType.DMA
    return pl.pallas_call(
        functools.partial(reduce_body, n, kinds),
        out_shape=(jax.ShapeDtypeStruct((tall, width), F32),) * kinds
        + (jax.ShapeDtypeStruct((2, 2, 3, groups // 2, rows, units), BF16),),
        in_specs=[VMEM] * kinds + [ANY] * 3,
        out_specs=(VMEM,) * kinds + (ANY,),
        scratch_shapes=[
            pltpu.VMEM((kinds, groups, tall, width), BF16),
            pltpu.VMEM((kinds, groups + 1, tall, width), BF16),
            dma((kinds, groups)),
            dma((kinds, groups)),
            dma((kinds, groups)),
            dma((kinds, groups + 1)),
            dma((3, 2, 2)),
            dma((3, 2, 2)),
        ],
        compiler_params=params(7, 60),
        name="reduce_tokens",
    )(*partials, *gradients)


def scatter_body(
    n,
    one_ref,
    mixed_ref,
    dy_ref,
    dxb_ref,
    branch_ref,
    gate_ref,
    dpar_ref,
    gain_one_ref,
    gain_two_ref,
    column_ref,
    out_ref,
    small_out,
    spread_ref,
    made,
    got_q,
    got_p,
    got_z,
    got_s,
    *sems,
):
    send_q, recv_q, send_p, recv_p, send_z, recv_z, send_s, recv_s, send_f, recv_f, here = sems
    groups = n // INNER
    me, outer, by_x, by_y, by_xy = whereabouts()
    rows = one_ref.shape[1]
    part_rows = gate_ref.shape[2]
    total, width = out_ref.shape
    half = width // 2

    def place_of(turn):
        return far_first(groups, outer, turn)

    def base_of(turn):
        return (place_of(turn) - outer) * INNER

    barrier = pltpu.get_barrier_semaphore()

    def hello(peer):
        pl.semaphore_signal(barrier, inc=1, device_id={"seq": peer}, device_id_type=MESH)

    hello(by_x)
    hello(by_y)

    def hello_outer(turn, carry):
        hello(me + base_of(turn))
        return carry

    lax.fori_loop(0, groups - 1, hello_outer, 0)
    core = lax.axis_index("ch")
    masks = [1 << bit for bit in range(n.bit_length() - 1)]
    pl.semaphore_signal(barrier, inc=1, device_id={"ch": 1 - core}, device_id_type=MESH)
    pl.semaphore_wait(barrier, groups + 2)

    flips = ((by_x, by_y), (by_y, by_x))
    units = Units(spread_ref.shape[2], groups, core)

    def exchange(turn, receive=False):
        place = lax.rem(outer + (groups - 1 - turn if receive else turn + 1), groups)
        owner = place if receive else outer
        return Sized(
            units,
            owner,
            lambda width: remote(
                column_ref.at[:, place, :, pl.ds(0, width)],
                spread_ref.at[:, :, units.columns(owner, width)],
                send_f.at[turn],
                recv_f.at[turn],
                me + (place - outer) * INNER,
            ),
        )

    def small(turn):
        place = me
        for at, mask in enumerate(masks):
            flipped = me + mask * (1 - 2 * lax.rem(me // mask, 2))
            place = jnp.where(turn == at, flipped, place)
        other = jnp.where(turn == len(masks), 1 - core, core)
        return pltpu.make_async_remote_copy(
            src_ref=small_out,
            dst_ref=got_s.at[turn],
            send_sem=send_s.at[turn],
            recv_sem=recv_s.at[turn],
            device_id=(place, other),
            device_id_type=MESH,
        )

    small_out[:8] = dpar_ref[...]
    small_out[8:] = jnp.zeros((8, width), F32)
    at = 8
    for gain_ref in (gain_one_ref, gain_two_ref):
        for start in range(0, gain_ref.shape[1], width):
            small_out[at : at + 1] = gain_ref[:, start : start + width]
            at += 1
    small_row = lax.broadcasted_iota(jnp.int32, small_out.shape, 0)

    def cols(h):
        return pl.ds(h * half, half)

    def along_q(turn, h, other):
        source = (by_xy if other else flips[h][1]) + base_of(turn)
        return remote(
            made.at[source, :, cols(h)],
            got_q.at[h, turn, other],
            send_q.at[h, turn, other],
            recv_q.at[h, turn, other],
            flips[h][1],
        )

    def along_p(turn, h):
        return remote(
            made.at[flips[h][0] + base_of(turn), :, cols(h)],
            got_p.at[h, turn],
            send_p.at[h, turn],
            recv_p.at[h, turn],
            flips[h][0],
        )

    def along_z(turn, h):
        place = place_of(turn)
        up = place > outer
        onto = jnp.where(up, outer + 1, outer - 1)
        slot = jnp.where(jnp.logical_and(place == onto, jnp.logical_not(up)), groups, place)
        return remote(
            made.at[me + base_of(turn), :, cols(h)],
            got_z.at[h, slot],
            send_z.at[h, turn],
            recv_z.at[h, slot],
            me + (onto - outer) * INNER,
        )

    def landed(slot, h):
        return remote(
            made.at[me, :, cols(h)], got_z.at[h, slot], send_z.at[h, 0], recv_z.at[h, slot], by_x
        )

    def has_incoming(turn):
        return jnp.where(place_of(turn) > outer, outer > 0, outer < groups - 1)

    def pass_on(turn):
        incoming = has_incoming(turn)
        for h in range(2):

            @pl.when(incoming)
            def _():
                landed(place_of(turn), h).wait_recv()
                add(me + base_of(turn), h, got_z, (h, place_of(turn)))

            along_z(turn, h).start()

    def make(block):
        left = one_ref[block]
        parts = [
            jnp.dot(left, dy_ref[...], preferred_element_type=F32),
            jnp.dot(left, dxb_ref[...], preferred_element_type=F32),
            jnp.dot(mixed_ref[block], branch_ref[...], preferred_element_type=F32),
        ]
        if rows % 16 == 0:
            for at, part in enumerate(parts):
                made[block, at * rows : (at + 1) * rows] = part.astype(BF16)
            for gate in range(2):
                at = 3 * rows + gate * part_rows
                made[block, at : at + part_rows] = gate_ref[block, gate]
        else:
            parts.extend(gate_ref[block, gate].astype(F32) for gate in range(2))
            made[block] = jnp.concatenate(parts, axis=0).astype(BF16)

    step = 32

    def add(block, h, ref, index):
        def one(at, carry):
            r = pl.ds(pl.multiple_of(at * step, step), step)
            made[block, r, cols(h)] = (
                made[block, r, cols(h)].astype(F32) + ref[index + (r,)].astype(F32)
            ).astype(BF16)
            return carry

        lax.fori_loop(0, total // step, one, 0)

    keep = Sized(
        units,
        outer,
        lambda width: pltpu.make_async_copy(
            column_ref.at[:, outer, :, pl.ds(0, width)],
            spread_ref.at[:, :, units.columns(outer, width)],
            here,
        ),
    )
    keep.start()

    def begin(turn, other):
        base = base_of(turn)
        if other:
            make(by_xy + base)
        else:
            for h in range(2):
                make(flips[h][1] + base)
        for h in range(2):
            along_q(turn, h, other).start()

    begin(0, 1)
    begin(0, 0)
    make(me + base_of(0))

    def turn_of(turn, carry):
        pl.when(turn <= len(masks))(lambda: small(turn).start())
        pl.when(turn < groups - 1)(lambda: exchange(turn).start())

        @pl.when(turn < groups)
        def _():
            base = base_of(turn)
            for h in range(2):
                along_q(turn, h, 1).wait_recv()
                add(flips[h][0] + base, h, got_q, (h, turn, 1))
                along_p(turn, h).start()
            pl.when(turn < groups - 1)(lambda: begin(turn + 1, 1))
            for h in range(2):
                along_q(turn, h, 0).wait_recv()
                add(me + base, h, got_q, (h, turn, 0))

            @pl.when(turn < groups - 1)
            def _():
                begin(turn + 1, 0)
                make(me + base_of(turn + 1))

            for h in range(2):
                along_p(turn, h).wait_recv()
                add(me + base, h, got_p, (h, turn))

            @pl.when(jnp.logical_and(turn < groups - 1, jnp.logical_not(has_incoming(turn))))
            def _():
                pass_on(turn)

            @pl.when(jnp.logical_and(turn >= 1, turn < groups - 1))
            def _():
                pl.when(has_incoming(turn - 1))(lambda: pass_on(turn - 1))

            @pl.when(jnp.logical_and(turn == groups - 2, has_incoming(turn)))
            def _():
                pass_on(turn)

        @pl.when(turn <= len(masks))
        def _():
            small(turn).wait()
            counts = jnp.logical_or(turn < len(masks), small_row >= 8)
            small_out[...] = small_out[...] + jnp.where(counts, got_s[turn], 0.0)

        return carry

    assert len(masks) < groups + 2
    lax.fori_loop(0, groups + 2, turn_of, 0)
    for condition, slots in (
        (jnp.logical_and(outer > 0, outer < groups - 1), (outer, groups)),
        (outer == groups - 1, (outer,)),
        (outer == 0, (groups,)),
    ):

        @pl.when(condition)
        def _(slots=slots):
            for h in range(2):
                for slot in slots:
                    landed(slot, h).wait_recv()

                def finish(at, carry):
                    r = pl.ds(pl.multiple_of(at * step, step), step)
                    value = made[me, r, cols(h)].astype(F32)
                    for slot in slots:
                        value = value + got_z[h, slot, r].astype(F32)
                    out_ref[r, cols(h)] = value
                    return carry

                lax.fori_loop(0, total // step, finish, 0)

    def clear(turn, carry):
        for h in range(2):
            along_q(turn, h, 0).wait_send()
            along_q(turn, h, 1).wait_send()
            along_p(turn, h).wait_send()

            @pl.when(turn < groups - 1)
            def _():
                along_z(turn, h).wait_send()

        @pl.when(turn < groups - 1)
        def _():
            exchange(turn, True).wait_recv()
            exchange(turn).wait_send()

        return carry

    lax.fori_loop(0, groups, clear, 0)
    keep.wait()


def scatter_mixer(one, mixed, dy, dxb, branch, gates, dpar, gain_one, gain_two, column, hidden_units):
    n, rows, _ = one.shape
    groups = n // INNER
    width = dy.shape[1]
    total = 3 * rows + 2 * gates.shape[2]
    kinds = column.shape[0]
    turns = n.bit_length()
    dma = pltpu.SemaphoreType.DMA
    return pl.pallas_call(
        functools.partial(scatter_body, n),
        out_shape=(
            jax.ShapeDtypeStruct((total, width), F32),
            jax.ShapeDtypeStruct((16, width), F32),
            jax.ShapeDtypeStruct((kinds, rows, hidden_units), BF16),
        ),
        in_specs=[VMEM] * 9 + [ANY],
        out_specs=(VMEM, VMEM, ANY),
        scratch_shapes=[
            pltpu.VMEM((n, total, width), BF16),
            pltpu.VMEM((2, groups, 2, total, width // 2), BF16),
            pltpu.VMEM((2, groups, total, width // 2), BF16),
            pltpu.VMEM((2, groups + 1, total, width // 2), BF16),
            pltpu.VMEM((turns, 16, width), F32),
            dma((2, groups, 2)),
            dma((2, groups, 2)),
            dma((2, groups)),
            dma((2, groups)),
            dma((2, groups)),
            dma((2, groups + 1)),
            dma((turns,)),
            dma((turns,)),
            dma((groups,)),
            dma((groups,)),
            dma(()),
        ],
        compiler_params=params(2, 62),
        name="scatter_mixer",
    )(one, mixed, dy, dxb, branch, gates, dpar, gain_one, gain_two, column)


GELU_A = 0.7978845608028654
GELU_B = 0.044715


def gelu_parts(v):
    t = jnp.tanh(GELU_A * (v + GELU_B * v * v * v))
    value = 0.5 * v * (1.0 + t)
    slope = 0.5 * (1.0 + t) + 0.5 * v * (1.0 - t * t) * GELU_A * (1.0 + 3.0 * GELU_B * v * v)
    return value, slope


def gates_of(conv_low, gate_ref, par_ref, head, cols, first):
    size = gate_ref.shape[-1]
    weight_x, weight_a = (gate_ref[gate, head].reshape(size, size) for gate in range(2))
    pre_x = jnp.dot(conv_low, weight_x, preferred_element_type=F32)
    pre_a = jnp.dot(conv_low, weight_a, preferred_element_type=F32)
    gate_x = jax.nn.sigmoid(pre_x + par_ref[5:6, cols])
    gate_a = jax.nn.sigmoid(pre_a + par_ref[6:7, cols])
    decay = jnp.exp(-8.0 * gate_a * par_ref[8:9, cols])
    room = 1.0 - decay * decay
    mult = jnp.where(first, 1.0, jnp.sqrt(jnp.maximum(room, 0.001)))
    return gate_x, gate_a, decay, room, mult


FLIPPED = (((1,), (1,)), ((), ()))


def by_columns(ref, cols):
    if len(ref.shape) == 2:
        return ref[:, cols]
    return ref[:, :, cols].reshape(ref.shape[0] * ref.shape[1], -1)


def by_rows(ref, start, size):
    if len(ref.shape) == 2:
        return ref[start : start + size]
    rows = ref.shape[1]
    parts, at = [], start
    while at < start + size:
        block, inside = divmod(at, rows)
        upto = min(rows, inside + start + size - at)
        parts.append(ref[block, inside:upto])
        at += upto - inside
    return jnp.concatenate(parts, axis=0)


def first_row(tokens):
    row = lax.broadcasted_iota(jnp.int32, (tokens, 1), 0)
    return jnp.logical_and(row == 0, lax.axis_index("seq") == 0)


def forward_body(
    n,
    hidden_units,
    gathered,
    one_ref,
    last_ref,
    w_in_ref,
    w_branch_ref,
    w_out_ref,
    gate_ref,
    par_ref,
    x_ref,
    gain_ref,
    column_ref,
    cot_ref,
    xb_ref,
    yp_ref,
    conv_ref,
    state_ref,
    branch_ref,
    edge_ref,
    resid_ref,
    two_ref,
    near_ref,
    cots_ref,
    w_in,
    w_branch,
    w_out,
    mixed,
    mixed_got,
    wide,
    fade,
    mine,
    theirs,
    *sems,
):
    send_tot, recv_tot, send_f, recv_f, send_m, recv_m, loaded, kept = sems[:8]
    tokens, width = xb_ref.shape
    model = one_ref.shape[1]
    me = lax.axis_index("seq")
    size = gate_ref.shape[-1]
    loads = [
        pltpu.make_async_copy(src, dst, loaded.at[at])
        for at, (src, dst) in enumerate(
            ((w_in_ref, w_in), (w_branch_ref, w_branch), (w_out_ref, w_out))
        )
    ]
    core = lax.axis_index("ch")
    half = tokens // 2
    if gathered is None:
        for load in loads:
            load.start()
        greet_all(n, me, True)
        x_start = 0
    else:
        last, columns, rows_before, gather_finish, gates_load = gathered
        last(0)
        loads[0].start()
        rows_before()
        x_start = core * half
    _, _, by_x, by_y, _ = whereabouts()
    part = column_ref.shape[1] // 2
    kinds = column_ref.shape[0]
    units = Units(hidden_units, n // INNER, lax.axis_index("ch"))
    outer = me // INNER
    hosted = [
        [
            Sized(
                units,
                outer,
                lambda width, kind=kind, h=h, part=part: remote(
                    column_ref.at[kind, pl.ds(h * part, part), :, pl.ds(0, width)],
                    near_ref.at[h, kind, :, :, pl.ds(0, width)],
                    send_f.at[kind, h],
                    recv_f.at[kind, h],
                    (by_x, by_y)[h],
                ),
            )
            for h in range(2)
        ]
        for kind in range(kinds)
    ]

    def host(pieces):
        for pair in pieces:
            for copy in pair:
                copy.start()

    chain = Chain(n, cot_ref, cots_ref, *sems[8:])
    keep = chain.keep(kept)
    chain.start()
    keep.start()
    if gathered is None:
        host(hosted[:1])
    loads[0].wait()
    for start in range(0, width, size):
        cols = slice(start, start + size)
        low = jnp.dot(one_ref[...], by_columns(w_in, cols), preferred_element_type=F32).astype(BF16)
        xb_ref[:, cols] = low
        wide[8:, cols] = low.astype(F32)
        low = jnp.dot(last_ref[...], by_columns(w_in, cols), preferred_element_type=F32).astype(BF16)
        wide[:8, cols] = low.astype(F32)[8:]
    if gathered is not None:
        last(1)
        loads[1].start()
        last(3)
        gates_load.start()
        columns()
        host(hosted[:1])
        gates_load.wait()
    loads[1].wait()
    for start in range(0, width, size):
        cols = slice(start, start + size)
        yp_ref[:, cols] = jnp.dot(one_ref[...], by_columns(w_branch, cols), preferred_element_type=F32)

    if gathered is not None:
        last(2)
        loads[2].start()
    edge_ref[:8] = wide[:8]
    first = first_row(tokens)
    for head in range(width // size):
        cols = slice(head * size, (head + 1) * size)
        conv = par_ref[4:5, cols]
        for tap in range(4):
            conv = conv + par_ref[tap : tap + 1, cols] * wide[8 - tap : 8 - tap + tokens, cols]
        conv_low = conv.astype(BF16)
        conv_ref[:, cols] = conv_low
        gate_x, _, decay, _, mult = gates_of(conv_low, gate_ref, par_ref, head, cols, first)
        fade[:, cols] = decay
        state_ref[:, cols] = conv_low.astype(F32) * gate_x * mult

    row = lax.broadcasted_iota(jnp.int32, (8, width), 0)

    def inside(at, carry):
        r = pl.ds(pl.multiple_of(at * 8, 8), 8)
        a, b = fade[r], state_ref[r]
        for by in (1, 2, 4):
            a_back = pltpu.roll(a, by, 0)
            b_back = pltpu.roll(b, by, 0)
            b = jnp.where(row >= by, a * b_back + b, b)
            a = jnp.where(row >= by, a * a_back, a)
        fade[r] = a
        state_ref[r] = b
        return a[7:8] * carry[0], a[7:8] * carry[1] + b[7:8]

    ones, zeros = jnp.ones((1, width), F32), jnp.zeros((1, width), F32)
    tot_a, tot_b = lax.fori_loop(0, tokens // 8, inside, (ones, zeros))
    mine[0:1] = tot_a
    mine[1:2] = tot_b

    def told(place):
        return remote(mine, theirs.at[me], send_tot.at[place], recv_tot.at[me], place)

    def heard(place):
        return remote(mine, theirs.at[place], send_tot.at[place], recv_tot.at[place], place)

    def tell(place, carry):
        told(place).start()
        return carry

    lax.fori_loop(me + 1, n, tell, 0)
    host(hosted[1:])

    def hear(place, state):
        heard(place).wait_recv()
        return theirs[place, 0:1] * state + theirs[place, 1:2]

    carry_in = lax.fori_loop(0, me, hear, zeros)
    edge_ref[8:] = jnp.broadcast_to(carry_in, (8, width))
    chain.step(1)

    def finish(at, carry):
        r = pl.ds(pl.multiple_of(at * 16, 16), 16)
        a, b = fade[r], state_ref[r]
        top = b[:8] + a[:8] * carry
        low = b[8:] + a[8:] * top[7:8]
        states = jnp.concatenate([top, low], axis=0)
        state_ref[r] = states
        branch_ref[r] = (states * gelu_parts(yp_ref[r])[0]).astype(BF16)
        return low[7:8]

    lax.fori_loop(0, tokens // 16, finish, carry_in)

    def sent(place, carry):
        told(place).wait_send()
        return carry

    lax.fori_loop(me + 1, n, sent, 0)
    loads[2].wait()
    for start in range(0, model, size):
        cols = slice(start, start + size)
        part = lax.dot_general(branch_ref[...], by_rows(w_out, start, size), FLIPPED, preferred_element_type=F32)
        mixed[0, :, cols] = part[:half]
        mixed[1, :, cols] = part[half:]
    exchange = pltpu.make_async_remote_copy(
        src_ref=mixed.at[1 - core],
        dst_ref=mixed_got,
        send_sem=send_m,
        recv_sem=recv_m,
        device_id={"ch": 1 - core},
        device_id_type=MESH,
    )
    exchange.start()
    exchange.wait_recv()

    def norm(at, carry):
        r = pl.ds(pl.multiple_of(at * 16, 16), 16)
        x = x_ref[pl.ds(pl.multiple_of(x_start + at * 16, 16), 16)]
        resid = x.astype(F32) + (mixed[core, r] + mixed_got[r])
        resid_ref[r] = resid
        scale = lax.rsqrt(jnp.mean(resid * resid, axis=-1, keepdims=True) + 1e-06)
        two_ref[r] = (resid * scale * gain_ref[...]).astype(BF16)
        return carry

    lax.fori_loop(0, half // 16, norm, 0)
    exchange.wait_send()
    for step in range(2, n // INNER):
        chain.step(step)
    for pair in hosted:
        for copy in pair:
            copy.wait()
    chain.finish()
    keep.wait()
    if gathered is not None:
        gather_finish()


def first_body(n, hidden_units, *refs):
    given, refs = refs[:13], refs[13:]
    weights, gates, ffn, (x_ref, norm_ref, par_ref, gain_ref, cot_ref) = (
        given[:3],
        given[3:5],
        given[5:8],
        given[8:],
    )
    outs, refs = refs[:18], refs[18:]
    scratch, sems = refs[:10], refs[10:]
    gather_sems, forward_sems, gate_sem = sems[:7], sems[7:-1], sems[-1]
    me = lax.axis_index("seq")
    greet_all(n, me, True)
    steps = gather_begin(
        n, (*weights, *gates, *ffn, x_ref, norm_ref, *outs[:8], *gather_sems), True
    )
    gate_s, scratch = scratch[0], scratch[1:]
    full_gates, column_ref, one_ref, _, last_ref = outs[3:8]
    gates_load = pltpu.make_async_copy(full_gates, gate_s, gate_sem)
    forward_body(
        n,
        hidden_units,
        (*steps, gates_load),
        one_ref,
        last_ref,
        *outs[:3],
        gate_s,
        par_ref,
        x_ref,
        gain_ref,
        column_ref,
        cot_ref,
        *outs[8:],
        *scratch,
        *forward_sems,
    )


def mixer_forward(one, last, weights, gates, par, x_half, gain, column, cotangent, hidden_units):
    n = lax.axis_size("seq")
    tokens, model = one.shape
    width = par.shape[1]
    half = tokens // 2
    kinds, groups, rows, units = column.shape
    dma = pltpu.SemaphoreType.DMA
    whole = jax.ShapeDtypeStruct((tokens, width), F32)
    low = jax.ShapeDtypeStruct((tokens, width), BF16)
    return pl.pallas_call(
        functools.partial(forward_body, n, hidden_units, None),
        out_shape=(
            low,
            whole,
            low,
            whole,
            low,
            jax.ShapeDtypeStruct((16, width), F32),
            jax.ShapeDtypeStruct((half, model), F32),
            jax.ShapeDtypeStruct((half, model), BF16),
            jax.ShapeDtypeStruct((2, kinds, groups // 2, rows, units), column.dtype),
            jax.ShapeDtypeStruct((groups, 2) + cotangent.shape, cotangent.dtype),
        ),
        in_specs=[VMEM] * 2 + [HBM] * 3 + [VMEM] * 4 + [HBM, HBM],
        out_specs=(VMEM,) * 8 + (HBM, HBM),
        scratch_shapes=[
            pltpu.VMEM((model, width), BF16),
            pltpu.VMEM((model, width), BF16),
            pltpu.VMEM((model, width), BF16),
            pltpu.VMEM((2, half, model), F32),
            pltpu.VMEM((half, model), F32),
            pltpu.VMEM((tokens + 8, width), F32),
            pltpu.VMEM((tokens, width), F32),
            pltpu.VMEM((2, width), F32),
            pltpu.VMEM((n, 2, width), F32),
            dma((n,)),
            dma((n,)),
            dma((kinds, 2)),
            dma((kinds, 2)),
            dma(()),
            dma(()),
            dma((3,)),
            dma(()),
            *chain_semaphores(groups),
        ],
        compiler_params=params(4, 60),
        name="mixer_forward",
    )(one, last, *weights, gates, par, x_half, gain, column, cotangent)


def gather_forward(weights, gates, ffn, x, norm_gain, par, gain, cotangent):
    n = lax.axis_size("seq")
    groups = n // INNER
    tokens, model = x.shape
    rows, width = weights[0].shape
    half = tokens // 2
    hidden_units = ffn[0].shape[1]
    most = Units(hidden_units, groups, 0).most
    heads, part, size = gates[0].shape
    dma = pltpu.SemaphoreType.DMA
    shape = jax.ShapeDtypeStruct
    whole, low = shape((tokens, width), F32), shape((tokens, width), BF16)
    weight = pltpu.VMEM((n, rows, width), BF16)
    return pl.pallas_call(
        functools.partial(first_body, n, hidden_units),
        out_shape=(
            *(shape((n, rows, width), BF16) for _ in range(3)),
            shape((2, heads, n, part, size), BF16),
            shape((3, groups, rows, most), BF16),
            shape((tokens, model), BF16),
            shape((model, tokens), BF16),
            shape((16, model), BF16),
            low,
            whole,
            low,
            whole,
            low,
            shape((16, width), F32),
            shape((half, model), F32),
            shape((half, model), BF16),
            shape((2, 3, groups // 2, rows, most), BF16),
            shape((groups, 2, half, model), BF16),
        ),
        in_specs=[HBM] * 8 + [VMEM] * 4 + [HBM],
        out_specs=(HBM,) * 5 + (VMEM,) * 11 + (HBM,) * 2,
        scratch_shapes=[
            pltpu.VMEM((2, heads, n, part, size), BF16),
            weight,
            weight,
            weight,
            pltpu.VMEM((2, half, model), F32),
            pltpu.VMEM((half, model), F32),
            pltpu.VMEM((tokens + 8, width), F32),
            pltpu.VMEM((tokens, width), F32),
            pltpu.VMEM((2, width), F32),
            pltpu.VMEM((n, 2, width), F32),
            dma((4, 2, n, 4)),
            dma((4, 2, n)),
            dma((3, groups)),
            dma((3, groups)),
            dma((8,)),
            dma(()),
            dma(()),
            dma((n,)),
            dma((n,)),
            dma((3, 2)),
            dma((3, 2)),
            dma(()),
            dma(()),
            dma((3,)),
            dma(()),
            *chain_semaphores(groups),
            dma(()),
        ],
        compiler_params=params(9, 60),
        name="gather_forward",
    )(*weights, *gates, *ffn, x, norm_gain, par, gain, cotangent)


def backward_body(
    n,
    hidden_units,
    mixed_ref,
    w_in_ref,
    w_branch_ref,
    w_out_ref,
    x_ref,
    gain_ref,
    resid_ref,
    yp_ref,
    state_ref,
    edge_ref,
    conv_ref,
    xb_ref,
    gate_ref,
    par_ref,
    half_ref,
    own_ref,
    dy_ref,
    dxb_ref,
    dgate_ref,
    dpar_ref,
    dx_ref,
    dgain_ref,
    column_ref,
    near_ref,
    own,
    w_in,
    w_branch,
    w_out,
    d_one,
    d_one_got,
    d_one_part,
    fade,
    shift,
    adj,
    gate_x_s,
    gate_a_s,
    dconv,
    wide,
    mine,
    theirs,
    head_rows,
    *sems,
):
    send_rows, recv_rows, send_tot, recv_tot, send_f, recv_f, send_m, recv_m, send_x, recv_x, loaded, own_sem, out_sem = sems
    tokens, width = xb_ref.shape
    model = gain_ref.shape[1]
    me = lax.axis_index("seq")
    size = gate_ref.shape[2]
    loads = [
        pltpu.make_async_copy(src, dst, loaded.at[at])
        for at, (src, dst) in enumerate(
            ((w_out_ref, w_out), (w_in_ref, w_in), (w_branch_ref, w_branch))
        )
    ]
    for load in loads:
        load.start()
    greet_all(n, me, True)
    _, _, by_x, by_y, _ = whereabouts()
    kinds, pieces = half_ref.shape[1:3]
    units = Units(hidden_units, n // INNER, lax.axis_index("ch"))
    outer = me // INNER
    hosted = [
        [
            Sized(
                units,
                outer,
                lambda width, kind=kind, at=at, h=h: remote(
                    half_ref.at[h, kind, at, :, pl.ds(0, width)],
                    near_ref.at[h, kind, at, :, pl.ds(0, width)],
                    send_f.at[kind, at, h],
                    recv_f.at[kind, at, h],
                    (by_x, by_y)[h],
                ),
            )
            for h in range(2)
        ]
        for kind in range(kinds)
        for at in range(pieces)
    ]

    def host(some):
        for pair in some:
            for copy in pair:
                copy.start()

    host(hosted[:2])
    own_load = pltpu.make_async_copy(own_ref, own, own_sem)
    own_load.start()
    first = first_row(tokens)
    fade[tokens:] = jnp.ones((8, width), F32)
    loads[0].wait()
    for head in range(width // size):
        cols = slice(head * size, (head + 1) * size)
        gate_x, gate_a, decay, _, _ = gates_of(conv_ref[:, cols], gate_ref, par_ref, head, cols, first)
        gate_x_s[:, cols] = gate_x
        gate_a_s[:, cols] = gate_a
        fade[:tokens, cols] = decay
        value, slope = gelu_parts(yp_ref[:, cols])
        grad = jnp.dot(mixed_ref[...], w_out[:, cols], preferred_element_type=F32)
        dy_ref[:, cols] = (grad * state_ref[:, cols] * slope).astype(BF16)
        adj[:, cols] = grad * value
        shift[:, cols] = fade[1 : tokens + 1, cols]

    row = lax.broadcasted_iota(jnp.int32, (8, width), 0)
    tiles = tokens // 8

    def inside(turn, carry):
        r = pl.ds(pl.multiple_of((tiles - 1 - turn) * 8, 8), 8)
        a, b = shift[r], adj[r]
        for by in (1, 2, 4):
            a_next = pltpu.roll(a, 8 - by, 0)
            b_next = pltpu.roll(b, 8 - by, 0)
            b = jnp.where(row < 8 - by, a * b_next + b, b)
            a = jnp.where(row < 8 - by, a * a_next, a)
        shift[r] = a
        adj[r] = b
        return a[0:1] * carry[0], a[0:1] * carry[1] + b[0:1]

    ones, zeros = jnp.ones((1, width), F32), jnp.zeros((1, width), F32)
    tot_a, tot_b = lax.fori_loop(0, tiles, inside, (ones, zeros))
    first_fade = fade[0:1]
    mine[0:1] = first_fade * tot_a
    mine[1:2] = first_fade * tot_b

    def told(place):
        return remote(mine, theirs.at[me], send_tot.at[place], recv_tot.at[me], place)

    def heard(place):
        return remote(mine, theirs.at[place], send_tot.at[place], recv_tot.at[place], place)

    def tell(place, carry):
        told(place).start()
        return carry

    lax.fori_loop(0, me, tell, 0)
    host(hosted[2:3])

    def hear(turn, state):
        place = n - 1 - turn
        heard(place).wait_recv()
        return theirs[place, 0:1] * state + theirs[place, 1:2]

    carry_in = lax.fori_loop(0, n - 1 - me, hear, zeros)

    def finish(turn, carry):
        r = pl.ds(pl.multiple_of((tiles - 1 - turn) * 8, 8), 8)
        value = adj[r] + shift[r] * carry
        adj[r] = value
        return value[0:1]

    lax.fori_loop(0, tiles, finish, carry_in)

    wide[:8] = edge_ref[:8]
    wide[8:] = xb_ref[...].astype(F32)
    at_first = lax.broadcasted_iota(jnp.int32, (tokens, 1), 0) == 0
    for head in range(width // size):
        cols = slice(head * size, (head + 1) * size)
        conv_low = conv_ref[:, cols]
        conv = conv_low.astype(F32)
        gate_x, gate_a, decay = gate_x_s[:, cols], gate_a_s[:, cols], fade[:tokens, cols]
        room = 1.0 - decay * decay
        mult = jnp.where(first, 1.0, jnp.sqrt(jnp.maximum(room, 0.001)))
        back = adj[:, cols]
        before = jnp.where(at_first, edge_ref[8:9, cols], pltpu.roll(state_ref[:, cols], 1, 0))
        d_mult = back * conv * gate_x
        moves = jnp.logical_and(room > 0.001, jnp.logical_not(first))
        d_decay = back * before - jnp.where(moves, d_mult * decay / mult, 0.0)
        d_log = d_decay * decay
        d_pre_x = back * conv * mult * gate_x * (1.0 - gate_x)
        d_pre_a = d_log * (-8.0 * par_ref[8:9, cols]) * gate_a * (1.0 - gate_a)
        dpar_ref[5:6, cols] = jnp.sum(d_pre_x, axis=0, keepdims=True)
        dpar_ref[6:7, cols] = jnp.sum(d_pre_a, axis=0, keepdims=True)
        dpar_ref[7:8, cols] = (
            jnp.sum(d_log * (-8.0 * gate_a), axis=0, keepdims=True) * par_ref[9:10, cols]
        )
        low_x, low_a = d_pre_x.astype(BF16), d_pre_a.astype(BF16)
        d_conv = (
            back * gate_x * mult
            + lax.dot_general(low_x, gate_ref[0, head], FLIPPED, preferred_element_type=F32)
            + lax.dot_general(low_a, gate_ref[1, head], FLIPPED, preferred_element_type=F32)
        )
        dconv[:tokens, cols] = d_conv
        over_rows = (((0,), (0,)), ((), ()))
        for gate, low in enumerate((low_x, low_a)):
            d_gate = lax.dot_general(conv_low, low, over_rows, preferred_element_type=F32)
            dgate_ref[:, gate, :, cols] = d_gate.astype(BF16).reshape(n, size // n, size)
        dpar_ref[4:5, cols] = jnp.sum(d_conv, axis=0, keepdims=True)
        for tap in range(4):
            dpar_ref[tap : tap + 1, cols] = jnp.sum(
                d_conv * wide[8 - tap : 8 - tap + tokens, cols], axis=0, keepdims=True
            )

    rows_copy = remote(
        dconv.at[pl.ds(0, 8)], head_rows, send_rows, recv_rows, lax.rem(me + n - 1, n)
    )
    pl.when(me > 0)(rows_copy.start)
    host(hosted[3:])
    loads[2].wait()
    for start in range(0, model, size):
        cols = slice(start, start + size)
        d_one_part[:, cols] = lax.dot_general(
            dy_ref[...], w_branch[cols], FLIPPED, preferred_element_type=F32
        )

    @pl.when(me + 1 < n)
    def _():
        rows_copy.wait_recv()
        dconv[tokens:] = head_rows[...]

    @pl.when(me + 1 == n)
    def _():
        dconv[tokens:] = jnp.zeros((8, width), F32)

    for head in range(width // size):
        cols = slice(head * size, (head + 1) * size)
        total = par_ref[0:1, cols] * dconv[:tokens, cols]
        for tap in range(1, 4):
            total = total + par_ref[tap : tap + 1, cols] * dconv[tap : tap + tokens, cols]
        dxb_ref[:, cols] = total.astype(BF16)

    pl.when(me > 0)(rows_copy.wait_send)

    def sent(place, carry):
        told(place).wait_send()
        return carry

    lax.fori_loop(0, me, sent, 0)
    core = lax.axis_index("ch")
    half = tokens // 2
    loads[1].wait()
    for start in range(0, model, size):
        cols = slice(start, start + size)
        part = (
            d_one_part[:, cols]
            + lax.dot_general(dxb_ref[...], w_in[cols], FLIPPED, preferred_element_type=F32)
        ).astype(BF16)
        d_one[0, :, cols] = part[:half]
        d_one[1, :, cols] = part[half:]
    exchange = pltpu.make_async_remote_copy(
        src_ref=d_one.at[1 - core],
        dst_ref=d_one_got,
        send_sem=send_m,
        recv_sem=recv_m,
        device_id={"ch": 1 - core},
        device_id_type=MESH,
    )
    exchange.start()
    exchange.wait_recv()

    def norm(at, total):
        r = pl.ds(pl.multiple_of(at * 16, 16), 16)
        x = x_ref[r].astype(F32)
        scale = lax.rsqrt(jnp.mean(x * x, axis=-1, keepdims=True) + 1e-06)
        grad = d_one[core, r].astype(F32) + d_one_got[r].astype(F32)
        back = grad * gain_ref[...]
        shrink = scale * scale * scale * jnp.mean(x * back, axis=-1, keepdims=True)
        dx_ref[core, r] = resid_ref[r] + (scale * back - x * shrink)
        return total + jnp.sum(grad * (x * scale), axis=0, keepdims=True)

    dgain_ref[...] = lax.fori_loop(0, half // 16, norm, jnp.zeros((1, model), F32))
    share = pltpu.make_async_remote_copy(
        src_ref=dx_ref.at[core],
        dst_ref=dx_ref.at[core],
        send_sem=send_x,
        recv_sem=recv_x,
        device_id={"ch": 1 - core},
        device_id_type=MESH,
    )
    share.start()
    exchange.wait_send()
    own_load.wait()
    part, rows = own.shape[2:4]
    chunk = 16 if rows % 16 == 0 else rows
    outs = []
    for kind in range(kinds):
        for h in range(2):
            for place in range(part):
                hosted[kind * part + place][h].wait()

                def add(at, carry, kind=kind, h=h, place=place):
                    r = pl.ds(pl.multiple_of(at * chunk, chunk), chunk)
                    own[h, kind, place, r] = (
                        own[h, kind, place, r].astype(F32) + near_ref[h, kind, place, r].astype(F32)
                    ).astype(BF16)
                    return carry

                lax.fori_loop(0, rows // chunk, add, 0)
            outs.append(
                pltpu.make_async_copy(
                    own.at[h, kind],
                    column_ref.at[kind, pl.ds(h * part, part)],
                    out_sem.at[kind, h],
                )
            )
            outs[-1].start()
    for copy in outs:
        copy.wait()
    pltpu.make_async_remote_copy(
        src_ref=dx_ref.at[core],
        dst_ref=dx_ref.at[1 - core],
        send_sem=send_x,
        recv_sem=recv_x,
        device_id={"ch": 1 - core},
        device_id_type=MESH,
    ).wait_recv()
    share.wait_send()


def mixer_backward(
    mixed, weights, x_half, gain, d_resid, y_pre, states, edge, conv, x_branch, gates, par, halves, own, hidden_units
):
    n = lax.axis_size("seq")
    tokens, width = x_branch.shape
    model = mixed.shape[1]
    size = gates.shape[2]
    half = tokens // 2
    _, kinds, part, rows, units = halves.shape
    dma = pltpu.SemaphoreType.DMA
    whole = pltpu.VMEM((tokens, width), F32)
    longer = pltpu.VMEM((tokens + 8, width), F32)
    weight = pltpu.VMEM((model, width), BF16)
    return pl.pallas_call(
        functools.partial(backward_body, n, hidden_units),
        out_shape=(
            jax.ShapeDtypeStruct((tokens, width), BF16),
            jax.ShapeDtypeStruct((tokens, width), BF16),
            jax.ShapeDtypeStruct((n, 2, size // n, width), BF16),
            jax.ShapeDtypeStruct((8, width), F32),
            jax.ShapeDtypeStruct((2, half, model), F32),
            jax.ShapeDtypeStruct((1, model), F32),
            jax.ShapeDtypeStruct((kinds, 2 * part, rows, units), BF16),
        ),
        in_specs=[VMEM] + [HBM] * 3 + [VMEM] * 10 + [HBM, HBM],
        out_specs=(VMEM,) * 6 + (HBM,),
        scratch_shapes=[
            pltpu.VMEM(halves.shape, BF16),
            pltpu.VMEM(halves.shape, BF16),
            weight,
            weight,
            weight,
            pltpu.VMEM((2, half, model), BF16),
            pltpu.VMEM((half, model), BF16),
            pltpu.VMEM((tokens, model), F32),
            longer,
            whole,
            whole,
            whole,
            whole,
            longer,
            longer,
            pltpu.VMEM((2, width), F32),
            pltpu.VMEM((n, 2, width), F32),
            pltpu.VMEM((8, width), F32),
            dma(()),
            dma(()),
            dma((n,)),
            dma((n,)),
            dma((kinds, part, 2)),
            dma((kinds, part, 2)),
            dma(()),
            dma(()),
            dma(()),
            dma(()),
            dma((3,)),
            dma(()),
            dma((kinds, 2)),
        ],
        compiler_params=params(5, 60),
        name="mixer_backward",
    )(mixed, *weights, x_half, gain, d_resid, y_pre, states, edge, conv, x_branch, gates, par, halves, own)


def ffn_body(n, hidden_units, *refs):
    own_ref, cots_ref, column_ref, near_ref, resid_ref, gain_ref = refs[:6]
    block_ref, d_resid_ref, mixed_ref, d_gain_ref, turned_ref = refs[6:11]
    halves_ref, mine_ref, far_ref = refs[11:14]
    tokens, cots, w, extra, hidden, box, sib, got, stage, turned, my_cot = refs[14:25]
    token_sems = refs[25:28]
    send_w, recv_w, keep_w, keep_c, keep_t, keep_m = refs[28:34]
    send_c, recv_s, send_z, recv_r, send_f, recv_f, send_m, recv_m, move, out_sem = refs[34:]
    groups = n // INNER
    half = groups // 2
    me, outer, by_x, by_y, by_xy = whereabouts()
    base = outer * INNER
    core = lax.axis_index("ch")
    above, below = outer + 1 < groups, outer > 0
    sibling = {"ch": 1 - core}
    barrier = pltpu.get_barrier_semaphore()

    def hello(peer):
        pl.semaphore_signal(barrier, inc=1, device_id=peer, device_id_type=MESH)

    hello({"seq": by_x})
    hello({"seq": by_y})
    hello(sibling)
    pl.when(above)(lambda: hello({"seq": me + INNER}))
    pl.when(below)(lambda: hello({"seq": me - INNER}))
    pl.semaphore_wait(barrier, 3 + above.astype(jnp.int32) + below.astype(jnp.int32))
    flips = ((by_x, by_y), (by_y, by_x))
    rows, units = w.shape[3], w.shape[4]
    split = Units(hidden_units, groups, core)
    tall, model = own_ref.shape
    count = 2 * tall
    deep = INNER * rows
    tile = 256

    def part(h):
        return pl.ds(h * half, half)


    chain_t = Chain(n, own_ref, tokens, *token_sems)

    def weight_copy(kind, h, far, receive=False):
        source = flips[h][0] if far else me
        if receive:
            source = by_xy if far else flips[h][1]
        src = near_ref.at[h, kind] if far else column_ref.at[kind, part(h)]
        return Sized(
            split,
            outer,
            lambda width: remote(
                src.at[:, :, pl.ds(0, width)],
                w.at[kind, part(h), source - base, :, pl.ds(0, width)],
                send_w.at[kind, h, far],
                recv_w.at[kind, h, far],
                flips[h][1],
            ),
        )

    keep = [
        [
            pltpu.make_async_copy(
                column_ref.at[kind], w.at[kind, :, me - base], keep_w.at[kind, 0]
            ),
            *(
                pltpu.make_async_copy(
                    near_ref.at[h, kind],
                    w.at[kind, part(h), flips[h][0] - base],
                    keep_w.at[kind, 1 + h],
                )
                for h in range(2)
            ),
        ]
        for kind in range(3)
    ]
    every = [(h, far) for far in range(2) for h in range(2)]
    own_t = chain_t.keep(keep_t)
    load_c = pltpu.make_async_copy(cots_ref, cots, keep_c)
    load_m = pltpu.make_async_copy(cots_ref.at[outer, core], my_cot, keep_m)
    chain_t.start()
    for kind in range(3):
        for h, far in every:
            weight_copy(kind, h, far).start()
    own_t.start()
    load_c.start()
    load_m.start()
    for kind in range(3):
        for copy in keep[kind]:
            copy.start()
    for step in range(1, groups):
        chain_t.step(step)
    chain_t.finish()
    own_t.wait()

    def weights_landed(kind):
        for h, far in every:
            weight_copy(kind, h, far, True).wait_recv()
        for copy in keep[kind]:
            copy.wait()
        if not split.even:

            @pl.when(jnp.logical_not(split.full(outer)))
            def _():
                rest = jnp.zeros((groups, INNER, rows, LANES), BF16)
                w[kind, :, :, :, units - LANES :] = rest

    def columns(kind, at):
        return w[kind, :, :, :, at : at + tile].reshape(model, tile)

    def token_rows(place):
        return pl.ds(pl.multiple_of(place * count, count), count)

    def each(limit, action):
        def one(turn, carry):
            action(turn)
            return carry

        lax.fori_loop(0, limit, one, 0)

    weights_landed(0)
    weights_landed(1)

    def middle(place):
        left = tokens[place].reshape(count, model)
        r = token_rows(place)
        for at in range(0, units, tile):
            c = slice(at, at + tile)
            gate = jnp.dot(left, columns(0, at), preferred_element_type=F32)
            up = jnp.dot(left, columns(1, at), preferred_element_type=F32)
            value, slope = gelu_parts(gate)
            hidden[0, r, c] = (value * up).astype(BF16)
            hidden[1, r, c] = (up * slope).astype(BF16)
            hidden[2, r, c] = value.astype(BF16)

    each(groups, middle)
    def back_hidden(place):
        left = cots[place].reshape(count, model)
        r = token_rows(place)
        for at in range(0, units, tile):
            c = slice(at, at + tile)
            back = jnp.dot(left, columns(2, at), preferred_element_type=F32)
            for kind in (1, 2):
                hidden[kind, r, c] = (back * hidden[kind, r, c].astype(F32)).astype(BF16)


    boxes = (cots, box)

    def partial(kind, place):
        r = token_rows(place)
        for at in range(groups):
            pairs = ((1, 0), (2, 1)) if kind == 0 else ((0, 2),)
            value = 0.0
            for left, right in pairs:
                value = value + lax.dot_general(
                    hidden[left, r],
                    w[right, at].reshape(deep, units),
                    FLIPPED,
                    preferred_element_type=F32,
                )
            value = value.astype(BF16)
            boxes[kind][place, 0, :, at * deep : (at + 1) * deep] = value[:tall]
            boxes[kind][place, 1, :, at * deep : (at + 1) * deep] = value[tall:]
        to_sibling(kind, place).start()

    def to_sibling(kind, place):
        return pltpu.make_async_remote_copy(
            src_ref=boxes[kind].at[place, 1 - core],
            dst_ref=sib.at[kind, place],
            send_sem=send_c.at[kind, place],
            recv_sem=recv_s.at[kind, place],
            device_id=sibling,
            device_id_type=MESH,
        )

    def along(kind, place, up):
        last = place == (outer + 1 if up else outer - 1)
        slot = place if up else jnp.where(last, groups, place)
        return remote(
            boxes[kind].at[place, core],
            got.at[kind, slot],
            send_z.at[kind, place],
            recv_r.at[kind, slot],
            me + (INNER if up else -INNER),
        )

    def landed(kind, slot):
        return remote(
            box.at[0, core], got.at[kind, slot], send_z.at[kind, 0], recv_r.at[kind, slot], by_x
        )

    chunk = 16

    def rows_of(at):
        return pl.ds(pl.multiple_of(at * chunk, chunk), chunk)

    def ready(kind, place, incoming):
        to_sibling(kind, place).wait_recv()

        def add(at, with_got):
            r = rows_of(at)
            value = boxes[kind][place, core, r].astype(F32) + sib[kind, place, r].astype(F32)
            if with_got:
                value = value + got[kind, place, r].astype(F32)
            boxes[kind][place, core, r] = value.astype(BF16)

        @pl.when(incoming)
        def _():
            landed(kind, place).wait_recv()
            each(tall // chunk, lambda at: add(at, True))

        @pl.when(jnp.logical_not(incoming))
        def _():
            each(tall // chunk, lambda at: add(at, False))

    def pass_on(kind, turn):
        ups = groups - 1 - outer
        upper = jnp.where(outer < half, turn < ups, turn >= outer)
        later = jnp.where(outer < half, turn, turn - outer)
        earlier = jnp.where(outer < half, turn - ups, turn)

        @pl.when(upper)
        def _():
            place = groups - 1 - later
            ready(kind, place, below)
            along(kind, place, True).start()

        @pl.when(jnp.logical_not(upper))
        def _():
            ready(kind, earlier, above)
            along(kind, earlier, False).start()

    at_end = jnp.logical_or(outer == 0, outer == groups - 1)

    def partials(kind, start, stop):
        def one(turn, carry):
            partial(kind, far_first(groups, outer, turn))

            @pl.when(jnp.logical_and(at_end, turn >= 1))
            def _():
                pass_on(kind, turn - 1)

            return carry

        lax.fori_loop(start, stop, one, 0)

    def between(kind, turns):
        @pl.when(jnp.logical_not(at_end))
        def _():
            for turn in turns:
                pass_on(kind, turn)

    def totals(kind, use):
        to_sibling(kind, outer).wait_recv()
        for condition, slots in (
            (jnp.logical_and(below, above), (outer, groups)),
            (jnp.logical_and(below, jnp.logical_not(above)), (outer,)),
            (jnp.logical_and(jnp.logical_not(below), above), (groups,)),
        ):

            @pl.when(condition)
            def _(slots=slots):
                for slot in slots:
                    landed(kind, slot).wait_recv()

                def one(at):
                    r = rows_of(at)
                    value = boxes[kind][outer, core, r].astype(F32) + sib[kind, outer, r].astype(F32)
                    for slot in slots:
                        value = value + got[kind, slot, r].astype(F32)
                    use(r, value)

                each(tall // chunk, one)

    def clear(kind):
        def one(place):
            to_sibling(kind, place).wait_send()

            @pl.when(place > outer)
            def _():
                along(kind, place, True).wait_send()

            @pl.when(place < outer)
            def _():
                along(kind, place, False).wait_send()

        each(groups, one)


    made = (w.at[0], w.at[1], extra)

    def gradient_copy(kind, h, far):
        source = by_xy if far else flips[h][1]
        return Sized(
            split,
            outer,
            lambda width: remote(
                made[kind].at[part(h), source - base, :, pl.ds(0, width)],
                far_ref.at[h, far, kind, :, :, pl.ds(0, width)],
                send_f.at[kind, h, far],
                recv_f.at[kind, h, far],
                flips[h][1],
            ),
        )

    def gradients(kinds, source, h):
        for at in range(h * half, (h + 1) * half):
            left = source[:, :, :, at * deep : (at + 1) * deep].reshape(groups * count, deep)
            turned[...] = left.T
            for kind, right in kinds:
                for start in range(0, units, tile):
                    c = slice(start, start + tile)
                    made[kind][at, :, :, c] = (
                        jnp.dot(turned[...], hidden[right, :, c], preferred_element_type=F32)
                        .astype(BF16)
                        .reshape(INNER, rows, tile)
                    )
        for kind, _ in kinds:
            for far in (1, 0):
                gradient_copy(kind, h, far).start()

    def collect(kind, h, far):
        inner = (flips[h][0] if far else me) - base
        gradient_copy(kind, h, far).wait_recv()
        load = pltpu.make_async_copy(far_ref.at[h, far, kind], stage, move)
        load.start()
        load.wait()
        for place in range(half):
            at = h * half + place

            def one(turn, place=place, at=at):
                r = rows_of(turn)
                made[kind][at, inner, r] = (
                    made[kind][at, inner, r].astype(F32) + stage[place, r].astype(F32)
                ).astype(BF16)

            each(rows // chunk, one)
        out_copy(kind, h, far).start()

    def out_copy(kind, h, far):
        inner = (flips[h][0] if far else me) - base
        return pltpu.make_async_copy(
            made[kind].at[part(h), inner],
            (halves_ref if far else mine_ref).at[h, kind],
            out_sem.at[kind, h, far],
        )

    load_c.wait()
    gradients(((2, 0),), cots, 0)
    gradients(((2, 0),), cots, 1)
    weights_landed(2)
    for kind in range(3):
        for h, far in every:
            weight_copy(kind, h, far).wait_send()
    partials(1, 0, groups)
    each(groups, back_hidden)
    load_m.wait()
    partials(0, 0, half)
    between(1, range(1))
    partials(0, half, groups)
    gradients(((0, 1),), tokens, 0)
    between(1, range(1, half))
    gradients(((0, 1),), tokens, 1)
    gradients(((1, 2),), tokens, 0)
    between(1, range(half, groups - 1))
    gradients(((1, 2),), tokens, 1)

    def shared(ref, at, part):
        return pltpu.make_async_remote_copy(
            src_ref=ref.at[core],
            dst_ref=ref.at[part],
            send_sem=send_m.at[at],
            recv_sem=recv_m.at[at],
            device_id=sibling,
            device_id_type=MESH,
        )

    def finish(r, value):
        block_ref[core, r] = (resid_ref[r] + value).astype(BF16)

    d_gain_ref[...] = jnp.zeros((1, model), F32)

    def norm(r, grad):
        resid = resid_ref[r]
        scale = lax.rsqrt(jnp.mean(resid * resid, axis=-1, keepdims=True) + 1e-06)
        back = grad * gain_ref[...]
        shrink = scale * scale * scale * jnp.mean(resid * back, axis=-1, keepdims=True)
        value = my_cot[r].astype(F32) + (scale * back - resid * shrink)
        d_resid_ref[r] = value
        mixed_ref[core, r] = value.astype(BF16)
        d_gain_ref[...] = d_gain_ref[...] + jnp.sum(grad * (resid * scale), axis=0, keepdims=True)

    for far in (1, 0):
        for h in range(2):
            collect(2, h, far)
    between(0, range(1))
    totals(1, finish)
    show = shared(block_ref, 1, core)
    show.start()
    for far in (1, 0):
        for h in range(2):
            collect(0, h, far)
    between(0, range(1, groups - 1))
    totals(0, norm)
    share = shared(mixed_ref, 0, core)
    share.start()
    shared(mixed_ref, 0, 1 - core).wait_recv()
    for start in range(0, model, tile):
        c = slice(start, start + tile)
        turned_ref[c, :tall] = mixed_ref[0, :, c].T
        turned_ref[c, tall:] = mixed_ref[1, :, c].T
    for far in (1, 0):
        for h in range(2):
            collect(1, h, far)
    clear(0)
    clear(1)
    shared(block_ref, 1, 1 - core).wait_recv()
    share.wait_send()
    show.wait_send()
    for kind in range(3):
        for h, far in every:
            gradient_copy(kind, h, far).wait_send()
            out_copy(kind, h, far).wait()


def feed_forward(own, cots, column, near, resid, gain, hidden_units):
    n = lax.axis_size("seq")
    groups = n // INNER
    tall, model = own.shape
    kinds, _, rows, units = column.shape
    half = groups // 2
    dma = pltpu.SemaphoreType.DMA
    part = jax.ShapeDtypeStruct((2, kinds, half, rows, units), BF16)
    return pl.pallas_call(
        functools.partial(ffn_body, n, hidden_units),
        out_shape=(
            jax.ShapeDtypeStruct((2, tall, model), BF16),
            jax.ShapeDtypeStruct((tall, model), F32),
            jax.ShapeDtypeStruct((2, tall, model), BF16),
            jax.ShapeDtypeStruct((1, model), F32),
            jax.ShapeDtypeStruct((model, 2 * tall), BF16),
            part,
            part,
            jax.ShapeDtypeStruct((2, 2, kinds, half, rows, units), BF16),
        ),
        in_specs=[HBM] * 4 + [VMEM] * 2,
        out_specs=(VMEM,) * 5 + (HBM,) * 3,
        scratch_shapes=[
            pltpu.VMEM((groups, 2, tall, model), BF16),
            pltpu.VMEM((groups, 2, tall, model), BF16),
            pltpu.VMEM((kinds, groups, INNER, rows, units), BF16),
            pltpu.VMEM((groups, INNER, rows, units), BF16),
            pltpu.VMEM((3, groups * 2 * tall, units), BF16),
            pltpu.VMEM((groups, 2, tall, model), BF16),
            pltpu.VMEM((2, groups, tall, model), BF16),
            pltpu.VMEM((2, groups + 1, tall, model), BF16),
            pltpu.VMEM((half, rows, units), BF16),
            pltpu.VMEM((INNER * rows, groups * 2 * tall), BF16),
            pltpu.VMEM((tall, model), BF16),
            *chain_semaphores(groups),
            dma((kinds, 2, 2)),
            dma((kinds, 2, 2)),
            dma((kinds, 3)),
            dma(()),
            dma(()),
            dma(()),
            dma((2, groups)),
            dma((2, groups)),
            dma((2, groups)),
            dma((2, groups + 1)),
            dma((kinds, 2, 2)),
            dma((kinds, 2, 2)),
            dma((2,)),
            dma((2,)),
            dma(()),
            dma((kinds, 2, 2)),
        ],
        compiler_params=params(8, 63),
        name="feed_forward",
    )(own, cots, column, near, resid, gain)


def my_half(values):
    half = values.shape[0] // 2
    return lax.dynamic_slice_in_dim(values, lax.axis_index("ch") * half, half, 0)


def join(own):
    other = swap(own, "ch", 1)
    core = lax.axis_index("ch")
    return jnp.concatenate(
        [jnp.where(core == 0, own, other), jnp.where(core == 0, other, own)], axis=0
    )


def tokens_out(partial, half):
    width = partial.shape[1]
    groups = lax.axis_size("seq") // INNER
    outer = lax.axis_index("seq") // INNER
    core = lax.axis_index("ch")
    parts = partial.reshape(groups, 2, half, width)
    theirs = pick(parts, 1 - core, 1).astype(BF16)
    summed = (pick(parts, core, 1).astype(F32) + swap(theirs, "ch", 1).astype(F32)).astype(BF16)
    total = pick(summed, outer).astype(F32)
    for step in range(1, groups):
        total = total + swap(pick(summed, outer ^ step), "seq", step * INNER).astype(F32)
    return total


def feed_forward_parts(n_two, cot_half, all_cot, column, near, resid, ffn_gain, hidden_units):
    f32, bf16 = F32, BF16
    _, groups, depth, units = column.shape
    half_rows, model = n_two.shape
    tok_rows = 2 * half_rows
    _, norm_back_two = jax.vjp(scaled_norm, resid, ffn_gain)
    all_two, *full_ffn = gather_tokens(n_two, column, near)
    all_two, all_cot = (v.reshape(groups * tok_rows, model) for v in (all_two, all_cot))
    own = Units(hidden_units, groups, lax.axis_index("ch")).width(lax.axis_index("seq") // INNER)
    valid = lax.broadcasted_iota(jnp.int32, (1, units), 1) < own
    full_ffn = [jnp.where(valid, w.reshape(model, units), 0) for w in full_ffn]
    gate_pre = jnp.dot(all_two, full_ffn[0], preferred_element_type=f32)
    up_pre = jnp.dot(all_two, full_ffn[1], preferred_element_type=f32)
    gate_act, gelu_back_gate = jax.vjp(gelu_tanh, gate_pre)
    hidden = (gate_act * up_pre).astype(bf16)
    ffn_term = jnp.einsum("tf,df->td", hidden, full_ffn[2], preferred_element_type=f32).astype(bf16)
    d_hidden = jnp.einsum("td,df->tf", all_cot, full_ffn[2], preferred_element_type=f32)
    d_gate = gelu_back_gate(d_hidden * up_pre)[0].astype(bf16)
    d_up = (d_hidden * gate_act).astype(bf16)
    d_n_two = (
        jnp.einsum("tf,df->td", d_gate, full_ffn[0], preferred_element_type=f32)
        + jnp.einsum("tf,df->td", d_up, full_ffn[1], preferred_element_type=f32)
    ).astype(bf16)
    terms = [
        jnp.einsum("td,tf->df", left, right, preferred_element_type=f32)
        .astype(bf16)
        .reshape(groups, INNER, depth, units)
        for left, right in ((all_two, d_gate), (all_two, d_up), (all_cot, hidden))
    ]
    split = [v.reshape(groups, 2, half_rows, model) for v in (d_n_two, ffn_term)]
    if groups <= 4:
        d_n_two, ffn_out, far = reduce_tokens(split, terms)
    else:
        d_n_two, far = reduce_tokens(split[:1], terms)
        ffn_out = tokens_out(ffn_term, half_rows)
    block_out = join((resid + ffn_out).astype(bf16))
    inner = lax.axis_index("seq") % INNER
    by_half = [t.reshape(2, groups // 2, INNER, depth, units) for t in terms]

    def block_at(h, place):
        return jnp.stack([pick(t[h], place, 1) for t in by_half]).astype(f32)

    mine = jnp.stack(
        [(block_at(h, inner) + far[h, 0].astype(f32)).astype(bf16) for h in range(2)]
    )
    halves = jnp.stack(
        [(block_at(h, inner ^ (1, 2)[h]) + far[h, 1].astype(f32)).astype(bf16) for h in range(2)]
    )
    d_resid_norm, d_ffn_gain_term = norm_back_two(d_n_two)
    d_resid = cot_half.astype(f32) + d_resid_norm
    d_mixed = join(d_resid.astype(bf16))
    return block_out, d_resid, d_mixed, d_ffn_gain_term.reshape(1, model), halves, mine


def shards(
    inputs,
    norm_gain,
    branch_weight,
    input_weight,
    channel_params,
    gate_x_blocks,
    gate_a_blocks,
    out_weight,
    ffn_gain,
    ffn_gate,
    ffn_up,
    ffn_down,
    cotangent,
):
    f32 = F32
    bf16 = BF16
    n = lax.axis_size("seq")
    tok_rows, model = inputs.shape
    half_rows = tok_rows // 2
    heads, part, size = gate_x_blocks.shape
    width = heads * size
    depth = ffn_gate.shape[0]
    groups = n // INNER
    hidden_units = ffn_gate.shape[1]
    x_half = my_half(inputs)
    cot_half = my_half(cotangent)
    par = jnp.concatenate(
        [
            channel_params,
            jax.nn.softplus(channel_params[7:8]),
            jax.nn.sigmoid(channel_params[7:8]),
            jnp.zeros((6, width), f32),
        ],
        axis=0,
    )
    mixer_set = [input_weight, branch_weight, out_weight.T]
    gate_set = [gate_x_blocks, gate_a_blocks]
    ffn_set = [ffn_gate, ffn_up, ffn_down.T]
    gain_one, gain_two = norm_gain.reshape(1, model), ffn_gain.reshape(1, model)
    if depth % 16 == 0 and part % 16 == 0:
        made = gather_forward(
            mixer_set, gate_set, ffn_set, inputs, gain_one, par, gain_two, cot_half
        )
        *full_mixer, full_gates, column, n_one, n_one_turned, _ = made[:8]
        full_mixer = [w.reshape(model, width) for w in full_mixer]
        gates = full_gates.reshape(2, heads, size, size)
        made = made[8:]
    else:
        *full_mixer, full_gates, column, n_one, n_one_turned, last_rows = gather_weights(
            mixer_set, gate_set, ffn_set, inputs, gain_one
        )
        full_mixer = [w.reshape(model, width) for w in full_mixer]
        gates = full_gates.reshape(2, heads, size, size)
        made = mixer_forward(
            n_one,
            last_rows,
            full_mixer,
            gates,
            par,
            x_half,
            gain_two,
            column,
            cot_half,
            hidden_units,
        )
    x_branch, y_pre, conv_out, states, branch_out, edge, resid, n_two, near, cots = made
    if groups <= 4 and depth % 16 == 0:
        block_out, d_resid, d_mixed, d_ffn_gain_term, d_mixed_turned, halves, mine, _ = feed_forward(
            n_two, cots, column, near, resid, ffn_gain.reshape(1, model), hidden_units
        )
        block_out = block_out.reshape(tok_rows, model)
        d_mixed = d_mixed.reshape(tok_rows, model)
    else:
        block_out, d_resid, d_mixed, d_ffn_gain_term, halves, mine = feed_forward_parts(
            n_two, cot_half, cots, column, near, resid, ffn_gain, hidden_units
        )
        d_mixed_turned = d_mixed.T
    d_y, d_xb, d_gates, d_par, d_inputs, d_norm_gain_term, column_back = mixer_backward(
        d_mixed,
        full_mixer,
        x_half,
        norm_gain.reshape(1, model),
        d_resid,
        y_pre,
        states,
        edge,
        conv_out,
        x_branch,
        gates,
        par,
        halves,
        mine,
        hidden_units,
    )
    d_inputs = d_inputs.reshape(tok_rows, model)
    gain_rows = model // width
    scattered, small, spread = scatter_mixer(
        n_one_turned.reshape(n, depth, tok_rows),
        d_mixed_turned.reshape(n, depth, tok_rows),
        d_y,
        d_xb,
        branch_out,
        d_gates,
        d_par,
        d_norm_gain_term,
        d_ffn_gain_term,
        column_back,
        hidden_units,
    )
    ffn_grads = [spread[kind].astype(f32) for kind in range(3)]
    d_gate_pair = scattered[3 * depth :].reshape(2, part, heads, size).transpose(0, 2, 1, 3)
    return (
        block_out,
        d_inputs,
        small[8 : 8 + gain_rows].reshape(model),
        scattered[:depth],
        scattered[depth : 2 * depth],
        small[:8],
        d_gate_pair[0],
        d_gate_pair[1],
        scattered[2 * depth : 3 * depth].T,
        small[8 + gain_rows : 8 + 2 * gain_rows].reshape(model),
        ffn_grads[0],
        ffn_grads[1],
        ffn_grads[2].T,
    )


def solution(mesh):
    placed = (
        P("seq", None),
        P(),
        P("seq", "ch"),
        P("seq", "ch"),
        P(None, "ch"),
        P("ch", "seq", None),
        P("ch", "seq", None),
        P("ch", "seq"),
        P(),
        P("seq", "ch"),
        P("seq", "ch"),
        P("ch", "seq"),
        P("seq", None),
    )
    return jax.shard_map(
        shards,
        mesh=mesh,
        in_specs=placed,
        out_specs=(
            P("seq", None),
            P("seq", None),
            P(),
            P("seq", "ch"),
            P("seq", "ch"),
            P(None, "ch"),
            P("ch", "seq", None),
            P("ch", "seq", None),
            P("ch", "seq"),
            P(),
            P("seq", "ch"),
            P("seq", "ch"),
            P("ch", "seq"),
        ),
        check_vma=False,
    )
```

```python
import functools

import jax
import jax.numpy as jnp
from jax import lax
from jax.experimental import pallas as pl
from jax.experimental.pallas import tpu as pltpu
from jax.sharding import PartitionSpec as P

F32 = jnp.float32
BF16 = jnp.bfloat16
INNER = 4
MESH = pl.DeviceIdType.MESH
VMEM = pl.BlockSpec(memory_space=pltpu.VMEM)
ANY = pl.BlockSpec(memory_space=pl.ANY)
HBM = pl.BlockSpec(memory_space=pltpu.HBM)


def swap(value, axis, mask):
    return lax.ppermute(value, axis, [(i, i ^ mask) for i in range(lax.axis_size(axis))])


def pick(array, index, axis=0):
    return lax.dynamic_index_in_dim(array, index, axis, False)


def scaled_norm(values, gain):
    return values * lax.rsqrt(jnp.mean(values * values, axis=-1, keepdims=True) + 1e-06) * gain


def gelu_tanh(values):
    return jax.nn.gelu(values, approximate=True)


def whereabouts():
    me = lax.axis_index("seq")
    outer = me // INNER
    inner = me - outer * INNER
    y = inner // 2
    x = inner - 2 * y
    by_x = me + 1 - 2 * x
    by_y = me + 2 - 4 * y
    return me, outer, by_x, by_y, by_x + 2 - 4 * y


def when(condition, action):
    if condition is None:
        action()
    else:
        pl.when(condition)(action)


def both(one, other):
    if one is None or other is None:
        return one if other is None else other
    return jnp.logical_and(one, other)


def greet(peers):
    barrier = pltpu.get_barrier_semaphore()
    for condition, peer in peers:
        when(
            condition,
            lambda peer=peer: pl.semaphore_signal(
                barrier, inc=1, device_id={"seq": peer}, device_id_type=MESH
            ),
        )
    count = 0
    for condition, _ in peers:
        count = count + (1 if condition is None else condition.astype(jnp.int32))
    pl.semaphore_wait(barrier, count)


def greet_all(n, me, sibling=False):
    barrier = pltpu.get_barrier_semaphore()

    def hello(step, carry):
        pl.semaphore_signal(
            barrier, inc=1, device_id={"seq": lax.rem(me + step, n)}, device_id_type=MESH
        )
        return carry

    lax.fori_loop(1, n, hello, 0)
    if sibling:
        pl.semaphore_signal(
            barrier, inc=1, device_id={"ch": 1 - lax.axis_index("ch")}, device_id_type=MESH
        )
    pl.semaphore_wait(barrier, n if sibling else n - 1)


def remote(src, dst, send_sem, recv_sem, place):
    return pltpu.make_async_remote_copy(
        src_ref=src,
        dst_ref=dst,
        send_sem=send_sem,
        recv_sem=recv_sem,
        device_id={"seq": place},
        device_id_type=MESH,
    )


def params(collective_id, mib):
    return pltpu.CompilerParams(
        collective_id=collective_id, has_side_effects=True, vmem_limit_bytes=mib * 2**20
    )


def gather_begin(n, refs, greeted):
    w_refs, g_refs, f_refs, x_ref, gain_ref = refs[:3], refs[3:5], refs[5:8], refs[8], refs[9]
    wo_refs, go_ref, column_ref, one_ref, turned_ref, last_ref = refs[10:13], *refs[13:18]
    send_m, recv_m, send_f, recv_f, here, send_l, recv_l = refs[18:]
    groups = n // INNER
    me, outer, by_x, by_y, by_xy = whereabouts()
    above, below = outer + 1 < groups, outer > 0
    def column_peer(turn):
        return lax.rem(outer + turn, groups)

    if not greeted:
        barrier = pltpu.get_barrier_semaphore()

        def hello(peer):
            pl.semaphore_signal(barrier, inc=1, device_id={"seq": peer}, device_id_type=MESH)

        hello(by_x)
        hello(by_y)

        def hello_column(turn, carry):
            hello(me + (column_peer(turn) - outer) * INNER)
            return carry

        lax.fori_loop(1, groups, hello_column, 0)
        pl.when(me + 1 < n)(lambda: hello(me + 1))
        pl.when(me > 0)(lambda: hello(me - 1))
        neighbours = (me + 1 < n).astype(jnp.int32) + (me > 0).astype(jnp.int32)
        pl.semaphore_wait(barrier, groups + 1 + neighbours)
    units = Units(f_refs[0].shape[1], groups, lax.axis_index("ch"))
    half = w_refs[0].shape[1] // 2

    keep = [
        pltpu.make_async_copy(w_refs[kind], wo_refs[kind].at[me], here.at[kind])
        for kind in range(3)
    ]
    for gate in range(2):
        keep.append(pltpu.make_async_copy(g_refs[gate], go_ref.at[gate, :, me], here.at[3 + gate]))
    for kind in range(3):
        keep.append(
            Sized(
                units,
                outer,
                lambda width, kind=kind: pltpu.make_async_copy(
                    f_refs[kind].at[:, units.columns(outer, width)],
                    column_ref.at[kind, outer, :, pl.ds(0, width)],
                    here.at[5 + kind],
                ),
            )
        )
    for copy in keep:
        copy.start()
    sent = []

    def copies(h, source, way, target, own, kinds=range(4)):
        cols = pl.ds(h * half, half)
        pairs = [
            (w_refs[kind].at[:, cols], wo_refs[kind].at[source, :, cols]) for kind in range(3)
        ]
        pairs.append((g_refs[h], go_ref.at[h, :, source]))
        return [
            remote(
                given if own else dst,
                dst,
                send_m.at[kind, h, source, way],
                recv_m.at[kind, h, source],
                target,
            )
            for kind, (given, dst) in enumerate(pairs)
            if kind in kinds
        ]

    def send(condition, *what):
        def go():
            for copy in copies(*what):
                copy.start()

        when(condition, go)
        sent.append((condition, what))

    def arrive(condition, h, source, kinds=range(4)):
        def go():
            for copy in copies(h, source, 0, by_x, False, kinds):
                copy.wait_recv()

        when(condition, go)

    def exchange(turn, receive):
        place = lax.rem(outer + groups - turn, groups) if receive else column_peer(turn)
        owner = outer if receive else place
        return [
            Sized(
                units,
                owner,
                lambda width, kind=kind: remote(
                    f_refs[kind].at[:, units.columns(owner, width)],
                    column_ref.at[kind, place if receive else outer, :, pl.ds(0, width)],
                    send_f.at[kind, turn],
                    recv_f.at[kind, turn],
                    me + (place - outer) * INNER,
                ),
            )
            for kind in range(3)
        ]

    def each_turn(action):
        def one(turn, carry):
            action(turn)
            return carry

        lax.fori_loop(1, groups, one, 0)

    tokens, model = x_ref.shape
    tall = last_ref.shape[0]
    last_copy = remote(one_ref.at[pl.ds(tokens - tall, tall)], last_ref, send_l, recv_l, me + 1)

    def norm(at, carry):
        r = pl.ds(pl.multiple_of(at * 16, 16), 16)
        x = x_ref[r].astype(F32)
        scale = lax.rsqrt(jnp.mean(x * x, axis=-1, keepdims=True) + 1e-06)
        one_ref[r] = (x * scale * gain_ref[...]).astype(BF16)
        return carry

    def norm_all():
        lax.fori_loop(0, tokens // 16, norm, 0)
        pl.when(me + 1 < n)(last_copy.start)
        for start in range(0, model, 256):
            cols = slice(start, start + 256)
            turned_ref[cols] = one_ref[:, cols].T

        @pl.when(me == 0)
        def _():
            last_ref[...] = jnp.zeros(last_ref.shape, BF16)

    for step in range(groups):
        if step == 1:
            norm_all()
        for h in range(2):
            flip_p, flip_q = (by_x, by_y) if h == 0 else (by_y, by_x)
            if step == 0:
                send(above, h, me, 0, me + INNER, True)
                send(below, h, me, 1, me - INNER, True)
                send(None, h, me, 2, flip_p, True)
                send(None, h, me, 3, flip_q, True)
                continue
            for source, there, onward, way, to in (
                (me - step * INNER, outer >= step, above, 0, me + INNER),
                (me + step * INNER, outer + step < groups, below, 1, me - INNER),
            ):
                arrive(there, h, source)
                send(both(there, onward), h, source, way, to, False)
                send(there, h, source, 2, flip_p, False)
                send(there, h, source, 3, flip_q, False)
    each_turn(lambda turn: [copy.start() for copy in exchange(turn, False)])
    for step in range(groups):
        for h in range(2):
            flip_p, flip_q = (by_x, by_y) if h == 0 else (by_y, by_x)
            if step == 0:
                arrive(None, h, flip_p)
                send(None, h, flip_p, 3, flip_q, False)
                continue
            for source, there in (
                (flip_p - step * INNER, outer >= step),
                (flip_p + step * INNER, outer + step < groups),
            ):
                arrive(there, h, source)
                send(there, h, source, 3, flip_q, False)

    def last(kind):
        for place in range(groups):
            shift = (place - outer) * INNER
            for h in range(2):
                arrive(None, h, (by_y if h == 0 else by_x) + shift, (kind,))
                arrive(None, h, by_xy + shift, (kind,))
        for copy in keep[kind : kind + 1] if kind < 3 else keep[3:5]:
            copy.wait()

    def columns():
        each_turn(lambda turn: [copy.wait_recv() for copy in exchange(turn, True)])
        for copy in keep[5:]:
            copy.wait()

    def rows_before():
        pl.when(me > 0)(last_copy.wait_recv)

    def finish():
        for condition, what in sent:

            def done(what=what):
                for copy in copies(*what):
                    copy.wait_send()

            when(condition, done)
        each_turn(lambda turn: [copy.wait_send() for copy in exchange(turn, False)])
        pl.when(me + 1 < n)(last_copy.wait_send)

    return last, columns, rows_before, finish


def gather_body(n, *refs):
    last, columns, rows_before, finish = gather_begin(n, refs, False)
    for kind in range(4):
        last(kind)
    columns()
    rows_before()
    finish()


def gather_weights(weights, gates, ffn, x, gain):
    n = lax.axis_size("seq")
    groups = n // INNER
    rows, hidden_units = ffn[0].shape
    most = Units(hidden_units, groups, 0).most
    dma = pltpu.SemaphoreType.DMA
    made = [jax.ShapeDtypeStruct((n,) + w.shape, w.dtype) for w in weights]
    heads, part, size = gates[0].shape
    made.append(jax.ShapeDtypeStruct((2, heads, n, part, size), BF16))
    made.append(jax.ShapeDtypeStruct((3, groups, rows, most), BF16))
    made.append(jax.ShapeDtypeStruct(x.shape, BF16))
    made.append(jax.ShapeDtypeStruct(x.shape[::-1], BF16))
    made.append(jax.ShapeDtypeStruct((16, x.shape[1]), BF16))
    return pl.pallas_call(
        functools.partial(gather_body, n),
        out_shape=tuple(made),
        in_specs=[HBM] * 8 + [VMEM] * 2,
        out_specs=(HBM,) * 5 + (VMEM,) * 3,
        scratch_shapes=[
            dma((4, 2, n, 4)),
            dma((4, 2, n)),
            dma((3, groups)),
            dma((3, groups)),
            dma((8,)),
            dma(()),
            dma(()),
        ],
        compiler_params=params(1, 60),
        name="gather_weights",
    )(*weights, *gates, *ffn, x, gain)


LANES = 128


class Units:
    def __init__(self, total, groups, core):
        self.tiles, self.groups, self.core = total // LANES, groups, core
        self.most = -(-self.tiles // groups) * LANES
        self.even = self.tiles % groups == 0

    def start(self, place):
        up = (1 - self.core) * (self.groups - 1)
        return (place * self.tiles + up) // self.groups

    def full(self, place):
        return (self.start(place + 1) - self.start(place)) * LANES == self.most

    def width(self, place):
        return (self.start(place + 1) - self.start(place)) * LANES

    def columns(self, place, width):
        return pl.ds(pl.multiple_of(self.start(place) * LANES, LANES), width)


class Sized:
    def __init__(self, units, place, make):
        self.units, self.place, self.make = units, place, make

    def each(self, action):
        most = self.units.most
        if self.units.even:
            action(self.make(most))
            return
        full = self.units.full(self.place)
        pl.when(full)(lambda: action(self.make(most)))
        pl.when(jnp.logical_not(full))(lambda: action(self.make(most - LANES)))

    def start(self):
        self.each(lambda copy: copy.start())

    def wait(self):
        self.each(lambda copy: copy.wait())

    def wait_send(self):
        self.each(lambda copy: copy.wait_send())

    def wait_recv(self):
        self.each(lambda copy: copy.wait_recv())


def far_first(groups, outer, turn):
    def order(at):
        alone = groups - 1 - 2 * at
        later = turn - alone
        step = later // 2
        return jnp.where(
            turn < alone, groups - 1 - turn, jnp.where(later - 2 * step == 0, step, 2 * at - step)
        )

    return jnp.where(
        outer < groups // 2, order(outer), groups - 1 - order(groups - 1 - outer)
    )


class Chain:
    def __init__(self, n, own, whole, send, recv_z, recv_c):
        me = lax.axis_index("seq")
        self.groups = n // INNER
        self.outer = outer = me // INNER
        self.core = lax.axis_index("ch")
        self.above, self.below = outer + 1 < self.groups, outer > 0
        self.sibling = {"ch": 1 - self.core}
        self.to = ({"seq": me + INNER}, {"seq": me - INNER}, self.sibling)
        self.own, self.whole = own, whole
        self.send, self.recv_z, self.recv_c = send, recv_z, recv_c

    def copy(self, source, way, own=False):
        dst = self.whole.at[source, self.core]
        return pltpu.make_async_remote_copy(
            src_ref=self.own if own else dst,
            dst_ref=dst,
            send_sem=self.send.at[source, way],
            recv_sem=(self.recv_c if way == 2 else self.recv_z).at[source],
            device_id=self.to[way],
            device_id_type=MESH,
        )

    def from_sibling(self, source):
        return pltpu.make_async_remote_copy(
            src_ref=self.own,
            dst_ref=self.whole.at[source, 1 - self.core],
            send_sem=self.send.at[source, 2],
            recv_sem=self.recv_c.at[source],
            device_id=self.sibling,
            device_id_type=MESH,
        )

    def keep(self, sem):
        return pltpu.make_async_copy(self.own, self.whole.at[self.outer, self.core], sem)

    def ways(self, step):
        return (
            (self.outer - step, self.outer >= step, self.above, 0),
            (self.outer + step, self.outer + step < self.groups, self.below, 1),
        )

    def start(self):
        pl.when(self.above)(self.copy(self.outer, 0, True).start)
        pl.when(self.below)(self.copy(self.outer, 1, True).start)
        self.copy(self.outer, 2, True).start()

    def step(self, step):
        for source, there, onward, way in self.ways(step):
            pl.when(there)(lambda: self.copy(source, way).wait_recv())
            pl.when(both(there, onward))(lambda: self.copy(source, way).start())
            pl.when(there)(lambda: self.copy(source, 2).start())

    def finish(self):
        for source in range(self.groups):
            self.from_sibling(source).wait_recv()
        pl.when(self.above)(self.copy(self.outer, 0, True).wait_send)
        pl.when(self.below)(self.copy(self.outer, 1, True).wait_send)
        self.copy(self.outer, 2, True).wait_send()
        for step in range(1, self.groups):
            for source, there, onward, way in self.ways(step):
                pl.when(both(there, onward))(lambda: self.copy(source, way).wait_send())
                pl.when(there)(lambda: self.copy(source, 2).wait_send())


def chain_semaphores(groups):
    dma = pltpu.SemaphoreType.DMA
    return [dma((groups, 3)), dma((groups,)), dma((groups,))]


def tokens_body(n, *refs):
    own_ref, column_ref, near_ref = refs[:3]
    all_ref, w_refs = refs[3], refs[4:7]
    send_t, recv_z, recv_c, send_w, recv_w, here = refs[7:]
    groups = n // INNER
    half = groups // 2
    me, outer, by_x, by_y, by_xy = whereabouts()
    base = outer * INNER
    core = lax.axis_index("ch")
    above, below = outer + 1 < groups, outer > 0
    sibling = {"ch": 1 - core}
    barrier = pltpu.get_barrier_semaphore()

    def hello(peer):
        pl.semaphore_signal(barrier, inc=1, device_id=peer, device_id_type=MESH)

    hello({"seq": by_x})
    hello({"seq": by_y})
    hello(sibling)
    pl.when(above)(lambda: hello({"seq": me + INNER}))
    pl.when(below)(lambda: hello({"seq": me - INNER}))
    pl.semaphore_wait(barrier, 3 + above.astype(jnp.int32) + below.astype(jnp.int32))

    chain = Chain(n, own_ref, all_ref, send_t, recv_z, recv_c)

    def part(h):
        return pl.ds(h * half, half)

    flips = ((by_x, by_y), (by_y, by_x))

    def weight_copy(kind, h, far, receive=False):
        source = flips[h][0] if far else me
        if receive:
            source = by_xy if far else flips[h][1]
        return remote(
            near_ref.at[h, kind] if far else column_ref.at[kind, part(h)],
            w_refs[kind].at[part(h), source - base],
            send_w.at[kind, h, far],
            recv_w.at[kind, h, far],
            flips[h][1],
        )

    keep = [chain.keep(here.at[0])]
    for kind in range(3):
        keep.append(
            pltpu.make_async_copy(
                column_ref.at[kind], w_refs[kind].at[:, me - base], here.at[1 + kind]
            )
        )
        for h in range(2):
            keep.append(
                pltpu.make_async_copy(
                    near_ref.at[h, kind],
                    w_refs[kind].at[part(h), flips[h][0] - base],
                    here.at[4 + 2 * kind + h],
                )
            )
    every_w = [(kind, h, far) for kind in range(3) for h in range(2) for far in range(2)]

    chain.start()
    for what in every_w:
        weight_copy(*what).start()
    for copy in keep:
        copy.start()
    for step in range(1, groups):
        chain.step(step)
    for what in every_w:
        weight_copy(*what, receive=True).wait_recv()
    chain.finish()
    for what in every_w:
        weight_copy(*what).wait_send()
    for copy in keep:
        copy.wait()


def gather_tokens(tokens, column, near):
    n = lax.axis_size("seq")
    groups = n // INNER
    kinds, _, rows, units = column.shape
    dma = pltpu.SemaphoreType.DMA
    wide = jax.ShapeDtypeStruct((groups, 2) + tokens.shape, tokens.dtype)
    weight = jax.ShapeDtypeStruct((groups, INNER, rows, units), column.dtype)
    return pl.pallas_call(
        functools.partial(tokens_body, n),
        out_shape=(wide, weight, weight, weight),
        in_specs=[ANY] * 3,
        out_specs=(ANY,) * 4,
        scratch_shapes=chain_semaphores(groups)
        + [dma((kinds, 2, 2)), dma((kinds, 2, 2)), dma((10,))],
        compiler_params=params(6, 16),
        name="gather_tokens",
    )(tokens, column, near)


def reduce_body(n, kinds, *refs):
    p_refs, t_refs = refs[:kinds], refs[kinds : kinds + 3]
    out_refs, far_ref = refs[kinds + 3 : 2 * kinds + 3], refs[2 * kinds + 3]
    summed, got, send_c, recv_c, send_z, recv_z, send_f, recv_f = refs[2 * kinds + 4 :]
    groups = n // INNER
    half = groups // 2
    me, outer, by_x, by_y, by_xy = whereabouts()
    base = outer * INNER
    core = lax.axis_index("ch")
    above, below = outer + 1 < groups, outer > 0
    sibling = {"ch": 1 - core}
    barrier = pltpu.get_barrier_semaphore()

    def hello(peer):
        pl.semaphore_signal(barrier, inc=1, device_id=peer, device_id_type=MESH)

    hello({"seq": by_x})
    hello({"seq": by_y})
    hello(sibling)
    pl.when(above)(lambda: hello({"seq": me + INNER}))
    pl.when(below)(lambda: hello({"seq": me - INNER}))
    pl.semaphore_wait(barrier, 3 + above.astype(jnp.int32) + below.astype(jnp.int32))
    flips = ((by_x, by_y), (by_y, by_x))

    def gradient_copy(kind, h, far):
        source = by_xy if far else flips[h][1]
        return remote(
            t_refs[kind].at[pl.ds(h * half, half), source - base],
            far_ref.at[h, far, kind],
            send_f.at[kind, h, far],
            recv_f.at[kind, h, far],
            flips[h][1],
        )

    def to_sibling(kind, place):
        return pltpu.make_async_remote_copy(
            src_ref=p_refs[kind].at[place, 1 - core],
            dst_ref=summed.at[kind, place],
            send_sem=send_c.at[kind, place],
            recv_sem=recv_c.at[kind, place],
            device_id=sibling,
            device_id_type=MESH,
        )

    def along(kind, place, up):
        last = place == (outer + 1 if up else outer - 1)
        slot = place if up else jnp.where(last, groups, place)
        return remote(
            summed.at[kind, place],
            got.at[kind, slot],
            send_z.at[kind, place],
            recv_z.at[kind, slot],
            me + (INNER if up else -INNER),
        )

    def landed(kind, slot):
        return remote(
            summed.at[kind, 0], got.at[kind, slot], send_z.at[kind, 0], recv_z.at[kind, slot], by_x
        )

    def each(limit, action):
        def one(turn, carry):
            action(turn)
            return carry

        lax.fori_loop(0, limit, one, 0)

    every_f = [(kind, h, far) for far in (1, 0) for kind in range(3) for h in range(2)]
    for kind in range(kinds):
        each(groups, lambda place, kind=kind: to_sibling(kind, place).start())
    for what in every_f:
        gradient_copy(*what).start()

    tall = summed.shape[2]
    chunk = 16

    def rows_of(at):
        return pl.ds(pl.multiple_of(at * chunk, chunk), chunk)

    def ready(kind, place, incoming):
        to_sibling(kind, place).wait_recv()

        def local(at):
            r = rows_of(at)
            summed[kind, place, r] = (
                summed[kind, place, r].astype(F32) + p_refs[kind][place, core, r].astype(F32)
            ).astype(BF16)

        def more(at):
            r = rows_of(at)
            summed[kind, place, r] = (
                summed[kind, place, r].astype(F32)
                + p_refs[kind][place, core, r].astype(F32)
                + got[kind, place, r].astype(F32)
            ).astype(BF16)

        @pl.when(incoming)
        def _():
            landed(kind, place).wait_recv()
            each(tall // chunk, more)

        @pl.when(jnp.logical_not(incoming))
        def _():
            each(tall // chunk, local)

    for kind in range(kinds):

        def climb(turn, kind=kind):
            place = groups - 1 - turn

            @pl.when(place > outer)
            def _():
                ready(kind, place, below)
                along(kind, place, True).start()

        def sink(turn, kind=kind):
            place = turn

            @pl.when(place < outer)
            def _():
                ready(kind, place, above)
                along(kind, place, False).start()

        def turns(turn):
            @pl.when(outer < half)
            def _():
                climb(turn)
                sink(turn)

            @pl.when(outer >= half)
            def _():
                sink(turn)
                climb(turn)

        each(groups - 1, turns)
    for kind in range(kinds):
        to_sibling(kind, outer).wait_recv()

        def own(at, kind=kind):
            r = rows_of(at)
            out_refs[kind][r] = summed[kind, outer, r].astype(F32) + p_refs[kind][
                outer, core, r
            ].astype(F32)

        each(tall // chunk, own)
        for there, slot in ((below, outer), (above, groups)):

            @pl.when(there)
            def _():
                landed(kind, slot).wait_recv()

                def plus(at):
                    r = rows_of(at)
                    out_refs[kind][r] = out_refs[kind][r] + got[kind, slot, r].astype(F32)

                each(tall // chunk, plus)

    for kind in range(kinds):

        def clear(place, kind=kind):
            to_sibling(kind, place).wait_send()

            @pl.when(place > outer)
            def _():
                along(kind, place, True).wait_send()

            @pl.when(place < outer)
            def _():
                along(kind, place, False).wait_send()

        each(groups, clear)
    for what in every_f:
        gradient_copy(*what).wait()


def reduce_tokens(partials, gradients):
    n = lax.axis_size("seq")
    groups = n // INNER
    kinds = len(partials)
    _, _, tall, width = partials[0].shape
    _, _, rows, units = gradients[0].shape
    dma = pltpu.SemaphoreType.DMA
    return pl.pallas_call(
        functools.partial(reduce_body, n, kinds),
        out_shape=(jax.ShapeDtypeStruct((tall, width), F32),) * kinds
        + (jax.ShapeDtypeStruct((2, 2, 3, groups // 2, rows, units), BF16),),
        in_specs=[VMEM] * kinds + [ANY] * 3,
        out_specs=(VMEM,) * kinds + (ANY,),
        scratch_shapes=[
            pltpu.VMEM((kinds, groups, tall, width), BF16),
            pltpu.VMEM((kinds, groups + 1, tall, width), BF16),
            dma((kinds, groups)),
            dma((kinds, groups)),
            dma((kinds, groups)),
            dma((kinds, groups + 1)),
            dma((3, 2, 2)),
            dma((3, 2, 2)),
        ],
        compiler_params=params(7, 60),
        name="reduce_tokens",
    )(*partials, *gradients)


def scatter_body(
    n,
    one_ref,
    mixed_ref,
    dy_ref,
    dxb_ref,
    branch_ref,
    gate_ref,
    dpar_ref,
    gain_one_ref,
    gain_two_ref,
    column_ref,
    out_ref,
    small_out,
    spread_ref,
    made,
    got_q,
    got_p,
    got_z,
    got_s,
    *sems,
):
    send_q, recv_q, send_p, recv_p, send_z, recv_z, send_s, recv_s, send_f, recv_f, here = sems
    groups = n // INNER
    me, outer, by_x, by_y, by_xy = whereabouts()
    rows = one_ref.shape[1]
    part_rows = gate_ref.shape[2]
    total, width = out_ref.shape
    half = width // 2

    def place_of(turn):
        return far_first(groups, outer, turn)

    def base_of(turn):
        return (place_of(turn) - outer) * INNER

    barrier = pltpu.get_barrier_semaphore()

    def hello(peer):
        pl.semaphore_signal(barrier, inc=1, device_id={"seq": peer}, device_id_type=MESH)

    hello(by_x)
    hello(by_y)

    def hello_outer(turn, carry):
        hello(me + base_of(turn))
        return carry

    lax.fori_loop(0, groups - 1, hello_outer, 0)
    core = lax.axis_index("ch")
    masks = [1 << bit for bit in range(n.bit_length() - 1)]
    pl.semaphore_signal(barrier, inc=1, device_id={"ch": 1 - core}, device_id_type=MESH)
    pl.semaphore_wait(barrier, groups + 2)

    flips = ((by_x, by_y), (by_y, by_x))
    units = Units(spread_ref.shape[2], groups, core)

    def exchange(turn, receive=False):
        place = lax.rem(outer + (groups - 1 - turn if receive else turn + 1), groups)
        owner = place if receive else outer
        return Sized(
            units,
            owner,
            lambda width: remote(
                column_ref.at[:, place, :, pl.ds(0, width)],
                spread_ref.at[:, :, units.columns(owner, width)],
                send_f.at[turn],
                recv_f.at[turn],
                me + (place - outer) * INNER,
            ),
        )

    def small(turn):
        place = me
        for at, mask in enumerate(masks):
            flipped = me + mask * (1 - 2 * lax.rem(me // mask, 2))
            place = jnp.where(turn == at, flipped, place)
        other = jnp.where(turn == len(masks), 1 - core, core)
        return pltpu.make_async_remote_copy(
            src_ref=small_out,
            dst_ref=got_s.at[turn],
            send_sem=send_s.at[turn],
            recv_sem=recv_s.at[turn],
            device_id=(place, other),
            device_id_type=MESH,
        )

    small_out[:8] = dpar_ref[...]
    small_out[8:] = jnp.zeros((8, width), F32)
    at = 8
    for gain_ref in (gain_one_ref, gain_two_ref):
        for start in range(0, gain_ref.shape[1], width):
            small_out[at : at + 1] = gain_ref[:, start : start + width]
            at += 1
    small_row = lax.broadcasted_iota(jnp.int32, small_out.shape, 0)

    def cols(h):
        return pl.ds(h * half, half)

    def along_q(turn, h, other):
        source = (by_xy if other else flips[h][1]) + base_of(turn)
        return remote(
            made.at[source, :, cols(h)],
            got_q.at[h, turn, other],
            send_q.at[h, turn, other],
            recv_q.at[h, turn, other],
            flips[h][1],
        )

    def along_p(turn, h):
        return remote(
            made.at[flips[h][0] + base_of(turn), :, cols(h)],
            got_p.at[h, turn],
            send_p.at[h, turn],
            recv_p.at[h, turn],
            flips[h][0],
        )

    def along_z(turn, h):
        place = place_of(turn)
        up = place > outer
        onto = jnp.where(up, outer + 1, outer - 1)
        slot = jnp.where(jnp.logical_and(place == onto, jnp.logical_not(up)), groups, place)
        return remote(
            made.at[me + base_of(turn), :, cols(h)],
            got_z.at[h, slot],
            send_z.at[h, turn],
            recv_z.at[h, slot],
            me + (onto - outer) * INNER,
        )

    def landed(slot, h):
        return remote(
            made.at[me, :, cols(h)], got_z.at[h, slot], send_z.at[h, 0], recv_z.at[h, slot], by_x
        )

    def has_incoming(turn):
        return jnp.where(place_of(turn) > outer, outer > 0, outer < groups - 1)

    def pass_on(turn):
        incoming = has_incoming(turn)
        for h in range(2):

            @pl.when(incoming)
            def _():
                landed(place_of(turn), h).wait_recv()
                add(me + base_of(turn), h, got_z, (h, place_of(turn)))

            along_z(turn, h).start()

    def make(block):
        left = one_ref[block]
        parts = [
            jnp.dot(left, dy_ref[...], preferred_element_type=F32),
            jnp.dot(left, dxb_ref[...], preferred_element_type=F32),
            jnp.dot(mixed_ref[block], branch_ref[...], preferred_element_type=F32),
        ]
        if rows % 16 == 0:
            for at, part in enumerate(parts):
                made[block, at * rows : (at + 1) * rows] = part.astype(BF16)
            for gate in range(2):
                at = 3 * rows + gate * part_rows
                made[block, at : at + part_rows] = gate_ref[block, gate]
        else:
            parts.extend(gate_ref[block, gate].astype(F32) for gate in range(2))
            made[block] = jnp.concatenate(parts, axis=0).astype(BF16)

    step = 32

    def add(block, h, ref, index):
        def one(at, carry):
            r = pl.ds(pl.multiple_of(at * step, step), step)
            made[block, r, cols(h)] = (
                made[block, r, cols(h)].astype(F32) + ref[index + (r,)].astype(F32)
            ).astype(BF16)
            return carry

        lax.fori_loop(0, total // step, one, 0)

    keep = Sized(
        units,
        outer,
        lambda width: pltpu.make_async_copy(
            column_ref.at[:, outer, :, pl.ds(0, width)],
            spread_ref.at[:, :, units.columns(outer, width)],
            here,
        ),
    )
    keep.start()

    def begin(turn, other):
        base = base_of(turn)
        if other:
            make(by_xy + base)
        else:
            for h in range(2):
                make(flips[h][1] + base)
        for h in range(2):
            along_q(turn, h, other).start()

    begin(0, 1)
    begin(0, 0)
    make(me + base_of(0))

    def turn_of(turn, carry):
        pl.when(turn <= len(masks))(lambda: small(turn).start())
        pl.when(turn < groups - 1)(lambda: exchange(turn).start())

        @pl.when(turn < groups)
        def _():
            base = base_of(turn)
            for h in range(2):
                along_q(turn, h, 1).wait_recv()
                add(flips[h][0] + base, h, got_q, (h, turn, 1))
                along_p(turn, h).start()
            pl.when(turn < groups - 1)(lambda: begin(turn + 1, 1))
            for h in range(2):
                along_q(turn, h, 0).wait_recv()
                add(me + base, h, got_q, (h, turn, 0))

            @pl.when(turn < groups - 1)
            def _():
                begin(turn + 1, 0)
                make(me + base_of(turn + 1))

            for h in range(2):
                along_p(turn, h).wait_recv()
                add(me + base, h, got_p, (h, turn))

            @pl.when(jnp.logical_and(turn < groups - 1, jnp.logical_not(has_incoming(turn))))
            def _():
                pass_on(turn)

            @pl.when(jnp.logical_and(turn >= 1, turn < groups - 1))
            def _():
                pl.when(has_incoming(turn - 1))(lambda: pass_on(turn - 1))

            @pl.when(jnp.logical_and(turn == groups - 2, has_incoming(turn)))
            def _():
                pass_on(turn)

        @pl.when(turn <= len(masks))
        def _():
            small(turn).wait()
            counts = jnp.logical_or(turn < len(masks), small_row >= 8)
            small_out[...] = small_out[...] + jnp.where(counts, got_s[turn], 0.0)

        return carry

    assert len(masks) < groups + 2
    lax.fori_loop(0, groups + 2, turn_of, 0)
    for condition, slots in (
        (jnp.logical_and(outer > 0, outer < groups - 1), (outer, groups)),
        (outer == groups - 1, (outer,)),
        (outer == 0, (groups,)),
    ):

        @pl.when(condition)
        def _(slots=slots):
            for h in range(2):
                for slot in slots:
                    landed(slot, h).wait_recv()

                def finish(at, carry):
                    r = pl.ds(pl.multiple_of(at * step, step), step)
                    value = made[me, r, cols(h)].astype(F32)
                    for slot in slots:
                        value = value + got_z[h, slot, r].astype(F32)
                    out_ref[r, cols(h)] = value
                    return carry

                lax.fori_loop(0, total // step, finish, 0)

    def clear(turn, carry):
        for h in range(2):
            along_q(turn, h, 0).wait_send()
            along_q(turn, h, 1).wait_send()
            along_p(turn, h).wait_send()

            @pl.when(turn < groups - 1)
            def _():
                along_z(turn, h).wait_send()

        @pl.when(turn < groups - 1)
        def _():
            exchange(turn, True).wait_recv()
            exchange(turn).wait_send()

        return carry

    lax.fori_loop(0, groups, clear, 0)
    keep.wait()


def scatter_mixer(one, mixed, dy, dxb, branch, gates, dpar, gain_one, gain_two, column, hidden_units):
    n, rows, _ = one.shape
    groups = n // INNER
    width = dy.shape[1]
    total = 3 * rows + 2 * gates.shape[2]
    kinds = column.shape[0]
    turns = n.bit_length()
    dma = pltpu.SemaphoreType.DMA
    return pl.pallas_call(
        functools.partial(scatter_body, n),
        out_shape=(
            jax.ShapeDtypeStruct((total, width), F32),
            jax.ShapeDtypeStruct((16, width), F32),
            jax.ShapeDtypeStruct((kinds, rows, hidden_units), BF16),
        ),
        in_specs=[VMEM] * 9 + [ANY],
        out_specs=(VMEM, VMEM, ANY),
        scratch_shapes=[
            pltpu.VMEM((n, total, width), BF16),
            pltpu.VMEM((2, groups, 2, total, width // 2), BF16),
            pltpu.VMEM((2, groups, total, width // 2), BF16),
            pltpu.VMEM((2, groups + 1, total, width // 2), BF16),
            pltpu.VMEM((turns, 16, width), F32),
            dma((2, groups, 2)),
            dma((2, groups, 2)),
            dma((2, groups)),
            dma((2, groups)),
            dma((2, groups)),
            dma((2, groups + 1)),
            dma((turns,)),
            dma((turns,)),
            dma((groups,)),
            dma((groups,)),
            dma(()),
        ],
        compiler_params=params(2, 62),
        name="scatter_mixer",
    )(one, mixed, dy, dxb, branch, gates, dpar, gain_one, gain_two, column)


GELU_A = 0.7978845608028654
GELU_B = 0.044715


def gelu_parts(v):
    t = jnp.tanh(GELU_A * (v + GELU_B * v * v * v))
    value = 0.5 * v * (1.0 + t)
    slope = 0.5 * (1.0 + t) + 0.5 * v * (1.0 - t * t) * GELU_A * (1.0 + 3.0 * GELU_B * v * v)
    return value, slope


def gates_of(conv_low, gate_ref, par_ref, head, cols, first):
    size = gate_ref.shape[-1]
    weight_x, weight_a = (gate_ref[gate, head].reshape(size, size) for gate in range(2))
    pre_x = jnp.dot(conv_low, weight_x, preferred_element_type=F32)
    pre_a = jnp.dot(conv_low, weight_a, preferred_element_type=F32)
    gate_x = jax.nn.sigmoid(pre_x + par_ref[5:6, cols])
    gate_a = jax.nn.sigmoid(pre_a + par_ref[6:7, cols])
    decay = jnp.exp(-8.0 * gate_a * par_ref[8:9, cols])
    room = 1.0 - decay * decay
    mult = jnp.where(first, 1.0, jnp.sqrt(jnp.maximum(room, 0.001)))
    return gate_x, gate_a, decay, room, mult


FLIPPED = (((1,), (1,)), ((), ()))


def by_columns(ref, cols):
    if len(ref.shape) == 2:
        return ref[:, cols]
    return ref[:, :, cols].reshape(ref.shape[0] * ref.shape[1], -1)


def by_rows(ref, start, size):
    if len(ref.shape) == 2:
        return ref[start : start + size]
    rows = ref.shape[1]
    parts, at = [], start
    while at < start + size:
        block, inside = divmod(at, rows)
        upto = min(rows, inside + start + size - at)
        parts.append(ref[block, inside:upto])
        at += upto - inside
    return jnp.concatenate(parts, axis=0)


def first_row(tokens):
    row = lax.broadcasted_iota(jnp.int32, (tokens, 1), 0)
    return jnp.logical_and(row == 0, lax.axis_index("seq") == 0)


def forward_body(
    n,
    hidden_units,
    gathered,
    one_ref,
    last_ref,
    w_in_ref,
    w_branch_ref,
    w_out_ref,
    gate_ref,
    par_ref,
    x_ref,
    gain_ref,
    column_ref,
    cot_ref,
    xb_ref,
    yp_ref,
    conv_ref,
    state_ref,
    branch_ref,
    edge_ref,
    resid_ref,
    two_ref,
    near_ref,
    cots_ref,
    w_in,
    w_branch,
    w_out,
    mixed,
    mixed_got,
    wide,
    fade,
    mine,
    theirs,
    *sems,
):
    send_tot, recv_tot, send_f, recv_f, send_m, recv_m, loaded, kept = sems[:8]
    tokens, width = xb_ref.shape
    model = one_ref.shape[1]
    me = lax.axis_index("seq")
    size = gate_ref.shape[-1]
    loads = [
        pltpu.make_async_copy(src, dst, loaded.at[at])
        for at, (src, dst) in enumerate(
            ((w_in_ref, w_in), (w_branch_ref, w_branch), (w_out_ref, w_out))
        )
    ]
    core = lax.axis_index("ch")
    half = tokens // 2
    if gathered is None:
        for load in loads:
            load.start()
        greet_all(n, me, True)
        x_start = 0
    else:
        last, columns, rows_before, gather_finish, gates_load = gathered
        last(0)
        loads[0].start()
        rows_before()
        x_start = core * half
    _, _, by_x, by_y, _ = whereabouts()
    part = column_ref.shape[1] // 2
    kinds = column_ref.shape[0]
    units = Units(hidden_units, n // INNER, lax.axis_index("ch"))
    outer = me // INNER
    hosted = [
        [
            Sized(
                units,
                outer,
                lambda width, kind=kind, h=h, part=part: remote(
                    column_ref.at[kind, pl.ds(h * part, part), :, pl.ds(0, width)],
                    near_ref.at[h, kind, :, :, pl.ds(0, width)],
                    send_f.at[kind, h],
                    recv_f.at[kind, h],
                    (by_x, by_y)[h],
                ),
            )
            for h in range(2)
        ]
        for kind in range(kinds)
    ]

    def host(pieces):
        for pair in pieces:
            for copy in pair:
                copy.start()

    chain = Chain(n, cot_ref, cots_ref, *sems[8:])
    keep = chain.keep(kept)
    chain.start()
    keep.start()
    if gathered is None:
        host(hosted[:1])
    loads[0].wait()
    for start in range(0, width, size):
        cols = slice(start, start + size)
        low = jnp.dot(one_ref[...], by_columns(w_in, cols), preferred_element_type=F32).astype(BF16)
        xb_ref[:, cols] = low
        wide[8:, cols] = low.astype(F32)
        low = jnp.dot(last_ref[...], by_columns(w_in, cols), preferred_element_type=F32).astype(BF16)
        wide[:8, cols] = low.astype(F32)[8:]
    if gathered is not None:
        last(1)
        loads[1].start()
        last(3)
        gates_load.start()
        columns()
        host(hosted[:1])
        gates_load.wait()
    loads[1].wait()
    for start in range(0, width, size):
        cols = slice(start, start + size)
        yp_ref[:, cols] = jnp.dot(one_ref[...], by_columns(w_branch, cols), preferred_element_type=F32)

    if gathered is not None:
        last(2)
        loads[2].start()
    edge_ref[:8] = wide[:8]
    first = first_row(tokens)
    for head in range(width // size):
        cols = slice(head * size, (head + 1) * size)
        conv = par_ref[4:5, cols]
        for tap in range(4):
            conv = conv + par_ref[tap : tap + 1, cols] * wide[8 - tap : 8 - tap + tokens, cols]
        conv_low = conv.astype(BF16)
        conv_ref[:, cols] = conv_low
        gate_x, _, decay, _, mult = gates_of(conv_low, gate_ref, par_ref, head, cols, first)
        fade[:, cols] = decay
        state_ref[:, cols] = conv_low.astype(F32) * gate_x * mult

    row = lax.broadcasted_iota(jnp.int32, (8, width), 0)

    def inside(at, carry):
        r = pl.ds(pl.multiple_of(at * 8, 8), 8)
        a, b = fade[r], state_ref[r]
        for by in (1, 2, 4):
            a_back = pltpu.roll(a, by, 0)
            b_back = pltpu.roll(b, by, 0)
            b = jnp.where(row >= by, a * b_back + b, b)
            a = jnp.where(row >= by, a * a_back, a)
        fade[r] = a
        state_ref[r] = b
        return a[7:8] * carry[0], a[7:8] * carry[1] + b[7:8]

    ones, zeros = jnp.ones((1, width), F32), jnp.zeros((1, width), F32)
    tot_a, tot_b = lax.fori_loop(0, tokens // 8, inside, (ones, zeros))
    mine[0:1] = tot_a
    mine[1:2] = tot_b

    def told(place):
        return remote(mine, theirs.at[me], send_tot.at[place], recv_tot.at[me], place)

    def heard(place):
        return remote(mine, theirs.at[place], send_tot.at[place], recv_tot.at[place], place)

    def tell(place, carry):
        told(place).start()
        return carry

    lax.fori_loop(me + 1, n, tell, 0)
    host(hosted[1:])

    def hear(place, carry):
        heard(place).wait_recv()
        return carry

    lax.fori_loop(0, me, hear, 0)
    carry_in = zeros
    for place in range(n):
        gone = place < me
        through = jnp.where(gone, theirs[place, 0:1], 1.0)
        carry_in = through * carry_in + jnp.where(gone, theirs[place, 1:2], 0.0)
    edge_ref[8:] = jnp.broadcast_to(carry_in, (8, width))
    chain.step(1)

    def finish(at, carry):
        r = pl.ds(pl.multiple_of(at * 16, 16), 16)
        a, b = fade[r], state_ref[r]
        top = b[:8] + a[:8] * carry
        low = b[8:] + a[8:] * top[7:8]
        states = jnp.concatenate([top, low], axis=0)
        state_ref[r] = states
        branch_ref[r] = (states * gelu_parts(yp_ref[r])[0]).astype(BF16)
        return low[7:8]

    lax.fori_loop(0, tokens // 16, finish, carry_in)

    def sent(place, carry):
        told(place).wait_send()
        return carry

    lax.fori_loop(me + 1, n, sent, 0)
    loads[2].wait()
    for start in range(0, model, size):
        cols = slice(start, start + size)
        part = lax.dot_general(branch_ref[...], by_rows(w_out, start, size), FLIPPED, preferred_element_type=F32)
        mixed[0, :, cols] = part[:half]
        mixed[1, :, cols] = part[half:]
    exchange = pltpu.make_async_remote_copy(
        src_ref=mixed.at[1 - core],
        dst_ref=mixed_got,
        send_sem=send_m,
        recv_sem=recv_m,
        device_id={"ch": 1 - core},
        device_id_type=MESH,
    )
    exchange.start()
    exchange.wait_recv()

    def norm(at, carry):
        r = pl.ds(pl.multiple_of(at * 16, 16), 16)
        x = x_ref[pl.ds(pl.multiple_of(x_start + at * 16, 16), 16)]
        resid = x.astype(F32) + (mixed[core, r] + mixed_got[r])
        resid_ref[r] = resid
        scale = lax.rsqrt(jnp.mean(resid * resid, axis=-1, keepdims=True) + 1e-06)
        two_ref[r] = (resid * scale * gain_ref[...]).astype(BF16)
        return carry

    lax.fori_loop(0, half // 16, norm, 0)
    exchange.wait_send()
    for step in range(2, n // INNER):
        chain.step(step)
    for pair in hosted:
        for copy in pair:
            copy.wait()
    chain.finish()
    keep.wait()
    if gathered is not None:
        gather_finish()


def first_body(n, hidden_units, *refs):
    given, refs = refs[:12], refs[12:]
    weights, gates, ffn, (x_ref, gains_ref, par_ref, all_cot_ref) = (
        given[:3],
        given[3:5],
        given[5:8],
        given[8:],
    )
    outs, refs = refs[:18], refs[18:]
    scratch, sems = refs[:10], refs[10:]
    gather_sems, forward_sems, gate_sem = sems[:7], sems[7:-1], sems[-1]
    me = lax.axis_index("seq")
    norm_ref, gain_ref = gains_ref.at[pl.ds(0, 1)], gains_ref.at[pl.ds(1, 1)]
    half = x_ref.shape[0] // 2
    start = pl.multiple_of(lax.axis_index("ch") * half, half)
    cot_ref = all_cot_ref.at[pl.ds(start, half)]
    greet_all(n, me, True)
    steps = gather_begin(
        n, (*weights, *gates, *ffn, x_ref, norm_ref, *outs[:8], *gather_sems), True
    )
    gate_s, scratch = scratch[0], scratch[1:]
    full_gates, column_ref, one_ref, _, last_ref = outs[3:8]
    gates_load = pltpu.make_async_copy(full_gates, gate_s, gate_sem)
    forward_body(
        n,
        hidden_units,
        (*steps, gates_load),
        one_ref,
        last_ref,
        *outs[:3],
        gate_s,
        par_ref,
        x_ref,
        gain_ref,
        column_ref,
        cot_ref,
        *outs[8:],
        *scratch,
        *forward_sems,
    )


def mixer_forward(one, last, weights, gates, par, x_half, gain, column, cotangent, hidden_units):
    n = lax.axis_size("seq")
    tokens, model = one.shape
    width = par.shape[1]
    half = tokens // 2
    kinds, groups, rows, units = column.shape
    dma = pltpu.SemaphoreType.DMA
    whole = jax.ShapeDtypeStruct((tokens, width), F32)
    low = jax.ShapeDtypeStruct((tokens, width), BF16)
    return pl.pallas_call(
        functools.partial(forward_body, n, hidden_units, None),
        out_shape=(
            low,
            whole,
            low,
            whole,
            low,
            jax.ShapeDtypeStruct((16, width), F32),
            jax.ShapeDtypeStruct((half, model), F32),
            jax.ShapeDtypeStruct((half, model), BF16),
            jax.ShapeDtypeStruct((2, kinds, groups // 2, rows, units), column.dtype),
            jax.ShapeDtypeStruct((groups, 2) + cotangent.shape, cotangent.dtype),
        ),
        in_specs=[VMEM] * 2 + [HBM] * 3 + [VMEM] * 4 + [HBM, HBM],
        out_specs=(VMEM,) * 8 + (HBM, HBM),
        scratch_shapes=[
            pltpu.VMEM((model, width), BF16),
            pltpu.VMEM((model, width), BF16),
            pltpu.VMEM((model, width), BF16),
            pltpu.VMEM((2, half, model), F32),
            pltpu.VMEM((half, model), F32),
            pltpu.VMEM((tokens + 8, width), F32),
            pltpu.VMEM((tokens, width), F32),
            pltpu.VMEM((2, width), F32),
            pltpu.VMEM((n, 2, width), F32),
            dma((n,)),
            dma((n,)),
            dma((kinds, 2)),
            dma((kinds, 2)),
            dma(()),
            dma(()),
            dma((3,)),
            dma(()),
            *chain_semaphores(groups),
        ],
        compiler_params=params(4, 60),
        name="mixer_forward",
    )(one, last, *weights, gates, par, x_half, gain, column, cotangent)


def gather_forward(weights, gates, ffn, x, gains, par, cotangent):
    n = lax.axis_size("seq")
    groups = n // INNER
    tokens, model = x.shape
    rows, width = weights[0].shape
    half = tokens // 2
    hidden_units = ffn[0].shape[1]
    most = Units(hidden_units, groups, 0).most
    heads, part, size = gates[0].shape
    dma = pltpu.SemaphoreType.DMA
    shape = jax.ShapeDtypeStruct
    whole, low = shape((tokens, width), F32), shape((tokens, width), BF16)
    weight = pltpu.VMEM((n, rows, width), BF16)
    return pl.pallas_call(
        functools.partial(first_body, n, hidden_units),
        out_shape=(
            *(shape((n, rows, width), BF16) for _ in range(3)),
            shape((2, heads, n, part, size), BF16),
            shape((3, groups, rows, most), BF16),
            shape((tokens, model), BF16),
            shape((model, tokens), BF16),
            shape((16, model), BF16),
            low,
            whole,
            low,
            whole,
            low,
            shape((16, width), F32),
            shape((half, model), F32),
            shape((half, model), BF16),
            shape((2, 3, groups // 2, rows, most), BF16),
            shape((groups, 2, half, model), BF16),
        ),
        in_specs=[HBM] * 8 + [VMEM] * 3 + [HBM],
        out_specs=(HBM,) * 5 + (VMEM,) * 11 + (HBM,) * 2,
        scratch_shapes=[
            pltpu.VMEM((2, heads, n, part, size), BF16),
            weight,
            weight,
            weight,
            pltpu.VMEM((2, half, model), F32),
            pltpu.VMEM((half, model), F32),
            pltpu.VMEM((tokens + 8, width), F32),
            pltpu.VMEM((tokens, width), F32),
            pltpu.VMEM((2, width), F32),
            pltpu.VMEM((n, 2, width), F32),
            dma((4, 2, n, 4)),
            dma((4, 2, n)),
            dma((3, groups)),
            dma((3, groups)),
            dma((8,)),
            dma(()),
            dma(()),
            dma((n,)),
            dma((n,)),
            dma((3, 2)),
            dma((3, 2)),
            dma(()),
            dma(()),
            dma((3,)),
            dma(()),
            *chain_semaphores(groups),
            dma(()),
        ],
        compiler_params=params(9, 60),
        name="gather_forward",
    )(*weights, *gates, *ffn, x, gains, par, cotangent)


def backward_body(
    n,
    hidden_units,
    mixed_ref,
    w_in_ref,
    w_branch_ref,
    w_out_ref,
    x_ref,
    gain_ref,
    resid_ref,
    yp_ref,
    state_ref,
    edge_ref,
    conv_ref,
    xb_ref,
    gate_ref,
    par_ref,
    half_ref,
    own_ref,
    dy_ref,
    dxb_ref,
    dgate_ref,
    dpar_ref,
    dx_ref,
    dgain_ref,
    column_ref,
    near_ref,
    own,
    w_in,
    w_branch,
    w_out,
    d_one,
    d_one_got,
    d_one_part,
    fade,
    shift,
    adj,
    gate_x_s,
    gate_a_s,
    dconv,
    wide,
    mine,
    theirs,
    head_rows,
    *sems,
):
    send_rows, recv_rows, send_tot, recv_tot, send_f, recv_f, send_m, recv_m, send_x, recv_x, loaded, own_sem, out_sem = sems
    tokens, width = xb_ref.shape
    model = gain_ref.shape[1]
    me = lax.axis_index("seq")
    size = gate_ref.shape[2]
    loads = [
        pltpu.make_async_copy(src, dst, loaded.at[at])
        for at, (src, dst) in enumerate(
            ((w_out_ref, w_out), (w_in_ref, w_in), (w_branch_ref, w_branch))
        )
    ]
    for load in loads:
        load.start()
    greet_all(n, me, True)
    _, _, by_x, by_y, _ = whereabouts()
    kinds, pieces = half_ref.shape[1:3]
    units = Units(hidden_units, n // INNER, lax.axis_index("ch"))
    outer = me // INNER
    hosted = [
        [
            Sized(
                units,
                outer,
                lambda width, kind=kind, at=at, h=h: remote(
                    half_ref.at[h, kind, at, :, pl.ds(0, width)],
                    near_ref.at[h, kind, at, :, pl.ds(0, width)],
                    send_f.at[kind, at, h],
                    recv_f.at[kind, at, h],
                    (by_x, by_y)[h],
                ),
            )
            for h in range(2)
        ]
        for kind in range(kinds)
        for at in range(pieces)
    ]

    def host(some):
        for pair in some:
            for copy in pair:
                copy.start()

    host(hosted[:2])
    own_load = pltpu.make_async_copy(own_ref, own, own_sem)
    own_load.start()
    first = first_row(tokens)
    fade[tokens:] = jnp.ones((8, width), F32)
    loads[0].wait()
    for head in range(width // size):
        cols = slice(head * size, (head + 1) * size)
        gate_x, gate_a, decay, _, _ = gates_of(conv_ref[:, cols], gate_ref, par_ref, head, cols, first)
        gate_x_s[:, cols] = gate_x
        gate_a_s[:, cols] = gate_a
        fade[:tokens, cols] = decay
        value, slope = gelu_parts(yp_ref[:, cols])
        grad = jnp.dot(mixed_ref[...], w_out[:, cols], preferred_element_type=F32)
        dy_ref[:, cols] = (grad * state_ref[:, cols] * slope).astype(BF16)
        adj[:, cols] = grad * value
        shift[:, cols] = fade[1 : tokens + 1, cols]

    row = lax.broadcasted_iota(jnp.int32, (8, width), 0)
    tiles = tokens // 8

    def inside(turn, carry):
        r = pl.ds(pl.multiple_of((tiles - 1 - turn) * 8, 8), 8)
        a, b = shift[r], adj[r]
        for by in (1, 2, 4):
            a_next = pltpu.roll(a, 8 - by, 0)
            b_next = pltpu.roll(b, 8 - by, 0)
            b = jnp.where(row < 8 - by, a * b_next + b, b)
            a = jnp.where(row < 8 - by, a * a_next, a)
        shift[r] = a
        adj[r] = b
        return a[0:1] * carry[0], a[0:1] * carry[1] + b[0:1]

    ones, zeros = jnp.ones((1, width), F32), jnp.zeros((1, width), F32)
    tot_a, tot_b = lax.fori_loop(0, tiles, inside, (ones, zeros))
    first_fade = fade[0:1]
    mine[0:1] = first_fade * tot_a
    mine[1:2] = first_fade * tot_b

    def told(place):
        return remote(mine, theirs.at[me], send_tot.at[place], recv_tot.at[me], place)

    def heard(place):
        return remote(mine, theirs.at[place], send_tot.at[place], recv_tot.at[place], place)

    def tell(place, carry):
        told(place).start()
        return carry

    lax.fori_loop(0, me, tell, 0)
    host(hosted[2:3])

    def hear(turn, carry):
        heard(n - 1 - turn).wait_recv()
        return carry

    lax.fori_loop(0, n - 1 - me, hear, 0)
    carry_in = zeros
    for place in reversed(range(n)):
        gone = place > me
        through = jnp.where(gone, theirs[place, 0:1], 1.0)
        carry_in = through * carry_in + jnp.where(gone, theirs[place, 1:2], 0.0)

    def finish(turn, carry):
        r = pl.ds(pl.multiple_of((tiles - 1 - turn) * 8, 8), 8)
        value = adj[r] + shift[r] * carry
        adj[r] = value
        return value[0:1]

    lax.fori_loop(0, tiles, finish, carry_in)

    wide[:8] = edge_ref[:8]
    wide[8:] = xb_ref[...].astype(F32)
    at_first = lax.broadcasted_iota(jnp.int32, (tokens, 1), 0) == 0
    for head in range(width // size):
        cols = slice(head * size, (head + 1) * size)
        conv_low = conv_ref[:, cols]
        conv = conv_low.astype(F32)
        gate_x, gate_a, decay = gate_x_s[:, cols], gate_a_s[:, cols], fade[:tokens, cols]
        room = 1.0 - decay * decay
        mult = jnp.where(first, 1.0, jnp.sqrt(jnp.maximum(room, 0.001)))
        back = adj[:, cols]
        before = jnp.where(at_first, edge_ref[8:9, cols], pltpu.roll(state_ref[:, cols], 1, 0))
        d_mult = back * conv * gate_x
        moves = jnp.logical_and(room > 0.001, jnp.logical_not(first))
        d_decay = back * before - jnp.where(moves, d_mult * decay / mult, 0.0)
        d_log = d_decay * decay
        d_pre_x = back * conv * mult * gate_x * (1.0 - gate_x)
        d_pre_a = d_log * (-8.0 * par_ref[8:9, cols]) * gate_a * (1.0 - gate_a)
        dpar_ref[5:6, cols] = jnp.sum(d_pre_x, axis=0, keepdims=True)
        dpar_ref[6:7, cols] = jnp.sum(d_pre_a, axis=0, keepdims=True)
        dpar_ref[7:8, cols] = (
            jnp.sum(d_log * (-8.0 * gate_a), axis=0, keepdims=True) * par_ref[9:10, cols]
        )
        low_x, low_a = d_pre_x.astype(BF16), d_pre_a.astype(BF16)
        d_conv = (
            back * gate_x * mult
            + lax.dot_general(low_x, gate_ref[0, head], FLIPPED, preferred_element_type=F32)
            + lax.dot_general(low_a, gate_ref[1, head], FLIPPED, preferred_element_type=F32)
        )
        dconv[:tokens, cols] = d_conv
        over_rows = (((0,), (0,)), ((), ()))
        for gate, low in enumerate((low_x, low_a)):
            d_gate = lax.dot_general(conv_low, low, over_rows, preferred_element_type=F32)
            dgate_ref[:, gate, :, cols] = d_gate.astype(BF16).reshape(n, size // n, size)
        dpar_ref[4:5, cols] = jnp.sum(d_conv, axis=0, keepdims=True)
        for tap in range(4):
            dpar_ref[tap : tap + 1, cols] = jnp.sum(
                d_conv * wide[8 - tap : 8 - tap + tokens, cols], axis=0, keepdims=True
            )

    rows_copy = remote(
        dconv.at[pl.ds(0, 8)], head_rows, send_rows, recv_rows, lax.rem(me + n - 1, n)
    )
    pl.when(me > 0)(rows_copy.start)
    host(hosted[3:])
    loads[2].wait()
    for start in range(0, model, size):
        cols = slice(start, start + size)
        d_one_part[:, cols] = lax.dot_general(
            dy_ref[...], w_branch[cols], FLIPPED, preferred_element_type=F32
        )

    rows = own.shape[3]
    chunk = 32 if rows % 32 == 0 else rows
    outs = []

    def collect(piece):
        kind, at = divmod(piece, pieces)
        for h in range(2):
            hosted[piece][h].wait()

            def add(turn, carry, h=h):
                r = pl.ds(pl.multiple_of(turn * chunk, chunk), chunk)
                own[h, kind, at, r] = (
                    own[h, kind, at, r].astype(F32) + near_ref[h, kind, at, r].astype(F32)
                ).astype(BF16)
                return carry

            lax.fori_loop(0, rows // chunk, add, 0)
            outs.append(
                pltpu.make_async_copy(
                    own.at[h, kind, at],
                    column_ref.at[kind, h * pieces + at],
                    out_sem.at[kind, at, h],
                )
            )
            outs[-1].start()

    own_load.wait()
    for piece in range(3):
        collect(piece)

    @pl.when(me + 1 < n)
    def _():
        rows_copy.wait_recv()
        dconv[tokens:] = head_rows[...]

    @pl.when(me + 1 == n)
    def _():
        dconv[tokens:] = jnp.zeros((8, width), F32)

    for head in range(width // size):
        cols = slice(head * size, (head + 1) * size)
        total = par_ref[0:1, cols] * dconv[:tokens, cols]
        for tap in range(1, 4):
            total = total + par_ref[tap : tap + 1, cols] * dconv[tap : tap + tokens, cols]
        dxb_ref[:, cols] = total.astype(BF16)

    pl.when(me > 0)(rows_copy.wait_send)

    def sent(place, carry):
        told(place).wait_send()
        return carry

    lax.fori_loop(0, me, sent, 0)
    core = lax.axis_index("ch")
    half = tokens // 2
    loads[1].wait()
    for start in range(0, model, size):
        cols = slice(start, start + size)
        part = (
            d_one_part[:, cols]
            + lax.dot_general(dxb_ref[...], w_in[cols], FLIPPED, preferred_element_type=F32)
        ).astype(BF16)
        d_one[0, :, cols] = part[:half]
        d_one[1, :, cols] = part[half:]
    exchange = pltpu.make_async_remote_copy(
        src_ref=d_one.at[1 - core],
        dst_ref=d_one_got,
        send_sem=send_m,
        recv_sem=recv_m,
        device_id={"ch": 1 - core},
        device_id_type=MESH,
    )
    exchange.start()
    exchange.wait_recv()

    def norm(at, total):
        r = pl.ds(pl.multiple_of(at * 16, 16), 16)
        x = x_ref[pl.ds(pl.multiple_of(core * half + at * 16, 16), 16)].astype(F32)
        scale = lax.rsqrt(jnp.mean(x * x, axis=-1, keepdims=True) + 1e-06)
        grad = d_one[core, r].astype(F32) + d_one_got[r].astype(F32)
        back = grad * gain_ref[...]
        shrink = scale * scale * scale * jnp.mean(x * back, axis=-1, keepdims=True)
        dx_ref[core, r] = resid_ref[r] + (scale * back - x * shrink)
        return total + jnp.sum(grad * (x * scale), axis=0, keepdims=True)

    dgain_ref[...] = lax.fori_loop(0, half // 16, norm, jnp.zeros((1, model), F32))
    share = pltpu.make_async_remote_copy(
        src_ref=dx_ref.at[core],
        dst_ref=dx_ref.at[core],
        send_sem=send_x,
        recv_sem=recv_x,
        device_id={"ch": 1 - core},
        device_id_type=MESH,
    )
    share.start()
    exchange.wait_send()
    for piece in range(3, len(hosted)):
        collect(piece)
    for copy in outs:
        copy.wait()
    pltpu.make_async_remote_copy(
        src_ref=dx_ref.at[core],
        dst_ref=dx_ref.at[1 - core],
        send_sem=send_x,
        recv_sem=recv_x,
        device_id={"ch": 1 - core},
        device_id_type=MESH,
    ).wait_recv()
    share.wait_send()


def mixer_backward(
    mixed, weights, x_half, gain, d_resid, y_pre, states, edge, conv, x_branch, gates, par, halves, own, hidden_units
):
    n = lax.axis_size("seq")
    tokens, width = x_branch.shape
    model = mixed.shape[1]
    size = gates.shape[2]
    half = tokens // 2
    _, kinds, part, rows, units = halves.shape
    dma = pltpu.SemaphoreType.DMA
    whole = pltpu.VMEM((tokens, width), F32)
    longer = pltpu.VMEM((tokens + 8, width), F32)
    weight = pltpu.VMEM((model, width), BF16)
    return pl.pallas_call(
        functools.partial(backward_body, n, hidden_units),
        out_shape=(
            jax.ShapeDtypeStruct((tokens, width), BF16),
            jax.ShapeDtypeStruct((tokens, width), BF16),
            jax.ShapeDtypeStruct((n, 2, size // n, width), BF16),
            jax.ShapeDtypeStruct((8, width), F32),
            jax.ShapeDtypeStruct((2, half, model), F32),
            jax.ShapeDtypeStruct((1, model), F32),
            jax.ShapeDtypeStruct((kinds, 2 * part, rows, units), BF16),
        ),
        in_specs=[VMEM] + [HBM] * 3 + [VMEM] * 10 + [HBM, HBM],
        out_specs=(VMEM,) * 6 + (HBM,),
        scratch_shapes=[
            pltpu.VMEM(halves.shape, BF16),
            pltpu.VMEM(halves.shape, BF16),
            weight,
            weight,
            weight,
            pltpu.VMEM((2, half, model), BF16),
            pltpu.VMEM((half, model), BF16),
            pltpu.VMEM((tokens, model), F32),
            longer,
            whole,
            whole,
            whole,
            whole,
            longer,
            longer,
            pltpu.VMEM((2, width), F32),
            pltpu.VMEM((n, 2, width), F32),
            pltpu.VMEM((8, width), F32),
            dma(()),
            dma(()),
            dma((n,)),
            dma((n,)),
            dma((kinds, part, 2)),
            dma((kinds, part, 2)),
            dma(()),
            dma(()),
            dma(()),
            dma(()),
            dma((3,)),
            dma(()),
            dma((kinds, part, 2)),
        ],
        compiler_params=params(5, 60),
        name="mixer_backward",
    )(mixed, *weights, x_half, gain, d_resid, y_pre, states, edge, conv, x_branch, gates, par, halves, own)


def ffn_body(n, hidden_units, *refs):
    own_ref, cots_ref, column_ref, near_ref, resid_ref, gain_ref = refs[:6]
    block_ref, d_resid_ref, mixed_ref, d_gain_ref, turned_ref = refs[6:11]
    halves_ref, mine_ref, far_ref = refs[11:14]
    tokens, cots, w, extra, hidden, box, sib, got, stage, turned, my_cot = refs[14:25]
    token_sems = refs[25:28]
    send_w, recv_w, keep_w, keep_c, keep_t, keep_m = refs[28:34]
    send_c, recv_s, send_z, recv_r, send_f, recv_f, send_m, recv_m, move, out_sem = refs[34:]
    groups = n // INNER
    half = groups // 2
    me, outer, by_x, by_y, by_xy = whereabouts()
    base = outer * INNER
    core = lax.axis_index("ch")
    above, below = outer + 1 < groups, outer > 0
    sibling = {"ch": 1 - core}
    barrier = pltpu.get_barrier_semaphore()

    def hello(peer):
        pl.semaphore_signal(barrier, inc=1, device_id=peer, device_id_type=MESH)

    hello({"seq": by_x})
    hello({"seq": by_y})
    hello(sibling)
    pl.when(above)(lambda: hello({"seq": me + INNER}))
    pl.when(below)(lambda: hello({"seq": me - INNER}))
    pl.semaphore_wait(barrier, 3 + above.astype(jnp.int32) + below.astype(jnp.int32))
    flips = ((by_x, by_y), (by_y, by_x))
    rows, units = w.shape[3], w.shape[4]
    split = Units(hidden_units, groups, core)
    tall, model = own_ref.shape
    count = 2 * tall
    deep = INNER * rows
    tile = 256

    def part(h):
        return pl.ds(h * half, half)


    chain_t = Chain(n, own_ref, tokens, *token_sems)

    def weight_copy(kind, h, far, receive=False):
        source = flips[h][0] if far else me
        if receive:
            source = by_xy if far else flips[h][1]
        src = near_ref.at[h, kind] if far else column_ref.at[kind, part(h)]
        return Sized(
            split,
            outer,
            lambda width: remote(
                src.at[:, :, pl.ds(0, width)],
                w.at[kind, part(h), source - base, :, pl.ds(0, width)],
                send_w.at[kind, h, far],
                recv_w.at[kind, h, far],
                flips[h][1],
            ),
        )

    keep = [
        [
            pltpu.make_async_copy(
                column_ref.at[kind], w.at[kind, :, me - base], keep_w.at[kind, 0]
            ),
            *(
                pltpu.make_async_copy(
                    near_ref.at[h, kind],
                    w.at[kind, part(h), flips[h][0] - base],
                    keep_w.at[kind, 1 + h],
                )
                for h in range(2)
            ),
        ]
        for kind in range(3)
    ]
    every = [(h, far) for far in range(2) for h in range(2)]
    own_t = chain_t.keep(keep_t)
    load_c = pltpu.make_async_copy(cots_ref, cots, keep_c)
    load_m = pltpu.make_async_copy(cots_ref.at[outer, core], my_cot, keep_m)
    chain_t.start()
    for kind in range(3):
        for h, far in every:
            weight_copy(kind, h, far).start()
    own_t.start()
    load_c.start()
    load_m.start()
    for kind in range(3):
        for copy in keep[kind]:
            copy.start()
    for step in range(1, groups):
        chain_t.step(step)
    chain_t.finish()
    own_t.wait()

    def weights_landed(kind):
        for h, far in every:
            weight_copy(kind, h, far, True).wait_recv()
        for copy in keep[kind]:
            copy.wait()
        if not split.even:

            @pl.when(jnp.logical_not(split.full(outer)))
            def _():
                rest = jnp.zeros((groups, INNER, rows, LANES), BF16)
                w[kind, :, :, :, units - LANES :] = rest

    def columns(kind, at):
        return w[kind, :, :, :, at : at + tile].reshape(model, tile)

    def token_rows(place):
        return pl.ds(pl.multiple_of(place * count, count), count)

    def each(limit, action):
        def one(turn, carry):
            action(turn)
            return carry

        lax.fori_loop(0, limit, one, 0)

    weights_landed(0)
    weights_landed(1)

    def middle(place):
        left = tokens[place].reshape(count, model)
        r = token_rows(place)
        for at in range(0, units, tile):
            c = slice(at, at + tile)
            gate = jnp.dot(left, columns(0, at), preferred_element_type=F32)
            up = jnp.dot(left, columns(1, at), preferred_element_type=F32)
            value, slope = gelu_parts(gate)
            hidden[0, r, c] = (value * up).astype(BF16)
            hidden[1, r, c] = (up * slope).astype(BF16)
            hidden[2, r, c] = value.astype(BF16)

    each(groups, middle)
    def back_hidden(place):
        left = cots[place].reshape(count, model)
        r = token_rows(place)
        for at in range(0, units, tile):
            c = slice(at, at + tile)
            back = jnp.dot(left, columns(2, at), preferred_element_type=F32)
            for kind in (1, 2):
                hidden[kind, r, c] = (back * hidden[kind, r, c].astype(F32)).astype(BF16)


    boxes = (cots, box)

    def partial(kind, place):
        r = token_rows(place)
        for at in range(groups):
            pairs = ((1, 0), (2, 1)) if kind == 0 else ((0, 2),)
            value = 0.0
            for left, right in pairs:
                value = value + lax.dot_general(
                    hidden[left, r],
                    w[right, at].reshape(deep, units),
                    FLIPPED,
                    preferred_element_type=F32,
                )
            value = value.astype(BF16)
            boxes[kind][place, 0, :, at * deep : (at + 1) * deep] = value[:tall]
            boxes[kind][place, 1, :, at * deep : (at + 1) * deep] = value[tall:]
        to_sibling(kind, place).start()

    def to_sibling(kind, place):
        return pltpu.make_async_remote_copy(
            src_ref=boxes[kind].at[place, 1 - core],
            dst_ref=sib.at[kind, place],
            send_sem=send_c.at[kind, place],
            recv_sem=recv_s.at[kind, place],
            device_id=sibling,
            device_id_type=MESH,
        )

    def along(kind, place, up):
        last = place == (outer + 1 if up else outer - 1)
        slot = place if up else jnp.where(last, groups, place)
        return remote(
            boxes[kind].at[place, core],
            got.at[kind, slot],
            send_z.at[kind, place],
            recv_r.at[kind, slot],
            me + (INNER if up else -INNER),
        )

    def landed(kind, slot):
        return remote(
            box.at[0, core], got.at[kind, slot], send_z.at[kind, 0], recv_r.at[kind, slot], by_x
        )

    chunk = 16

    def rows_of(at):
        return pl.ds(pl.multiple_of(at * chunk, chunk), chunk)

    def ready(kind, place, incoming):
        to_sibling(kind, place).wait_recv()

        def add(at, with_got):
            r = rows_of(at)
            value = boxes[kind][place, core, r].astype(F32) + sib[kind, place, r].astype(F32)
            if with_got:
                value = value + got[kind, place, r].astype(F32)
            boxes[kind][place, core, r] = value.astype(BF16)

        @pl.when(incoming)
        def _():
            landed(kind, place).wait_recv()
            each(tall // chunk, lambda at: add(at, True))

        @pl.when(jnp.logical_not(incoming))
        def _():
            each(tall // chunk, lambda at: add(at, False))

    def pass_on(kind, turn):
        ups = groups - 1 - outer
        upper = jnp.where(outer < half, turn < ups, turn >= outer)
        later = jnp.where(outer < half, turn, turn - outer)
        earlier = jnp.where(outer < half, turn - ups, turn)

        @pl.when(upper)
        def _():
            place = groups - 1 - later
            ready(kind, place, below)
            along(kind, place, True).start()

        @pl.when(jnp.logical_not(upper))
        def _():
            ready(kind, earlier, above)
            along(kind, earlier, False).start()

    at_end = jnp.logical_or(outer == 0, outer == groups - 1)

    def partials(kind, start, stop):
        def one(turn, carry):
            partial(kind, far_first(groups, outer, turn))

            @pl.when(jnp.logical_and(at_end, turn >= 1))
            def _():
                pass_on(kind, turn - 1)

            return carry

        lax.fori_loop(start, stop, one, 0)

    def between(kind, turns):
        @pl.when(jnp.logical_not(at_end))
        def _():
            for turn in turns:
                pass_on(kind, turn)

    def totals(kind, use):
        to_sibling(kind, outer).wait_recv()
        for condition, slots in (
            (jnp.logical_and(below, above), (outer, groups)),
            (jnp.logical_and(below, jnp.logical_not(above)), (outer,)),
            (jnp.logical_and(jnp.logical_not(below), above), (groups,)),
        ):

            @pl.when(condition)
            def _(slots=slots):
                for slot in slots:
                    landed(kind, slot).wait_recv()

                def one(at):
                    r = rows_of(at)
                    value = boxes[kind][outer, core, r].astype(F32) + sib[kind, outer, r].astype(F32)
                    for slot in slots:
                        value = value + got[kind, slot, r].astype(F32)
                    use(r, value)

                each(tall // chunk, one)

    def clear(kind):
        def one(place):
            to_sibling(kind, place).wait_send()

            @pl.when(place > outer)
            def _():
                along(kind, place, True).wait_send()

            @pl.when(place < outer)
            def _():
                along(kind, place, False).wait_send()

        each(groups, one)


    made = (w.at[0], w.at[1], extra)

    def gradient_copy(kind, h, far):
        source = by_xy if far else flips[h][1]
        return Sized(
            split,
            outer,
            lambda width: remote(
                made[kind].at[part(h), source - base, :, pl.ds(0, width)],
                far_ref.at[h, far, kind, :, :, pl.ds(0, width)],
                send_f.at[kind, h, far],
                recv_f.at[kind, h, far],
                flips[h][1],
            ),
        )

    def gradients(kinds, source, h):
        for at in range(h * half, (h + 1) * half):
            left = source[:, :, :, at * deep : (at + 1) * deep].reshape(groups * count, deep)
            turned[...] = left.T
            for kind, right in kinds:
                for start in range(0, units, tile):
                    c = slice(start, start + tile)
                    made[kind][at, :, :, c] = (
                        jnp.dot(turned[...], hidden[right, :, c], preferred_element_type=F32)
                        .astype(BF16)
                        .reshape(INNER, rows, tile)
                    )
        for kind, _ in kinds:
            for far in (1, 0):
                gradient_copy(kind, h, far).start()

    def collect(kind, h, far):
        inner = (flips[h][0] if far else me) - base
        gradient_copy(kind, h, far).wait_recv()
        load = pltpu.make_async_copy(far_ref.at[h, far, kind], stage, move)
        load.start()
        load.wait()
        for place in range(half):
            at = h * half + place

            def one(turn, place=place, at=at):
                r = rows_of(turn)
                made[kind][at, inner, r] = (
                    made[kind][at, inner, r].astype(F32) + stage[place, r].astype(F32)
                ).astype(BF16)

            each(rows // chunk, one)
        out_copy(kind, h, far).start()

    def out_copy(kind, h, far):
        inner = (flips[h][0] if far else me) - base
        return pltpu.make_async_copy(
            made[kind].at[part(h), inner],
            (halves_ref if far else mine_ref).at[h, kind],
            out_sem.at[kind, h, far],
        )

    load_c.wait()
    gradients(((2, 0),), cots, 0)
    gradients(((2, 0),), cots, 1)
    weights_landed(2)
    for kind in range(3):
        for h, far in every:
            weight_copy(kind, h, far).wait_send()
    partials(1, 0, groups)
    each(groups, back_hidden)
    load_m.wait()
    partials(0, 0, half)
    between(1, range(1))
    partials(0, half, groups)
    gradients(((0, 1),), tokens, 0)
    between(1, range(1, half))
    gradients(((0, 1),), tokens, 1)
    gradients(((1, 2),), tokens, 0)
    between(1, range(half, groups - 1))
    gradients(((1, 2),), tokens, 1)

    def shared(ref, at, part):
        return pltpu.make_async_remote_copy(
            src_ref=ref.at[core],
            dst_ref=ref.at[part],
            send_sem=send_m.at[at],
            recv_sem=recv_m.at[at],
            device_id=sibling,
            device_id_type=MESH,
        )

    def finish(r, value):
        block_ref[core, r] = (resid_ref[r] + value).astype(BF16)

    d_gain_ref[...] = jnp.zeros((1, model), F32)

    def norm(r, grad):
        resid = resid_ref[r]
        scale = lax.rsqrt(jnp.mean(resid * resid, axis=-1, keepdims=True) + 1e-06)
        back = grad * gain_ref[...]
        shrink = scale * scale * scale * jnp.mean(resid * back, axis=-1, keepdims=True)
        value = my_cot[r].astype(F32) + (scale * back - resid * shrink)
        d_resid_ref[r] = value
        mixed_ref[core, r] = value.astype(BF16)
        d_gain_ref[...] = d_gain_ref[...] + jnp.sum(grad * (resid * scale), axis=0, keepdims=True)

    for far in (1, 0):
        for h in range(2):
            collect(2, h, far)
    between(0, range(1))
    totals(1, finish)
    show = shared(block_ref, 1, core)
    show.start()
    for far in (1, 0):
        for h in range(2):
            collect(0, h, far)
    between(0, range(1, groups - 1))
    totals(0, norm)
    share = shared(mixed_ref, 0, core)
    share.start()
    shared(mixed_ref, 0, 1 - core).wait_recv()
    for start in range(0, model, tile):
        c = slice(start, start + tile)
        turned_ref[c, :tall] = mixed_ref[0, :, c].T
        turned_ref[c, tall:] = mixed_ref[1, :, c].T
    for far in (1, 0):
        for h in range(2):
            collect(1, h, far)
    clear(0)
    clear(1)
    shared(block_ref, 1, 1 - core).wait_recv()
    share.wait_send()
    show.wait_send()
    for kind in range(3):
        for h, far in every:
            gradient_copy(kind, h, far).wait_send()
            out_copy(kind, h, far).wait()


def feed_forward(own, cots, column, near, resid, gain, hidden_units):
    n = lax.axis_size("seq")
    groups = n // INNER
    tall, model = own.shape
    kinds, _, rows, units = column.shape
    half = groups // 2
    dma = pltpu.SemaphoreType.DMA
    part = jax.ShapeDtypeStruct((2, kinds, half, rows, units), BF16)
    return pl.pallas_call(
        functools.partial(ffn_body, n, hidden_units),
        out_shape=(
            jax.ShapeDtypeStruct((2, tall, model), BF16),
            jax.ShapeDtypeStruct((tall, model), F32),
            jax.ShapeDtypeStruct((2, tall, model), BF16),
            jax.ShapeDtypeStruct((1, model), F32),
            jax.ShapeDtypeStruct((model, 2 * tall), BF16),
            part,
            part,
            jax.ShapeDtypeStruct((2, 2, kinds, half, rows, units), BF16),
        ),
        in_specs=[HBM] * 4 + [VMEM] * 2,
        out_specs=(VMEM,) * 5 + (HBM,) * 3,
        scratch_shapes=[
            pltpu.VMEM((groups, 2, tall, model), BF16),
            pltpu.VMEM((groups, 2, tall, model), BF16),
            pltpu.VMEM((kinds, groups, INNER, rows, units), BF16),
            pltpu.VMEM((groups, INNER, rows, units), BF16),
            pltpu.VMEM((3, groups * 2 * tall, units), BF16),
            pltpu.VMEM((groups, 2, tall, model), BF16),
            pltpu.VMEM((2, groups, tall, model), BF16),
            pltpu.VMEM((2, groups + 1, tall, model), BF16),
            pltpu.VMEM((half, rows, units), BF16),
            pltpu.VMEM((INNER * rows, groups * 2 * tall), BF16),
            pltpu.VMEM((tall, model), BF16),
            *chain_semaphores(groups),
            dma((kinds, 2, 2)),
            dma((kinds, 2, 2)),
            dma((kinds, 3)),
            dma(()),
            dma(()),
            dma(()),
            dma((2, groups)),
            dma((2, groups)),
            dma((2, groups)),
            dma((2, groups + 1)),
            dma((kinds, 2, 2)),
            dma((kinds, 2, 2)),
            dma((2,)),
            dma((2,)),
            dma(()),
            dma((kinds, 2, 2)),
        ],
        compiler_params=params(8, 63),
        name="feed_forward",
    )(own, cots, column, near, resid, gain)


def my_half(values):
    half = values.shape[0] // 2
    return lax.dynamic_slice_in_dim(values, lax.axis_index("ch") * half, half, 0)


def join(own):
    other = swap(own, "ch", 1)
    core = lax.axis_index("ch")
    return jnp.concatenate(
        [jnp.where(core == 0, own, other), jnp.where(core == 0, other, own)], axis=0
    )


def tokens_out(partial, half):
    width = partial.shape[1]
    groups = lax.axis_size("seq") // INNER
    outer = lax.axis_index("seq") // INNER
    core = lax.axis_index("ch")
    parts = partial.reshape(groups, 2, half, width)
    theirs = pick(parts, 1 - core, 1).astype(BF16)
    summed = (pick(parts, core, 1).astype(F32) + swap(theirs, "ch", 1).astype(F32)).astype(BF16)
    total = pick(summed, outer).astype(F32)
    for step in range(1, groups):
        total = total + swap(pick(summed, outer ^ step), "seq", step * INNER).astype(F32)
    return total


def feed_forward_parts(n_two, cot_half, all_cot, column, near, resid, ffn_gain, hidden_units):
    f32, bf16 = F32, BF16
    _, groups, depth, units = column.shape
    half_rows, model = n_two.shape
    tok_rows = 2 * half_rows
    _, norm_back_two = jax.vjp(scaled_norm, resid, ffn_gain)
    all_two, *full_ffn = gather_tokens(n_two, column, near)
    all_two, all_cot = (v.reshape(groups * tok_rows, model) for v in (all_two, all_cot))
    own = Units(hidden_units, groups, lax.axis_index("ch")).width(lax.axis_index("seq") // INNER)
    valid = lax.broadcasted_iota(jnp.int32, (1, units), 1) < own
    full_ffn = [jnp.where(valid, w.reshape(model, units), 0) for w in full_ffn]
    gate_pre = jnp.dot(all_two, full_ffn[0], preferred_element_type=f32)
    up_pre = jnp.dot(all_two, full_ffn[1], preferred_element_type=f32)
    gate_act, gelu_back_gate = jax.vjp(gelu_tanh, gate_pre)
    hidden = (gate_act * up_pre).astype(bf16)
    ffn_term = jnp.einsum("tf,df->td", hidden, full_ffn[2], preferred_element_type=f32).astype(bf16)
    d_hidden = jnp.einsum("td,df->tf", all_cot, full_ffn[2], preferred_element_type=f32)
    d_gate = gelu_back_gate(d_hidden * up_pre)[0].astype(bf16)
    d_up = (d_hidden * gate_act).astype(bf16)
    d_n_two = (
        jnp.einsum("tf,df->td", d_gate, full_ffn[0], preferred_element_type=f32)
        + jnp.einsum("tf,df->td", d_up, full_ffn[1], preferred_element_type=f32)
    ).astype(bf16)
    terms = [
        jnp.einsum("td,tf->df", left, right, preferred_element_type=f32)
        .astype(bf16)
        .reshape(groups, INNER, depth, units)
        for left, right in ((all_two, d_gate), (all_two, d_up), (all_cot, hidden))
    ]
    split = [v.reshape(groups, 2, half_rows, model) for v in (d_n_two, ffn_term)]
    if groups <= 4:
        d_n_two, ffn_out, far = reduce_tokens(split, terms)
    else:
        d_n_two, far = reduce_tokens(split[:1], terms)
        ffn_out = tokens_out(ffn_term, half_rows)
    block_out = join((resid + ffn_out).astype(bf16))
    inner = lax.axis_index("seq") % INNER
    by_half = [t.reshape(2, groups // 2, INNER, depth, units) for t in terms]

    def block_at(h, place):
        return jnp.stack([pick(t[h], place, 1) for t in by_half]).astype(f32)

    mine = jnp.stack(
        [(block_at(h, inner) + far[h, 0].astype(f32)).astype(bf16) for h in range(2)]
    )
    halves = jnp.stack(
        [(block_at(h, inner ^ (1, 2)[h]) + far[h, 1].astype(f32)).astype(bf16) for h in range(2)]
    )
    d_resid_norm, d_ffn_gain_term = norm_back_two(d_n_two)
    d_resid = cot_half.astype(f32) + d_resid_norm
    d_mixed = join(d_resid.astype(bf16))
    return block_out, d_resid, d_mixed, d_ffn_gain_term.reshape(1, model), halves, mine


def shards(
    inputs,
    norm_gain,
    branch_weight,
    input_weight,
    channel_params,
    gate_x_blocks,
    gate_a_blocks,
    out_weight,
    ffn_gain,
    ffn_gate,
    ffn_up,
    ffn_down,
    cotangent,
):
    f32 = F32
    bf16 = BF16
    n = lax.axis_size("seq")
    tok_rows, model = inputs.shape
    half_rows = tok_rows // 2
    heads, part, size = gate_x_blocks.shape
    width = heads * size
    depth = ffn_gate.shape[0]
    groups = n // INNER
    hidden_units = ffn_gate.shape[1]
    par = jnp.concatenate(
        [
            channel_params,
            jax.nn.softplus(channel_params[7:8]),
            jax.nn.sigmoid(channel_params[7:8]),
            jnp.zeros((6, width), f32),
        ],
        axis=0,
    )
    mixer_set = [input_weight, branch_weight, out_weight.T]
    gate_set = [gate_x_blocks, gate_a_blocks]
    ffn_set = [ffn_gate, ffn_up, ffn_down.T]
    gains = jnp.stack([norm_gain, ffn_gain])
    gain_one, gain_two = gains[:1], gains[1:]
    if depth % 16 == 0 and part % 16 == 0:
        made = gather_forward(
            mixer_set, gate_set, ffn_set, inputs, gains, par, cotangent
        )
        *full_mixer, full_gates, column, n_one, n_one_turned, _ = made[:8]
        full_mixer = [w.reshape(model, width) for w in full_mixer]
        gates = full_gates.reshape(2, heads, size, size)
        made = made[8:]
    else:
        cot_half = my_half(cotangent)
        *full_mixer, full_gates, column, n_one, n_one_turned, last_rows = gather_weights(
            mixer_set, gate_set, ffn_set, inputs, gain_one
        )
        full_mixer = [w.reshape(model, width) for w in full_mixer]
        gates = full_gates.reshape(2, heads, size, size)
        made = mixer_forward(
            n_one,
            last_rows,
            full_mixer,
            gates,
            par,
            my_half(inputs),
            gain_two,
            column,
            cot_half,
            hidden_units,
        )
    x_branch, y_pre, conv_out, states, branch_out, edge, resid, n_two, near, cots = made
    if groups <= 4 and depth % 16 == 0:
        block_out, d_resid, d_mixed, d_ffn_gain_term, d_mixed_turned, halves, mine, _ = feed_forward(
            n_two, cots, column, near, resid, gain_two, hidden_units
        )
        block_out = block_out.reshape(tok_rows, model)
        d_mixed = d_mixed.reshape(tok_rows, model)
    else:
        block_out, d_resid, d_mixed, d_ffn_gain_term, halves, mine = feed_forward_parts(
            n_two, cot_half, cots, column, near, resid, ffn_gain, hidden_units
        )
        d_mixed_turned = d_mixed.T
    d_y, d_xb, d_gates, d_par, d_inputs, d_norm_gain_term, column_back = mixer_backward(
        d_mixed,
        full_mixer,
        inputs,
        gain_one,
        d_resid,
        y_pre,
        states,
        edge,
        conv_out,
        x_branch,
        gates,
        par,
        halves,
        mine,
        hidden_units,
    )
    d_inputs = d_inputs.reshape(tok_rows, model)
    gain_rows = model // width
    scattered, small, spread = scatter_mixer(
        n_one_turned.reshape(n, depth, tok_rows),
        d_mixed_turned.reshape(n, depth, tok_rows),
        d_y,
        d_xb,
        branch_out,
        d_gates,
        d_par,
        d_norm_gain_term,
        d_ffn_gain_term,
        column_back,
        hidden_units,
    )
    ffn_grads = [spread[kind].astype(f32) for kind in range(3)]
    d_gate_pair = scattered[3 * depth :].reshape(2, part, heads, size).transpose(0, 2, 1, 3)
    return (
        block_out,
        d_inputs,
        small[8 : 8 + gain_rows].reshape(model),
        scattered[:depth],
        scattered[depth : 2 * depth],
        small[:8],
        d_gate_pair[0],
        d_gate_pair[1],
        scattered[2 * depth : 3 * depth].T,
        small[8 + gain_rows : 8 + 2 * gain_rows].reshape(model),
        ffn_grads[0],
        ffn_grads[1],
        ffn_grads[2].T,
    )


def solution(mesh):
    placed = (
        P("seq", None),
        P(),
        P("seq", "ch"),
        P("seq", "ch"),
        P(None, "ch"),
        P("ch", "seq", None),
        P("ch", "seq", None),
        P("ch", "seq"),
        P(),
        P("seq", "ch"),
        P("seq", "ch"),
        P("ch", "seq"),
        P("seq", None),
    )
    return jax.shard_map(
        shards,
        mesh=mesh,
        in_specs=placed,
        out_specs=(
            P("seq", None),
            P("seq", None),
            P(),
            P("seq", "ch"),
            P("seq", "ch"),
            P(None, "ch"),
            P("ch", "seq", None),
            P("ch", "seq", None),
            P("ch", "seq"),
            P(),
            P("seq", "ch"),
            P("seq", "ch"),
            P("ch", "seq"),
        ),
        check_vma=False,
    )
```

```python
import functools

import jax
import jax.numpy as jnp
from jax import lax
from jax.experimental import pallas as pl
from jax.experimental.pallas import tpu as pltpu
from jax.sharding import PartitionSpec as P

F32 = jnp.float32
BF16 = jnp.bfloat16
INNER = 4
MESH = pl.DeviceIdType.MESH
VMEM = pl.BlockSpec(memory_space=pltpu.VMEM)
ANY = pl.BlockSpec(memory_space=pl.ANY)
HBM = pl.BlockSpec(memory_space=pltpu.HBM)


def swap(value, axis, mask):
    return lax.ppermute(value, axis, [(i, i ^ mask) for i in range(lax.axis_size(axis))])


def pick(array, index, axis=0):
    return lax.dynamic_index_in_dim(array, index, axis, False)


def scaled_norm(values, gain):
    return values * lax.rsqrt(jnp.mean(values * values, axis=-1, keepdims=True) + 1e-06) * gain


def gelu_tanh(values):
    return jax.nn.gelu(values, approximate=True)


def whereabouts():
    me = lax.axis_index("seq")
    outer = me // INNER
    inner = me - outer * INNER
    y = inner // 2
    x = inner - 2 * y
    by_x = me + 1 - 2 * x
    by_y = me + 2 - 4 * y
    return me, outer, by_x, by_y, by_x + 2 - 4 * y


def when(condition, action):
    if condition is None:
        action()
    else:
        pl.when(condition)(action)


def both(one, other):
    if one is None or other is None:
        return one if other is None else other
    return jnp.logical_and(one, other)


def greet(peers):
    barrier = pltpu.get_barrier_semaphore()
    for condition, peer in peers:
        when(
            condition,
            lambda peer=peer: pl.semaphore_signal(
                barrier, inc=1, device_id={"seq": peer}, device_id_type=MESH
            ),
        )
    count = 0
    for condition, _ in peers:
        count = count + (1 if condition is None else condition.astype(jnp.int32))
    pl.semaphore_wait(barrier, count)


def greet_all(n, me, sibling=False):
    barrier = pltpu.get_barrier_semaphore()

    def hello(step, carry):
        pl.semaphore_signal(
            barrier, inc=1, device_id={"seq": lax.rem(me + step, n)}, device_id_type=MESH
        )
        return carry

    lax.fori_loop(1, n, hello, 0)
    if sibling:
        pl.semaphore_signal(
            barrier, inc=1, device_id={"ch": 1 - lax.axis_index("ch")}, device_id_type=MESH
        )
    pl.semaphore_wait(barrier, n if sibling else n - 1)


def remote(src, dst, send_sem, recv_sem, place):
    return pltpu.make_async_remote_copy(
        src_ref=src,
        dst_ref=dst,
        send_sem=send_sem,
        recv_sem=recv_sem,
        device_id={"seq": place},
        device_id_type=MESH,
    )


def params(collective_id, mib):
    return pltpu.CompilerParams(
        collective_id=collective_id, has_side_effects=True, vmem_limit_bytes=mib * 2**20
    )


def gather_begin(n, refs, greeted):
    w_refs, g_refs, f_refs, x_ref, gain_ref = refs[:3], refs[3:5], refs[5:8], refs[8], refs[9]
    wo_refs, go_ref, column_ref, one_ref, turned_ref, last_ref = refs[10:13], *refs[13:18]
    send_m, recv_m, send_f, recv_f, here, send_l, recv_l = refs[18:]
    groups = n // INNER
    me, outer, by_x, by_y, by_xy = whereabouts()
    above, below = outer + 1 < groups, outer > 0
    def column_peer(turn):
        return lax.rem(outer + turn, groups)

    if not greeted:
        barrier = pltpu.get_barrier_semaphore()

        def hello(peer):
            pl.semaphore_signal(barrier, inc=1, device_id={"seq": peer}, device_id_type=MESH)

        hello(by_x)
        hello(by_y)

        def hello_column(turn, carry):
            hello(me + (column_peer(turn) - outer) * INNER)
            return carry

        lax.fori_loop(1, groups, hello_column, 0)
        pl.when(me + 1 < n)(lambda: hello(me + 1))
        pl.when(me > 0)(lambda: hello(me - 1))
        neighbours = (me + 1 < n).astype(jnp.int32) + (me > 0).astype(jnp.int32)
        pl.semaphore_wait(barrier, groups + 1 + neighbours)
    units = Units(f_refs[0].shape[1], groups, lax.axis_index("ch"))
    half = w_refs[0].shape[1] // 2

    keep = [
        pltpu.make_async_copy(w_refs[kind], wo_refs[kind].at[me], here.at[kind])
        for kind in range(3)
    ]
    for gate in range(2):
        keep.append(pltpu.make_async_copy(g_refs[gate], go_ref.at[gate, :, me], here.at[3 + gate]))
    for kind in range(3):
        keep.append(
            Sized(
                units,
                outer,
                lambda width, kind=kind: pltpu.make_async_copy(
                    f_refs[kind].at[:, units.columns(outer, width)],
                    column_ref.at[kind, outer, :, pl.ds(0, width)],
                    here.at[5 + kind],
                ),
            )
        )
    for copy in keep:
        copy.start()
    sent = []

    def copies(h, source, way, target, own, kinds=range(4)):
        cols = pl.ds(h * half, half)
        pairs = [
            (w_refs[kind].at[:, cols], wo_refs[kind].at[source, :, cols]) for kind in range(3)
        ]
        pairs.append((g_refs[h], go_ref.at[h, :, source]))
        return [
            remote(
                given if own else dst,
                dst,
                send_m.at[kind, h, source, way],
                recv_m.at[kind, h, source],
                target,
            )
            for kind, (given, dst) in ((at, pairs[at]) for at in (3, 0, 1, 2))
            if kind in kinds
        ]

    def send(condition, *what):
        def go():
            for copy in copies(*what):
                copy.start()

        when(condition, go)
        sent.append((condition, what))

    def arrive(condition, h, source, kinds=range(4)):
        def go():
            for copy in copies(h, source, 0, by_x, False, kinds):
                copy.wait_recv()

        when(condition, go)

    def exchange(turn, receive):
        place = lax.rem(outer + groups - turn, groups) if receive else column_peer(turn)
        owner = outer if receive else place
        return [
            Sized(
                units,
                owner,
                lambda width, kind=kind: remote(
                    f_refs[kind].at[:, units.columns(owner, width)],
                    column_ref.at[kind, place if receive else outer, :, pl.ds(0, width)],
                    send_f.at[kind, turn],
                    recv_f.at[kind, turn],
                    me + (place - outer) * INNER,
                ),
            )
            for kind in range(3)
        ]

    def each_turn(action):
        def one(turn, carry):
            action(turn)
            return carry

        lax.fori_loop(1, groups, one, 0)

    tokens, model = x_ref.shape
    tall = last_ref.shape[0]
    last_copy = remote(one_ref.at[pl.ds(tokens - tall, tall)], last_ref, send_l, recv_l, me + 1)

    def norm(at, carry):
        r = pl.ds(pl.multiple_of(at * 16, 16), 16)
        x = x_ref[r].astype(F32)
        scale = lax.rsqrt(jnp.mean(x * x, axis=-1, keepdims=True) + 1e-06)
        one_ref[r] = (x * scale * gain_ref[...]).astype(BF16)
        return carry

    def norm_all():
        lax.fori_loop(0, tokens // 16, norm, 0)
        pl.when(me + 1 < n)(last_copy.start)
        for start in range(0, model, 256):
            cols = slice(start, start + 256)
            turned_ref[cols] = one_ref[:, cols].T

        @pl.when(me == 0)
        def _():
            last_ref[...] = jnp.zeros(last_ref.shape, BF16)

    for step in range(groups):
        if step == 1:
            norm_all()
        for h in range(2):
            flip_p, flip_q = (by_x, by_y) if h == 0 else (by_y, by_x)
            if step == 0:
                send(above, h, me, 0, me + INNER, True)
                send(below, h, me, 1, me - INNER, True)
                send(None, h, me, 2, flip_p, True)
                send(None, h, me, 3, flip_q, True)
                continue
            for source, there, onward, way, to in (
                (me - step * INNER, outer >= step, above, 0, me + INNER),
                (me + step * INNER, outer + step < groups, below, 1, me - INNER),
            ):
                arrive(there, h, source)
                send(both(there, onward), h, source, way, to, False)
                send(there, h, source, 2, flip_p, False)
                send(there, h, source, 3, flip_q, False)
    each_turn(lambda turn: [copy.start() for copy in exchange(turn, False)])
    for step in range(groups):
        for h in range(2):
            flip_p, flip_q = (by_x, by_y) if h == 0 else (by_y, by_x)
            if step == 0:
                arrive(None, h, flip_p)
                send(None, h, flip_p, 3, flip_q, False)
                continue
            for source, there in (
                (flip_p - step * INNER, outer >= step),
                (flip_p + step * INNER, outer + step < groups),
            ):
                arrive(there, h, source)
                send(there, h, source, 3, flip_q, False)

    def last(kind):
        for place in range(groups):
            shift = (place - outer) * INNER
            for h in range(2):
                arrive(None, h, (by_y if h == 0 else by_x) + shift, (kind,))
                arrive(None, h, by_xy + shift, (kind,))
        for copy in keep[kind : kind + 1] if kind < 3 else keep[3:5]:
            copy.wait()

    def columns():
        each_turn(lambda turn: [copy.wait_recv() for copy in exchange(turn, True)])
        for copy in keep[5:]:
            copy.wait()

    def rows_before():
        pl.when(me > 0)(last_copy.wait_recv)

    def finish():
        for condition, what in sent:

            def done(what=what):
                for copy in copies(*what):
                    copy.wait_send()

            when(condition, done)
        each_turn(lambda turn: [copy.wait_send() for copy in exchange(turn, False)])
        pl.when(me + 1 < n)(last_copy.wait_send)

    return last, columns, rows_before, finish


def gather_body(n, *refs):
    last, columns, rows_before, finish = gather_begin(n, refs, False)
    for kind in range(4):
        last(kind)
    columns()
    rows_before()
    finish()


def gather_weights(weights, gates, ffn, x, gain):
    n = lax.axis_size("seq")
    groups = n // INNER
    rows, hidden_units = ffn[0].shape
    most = Units(hidden_units, groups, 0).most
    dma = pltpu.SemaphoreType.DMA
    made = [jax.ShapeDtypeStruct((n,) + w.shape, w.dtype) for w in weights]
    heads, part, size = gates[0].shape
    made.append(jax.ShapeDtypeStruct((2, heads, n, part, size), BF16))
    made.append(jax.ShapeDtypeStruct((3, groups, rows, most), BF16))
    made.append(jax.ShapeDtypeStruct(x.shape, BF16))
    made.append(jax.ShapeDtypeStruct(x.shape[::-1], BF16))
    made.append(jax.ShapeDtypeStruct((16, x.shape[1]), BF16))
    return pl.pallas_call(
        functools.partial(gather_body, n),
        out_shape=tuple(made),
        in_specs=[HBM] * 8 + [VMEM] * 2,
        out_specs=(HBM,) * 5 + (VMEM,) * 3,
        scratch_shapes=[
            dma((4, 2, n, 4)),
            dma((4, 2, n)),
            dma((3, groups)),
            dma((3, groups)),
            dma((8,)),
            dma(()),
            dma(()),
        ],
        compiler_params=params(1, 60),
        name="gather_weights",
    )(*weights, *gates, *ffn, x, gain)


LANES = 128


class Units:
    def __init__(self, total, groups, core):
        self.tiles, self.groups, self.core = total // LANES, groups, core
        self.most = -(-self.tiles // groups) * LANES
        self.even = self.tiles % groups == 0

    def start(self, place):
        up = (1 - self.core) * (self.groups - 1)
        return (place * self.tiles + up) // self.groups

    def full(self, place):
        return (self.start(place + 1) - self.start(place)) * LANES == self.most

    def width(self, place):
        return (self.start(place + 1) - self.start(place)) * LANES

    def columns(self, place, width):
        return pl.ds(pl.multiple_of(self.start(place) * LANES, LANES), width)


class Sized:
    def __init__(self, units, place, make):
        self.units, self.place, self.make = units, place, make

    def each(self, action):
        most = self.units.most
        if self.units.even:
            action(self.make(most))
            return
        full = self.units.full(self.place)
        pl.when(full)(lambda: action(self.make(most)))
        pl.when(jnp.logical_not(full))(lambda: action(self.make(most - LANES)))

    def start(self):
        self.each(lambda copy: copy.start())

    def wait(self):
        self.each(lambda copy: copy.wait())

    def wait_send(self):
        self.each(lambda copy: copy.wait_send())

    def wait_recv(self):
        self.each(lambda copy: copy.wait_recv())


def far_first(groups, outer, turn):
    def order(at):
        alone = groups - 1 - 2 * at
        later = turn - alone
        step = later // 2
        return jnp.where(
            turn < alone, groups - 1 - turn, jnp.where(later - 2 * step == 0, step, 2 * at - step)
        )

    return jnp.where(
        outer < groups // 2, order(outer), groups - 1 - order(groups - 1 - outer)
    )


class Chain:
    def __init__(self, n, own, whole, send, recv_z, recv_c):
        me = lax.axis_index("seq")
        self.groups = n // INNER
        self.outer = outer = me // INNER
        self.core = lax.axis_index("ch")
        self.above, self.below = outer + 1 < self.groups, outer > 0
        self.sibling = {"ch": 1 - self.core}
        self.to = ({"seq": me + INNER}, {"seq": me - INNER}, self.sibling)
        self.own, self.whole = own, whole
        self.send, self.recv_z, self.recv_c = send, recv_z, recv_c

    def copy(self, source, way, own=False):
        dst = self.whole.at[source, self.core]
        return pltpu.make_async_remote_copy(
            src_ref=self.own if own else dst,
            dst_ref=dst,
            send_sem=self.send.at[source, way],
            recv_sem=(self.recv_c if way == 2 else self.recv_z).at[source],
            device_id=self.to[way],
            device_id_type=MESH,
        )

    def from_sibling(self, source):
        return pltpu.make_async_remote_copy(
            src_ref=self.own,
            dst_ref=self.whole.at[source, 1 - self.core],
            send_sem=self.send.at[source, 2],
            recv_sem=self.recv_c.at[source],
            device_id=self.sibling,
            device_id_type=MESH,
        )

    def keep(self, sem):
        return pltpu.make_async_copy(self.own, self.whole.at[self.outer, self.core], sem)

    def ways(self, step):
        return (
            (self.outer - step, self.outer >= step, self.above, 0),
            (self.outer + step, self.outer + step < self.groups, self.below, 1),
        )

    def start(self):
        pl.when(self.above)(self.copy(self.outer, 0, True).start)
        pl.when(self.below)(self.copy(self.outer, 1, True).start)
        self.copy(self.outer, 2, True).start()

    def step(self, step):
        for source, there, onward, way in self.ways(step):
            pl.when(there)(lambda: self.copy(source, way).wait_recv())
            pl.when(both(there, onward))(lambda: self.copy(source, way).start())
            pl.when(there)(lambda: self.copy(source, 2).start())

    def finish(self):
        for source in range(self.groups):
            self.from_sibling(source).wait_recv()
        pl.when(self.above)(self.copy(self.outer, 0, True).wait_send)
        pl.when(self.below)(self.copy(self.outer, 1, True).wait_send)
        self.copy(self.outer, 2, True).wait_send()
        for step in range(1, self.groups):
            for source, there, onward, way in self.ways(step):
                pl.when(both(there, onward))(lambda: self.copy(source, way).wait_send())
                pl.when(there)(lambda: self.copy(source, 2).wait_send())


def chain_semaphores(groups):
    dma = pltpu.SemaphoreType.DMA
    return [dma((groups, 3)), dma((groups,)), dma((groups,))]


def tokens_body(n, *refs):
    own_ref, column_ref, near_ref = refs[:3]
    all_ref, w_refs = refs[3], refs[4:7]
    send_t, recv_z, recv_c, send_w, recv_w, here = refs[7:]
    groups = n // INNER
    half = groups // 2
    me, outer, by_x, by_y, by_xy = whereabouts()
    base = outer * INNER
    core = lax.axis_index("ch")
    above, below = outer + 1 < groups, outer > 0
    sibling = {"ch": 1 - core}
    barrier = pltpu.get_barrier_semaphore()

    def hello(peer):
        pl.semaphore_signal(barrier, inc=1, device_id=peer, device_id_type=MESH)

    hello({"seq": by_x})
    hello({"seq": by_y})
    hello(sibling)
    pl.when(above)(lambda: hello({"seq": me + INNER}))
    pl.when(below)(lambda: hello({"seq": me - INNER}))
    pl.semaphore_wait(barrier, 3 + above.astype(jnp.int32) + below.astype(jnp.int32))

    chain = Chain(n, own_ref, all_ref, send_t, recv_z, recv_c)

    def part(h):
        return pl.ds(h * half, half)

    flips = ((by_x, by_y), (by_y, by_x))

    def weight_copy(kind, h, far, receive=False):
        source = flips[h][0] if far else me
        if receive:
            source = by_xy if far else flips[h][1]
        return remote(
            near_ref.at[h, kind] if far else column_ref.at[kind, part(h)],
            w_refs[kind].at[part(h), source - base],
            send_w.at[kind, h, far],
            recv_w.at[kind, h, far],
            flips[h][1],
        )

    keep = [chain.keep(here.at[0])]
    for kind in range(3):
        keep.append(
            pltpu.make_async_copy(
                column_ref.at[kind], w_refs[kind].at[:, me - base], here.at[1 + kind]
            )
        )
        for h in range(2):
            keep.append(
                pltpu.make_async_copy(
                    near_ref.at[h, kind],
                    w_refs[kind].at[part(h), flips[h][0] - base],
                    here.at[4 + 2 * kind + h],
                )
            )
    every_w = [(kind, h, far) for kind in range(3) for h in range(2) for far in range(2)]

    chain.start()
    for what in every_w:
        weight_copy(*what).start()
    for copy in keep:
        copy.start()
    for step in range(1, groups):
        chain.step(step)
    for what in every_w:
        weight_copy(*what, receive=True).wait_recv()
    chain.finish()
    for what in every_w:
        weight_copy(*what).wait_send()
    for copy in keep:
        copy.wait()


def gather_tokens(tokens, column, near):
    n = lax.axis_size("seq")
    groups = n // INNER
    kinds, _, rows, units = column.shape
    dma = pltpu.SemaphoreType.DMA
    wide = jax.ShapeDtypeStruct((groups, 2) + tokens.shape, tokens.dtype)
    weight = jax.ShapeDtypeStruct((groups, INNER, rows, units), column.dtype)
    return pl.pallas_call(
        functools.partial(tokens_body, n),
        out_shape=(wide, weight, weight, weight),
        in_specs=[ANY] * 3,
        out_specs=(ANY,) * 4,
        scratch_shapes=chain_semaphores(groups)
        + [dma((kinds, 2, 2)), dma((kinds, 2, 2)), dma((10,))],
        compiler_params=params(6, 16),
        name="gather_tokens",
    )(tokens, column, near)


def reduce_body(n, kinds, *refs):
    p_refs, t_refs = refs[:kinds], refs[kinds : kinds + 3]
    out_refs, far_ref = refs[kinds + 3 : 2 * kinds + 3], refs[2 * kinds + 3]
    summed, got, send_c, recv_c, send_z, recv_z, send_f, recv_f = refs[2 * kinds + 4 :]
    groups = n // INNER
    half = groups // 2
    me, outer, by_x, by_y, by_xy = whereabouts()
    base = outer * INNER
    core = lax.axis_index("ch")
    above, below = outer + 1 < groups, outer > 0
    sibling = {"ch": 1 - core}
    barrier = pltpu.get_barrier_semaphore()

    def hello(peer):
        pl.semaphore_signal(barrier, inc=1, device_id=peer, device_id_type=MESH)

    hello({"seq": by_x})
    hello({"seq": by_y})
    hello(sibling)
    pl.when(above)(lambda: hello({"seq": me + INNER}))
    pl.when(below)(lambda: hello({"seq": me - INNER}))
    pl.semaphore_wait(barrier, 3 + above.astype(jnp.int32) + below.astype(jnp.int32))
    flips = ((by_x, by_y), (by_y, by_x))

    def gradient_copy(kind, h, far):
        source = by_xy if far else flips[h][1]
        return remote(
            t_refs[kind].at[pl.ds(h * half, half), source - base],
            far_ref.at[h, far, kind],
            send_f.at[kind, h, far],
            recv_f.at[kind, h, far],
            flips[h][1],
        )

    def to_sibling(kind, place):
        return pltpu.make_async_remote_copy(
            src_ref=p_refs[kind].at[place, 1 - core],
            dst_ref=summed.at[kind, place],
            send_sem=send_c.at[kind, place],
            recv_sem=recv_c.at[kind, place],
            device_id=sibling,
            device_id_type=MESH,
        )

    def along(kind, place, up):
        last = place == (outer + 1 if up else outer - 1)
        slot = place if up else jnp.where(last, groups, place)
        return remote(
            summed.at[kind, place],
            got.at[kind, slot],
            send_z.at[kind, place],
            recv_z.at[kind, slot],
            me + (INNER if up else -INNER),
        )

    def landed(kind, slot):
        return remote(
            summed.at[kind, 0], got.at[kind, slot], send_z.at[kind, 0], recv_z.at[kind, slot], by_x
        )

    def each(limit, action):
        def one(turn, carry):
            action(turn)
            return carry

        lax.fori_loop(0, limit, one, 0)

    every_f = [(kind, h, far) for far in (1, 0) for kind in range(3) for h in range(2)]
    for kind in range(kinds):
        each(groups, lambda place, kind=kind: to_sibling(kind, place).start())
    for what in every_f:
        gradient_copy(*what).start()

    tall = summed.shape[2]
    chunk = 16

    def rows_of(at):
        return pl.ds(pl.multiple_of(at * chunk, chunk), chunk)

    def ready(kind, place, incoming):
        to_sibling(kind, place).wait_recv()

        def local(at):
            r = rows_of(at)
            summed[kind, place, r] = (
                summed[kind, place, r].astype(F32) + p_refs[kind][place, core, r].astype(F32)
            ).astype(BF16)

        def more(at):
            r = rows_of(at)
            summed[kind, place, r] = (
                summed[kind, place, r].astype(F32)
                + p_refs[kind][place, core, r].astype(F32)
                + got[kind, place, r].astype(F32)
            ).astype(BF16)

        @pl.when(incoming)
        def _():
            landed(kind, place).wait_recv()
            each(tall // chunk, more)

        @pl.when(jnp.logical_not(incoming))
        def _():
            each(tall // chunk, local)

    for kind in range(kinds):

        def climb(turn, kind=kind):
            place = groups - 1 - turn

            @pl.when(place > outer)
            def _():
                ready(kind, place, below)
                along(kind, place, True).start()

        def sink(turn, kind=kind):
            place = turn

            @pl.when(place < outer)
            def _():
                ready(kind, place, above)
                along(kind, place, False).start()

        def turns(turn):
            @pl.when(outer < half)
            def _():
                climb(turn)
                sink(turn)

            @pl.when(outer >= half)
            def _():
                sink(turn)
                climb(turn)

        each(groups - 1, turns)
    for kind in range(kinds):
        to_sibling(kind, outer).wait_recv()

        def own(at, kind=kind):
            r = rows_of(at)
            out_refs[kind][r] = summed[kind, outer, r].astype(F32) + p_refs[kind][
                outer, core, r
            ].astype(F32)

        each(tall // chunk, own)
        for there, slot in ((below, outer), (above, groups)):

            @pl.when(there)
            def _():
                landed(kind, slot).wait_recv()

                def plus(at):
                    r = rows_of(at)
                    out_refs[kind][r] = out_refs[kind][r] + got[kind, slot, r].astype(F32)

                each(tall // chunk, plus)

    for kind in range(kinds):

        def clear(place, kind=kind):
            to_sibling(kind, place).wait_send()

            @pl.when(place > outer)
            def _():
                along(kind, place, True).wait_send()

            @pl.when(place < outer)
            def _():
                along(kind, place, False).wait_send()

        each(groups, clear)
    for what in every_f:
        gradient_copy(*what).wait()


def reduce_tokens(partials, gradients):
    n = lax.axis_size("seq")
    groups = n // INNER
    kinds = len(partials)
    _, _, tall, width = partials[0].shape
    _, _, rows, units = gradients[0].shape
    dma = pltpu.SemaphoreType.DMA
    return pl.pallas_call(
        functools.partial(reduce_body, n, kinds),
        out_shape=(jax.ShapeDtypeStruct((tall, width), F32),) * kinds
        + (jax.ShapeDtypeStruct((2, 2, 3, groups // 2, rows, units), BF16),),
        in_specs=[VMEM] * kinds + [ANY] * 3,
        out_specs=(VMEM,) * kinds + (ANY,),
        scratch_shapes=[
            pltpu.VMEM((kinds, groups, tall, width), BF16),
            pltpu.VMEM((kinds, groups + 1, tall, width), BF16),
            dma((kinds, groups)),
            dma((kinds, groups)),
            dma((kinds, groups)),
            dma((kinds, groups + 1)),
            dma((3, 2, 2)),
            dma((3, 2, 2)),
        ],
        compiler_params=params(7, 60),
        name="reduce_tokens",
    )(*partials, *gradients)


def scatter_body(
    n,
    one_ref,
    mixed_ref,
    dy_ref,
    dxb_ref,
    branch_ref,
    gate_ref,
    dpar_ref,
    gain_one_ref,
    gain_two_ref,
    column_ref,
    out_ref,
    small_out,
    spread_ref,
    made,
    got_q,
    got_p,
    got_z,
    got_s,
    *sems,
):
    send_q, recv_q, send_p, recv_p, send_z, recv_z, send_s, recv_s, send_f, recv_f, here = sems
    groups = n // INNER
    me, outer, by_x, by_y, by_xy = whereabouts()
    rows = one_ref.shape[1]
    part_rows = gate_ref.shape[2]
    total, width = out_ref.shape
    half = width // 2

    def place_of(turn):
        return far_first(groups, outer, turn)

    def base_of(turn):
        return (place_of(turn) - outer) * INNER

    barrier = pltpu.get_barrier_semaphore()

    def hello(peer):
        pl.semaphore_signal(barrier, inc=1, device_id={"seq": peer}, device_id_type=MESH)

    hello(by_x)
    hello(by_y)

    def hello_outer(turn, carry):
        hello(me + base_of(turn))
        return carry

    lax.fori_loop(0, groups - 1, hello_outer, 0)
    core = lax.axis_index("ch")
    masks = [1 << bit for bit in range(n.bit_length() - 1)]
    pl.semaphore_signal(barrier, inc=1, device_id={"ch": 1 - core}, device_id_type=MESH)
    pl.semaphore_wait(barrier, groups + 2)

    flips = ((by_x, by_y), (by_y, by_x))
    units = Units(spread_ref.shape[2], groups, core)

    def exchange(turn, receive=False):
        place = lax.rem(outer + (groups - 1 - turn if receive else turn + 1), groups)
        owner = place if receive else outer
        return Sized(
            units,
            owner,
            lambda width: remote(
                column_ref.at[:, place, :, pl.ds(0, width)],
                spread_ref.at[:, :, units.columns(owner, width)],
                send_f.at[turn],
                recv_f.at[turn],
                me + (place - outer) * INNER,
            ),
        )

    def small(turn):
        place = me
        for at, mask in enumerate(masks):
            flipped = me + mask * (1 - 2 * lax.rem(me // mask, 2))
            place = jnp.where(turn == at, flipped, place)
        other = jnp.where(turn == len(masks), 1 - core, core)
        return pltpu.make_async_remote_copy(
            src_ref=small_out,
            dst_ref=got_s.at[turn],
            send_sem=send_s.at[turn],
            recv_sem=recv_s.at[turn],
            device_id=(place, other),
            device_id_type=MESH,
        )

    small_out[:8] = dpar_ref[...]
    small_out[8:] = jnp.zeros((8, width), F32)
    at = 8
    for gain_ref in (gain_one_ref, gain_two_ref):
        for start in range(0, gain_ref.shape[1], width):
            small_out[at : at + 1] = gain_ref[:, start : start + width]
            at += 1
    small_row = lax.broadcasted_iota(jnp.int32, small_out.shape, 0)

    def cols(h):
        return pl.ds(h * half, half)

    def along_q(turn, h, other):
        source = (by_xy if other else flips[h][1]) + base_of(turn)
        return remote(
            made.at[source, :, cols(h)],
            got_q.at[h, turn, other],
            send_q.at[h, turn, other],
            recv_q.at[h, turn, other],
            flips[h][1],
        )

    def along_p(turn, h):
        return remote(
            made.at[flips[h][0] + base_of(turn), :, cols(h)],
            got_p.at[h, turn],
            send_p.at[h, turn],
            recv_p.at[h, turn],
            flips[h][0],
        )

    def along_z(turn, h):
        place = place_of(turn)
        up = place > outer
        onto = jnp.where(up, outer + 1, outer - 1)
        slot = jnp.where(jnp.logical_and(place == onto, jnp.logical_not(up)), groups, place)
        return remote(
            made.at[me + base_of(turn), :, cols(h)],
            got_z.at[h, slot],
            send_z.at[h, turn],
            recv_z.at[h, slot],
            me + (onto - outer) * INNER,
        )

    def landed(slot, h):
        return remote(
            made.at[me, :, cols(h)], got_z.at[h, slot], send_z.at[h, 0], recv_z.at[h, slot], by_x
        )

    def has_incoming(turn):
        return jnp.where(place_of(turn) > outer, outer > 0, outer < groups - 1)

    def pass_on(turn):
        incoming = has_incoming(turn)
        for h in range(2):

            @pl.when(incoming)
            def _():
                landed(place_of(turn), h).wait_recv()
                add(me + base_of(turn), h, got_z, (h, place_of(turn)))

            along_z(turn, h).start()

    def make(block):
        left = one_ref[block]
        parts = [
            jnp.dot(left, dy_ref[...], preferred_element_type=F32),
            jnp.dot(left, dxb_ref[...], preferred_element_type=F32),
            jnp.dot(mixed_ref[block], branch_ref[...], preferred_element_type=F32),
        ]
        if rows % 16 == 0:
            for at, part in enumerate(parts):
                made[block, at * rows : (at + 1) * rows] = part.astype(BF16)
            for gate in range(2):
                at = 3 * rows + gate * part_rows
                made[block, at : at + part_rows] = gate_ref[block, gate]
        else:
            parts.extend(gate_ref[block, gate].astype(F32) for gate in range(2))
            made[block] = jnp.concatenate(parts, axis=0).astype(BF16)

    step = 32

    def add(block, h, ref, index):
        def one(at, carry):
            r = pl.ds(pl.multiple_of(at * step, step), step)
            made[block, r, cols(h)] = (
                made[block, r, cols(h)].astype(F32) + ref[index + (r,)].astype(F32)
            ).astype(BF16)
            return carry

        lax.fori_loop(0, total // step, one, 0)

    keep = Sized(
        units,
        outer,
        lambda width: pltpu.make_async_copy(
            column_ref.at[:, outer, :, pl.ds(0, width)],
            spread_ref.at[:, :, units.columns(outer, width)],
            here,
        ),
    )
    keep.start()

    def begin(turn, other):
        base = base_of(turn)
        if other:
            make(by_xy + base)
        else:
            for h in range(2):
                make(flips[h][1] + base)
        for h in range(2):
            along_q(turn, h, other).start()

    begin(0, 1)
    begin(0, 0)
    make(me + base_of(0))

    def turn_of(turn, carry):
        pl.when(turn <= len(masks))(lambda: small(turn).start())
        pl.when(turn < groups - 1)(lambda: exchange(turn).start())

        @pl.when(turn < groups)
        def _():
            base = base_of(turn)
            for h in range(2):
                along_q(turn, h, 1).wait_recv()
                add(flips[h][0] + base, h, got_q, (h, turn, 1))
                along_p(turn, h).start()
            pl.when(turn < groups - 1)(lambda: begin(turn + 1, 1))
            for h in range(2):
                along_q(turn, h, 0).wait_recv()
                add(me + base, h, got_q, (h, turn, 0))

            @pl.when(turn < groups - 1)
            def _():
                begin(turn + 1, 0)
                make(me + base_of(turn + 1))

            for h in range(2):
                along_p(turn, h).wait_recv()
                add(me + base, h, got_p, (h, turn))

            @pl.when(jnp.logical_and(turn < groups - 1, jnp.logical_not(has_incoming(turn))))
            def _():
                pass_on(turn)

            @pl.when(jnp.logical_and(turn >= 1, turn < groups - 1))
            def _():
                pl.when(has_incoming(turn - 1))(lambda: pass_on(turn - 1))

            @pl.when(jnp.logical_and(turn == groups - 2, has_incoming(turn)))
            def _():
                pass_on(turn)

        @pl.when(turn <= len(masks))
        def _():
            small(turn).wait()
            counts = jnp.logical_or(turn < len(masks), small_row >= 8)
            small_out[...] = small_out[...] + jnp.where(counts, got_s[turn], 0.0)

        return carry

    assert len(masks) < groups + 2
    lax.fori_loop(0, groups + 2, turn_of, 0)
    for condition, slots in (
        (jnp.logical_and(outer > 0, outer < groups - 1), (outer, groups)),
        (outer == groups - 1, (outer,)),
        (outer == 0, (groups,)),
    ):

        @pl.when(condition)
        def _(slots=slots):
            for h in range(2):
                for slot in slots:
                    landed(slot, h).wait_recv()

                def finish(at, carry):
                    r = pl.ds(pl.multiple_of(at * step, step), step)
                    value = made[me, r, cols(h)].astype(F32)
                    for slot in slots:
                        value = value + got_z[h, slot, r].astype(F32)
                    out_ref[r, cols(h)] = value
                    return carry

                lax.fori_loop(0, total // step, finish, 0)

    def clear(turn, carry):
        for h in range(2):
            along_q(turn, h, 0).wait_send()
            along_q(turn, h, 1).wait_send()
            along_p(turn, h).wait_send()

            @pl.when(turn < groups - 1)
            def _():
                along_z(turn, h).wait_send()

        @pl.when(turn < groups - 1)
        def _():
            exchange(turn, True).wait_recv()
            exchange(turn).wait_send()

        return carry

    lax.fori_loop(0, groups, clear, 0)
    keep.wait()


def scatter_mixer(one, mixed, dy, dxb, branch, gates, dpar, gain_one, gain_two, column, hidden_units):
    n, rows, _ = one.shape
    groups = n // INNER
    width = dy.shape[1]
    total = 3 * rows + 2 * gates.shape[2]
    kinds = column.shape[0]
    turns = n.bit_length()
    dma = pltpu.SemaphoreType.DMA
    return pl.pallas_call(
        functools.partial(scatter_body, n),
        out_shape=(
            jax.ShapeDtypeStruct((total, width), F32),
            jax.ShapeDtypeStruct((16, width), F32),
            jax.ShapeDtypeStruct((kinds, rows, hidden_units), BF16),
        ),
        in_specs=[VMEM] * 9 + [ANY],
        out_specs=(VMEM, VMEM, ANY),
        scratch_shapes=[
            pltpu.VMEM((n, total, width), BF16),
            pltpu.VMEM((2, groups, 2, total, width // 2), BF16),
            pltpu.VMEM((2, groups, total, width // 2), BF16),
            pltpu.VMEM((2, groups + 1, total, width // 2), BF16),
            pltpu.VMEM((turns, 16, width), F32),
            dma((2, groups, 2)),
            dma((2, groups, 2)),
            dma((2, groups)),
            dma((2, groups)),
            dma((2, groups)),
            dma((2, groups + 1)),
            dma((turns,)),
            dma((turns,)),
            dma((groups,)),
            dma((groups,)),
            dma(()),
        ],
        compiler_params=params(2, 62),
        name="scatter_mixer",
    )(one, mixed, dy, dxb, branch, gates, dpar, gain_one, gain_two, column)


GELU_A = 0.7978845608028654
GELU_B = 0.044715


def gelu_parts(v):
    t = jnp.tanh(GELU_A * (v + GELU_B * v * v * v))
    value = 0.5 * v * (1.0 + t)
    slope = 0.5 * (1.0 + t) + 0.5 * v * (1.0 - t * t) * GELU_A * (1.0 + 3.0 * GELU_B * v * v)
    return value, slope


def gates_of(conv_low, gate_ref, par_ref, head, cols, first):
    size = gate_ref.shape[-1]
    weight_x, weight_a = (gate_ref[gate, head].reshape(size, size) for gate in range(2))
    pre_x = jnp.dot(conv_low, weight_x, preferred_element_type=F32)
    pre_a = jnp.dot(conv_low, weight_a, preferred_element_type=F32)
    gate_x = jax.nn.sigmoid(pre_x + par_ref[5:6, cols])
    gate_a = jax.nn.sigmoid(pre_a + par_ref[6:7, cols])
    decay = jnp.exp(-8.0 * gate_a * par_ref[8:9, cols])
    room = 1.0 - decay * decay
    mult = jnp.where(first, 1.0, jnp.sqrt(jnp.maximum(room, 0.001)))
    return gate_x, gate_a, decay, room, mult


FLIPPED = (((1,), (1,)), ((), ()))


def by_columns(ref, cols):
    if len(ref.shape) == 2:
        return ref[:, cols]
    return ref[:, :, cols].reshape(ref.shape[0] * ref.shape[1], -1)


def by_rows(ref, start, size):
    if len(ref.shape) == 2:
        return ref[start : start + size]
    rows = ref.shape[1]
    parts, at = [], start
    while at < start + size:
        block, inside = divmod(at, rows)
        upto = min(rows, inside + start + size - at)
        parts.append(ref[block, inside:upto])
        at += upto - inside
    return jnp.concatenate(parts, axis=0)


def first_row(tokens):
    row = lax.broadcasted_iota(jnp.int32, (tokens, 1), 0)
    return jnp.logical_and(row == 0, lax.axis_index("seq") == 0)


def forward_body(
    n,
    hidden_units,
    gathered,
    one_ref,
    last_ref,
    w_in_ref,
    w_branch_ref,
    w_out_ref,
    gate_ref,
    par_ref,
    x_ref,
    gain_ref,
    column_ref,
    cot_ref,
    xb_ref,
    yp_ref,
    conv_ref,
    state_ref,
    branch_ref,
    edge_ref,
    resid_ref,
    two_ref,
    near_ref,
    cots_ref,
    w_in,
    w_branch,
    w_out,
    mixed,
    mixed_got,
    wide,
    fade,
    mine,
    theirs,
    *sems,
):
    send_tot, recv_tot, send_f, recv_f, send_m, recv_m, loaded, kept = sems[:8]
    tokens, width = xb_ref.shape
    model = one_ref.shape[1]
    me = lax.axis_index("seq")
    size = gate_ref.shape[-1]
    loads = [
        pltpu.make_async_copy(src, dst, loaded.at[at])
        for at, (src, dst) in enumerate(
            ((w_in_ref, w_in), (w_branch_ref, w_branch), (w_out_ref, w_out))
        )
    ]
    core = lax.axis_index("ch")
    half = tokens // 2
    if gathered is None:
        for load in loads:
            load.start()
        greet_all(n, me, True)
        x_start = 0
    else:
        last, columns, rows_before, gather_finish, gates_load = gathered
        last(0)
        loads[0].start()
        last(3)
        gates_load.start()
        rows_before()
        columns()
        x_start = core * half
    _, _, by_x, by_y, _ = whereabouts()
    part = column_ref.shape[1] // 2
    kinds = column_ref.shape[0]
    units = Units(hidden_units, n // INNER, lax.axis_index("ch"))
    outer = me // INNER
    hosted = [
        [
            Sized(
                units,
                outer,
                lambda width, kind=kind, h=h, part=part: remote(
                    column_ref.at[kind, pl.ds(h * part, part), :, pl.ds(0, width)],
                    near_ref.at[h, kind, :, :, pl.ds(0, width)],
                    send_f.at[kind, h],
                    recv_f.at[kind, h],
                    (by_x, by_y)[h],
                ),
            )
            for h in range(2)
        ]
        for kind in range(kinds)
    ]

    def host(pieces):
        for pair in pieces:
            for copy in pair:
                copy.start()

    chain = Chain(n, cot_ref, cots_ref, *sems[8:])
    keep = chain.keep(kept)
    chain.start()
    keep.start()
    host(hosted[:1])
    loads[0].wait()
    for start in range(0, width, size):
        cols = slice(start, start + size)
        low = jnp.dot(one_ref[...], by_columns(w_in, cols), preferred_element_type=F32).astype(BF16)
        xb_ref[:, cols] = low
        wide[8:, cols] = low.astype(F32)
        low = jnp.dot(last_ref[...], by_columns(w_in, cols), preferred_element_type=F32).astype(BF16)
        wide[:8, cols] = low.astype(F32)[8:]

    def branch():
        loads[1].wait()
        for start in range(0, width, size):
            cols = slice(start, start + size)
            yp_ref[:, cols] = jnp.dot(
                one_ref[...], by_columns(w_branch, cols), preferred_element_type=F32
            )

    if gathered is None:
        branch()
    else:
        gates_load.wait()
    edge_ref[:8] = wide[:8]
    first = first_row(tokens)
    for head in range(width // size):
        cols = slice(head * size, (head + 1) * size)
        conv = par_ref[4:5, cols]
        for tap in range(4):
            conv = conv + par_ref[tap : tap + 1, cols] * wide[8 - tap : 8 - tap + tokens, cols]
        conv_low = conv.astype(BF16)
        conv_ref[:, cols] = conv_low
        gate_x, _, decay, _, mult = gates_of(conv_low, gate_ref, par_ref, head, cols, first)
        fade[:, cols] = decay
        state_ref[:, cols] = conv_low.astype(F32) * gate_x * mult

    row = lax.broadcasted_iota(jnp.int32, (8, width), 0)

    def inside(at, carry):
        r = pl.ds(pl.multiple_of(at * 8, 8), 8)
        a, b = fade[r], state_ref[r]
        for by in (1, 2, 4):
            a_back = pltpu.roll(a, by, 0)
            b_back = pltpu.roll(b, by, 0)
            b = jnp.where(row >= by, a * b_back + b, b)
            a = jnp.where(row >= by, a * a_back, a)
        fade[r] = a
        state_ref[r] = b
        return a[7:8] * carry[0], a[7:8] * carry[1] + b[7:8]

    ones, zeros = jnp.ones((1, width), F32), jnp.zeros((1, width), F32)
    tot_a, tot_b = lax.fori_loop(0, tokens // 8, inside, (ones, zeros))
    mine[0:1] = tot_a
    mine[1:2] = tot_b

    def told(place):
        return remote(mine, theirs.at[me], send_tot.at[place], recv_tot.at[me], place)

    def heard(place):
        return remote(mine, theirs.at[place], send_tot.at[place], recv_tot.at[place], place)

    def tell(place, carry):
        told(place).start()
        return carry

    lax.fori_loop(me + 1, n, tell, 0)
    host(hosted[1:])
    if gathered is not None:
        last(1)
        loads[1].start()
        last(2)
        loads[2].start()
        branch()

    def hear(place, carry):
        heard(place).wait_recv()
        return carry

    lax.fori_loop(0, me, hear, 0)
    carry_in = zeros
    for place in range(n):
        gone = place < me
        through = jnp.where(gone, theirs[place, 0:1], 1.0)
        carry_in = through * carry_in + jnp.where(gone, theirs[place, 1:2], 0.0)
    edge_ref[8:] = jnp.broadcast_to(carry_in, (8, width))
    chain.step(1)

    def finish(at, carry):
        r = pl.ds(pl.multiple_of(at * 16, 16), 16)
        a, b = fade[r], state_ref[r]
        top = b[:8] + a[:8] * carry
        low = b[8:] + a[8:] * top[7:8]
        states = jnp.concatenate([top, low], axis=0)
        state_ref[r] = states
        branch_ref[r] = (states * gelu_parts(yp_ref[r])[0]).astype(BF16)
        return low[7:8]

    lax.fori_loop(0, tokens // 16, finish, carry_in)

    def sent(place, carry):
        told(place).wait_send()
        return carry

    lax.fori_loop(me + 1, n, sent, 0)
    loads[2].wait()
    for start in range(0, model, size):
        cols = slice(start, start + size)
        part = lax.dot_general(branch_ref[...], by_rows(w_out, start, size), FLIPPED, preferred_element_type=F32)
        mixed[0, :, cols] = part[:half]
        mixed[1, :, cols] = part[half:]
    exchange = pltpu.make_async_remote_copy(
        src_ref=mixed.at[1 - core],
        dst_ref=mixed_got,
        send_sem=send_m,
        recv_sem=recv_m,
        device_id={"ch": 1 - core},
        device_id_type=MESH,
    )
    exchange.start()
    exchange.wait_recv()

    def norm(at, carry):
        r = pl.ds(pl.multiple_of(at * 16, 16), 16)
        x = x_ref[pl.ds(pl.multiple_of(x_start + at * 16, 16), 16)]
        resid = x.astype(F32) + (mixed[core, r] + mixed_got[r])
        resid_ref[r] = resid
        scale = lax.rsqrt(jnp.mean(resid * resid, axis=-1, keepdims=True) + 1e-06)
        two_ref[r] = (resid * scale * gain_ref[...]).astype(BF16)
        return carry

    lax.fori_loop(0, half // 16, norm, 0)
    exchange.wait_send()
    for step in range(2, n // INNER):
        chain.step(step)
    for pair in hosted:
        for copy in pair:
            copy.wait()
    chain.finish()
    keep.wait()
    if gathered is not None:
        gather_finish()


def first_body(n, hidden_units, *refs):
    given, refs = refs[:12], refs[12:]
    weights, gates, ffn, (x_ref, gains_ref, par_ref, all_cot_ref) = (
        given[:3],
        given[3:5],
        given[5:8],
        given[8:],
    )
    outs, refs = refs[:18], refs[18:]
    scratch, sems = refs[:10], refs[10:]
    gather_sems, forward_sems, gate_sem = sems[:7], sems[7:-1], sems[-1]
    me = lax.axis_index("seq")
    norm_ref, gain_ref = gains_ref.at[pl.ds(0, 1)], gains_ref.at[pl.ds(1, 1)]
    half = x_ref.shape[0] // 2
    start = pl.multiple_of(lax.axis_index("ch") * half, half)
    cot_ref = all_cot_ref.at[pl.ds(start, half)]
    greet_all(n, me, True)
    steps = gather_begin(
        n, (*weights, *gates, *ffn, x_ref, norm_ref, *outs[:8], *gather_sems), True
    )
    gate_s, scratch = scratch[0], scratch[1:]
    full_gates, column_ref, one_ref, _, last_ref = outs[3:8]
    gates_load = pltpu.make_async_copy(full_gates, gate_s, gate_sem)
    forward_body(
        n,
        hidden_units,
        (*steps, gates_load),
        one_ref,
        last_ref,
        *outs[:3],
        gate_s,
        par_ref,
        x_ref,
        gain_ref,
        column_ref,
        cot_ref,
        *outs[8:],
        *scratch,
        *forward_sems,
    )


def mixer_forward(one, last, weights, gates, par, x_half, gain, column, cotangent, hidden_units):
    n = lax.axis_size("seq")
    tokens, model = one.shape
    width = par.shape[1]
    half = tokens // 2
    kinds, groups, rows, units = column.shape
    dma = pltpu.SemaphoreType.DMA
    whole = jax.ShapeDtypeStruct((tokens, width), F32)
    low = jax.ShapeDtypeStruct((tokens, width), BF16)
    return pl.pallas_call(
        functools.partial(forward_body, n, hidden_units, None),
        out_shape=(
            low,
            whole,
            low,
            whole,
            low,
            jax.ShapeDtypeStruct((16, width), F32),
            jax.ShapeDtypeStruct((half, model), F32),
            jax.ShapeDtypeStruct((half, model), BF16),
            jax.ShapeDtypeStruct((2, kinds, groups // 2, rows, units), column.dtype),
            jax.ShapeDtypeStruct((groups, 2) + cotangent.shape, cotangent.dtype),
        ),
        in_specs=[VMEM] * 2 + [HBM] * 3 + [VMEM] * 4 + [HBM, HBM],
        out_specs=(VMEM,) * 8 + (HBM, HBM),
        scratch_shapes=[
            pltpu.VMEM((model, width), BF16),
            pltpu.VMEM((model, width), BF16),
            pltpu.VMEM((model, width), BF16),
            pltpu.VMEM((2, half, model), F32),
            pltpu.VMEM((half, model), F32),
            pltpu.VMEM((tokens + 8, width), F32),
            pltpu.VMEM((tokens, width), F32),
            pltpu.VMEM((2, width), F32),
            pltpu.VMEM((n, 2, width), F32),
            dma((n,)),
            dma((n,)),
            dma((kinds, 2)),
            dma((kinds, 2)),
            dma(()),
            dma(()),
            dma((3,)),
            dma(()),
            *chain_semaphores(groups),
        ],
        compiler_params=params(4, 60),
        name="mixer_forward",
    )(one, last, *weights, gates, par, x_half, gain, column, cotangent)


def gather_forward(weights, gates, ffn, x, gains, par, cotangent):
    n = lax.axis_size("seq")
    groups = n // INNER
    tokens, model = x.shape
    rows, width = weights[0].shape
    half = tokens // 2
    hidden_units = ffn[0].shape[1]
    most = Units(hidden_units, groups, 0).most
    heads, part, size = gates[0].shape
    dma = pltpu.SemaphoreType.DMA
    shape = jax.ShapeDtypeStruct
    whole, low = shape((tokens, width), F32), shape((tokens, width), BF16)
    weight = pltpu.VMEM((n, rows, width), BF16)
    return pl.pallas_call(
        functools.partial(first_body, n, hidden_units),
        out_shape=(
            *(shape((n, rows, width), BF16) for _ in range(3)),
            shape((2, heads, n, part, size), BF16),
            shape((3, groups, rows, most), BF16),
            shape((tokens, model), BF16),
            shape((model, tokens), BF16),
            shape((16, model), BF16),
            low,
            whole,
            low,
            whole,
            low,
            shape((16, width), F32),
            shape((half, model), F32),
            shape((half, model), BF16),
            shape((2, 3, groups // 2, rows, most), BF16),
            shape((groups, 2, half, model), BF16),
        ),
        in_specs=[HBM] * 8 + [VMEM] * 3 + [HBM],
        out_specs=(HBM,) * 5 + (VMEM,) * 11 + (HBM,) * 2,
        scratch_shapes=[
            pltpu.VMEM((2, heads, n, part, size), BF16),
            weight,
            weight,
            weight,
            pltpu.VMEM((2, half, model), F32),
            pltpu.VMEM((half, model), F32),
            pltpu.VMEM((tokens + 8, width), F32),
            pltpu.VMEM((tokens, width), F32),
            pltpu.VMEM((2, width), F32),
            pltpu.VMEM((n, 2, width), F32),
            dma((4, 2, n, 4)),
            dma((4, 2, n)),
            dma((3, groups)),
            dma((3, groups)),
            dma((8,)),
            dma(()),
            dma(()),
            dma((n,)),
            dma((n,)),
            dma((3, 2)),
            dma((3, 2)),
            dma(()),
            dma(()),
            dma((3,)),
            dma(()),
            *chain_semaphores(groups),
            dma(()),
        ],
        compiler_params=params(9, 60),
        name="gather_forward",
    )(*weights, *gates, *ffn, x, gains, par, cotangent)


def backward_body(
    n,
    hidden_units,
    mixed_ref,
    w_in_ref,
    w_branch_ref,
    w_out_ref,
    x_ref,
    gain_ref,
    resid_ref,
    yp_ref,
    state_ref,
    edge_ref,
    conv_ref,
    xb_ref,
    gate_ref,
    par_ref,
    half_ref,
    own_ref,
    dy_ref,
    dxb_ref,
    dgate_ref,
    dpar_ref,
    dx_ref,
    dgain_ref,
    column_ref,
    near_ref,
    own,
    w_in,
    w_branch,
    w_out,
    d_one,
    d_one_got,
    d_one_part,
    fade,
    shift,
    adj,
    gate_x_s,
    gate_a_s,
    dconv,
    wide,
    mine,
    theirs,
    head_rows,
    *sems,
):
    send_rows, recv_rows, send_tot, recv_tot, send_f, recv_f, send_m, recv_m, send_x, recv_x, loaded, own_sem, out_sem = sems
    tokens, width = xb_ref.shape
    model = gain_ref.shape[1]
    me = lax.axis_index("seq")
    size = gate_ref.shape[2]
    loads = [
        pltpu.make_async_copy(src, dst, loaded.at[at])
        for at, (src, dst) in enumerate(
            ((w_out_ref, w_out), (w_in_ref, w_in), (w_branch_ref, w_branch))
        )
    ]
    for load in loads:
        load.start()
    greet_all(n, me, True)
    _, _, by_x, by_y, _ = whereabouts()
    kinds, pieces = half_ref.shape[1:3]
    units = Units(hidden_units, n // INNER, lax.axis_index("ch"))
    outer = me // INNER
    hosted = [
        [
            Sized(
                units,
                outer,
                lambda width, kind=kind, at=at, h=h: remote(
                    half_ref.at[h, kind, at, :, pl.ds(0, width)],
                    near_ref.at[h, kind, at, :, pl.ds(0, width)],
                    send_f.at[kind, at, h],
                    recv_f.at[kind, at, h],
                    (by_x, by_y)[h],
                ),
            )
            for h in range(2)
        ]
        for kind in range(kinds)
        for at in range(pieces)
    ]

    def host(some):
        for pair in some:
            for copy in pair:
                copy.start()

    host(hosted[:2])
    own_load = pltpu.make_async_copy(own_ref, own, own_sem)
    own_load.start()
    first = first_row(tokens)
    fade[tokens:] = jnp.ones((8, width), F32)
    loads[0].wait()
    for head in range(width // size):
        cols = slice(head * size, (head + 1) * size)
        gate_x, gate_a, decay, _, _ = gates_of(conv_ref[:, cols], gate_ref, par_ref, head, cols, first)
        gate_x_s[:, cols] = gate_x
        gate_a_s[:, cols] = gate_a
        fade[:tokens, cols] = decay
        value, slope = gelu_parts(yp_ref[:, cols])
        grad = jnp.dot(mixed_ref[...], w_out[:, cols], preferred_element_type=F32)
        dy_ref[:, cols] = (grad * state_ref[:, cols] * slope).astype(BF16)
        adj[:, cols] = grad * value
        shift[:, cols] = fade[1 : tokens + 1, cols]

    row = lax.broadcasted_iota(jnp.int32, (8, width), 0)
    tiles = tokens // 8

    def inside(turn, carry):
        r = pl.ds(pl.multiple_of((tiles - 1 - turn) * 8, 8), 8)
        a, b = shift[r], adj[r]
        for by in (1, 2, 4):
            a_next = pltpu.roll(a, 8 - by, 0)
            b_next = pltpu.roll(b, 8 - by, 0)
            b = jnp.where(row < 8 - by, a * b_next + b, b)
            a = jnp.where(row < 8 - by, a * a_next, a)
        shift[r] = a
        adj[r] = b
        return a[0:1] * carry[0], a[0:1] * carry[1] + b[0:1]

    ones, zeros = jnp.ones((1, width), F32), jnp.zeros((1, width), F32)
    tot_a, tot_b = lax.fori_loop(0, tiles, inside, (ones, zeros))
    first_fade = fade[0:1]
    mine[0:1] = first_fade * tot_a
    mine[1:2] = first_fade * tot_b

    def told(place):
        return remote(mine, theirs.at[me], send_tot.at[place], recv_tot.at[me], place)

    def heard(place):
        return remote(mine, theirs.at[place], send_tot.at[place], recv_tot.at[place], place)

    def tell(place, carry):
        told(place).start()
        return carry

    lax.fori_loop(0, me, tell, 0)
    host(hosted[2:3])

    def hear(turn, carry):
        heard(n - 1 - turn).wait_recv()
        return carry

    lax.fori_loop(0, n - 1 - me, hear, 0)
    carry_in = zeros
    for place in reversed(range(n)):
        gone = place > me
        through = jnp.where(gone, theirs[place, 0:1], 1.0)
        carry_in = through * carry_in + jnp.where(gone, theirs[place, 1:2], 0.0)

    def finish(turn, carry):
        r = pl.ds(pl.multiple_of((tiles - 1 - turn) * 8, 8), 8)
        value = adj[r] + shift[r] * carry
        adj[r] = value
        return value[0:1]

    lax.fori_loop(0, tiles, finish, carry_in)

    wide[:8] = edge_ref[:8]
    wide[8:] = xb_ref[...].astype(F32)
    at_first = lax.broadcasted_iota(jnp.int32, (tokens, 1), 0) == 0
    for head in range(width // size):
        cols = slice(head * size, (head + 1) * size)
        conv_low = conv_ref[:, cols]
        conv = conv_low.astype(F32)
        gate_x, gate_a, decay = gate_x_s[:, cols], gate_a_s[:, cols], fade[:tokens, cols]
        room = 1.0 - decay * decay
        mult = jnp.where(first, 1.0, jnp.sqrt(jnp.maximum(room, 0.001)))
        back = adj[:, cols]
        before = jnp.where(at_first, edge_ref[8:9, cols], pltpu.roll(state_ref[:, cols], 1, 0))
        d_mult = back * conv * gate_x
        moves = jnp.logical_and(room > 0.001, jnp.logical_not(first))
        d_decay = back * before - jnp.where(moves, d_mult * decay / mult, 0.0)
        d_log = d_decay * decay
        d_pre_x = back * conv * mult * gate_x * (1.0 - gate_x)
        d_pre_a = d_log * (-8.0 * par_ref[8:9, cols]) * gate_a * (1.0 - gate_a)
        dpar_ref[5:6, cols] = jnp.sum(d_pre_x, axis=0, keepdims=True)
        dpar_ref[6:7, cols] = jnp.sum(d_pre_a, axis=0, keepdims=True)
        dpar_ref[7:8, cols] = (
            jnp.sum(d_log * (-8.0 * gate_a), axis=0, keepdims=True) * par_ref[9:10, cols]
        )
        low_x, low_a = d_pre_x.astype(BF16), d_pre_a.astype(BF16)
        d_conv = (
            back * gate_x * mult
            + lax.dot_general(low_x, gate_ref[0, head], FLIPPED, preferred_element_type=F32)
            + lax.dot_general(low_a, gate_ref[1, head], FLIPPED, preferred_element_type=F32)
        )
        dconv[:tokens, cols] = d_conv
        over_rows = (((0,), (0,)), ((), ()))
        for gate, low in enumerate((low_x, low_a)):
            d_gate = lax.dot_general(conv_low, low, over_rows, preferred_element_type=F32)
            dgate_ref[:, gate, :, cols] = d_gate.astype(BF16).reshape(n, size // n, size)
        dpar_ref[4:5, cols] = jnp.sum(d_conv, axis=0, keepdims=True)
        for tap in range(4):
            dpar_ref[tap : tap + 1, cols] = jnp.sum(
                d_conv * wide[8 - tap : 8 - tap + tokens, cols], axis=0, keepdims=True
            )

    rows_copy = remote(
        dconv.at[pl.ds(0, 8)], head_rows, send_rows, recv_rows, lax.rem(me + n - 1, n)
    )
    pl.when(me > 0)(rows_copy.start)
    host(hosted[3:])
    loads[2].wait()
    for start in range(0, model, size):
        cols = slice(start, start + size)
        d_one_part[:, cols] = lax.dot_general(
            dy_ref[...], w_branch[cols], FLIPPED, preferred_element_type=F32
        )

    rows = own.shape[3]
    chunk = 32 if rows % 32 == 0 else rows
    outs = []

    def collect(piece):
        kind, at = divmod(piece, pieces)
        for h in range(2):
            hosted[piece][h].wait()

            def add(turn, carry, h=h):
                r = pl.ds(pl.multiple_of(turn * chunk, chunk), chunk)
                own[h, kind, at, r] = (
                    own[h, kind, at, r].astype(F32) + near_ref[h, kind, at, r].astype(F32)
                ).astype(BF16)
                return carry

            lax.fori_loop(0, rows // chunk, add, 0)
            outs.append(
                pltpu.make_async_copy(
                    own.at[h, kind, at],
                    column_ref.at[kind, h * pieces + at],
                    out_sem.at[kind, at, h],
                )
            )
            outs[-1].start()

    own_load.wait()
    for piece in range(3):
        collect(piece)

    @pl.when(me + 1 < n)
    def _():
        rows_copy.wait_recv()
        dconv[tokens:] = head_rows[...]

    @pl.when(me + 1 == n)
    def _():
        dconv[tokens:] = jnp.zeros((8, width), F32)

    for head in range(width // size):
        cols = slice(head * size, (head + 1) * size)
        total = par_ref[0:1, cols] * dconv[:tokens, cols]
        for tap in range(1, 4):
            total = total + par_ref[tap : tap + 1, cols] * dconv[tap : tap + tokens, cols]
        dxb_ref[:, cols] = total.astype(BF16)

    pl.when(me > 0)(rows_copy.wait_send)

    def sent(place, carry):
        told(place).wait_send()
        return carry

    lax.fori_loop(0, me, sent, 0)
    core = lax.axis_index("ch")
    half = tokens // 2
    loads[1].wait()
    for start in range(0, model, size):
        cols = slice(start, start + size)
        part = (
            d_one_part[:, cols]
            + lax.dot_general(dxb_ref[...], w_in[cols], FLIPPED, preferred_element_type=F32)
        ).astype(BF16)
        d_one[0, :, cols] = part[:half]
        d_one[1, :, cols] = part[half:]
    exchange = pltpu.make_async_remote_copy(
        src_ref=d_one.at[1 - core],
        dst_ref=d_one_got,
        send_sem=send_m,
        recv_sem=recv_m,
        device_id={"ch": 1 - core},
        device_id_type=MESH,
    )
    exchange.start()
    exchange.wait_recv()

    def norm(at, total):
        r = pl.ds(pl.multiple_of(at * 16, 16), 16)
        x = x_ref[pl.ds(pl.multiple_of(core * half + at * 16, 16), 16)].astype(F32)
        scale = lax.rsqrt(jnp.mean(x * x, axis=-1, keepdims=True) + 1e-06)
        grad = d_one[core, r].astype(F32) + d_one_got[r].astype(F32)
        back = grad * gain_ref[...]
        shrink = scale * scale * scale * jnp.mean(x * back, axis=-1, keepdims=True)
        dx_ref[core, r] = resid_ref[r] + (scale * back - x * shrink)
        return total + jnp.sum(grad * (x * scale), axis=0, keepdims=True)

    dgain_ref[...] = lax.fori_loop(0, half // 16, norm, jnp.zeros((1, model), F32))
    share = pltpu.make_async_remote_copy(
        src_ref=dx_ref.at[core],
        dst_ref=dx_ref.at[core],
        send_sem=send_x,
        recv_sem=recv_x,
        device_id={"ch": 1 - core},
        device_id_type=MESH,
    )
    share.start()
    exchange.wait_send()
    for piece in range(3, len(hosted)):
        collect(piece)
    for copy in outs:
        copy.wait()
    pltpu.make_async_remote_copy(
        src_ref=dx_ref.at[core],
        dst_ref=dx_ref.at[1 - core],
        send_sem=send_x,
        recv_sem=recv_x,
        device_id={"ch": 1 - core},
        device_id_type=MESH,
    ).wait_recv()
    share.wait_send()


def mixer_backward(
    mixed, weights, x_half, gain, d_resid, y_pre, states, edge, conv, x_branch, gates, par, halves, own, hidden_units
):
    n = lax.axis_size("seq")
    tokens, width = x_branch.shape
    model = mixed.shape[1]
    size = gates.shape[2]
    half = tokens // 2
    _, kinds, part, rows, units = halves.shape
    dma = pltpu.SemaphoreType.DMA
    whole = pltpu.VMEM((tokens, width), F32)
    longer = pltpu.VMEM((tokens + 8, width), F32)
    weight = pltpu.VMEM((model, width), BF16)
    return pl.pallas_call(
        functools.partial(backward_body, n, hidden_units),
        out_shape=(
            jax.ShapeDtypeStruct((tokens, width), BF16),
            jax.ShapeDtypeStruct((tokens, width), BF16),
            jax.ShapeDtypeStruct((n, 2, size // n, width), BF16),
            jax.ShapeDtypeStruct((8, width), F32),
            jax.ShapeDtypeStruct((2, half, model), F32),
            jax.ShapeDtypeStruct((1, model), F32),
            jax.ShapeDtypeStruct((kinds, 2 * part, rows, units), BF16),
        ),
        in_specs=[VMEM] + [HBM] * 3 + [VMEM] * 10 + [HBM, HBM],
        out_specs=(VMEM,) * 6 + (HBM,),
        scratch_shapes=[
            pltpu.VMEM(halves.shape, BF16),
            pltpu.VMEM(halves.shape, BF16),
            weight,
            weight,
            weight,
            pltpu.VMEM((2, half, model), BF16),
            pltpu.VMEM((half, model), BF16),
            pltpu.VMEM((tokens, model), F32),
            longer,
            whole,
            whole,
            whole,
            whole,
            longer,
            longer,
            pltpu.VMEM((2, width), F32),
            pltpu.VMEM((n, 2, width), F32),
            pltpu.VMEM((8, width), F32),
            dma(()),
            dma(()),
            dma((n,)),
            dma((n,)),
            dma((kinds, part, 2)),
            dma((kinds, part, 2)),
            dma(()),
            dma(()),
            dma(()),
            dma(()),
            dma((3,)),
            dma(()),
            dma((kinds, part, 2)),
        ],
        compiler_params=params(5, 60),
        name="mixer_backward",
    )(mixed, *weights, x_half, gain, d_resid, y_pre, states, edge, conv, x_branch, gates, par, halves, own)


def ffn_body(n, hidden_units, *refs):
    own_ref, cots_ref, column_ref, near_ref, resid_ref, gain_ref = refs[:6]
    block_ref, d_resid_ref, mixed_ref, d_gain_ref, turned_ref = refs[6:11]
    halves_ref, mine_ref, far_ref = refs[11:14]
    tokens, cots, w, extra, hidden, box, sib, got, stage, turned, my_cot = refs[14:25]
    token_sems = refs[25:28]
    send_w, recv_w, keep_w, keep_c, keep_t, keep_m = refs[28:34]
    send_c, recv_s, send_z, recv_r, send_f, recv_f, send_m, recv_m, move, out_sem = refs[34:]
    groups = n // INNER
    half = groups // 2
    me, outer, by_x, by_y, by_xy = whereabouts()
    base = outer * INNER
    core = lax.axis_index("ch")
    above, below = outer + 1 < groups, outer > 0
    sibling = {"ch": 1 - core}
    barrier = pltpu.get_barrier_semaphore()

    def hello(peer):
        pl.semaphore_signal(barrier, inc=1, device_id=peer, device_id_type=MESH)

    hello({"seq": by_x})
    hello({"seq": by_y})
    hello(sibling)
    pl.when(above)(lambda: hello({"seq": me + INNER}))
    pl.when(below)(lambda: hello({"seq": me - INNER}))
    pl.semaphore_wait(barrier, 3 + above.astype(jnp.int32) + below.astype(jnp.int32))
    flips = ((by_x, by_y), (by_y, by_x))
    rows, units = w.shape[3], w.shape[4]
    split = Units(hidden_units, groups, core)
    tall, model = own_ref.shape
    count = 2 * tall
    deep = INNER * rows
    tile = 256

    def part(h):
        return pl.ds(h * half, half)


    chain_t = Chain(n, own_ref, tokens, *token_sems)

    def weight_copy(kind, h, far, receive=False):
        source = flips[h][0] if far else me
        if receive:
            source = by_xy if far else flips[h][1]
        src = near_ref.at[h, kind] if far else column_ref.at[kind, part(h)]
        return Sized(
            split,
            outer,
            lambda width: remote(
                src.at[:, :, pl.ds(0, width)],
                w.at[kind, part(h), source - base, :, pl.ds(0, width)],
                send_w.at[kind, h, far],
                recv_w.at[kind, h, far],
                flips[h][1],
            ),
        )

    keep = [
        [
            pltpu.make_async_copy(
                column_ref.at[kind], w.at[kind, :, me - base], keep_w.at[kind, 0]
            ),
            *(
                pltpu.make_async_copy(
                    near_ref.at[h, kind],
                    w.at[kind, part(h), flips[h][0] - base],
                    keep_w.at[kind, 1 + h],
                )
                for h in range(2)
            ),
        ]
        for kind in range(3)
    ]
    every = [(h, far) for far in range(2) for h in range(2)]
    own_t = chain_t.keep(keep_t)
    load_c = pltpu.make_async_copy(cots_ref, cots, keep_c)
    load_m = pltpu.make_async_copy(cots_ref.at[outer, core], my_cot, keep_m)
    chain_t.start()
    for kind in range(3):
        for h, far in every:
            weight_copy(kind, h, far).start()
    own_t.start()
    load_c.start()
    load_m.start()
    for kind in range(3):
        for copy in keep[kind]:
            copy.start()
    for step in range(1, groups):
        chain_t.step(step)
    chain_t.finish()
    own_t.wait()

    def weights_landed(kind):
        for h, far in every:
            weight_copy(kind, h, far, True).wait_recv()
        for copy in keep[kind]:
            copy.wait()
        if not split.even:

            @pl.when(jnp.logical_not(split.full(outer)))
            def _():
                rest = jnp.zeros((groups, INNER, rows, LANES), BF16)
                w[kind, :, :, :, units - LANES :] = rest

    def columns(kind, at):
        return w[kind, :, :, :, at : at + tile].reshape(model, tile)

    def token_rows(place):
        return pl.ds(pl.multiple_of(place * count, count), count)

    def each(limit, action):
        def one(turn, carry):
            action(turn)
            return carry

        lax.fori_loop(0, limit, one, 0)

    weights_landed(0)
    weights_landed(1)

    def middle(place):
        left = tokens[place].reshape(count, model)
        r = token_rows(place)
        for at in range(0, units, tile):
            c = slice(at, at + tile)
            gate = jnp.dot(left, columns(0, at), preferred_element_type=F32)
            up = jnp.dot(left, columns(1, at), preferred_element_type=F32)
            value, slope = gelu_parts(gate)
            hidden[0, r, c] = (value * up).astype(BF16)
            hidden[1, r, c] = (up * slope).astype(BF16)
            hidden[2, r, c] = value.astype(BF16)

    each(groups, middle)
    def back_hidden(place):
        left = cots[place].reshape(count, model)
        r = token_rows(place)
        for at in range(0, units, tile):
            c = slice(at, at + tile)
            back = jnp.dot(left, columns(2, at), preferred_element_type=F32)
            for kind in (1, 2):
                hidden[kind, r, c] = (back * hidden[kind, r, c].astype(F32)).astype(BF16)


    boxes = (cots, box)

    def partial(kind, place):
        r = token_rows(place)
        for at in range(groups):
            pairs = ((1, 0), (2, 1)) if kind == 0 else ((0, 2),)
            value = 0.0
            for left, right in pairs:
                value = value + lax.dot_general(
                    hidden[left, r],
                    w[right, at].reshape(deep, units),
                    FLIPPED,
                    preferred_element_type=F32,
                )
            value = value.astype(BF16)
            boxes[kind][place, 0, :, at * deep : (at + 1) * deep] = value[:tall]
            boxes[kind][place, 1, :, at * deep : (at + 1) * deep] = value[tall:]
        to_sibling(kind, place).start()

    def to_sibling(kind, place):
        return pltpu.make_async_remote_copy(
            src_ref=boxes[kind].at[place, 1 - core],
            dst_ref=sib.at[kind, place],
            send_sem=send_c.at[kind, place],
            recv_sem=recv_s.at[kind, place],
            device_id=sibling,
            device_id_type=MESH,
        )

    def along(kind, place, up):
        last = place == (outer + 1 if up else outer - 1)
        slot = place if up else jnp.where(last, groups, place)
        return remote(
            boxes[kind].at[place, core],
            got.at[kind, slot],
            send_z.at[kind, place],
            recv_r.at[kind, slot],
            me + (INNER if up else -INNER),
        )

    def landed(kind, slot):
        return remote(
            box.at[0, core], got.at[kind, slot], send_z.at[kind, 0], recv_r.at[kind, slot], by_x
        )

    chunk = 16

    def rows_of(at):
        return pl.ds(pl.multiple_of(at * chunk, chunk), chunk)

    def ready(kind, place, incoming):
        to_sibling(kind, place).wait_recv()

        def add(at, with_got):
            r = rows_of(at)
            value = boxes[kind][place, core, r].astype(F32) + sib[kind, place, r].astype(F32)
            if with_got:
                value = value + got[kind, place, r].astype(F32)
            boxes[kind][place, core, r] = value.astype(BF16)

        @pl.when(incoming)
        def _():
            landed(kind, place).wait_recv()
            each(tall // chunk, lambda at: add(at, True))

        @pl.when(jnp.logical_not(incoming))
        def _():
            each(tall // chunk, lambda at: add(at, False))

    def pass_on(kind, turn):
        ups = groups - 1 - outer
        upper = jnp.where(outer < half, turn < ups, turn >= outer)
        later = jnp.where(outer < half, turn, turn - outer)
        earlier = jnp.where(outer < half, turn - ups, turn)

        @pl.when(upper)
        def _():
            place = groups - 1 - later
            ready(kind, place, below)
            along(kind, place, True).start()

        @pl.when(jnp.logical_not(upper))
        def _():
            ready(kind, earlier, above)
            along(kind, earlier, False).start()

    at_end = jnp.logical_or(outer == 0, outer == groups - 1)

    def partials(kind, start, stop):
        def one(turn, carry):
            partial(kind, far_first(groups, outer, turn))

            @pl.when(jnp.logical_and(at_end, turn >= 1))
            def _():
                pass_on(kind, turn - 1)

            return carry

        lax.fori_loop(start, stop, one, 0)

    def between(kind, turns):
        @pl.when(jnp.logical_not(at_end))
        def _():
            for turn in turns:
                pass_on(kind, turn)

    def totals(kind, use):
        to_sibling(kind, outer).wait_recv()
        for condition, slots in (
            (jnp.logical_and(below, above), (outer, groups)),
            (jnp.logical_and(below, jnp.logical_not(above)), (outer,)),
            (jnp.logical_and(jnp.logical_not(below), above), (groups,)),
        ):

            @pl.when(condition)
            def _(slots=slots):
                for slot in slots:
                    landed(kind, slot).wait_recv()

                def one(at):
                    r = rows_of(at)
                    value = boxes[kind][outer, core, r].astype(F32) + sib[kind, outer, r].astype(F32)
                    for slot in slots:
                        value = value + got[kind, slot, r].astype(F32)
                    use(r, value)

                each(tall // chunk, one)

    def clear(kind):
        def one(place):
            to_sibling(kind, place).wait_send()

            @pl.when(place > outer)
            def _():
                along(kind, place, True).wait_send()

            @pl.when(place < outer)
            def _():
                along(kind, place, False).wait_send()

        each(groups, one)


    made = (w.at[0], w.at[1], extra)

    def gradient_copy(kind, h, far):
        source = by_xy if far else flips[h][1]
        return Sized(
            split,
            outer,
            lambda width: remote(
                made[kind].at[part(h), source - base, :, pl.ds(0, width)],
                far_ref.at[h, far, kind, :, :, pl.ds(0, width)],
                send_f.at[kind, h, far],
                recv_f.at[kind, h, far],
                flips[h][1],
            ),
        )

    def gradients(kinds, source, h):
        for at in range(h * half, (h + 1) * half):
            left = source[:, :, :, at * deep : (at + 1) * deep].reshape(groups * count, deep)
            turned[...] = left.T
            for kind, right in kinds:
                for start in range(0, units, tile):
                    c = slice(start, start + tile)
                    made[kind][at, :, :, c] = (
                        jnp.dot(turned[...], hidden[right, :, c], preferred_element_type=F32)
                        .astype(BF16)
                        .reshape(INNER, rows, tile)
                    )
        for kind, _ in kinds:
            for far in (1, 0):
                gradient_copy(kind, h, far).start()

    def collect(kind, h, far):
        inner = (flips[h][0] if far else me) - base
        gradient_copy(kind, h, far).wait_recv()
        load = pltpu.make_async_copy(far_ref.at[h, far, kind], stage, move)
        load.start()
        load.wait()
        for place in range(half):
            at = h * half + place

            def one(turn, place=place, at=at):
                r = rows_of(turn)
                made[kind][at, inner, r] = (
                    made[kind][at, inner, r].astype(F32) + stage[place, r].astype(F32)
                ).astype(BF16)

            each(rows // chunk, one)
        out_copy(kind, h, far).start()

    def out_copy(kind, h, far):
        inner = (flips[h][0] if far else me) - base
        return pltpu.make_async_copy(
            made[kind].at[part(h), inner],
            (halves_ref if far else mine_ref).at[h, kind],
            out_sem.at[kind, h, far],
        )

    load_c.wait()
    gradients(((2, 0),), cots, 0)
    gradients(((2, 0),), cots, 1)
    weights_landed(2)
    for kind in range(3):
        for h, far in every:
            weight_copy(kind, h, far).wait_send()
    partials(1, 0, groups)
    each(groups, back_hidden)
    load_m.wait()
    partials(0, 0, half)
    between(1, range(1))
    partials(0, half, groups)
    gradients(((0, 1),), tokens, 0)
    between(1, range(1, half))
    gradients(((0, 1),), tokens, 1)
    gradients(((1, 2),), tokens, 0)
    between(1, range(half, groups - 1))
    gradients(((1, 2),), tokens, 1)

    def shared(ref, at, part):
        return pltpu.make_async_remote_copy(
            src_ref=ref.at[core],
            dst_ref=ref.at[part],
            send_sem=send_m.at[at],
            recv_sem=recv_m.at[at],
            device_id=sibling,
            device_id_type=MESH,
        )

    def finish(r, value):
        block_ref[core, r] = (resid_ref[r] + value).astype(BF16)

    d_gain_ref[...] = jnp.zeros((1, model), F32)

    def norm(r, grad):
        resid = resid_ref[r]
        scale = lax.rsqrt(jnp.mean(resid * resid, axis=-1, keepdims=True) + 1e-06)
        back = grad * gain_ref[...]
        shrink = scale * scale * scale * jnp.mean(resid * back, axis=-1, keepdims=True)
        value = my_cot[r].astype(F32) + (scale * back - resid * shrink)
        d_resid_ref[r] = value
        mixed_ref[core, r] = value.astype(BF16)
        d_gain_ref[...] = d_gain_ref[...] + jnp.sum(grad * (resid * scale), axis=0, keepdims=True)

    for far in (1, 0):
        for h in range(2):
            collect(2, h, far)
    between(0, range(1))
    totals(1, finish)
    show = shared(block_ref, 1, core)
    show.start()
    for far in (1, 0):
        for h in range(2):
            collect(0, h, far)
    between(0, range(1, groups - 1))
    totals(0, norm)
    share = shared(mixed_ref, 0, core)
    share.start()
    shared(mixed_ref, 0, 1 - core).wait_recv()
    for start in range(0, model, tile):
        c = slice(start, start + tile)
        turned_ref[c, :tall] = mixed_ref[0, :, c].T
        turned_ref[c, tall:] = mixed_ref[1, :, c].T
    for far in (1, 0):
        for h in range(2):
            collect(1, h, far)
    clear(0)
    clear(1)
    shared(block_ref, 1, 1 - core).wait_recv()
    share.wait_send()
    show.wait_send()
    for kind in range(3):
        for h, far in every:
            gradient_copy(kind, h, far).wait_send()
            out_copy(kind, h, far).wait()


def feed_forward(own, cots, column, near, resid, gain, hidden_units):
    n = lax.axis_size("seq")
    groups = n // INNER
    tall, model = own.shape
    kinds, _, rows, units = column.shape
    half = groups // 2
    dma = pltpu.SemaphoreType.DMA
    part = jax.ShapeDtypeStruct((2, kinds, half, rows, units), BF16)
    return pl.pallas_call(
        functools.partial(ffn_body, n, hidden_units),
        out_shape=(
            jax.ShapeDtypeStruct((2, tall, model), BF16),
            jax.ShapeDtypeStruct((tall, model), F32),
            jax.ShapeDtypeStruct((2, tall, model), BF16),
            jax.ShapeDtypeStruct((1, model), F32),
            jax.ShapeDtypeStruct((model, 2 * tall), BF16),
            part,
            part,
            jax.ShapeDtypeStruct((2, 2, kinds, half, rows, units), BF16),
        ),
        in_specs=[HBM] * 4 + [VMEM] * 2,
        out_specs=(VMEM,) * 5 + (HBM,) * 3,
        scratch_shapes=[
            pltpu.VMEM((groups, 2, tall, model), BF16),
            pltpu.VMEM((groups, 2, tall, model), BF16),
            pltpu.VMEM((kinds, groups, INNER, rows, units), BF16),
            pltpu.VMEM((groups, INNER, rows, units), BF16),
            pltpu.VMEM((3, groups * 2 * tall, units), BF16),
            pltpu.VMEM((groups, 2, tall, model), BF16),
            pltpu.VMEM((2, groups, tall, model), BF16),
            pltpu.VMEM((2, groups + 1, tall, model), BF16),
            pltpu.VMEM((half, rows, units), BF16),
            pltpu.VMEM((INNER * rows, groups * 2 * tall), BF16),
            pltpu.VMEM((tall, model), BF16),
            *chain_semaphores(groups),
            dma((kinds, 2, 2)),
            dma((kinds, 2, 2)),
            dma((kinds, 3)),
            dma(()),
            dma(()),
            dma(()),
            dma((2, groups)),
            dma((2, groups)),
            dma((2, groups)),
            dma((2, groups + 1)),
            dma((kinds, 2, 2)),
            dma((kinds, 2, 2)),
            dma((2,)),
            dma((2,)),
            dma(()),
            dma((kinds, 2, 2)),
        ],
        compiler_params=params(8, 63),
        name="feed_forward",
    )(own, cots, column, near, resid, gain)


def my_half(values):
    half = values.shape[0] // 2
    return lax.dynamic_slice_in_dim(values, lax.axis_index("ch") * half, half, 0)


def join(own):
    other = swap(own, "ch", 1)
    core = lax.axis_index("ch")
    return jnp.concatenate(
        [jnp.where(core == 0, own, other), jnp.where(core == 0, other, own)], axis=0
    )


def tokens_out(partial, half):
    width = partial.shape[1]
    groups = lax.axis_size("seq") // INNER
    outer = lax.axis_index("seq") // INNER
    core = lax.axis_index("ch")
    parts = partial.reshape(groups, 2, half, width)
    theirs = pick(parts, 1 - core, 1).astype(BF16)
    summed = (pick(parts, core, 1).astype(F32) + swap(theirs, "ch", 1).astype(F32)).astype(BF16)
    total = pick(summed, outer).astype(F32)
    for step in range(1, groups):
        total = total + swap(pick(summed, outer ^ step), "seq", step * INNER).astype(F32)
    return total


def feed_forward_parts(n_two, cot_half, all_cot, column, near, resid, ffn_gain, hidden_units):
    f32, bf16 = F32, BF16
    _, groups, depth, units = column.shape
    half_rows, model = n_two.shape
    tok_rows = 2 * half_rows
    _, norm_back_two = jax.vjp(scaled_norm, resid, ffn_gain)
    all_two, *full_ffn = gather_tokens(n_two, column, near)
    all_two, all_cot = (v.reshape(groups * tok_rows, model) for v in (all_two, all_cot))
    own = Units(hidden_units, groups, lax.axis_index("ch")).width(lax.axis_index("seq") // INNER)
    valid = lax.broadcasted_iota(jnp.int32, (1, units), 1) < own
    full_ffn = [jnp.where(valid, w.reshape(model, units), 0) for w in full_ffn]
    gate_pre = jnp.dot(all_two, full_ffn[0], preferred_element_type=f32)
    up_pre = jnp.dot(all_two, full_ffn[1], preferred_element_type=f32)
    gate_act, gelu_back_gate = jax.vjp(gelu_tanh, gate_pre)
    hidden = (gate_act * up_pre).astype(bf16)
    ffn_term = jnp.einsum("tf,df->td", hidden, full_ffn[2], preferred_element_type=f32).astype(bf16)
    d_hidden = jnp.einsum("td,df->tf", all_cot, full_ffn[2], preferred_element_type=f32)
    d_gate = gelu_back_gate(d_hidden * up_pre)[0].astype(bf16)
    d_up = (d_hidden * gate_act).astype(bf16)
    d_n_two = (
        jnp.einsum("tf,df->td", d_gate, full_ffn[0], preferred_element_type=f32)
        + jnp.einsum("tf,df->td", d_up, full_ffn[1], preferred_element_type=f32)
    ).astype(bf16)
    terms = [
        jnp.einsum("td,tf->df", left, right, preferred_element_type=f32)
        .astype(bf16)
        .reshape(groups, INNER, depth, units)
        for left, right in ((all_two, d_gate), (all_two, d_up), (all_cot, hidden))
    ]
    split = [v.reshape(groups, 2, half_rows, model) for v in (d_n_two, ffn_term)]
    if groups <= 4:
        d_n_two, ffn_out, far = reduce_tokens(split, terms)
    else:
        d_n_two, far = reduce_tokens(split[:1], terms)
        ffn_out = tokens_out(ffn_term, half_rows)
    block_out = join((resid + ffn_out).astype(bf16))
    inner = lax.axis_index("seq") % INNER
    by_half = [t.reshape(2, groups // 2, INNER, depth, units) for t in terms]

    def block_at(h, place):
        return jnp.stack([pick(t[h], place, 1) for t in by_half]).astype(f32)

    mine = jnp.stack(
        [(block_at(h, inner) + far[h, 0].astype(f32)).astype(bf16) for h in range(2)]
    )
    halves = jnp.stack(
        [(block_at(h, inner ^ (1, 2)[h]) + far[h, 1].astype(f32)).astype(bf16) for h in range(2)]
    )
    d_resid_norm, d_ffn_gain_term = norm_back_two(d_n_two)
    d_resid = cot_half.astype(f32) + d_resid_norm
    d_mixed = join(d_resid.astype(bf16))
    return block_out, d_resid, d_mixed, d_ffn_gain_term.reshape(1, model), halves, mine


def shards(
    inputs,
    norm_gain,
    branch_weight,
    input_weight,
    channel_params,
    gate_x_blocks,
    gate_a_blocks,
    out_weight,
    ffn_gain,
    ffn_gate,
    ffn_up,
    ffn_down,
    cotangent,
):
    f32 = F32
    bf16 = BF16
    n = lax.axis_size("seq")
    tok_rows, model = inputs.shape
    half_rows = tok_rows // 2
    heads, part, size = gate_x_blocks.shape
    width = heads * size
    depth = ffn_gate.shape[0]
    groups = n // INNER
    hidden_units = ffn_gate.shape[1]
    par = jnp.concatenate(
        [
            channel_params,
            jax.nn.softplus(channel_params[7:8]),
            jax.nn.sigmoid(channel_params[7:8]),
            jnp.zeros((6, width), f32),
        ],
        axis=0,
    )
    mixer_set = [input_weight, branch_weight, out_weight.T]
    gate_set = [gate_x_blocks, gate_a_blocks]
    ffn_set = [ffn_gate, ffn_up, ffn_down.T]
    gains = jnp.stack([norm_gain, ffn_gain])
    gain_one, gain_two = gains[:1], gains[1:]
    if depth % 16 == 0 and part % 16 == 0:
        made = gather_forward(
            mixer_set, gate_set, ffn_set, inputs, gains, par, cotangent
        )
        *full_mixer, full_gates, column, n_one, n_one_turned, _ = made[:8]
        full_mixer = [w.reshape(model, width) for w in full_mixer]
        gates = full_gates.reshape(2, heads, size, size)
        made = made[8:]
    else:
        cot_half = my_half(cotangent)
        *full_mixer, full_gates, column, n_one, n_one_turned, last_rows = gather_weights(
            mixer_set, gate_set, ffn_set, inputs, gain_one
        )
        full_mixer = [w.reshape(model, width) for w in full_mixer]
        gates = full_gates.reshape(2, heads, size, size)
        made = mixer_forward(
            n_one,
            last_rows,
            full_mixer,
            gates,
            par,
            my_half(inputs),
            gain_two,
            column,
            cot_half,
            hidden_units,
        )
    x_branch, y_pre, conv_out, states, branch_out, edge, resid, n_two, near, cots = made
    if groups <= 4 and depth % 16 == 0:
        block_out, d_resid, d_mixed, d_ffn_gain_term, d_mixed_turned, halves, mine, _ = feed_forward(
            n_two, cots, column, near, resid, gain_two, hidden_units
        )
        block_out = block_out.reshape(tok_rows, model)
        d_mixed = d_mixed.reshape(tok_rows, model)
    else:
        block_out, d_resid, d_mixed, d_ffn_gain_term, halves, mine = feed_forward_parts(
            n_two, cot_half, cots, column, near, resid, ffn_gain, hidden_units
        )
        d_mixed_turned = d_mixed.T
    d_y, d_xb, d_gates, d_par, d_inputs, d_norm_gain_term, column_back = mixer_backward(
        d_mixed,
        full_mixer,
        inputs,
        gain_one,
        d_resid,
        y_pre,
        states,
        edge,
        conv_out,
        x_branch,
        gates,
        par,
        halves,
        mine,
        hidden_units,
    )
    d_inputs = d_inputs.reshape(tok_rows, model)
    gain_rows = model // width
    scattered, small, spread = scatter_mixer(
        n_one_turned.reshape(n, depth, tok_rows),
        d_mixed_turned.reshape(n, depth, tok_rows),
        d_y,
        d_xb,
        branch_out,
        d_gates,
        d_par,
        d_norm_gain_term,
        d_ffn_gain_term,
        column_back,
        hidden_units,
    )
    ffn_grads = [spread[kind].astype(f32) for kind in range(3)]
    d_gate_pair = scattered[3 * depth :].reshape(2, part, heads, size).transpose(0, 2, 1, 3)
    return (
        block_out,
        d_inputs,
        small[8 : 8 + gain_rows].reshape(model),
        scattered[:depth],
        scattered[depth : 2 * depth],
        small[:8],
        d_gate_pair[0],
        d_gate_pair[1],
        scattered[2 * depth : 3 * depth].T,
        small[8 + gain_rows : 8 + 2 * gain_rows].reshape(model),
        ffn_grads[0],
        ffn_grads[1],
        ffn_grads[2].T,
    )


def solution(mesh):
    placed = (
        P("seq", None),
        P(),
        P("seq", "ch"),
        P("seq", "ch"),
        P(None, "ch"),
        P("ch", "seq", None),
        P("ch", "seq", None),
        P("ch", "seq"),
        P(),
        P("seq", "ch"),
        P("seq", "ch"),
        P("ch", "seq"),
        P("seq", None),
    )
    return jax.shard_map(
        shards,
        mesh=mesh,
        in_specs=placed,
        out_specs=(
            P("seq", None),
            P("seq", None),
            P(),
            P("seq", "ch"),
            P("seq", "ch"),
            P(None, "ch"),
            P("ch", "seq", None),
            P("ch", "seq", None),
            P("ch", "seq"),
            P(),
            P("seq", "ch"),
            P("seq", "ch"),
            P("ch", "seq"),
        ),
        check_vma=False,
    )
```

```python
import functools

import jax
import jax.numpy as jnp
from jax import lax
from jax.experimental import pallas as pl
from jax.experimental.pallas import tpu as pltpu
from jax.sharding import PartitionSpec as P

F32 = jnp.float32
BF16 = jnp.bfloat16
INNER = 4
MESH = pl.DeviceIdType.MESH
VMEM = pl.BlockSpec(memory_space=pltpu.VMEM)
ANY = pl.BlockSpec(memory_space=pl.ANY)
HBM = pl.BlockSpec(memory_space=pltpu.HBM)


def swap(value, axis, mask):
    return lax.ppermute(value, axis, [(i, i ^ mask) for i in range(lax.axis_size(axis))])


def pick(array, index, axis=0):
    return lax.dynamic_index_in_dim(array, index, axis, False)


def scaled_norm(values, gain):
    return values * lax.rsqrt(jnp.mean(values * values, axis=-1, keepdims=True) + 1e-06) * gain


def gelu_tanh(values):
    return jax.nn.gelu(values, approximate=True)


def whereabouts():
    me = lax.axis_index("seq")
    outer = me // INNER
    inner = me - outer * INNER
    y = inner // 2
    x = inner - 2 * y
    by_x = me + 1 - 2 * x
    by_y = me + 2 - 4 * y
    return me, outer, by_x, by_y, by_x + 2 - 4 * y


def when(condition, action):
    if condition is None:
        action()
    else:
        pl.when(condition)(action)


def both(one, other):
    if one is None or other is None:
        return one if other is None else other
    return jnp.logical_and(one, other)


def greet(peers):
    barrier = pltpu.get_barrier_semaphore()
    for condition, peer in peers:
        when(
            condition,
            lambda peer=peer: pl.semaphore_signal(
                barrier, inc=1, device_id={"seq": peer}, device_id_type=MESH
            ),
        )
    count = 0
    for condition, _ in peers:
        count = count + (1 if condition is None else condition.astype(jnp.int32))
    pl.semaphore_wait(barrier, count)


def greet_all(n, me, sibling=False):
    barrier = pltpu.get_barrier_semaphore()

    def hello(step, carry):
        pl.semaphore_signal(
            barrier, inc=1, device_id={"seq": lax.rem(me + step, n)}, device_id_type=MESH
        )
        return carry

    lax.fori_loop(1, n, hello, 0)
    if sibling:
        pl.semaphore_signal(
            barrier, inc=1, device_id={"ch": 1 - lax.axis_index("ch")}, device_id_type=MESH
        )
    pl.semaphore_wait(barrier, n if sibling else n - 1)


def remote(src, dst, send_sem, recv_sem, place):
    return pltpu.make_async_remote_copy(
        src_ref=src,
        dst_ref=dst,
        send_sem=send_sem,
        recv_sem=recv_sem,
        device_id={"seq": place},
        device_id_type=MESH,
    )


def params(collective_id, mib):
    return pltpu.CompilerParams(
        collective_id=collective_id, has_side_effects=True, vmem_limit_bytes=mib * 2**20
    )


def gather_begin(n, refs, greeted):
    w_refs, g_refs, f_refs, x_ref, gain_ref = refs[:3], refs[3:5], refs[5:8], refs[8], refs[9]
    wo_refs, go_ref, column_ref, one_ref, turned_ref, last_ref = refs[10:13], *refs[13:18]
    send_m, recv_m, send_f, recv_f, here, send_l, recv_l = refs[18:]
    groups = n // INNER
    me, outer, by_x, by_y, by_xy = whereabouts()
    above, below = outer + 1 < groups, outer > 0
    def column_peer(turn):
        return lax.rem(outer + turn, groups)

    if not greeted:
        barrier = pltpu.get_barrier_semaphore()

        def hello(peer):
            pl.semaphore_signal(barrier, inc=1, device_id={"seq": peer}, device_id_type=MESH)

        hello(by_x)
        hello(by_y)

        def hello_column(turn, carry):
            hello(me + (column_peer(turn) - outer) * INNER)
            return carry

        lax.fori_loop(1, groups, hello_column, 0)
        pl.when(me + 1 < n)(lambda: hello(me + 1))
        pl.when(me > 0)(lambda: hello(me - 1))
        neighbours = (me + 1 < n).astype(jnp.int32) + (me > 0).astype(jnp.int32)
        pl.semaphore_wait(barrier, groups + 1 + neighbours)
    units = Units(f_refs[0].shape[1], groups, lax.axis_index("ch"))
    half = w_refs[0].shape[1] // 2

    keep = [
        pltpu.make_async_copy(w_refs[kind], wo_refs[kind].at[me], here.at[kind])
        for kind in range(3)
    ]
    for gate in range(2):
        keep.append(pltpu.make_async_copy(g_refs[gate], go_ref.at[gate, :, me], here.at[3 + gate]))
    for kind in range(3):
        keep.append(
            Sized(
                units,
                outer,
                lambda width, kind=kind: pltpu.make_async_copy(
                    f_refs[kind].at[:, units.columns(outer, width)],
                    column_ref.at[kind, outer, :, pl.ds(0, width)],
                    here.at[5 + kind],
                ),
            )
        )
    for copy in keep:
        copy.start()
    sent = []

    def copies(h, source, way, target, own, kinds=range(4)):
        cols = pl.ds(h * half, half)
        pairs = [
            (w_refs[kind].at[:, cols], wo_refs[kind].at[source, :, cols]) for kind in range(3)
        ]
        pairs.append((g_refs[h], go_ref.at[h, :, source]))
        return [
            remote(
                given if own else dst,
                dst,
                send_m.at[kind, h, source, way],
                recv_m.at[kind, h, source],
                target,
            )
            for kind, (given, dst) in enumerate(pairs)
            if kind in kinds
        ]

    def send(condition, *what):
        def go():
            for copy in copies(*what):
                copy.start()

        when(condition, go)
        sent.append((condition, what))

    def arrive(condition, h, source, kinds=range(4)):
        def go():
            for copy in copies(h, source, 0, by_x, False, kinds):
                copy.wait_recv()

        when(condition, go)

    def exchange(turn, receive):
        place = lax.rem(outer + groups - turn, groups) if receive else column_peer(turn)
        owner = outer if receive else place
        return [
            Sized(
                units,
                owner,
                lambda width, kind=kind: remote(
                    f_refs[kind].at[:, units.columns(owner, width)],
                    column_ref.at[kind, place if receive else outer, :, pl.ds(0, width)],
                    send_f.at[kind, turn],
                    recv_f.at[kind, turn],
                    me + (place - outer) * INNER,
                ),
            )
            for kind in range(3)
        ]

    def each_turn(action):
        def one(turn, carry):
            action(turn)
            return carry

        lax.fori_loop(1, groups, one, 0)

    tokens, model = x_ref.shape
    tall = last_ref.shape[0]
    last_copy = remote(one_ref.at[pl.ds(tokens - tall, tall)], last_ref, send_l, recv_l, me + 1)

    def norm(at, carry):
        r = pl.ds(pl.multiple_of(at * 16, 16), 16)
        x = x_ref[r].astype(F32)
        scale = lax.rsqrt(jnp.mean(x * x, axis=-1, keepdims=True) + 1e-06)
        one_ref[r] = (x * scale * gain_ref[...]).astype(BF16)
        return carry

    def norm_all():
        lax.fori_loop(0, tokens // 16, norm, 0)
        pl.when(me + 1 < n)(last_copy.start)
        for start in range(0, model, 256):
            cols = slice(start, start + 256)
            turned_ref[cols] = one_ref[:, cols].T

        @pl.when(me == 0)
        def _():
            last_ref[...] = jnp.zeros(last_ref.shape, BF16)

    for step in range(groups):
        if step == 1:
            norm_all()
        for h in range(2):
            flip_p, flip_q = (by_x, by_y) if h == 0 else (by_y, by_x)
            if step == 0:
                send(above, h, me, 0, me + INNER, True)
                send(below, h, me, 1, me - INNER, True)
                send(None, h, me, 2, flip_p, True)
                send(None, h, me, 3, flip_q, True)
                continue
            for source, there, onward, way, to in (
                (me - step * INNER, outer >= step, above, 0, me + INNER),
                (me + step * INNER, outer + step < groups, below, 1, me - INNER),
            ):
                arrive(there, h, source)
                send(both(there, onward), h, source, way, to, False)
                send(there, h, source, 2, flip_p, False)
                send(there, h, source, 3, flip_q, False)
    each_turn(lambda turn: [copy.start() for copy in exchange(turn, False)])
    for step in range(groups):
        for h in range(2):
            flip_p, flip_q = (by_x, by_y) if h == 0 else (by_y, by_x)
            if step == 0:
                arrive(None, h, flip_p)
                send(None, h, flip_p, 3, flip_q, False)
                continue
            for source, there in (
                (flip_p - step * INNER, outer >= step),
                (flip_p + step * INNER, outer + step < groups),
            ):
                arrive(there, h, source)
                send(there, h, source, 3, flip_q, False)

    def last(kind):
        for place in range(groups):
            shift = (place - outer) * INNER
            for h in range(2):
                arrive(None, h, (by_y if h == 0 else by_x) + shift, (kind,))
                arrive(None, h, by_xy + shift, (kind,))
        for copy in keep[kind : kind + 1] if kind < 3 else keep[3:5]:
            copy.wait()

    def columns():
        each_turn(lambda turn: [copy.wait_recv() for copy in exchange(turn, True)])
        for copy in keep[5:]:
            copy.wait()

    def rows_before():
        pl.when(me > 0)(last_copy.wait_recv)

    def finish():
        for condition, what in sent:

            def done(what=what):
                for copy in copies(*what):
                    copy.wait_send()

            when(condition, done)
        each_turn(lambda turn: [copy.wait_send() for copy in exchange(turn, False)])
        pl.when(me + 1 < n)(last_copy.wait_send)

    return last, columns, rows_before, finish


def gather_body(n, *refs):
    last, columns, rows_before, finish = gather_begin(n, refs, False)
    for kind in range(4):
        last(kind)
    columns()
    rows_before()
    finish()


def gather_weights(weights, gates, ffn, x, gain):
    n = lax.axis_size("seq")
    groups = n // INNER
    rows, hidden_units = ffn[0].shape
    most = Units(hidden_units, groups, 0).most
    dma = pltpu.SemaphoreType.DMA
    made = [jax.ShapeDtypeStruct((n,) + w.shape, w.dtype) for w in weights]
    heads, part, size = gates[0].shape
    made.append(jax.ShapeDtypeStruct((2, heads, n, part, size), BF16))
    made.append(jax.ShapeDtypeStruct((3, groups, rows, most), BF16))
    made.append(jax.ShapeDtypeStruct(x.shape, BF16))
    made.append(jax.ShapeDtypeStruct(x.shape[::-1], BF16))
    made.append(jax.ShapeDtypeStruct((16, x.shape[1]), BF16))
    return pl.pallas_call(
        functools.partial(gather_body, n),
        out_shape=tuple(made),
        in_specs=[HBM] * 8 + [VMEM] * 2,
        out_specs=(HBM,) * 5 + (VMEM,) * 3,
        scratch_shapes=[
            dma((4, 2, n, 4)),
            dma((4, 2, n)),
            dma((3, groups)),
            dma((3, groups)),
            dma((8,)),
            dma(()),
            dma(()),
        ],
        compiler_params=params(1, 60),
        name="gather_weights",
    )(*weights, *gates, *ffn, x, gain)


LANES = 128


class Units:
    def __init__(self, total, groups, core):
        self.tiles, self.groups, self.core = total // LANES, groups, core
        self.most = -(-self.tiles // groups) * LANES
        self.even = self.tiles % groups == 0

    def start(self, place):
        up = (1 - self.core) * (self.groups - 1)
        return (place * self.tiles + up) // self.groups

    def full(self, place):
        return (self.start(place + 1) - self.start(place)) * LANES == self.most

    def width(self, place):
        return (self.start(place + 1) - self.start(place)) * LANES

    def columns(self, place, width):
        return pl.ds(pl.multiple_of(self.start(place) * LANES, LANES), width)


class Sized:
    def __init__(self, units, place, make):
        self.units, self.place, self.make = units, place, make

    def each(self, action):
        most = self.units.most
        if self.units.even:
            action(self.make(most))
            return
        full = self.units.full(self.place)
        pl.when(full)(lambda: action(self.make(most)))
        pl.when(jnp.logical_not(full))(lambda: action(self.make(most - LANES)))

    def start(self):
        self.each(lambda copy: copy.start())

    def wait(self):
        self.each(lambda copy: copy.wait())

    def wait_send(self):
        self.each(lambda copy: copy.wait_send())

    def wait_recv(self):
        self.each(lambda copy: copy.wait_recv())


def far_first(groups, outer, turn):
    def order(at):
        alone = groups - 1 - 2 * at
        later = turn - alone
        step = later // 2
        return jnp.where(
            turn < alone, groups - 1 - turn, jnp.where(later - 2 * step == 0, step, 2 * at - step)
        )

    return jnp.where(
        outer < groups // 2, order(outer), groups - 1 - order(groups - 1 - outer)
    )


class Chain:
    def __init__(self, n, own, whole, send, recv_z, recv_c):
        me = lax.axis_index("seq")
        self.groups = n // INNER
        self.outer = outer = me // INNER
        self.core = lax.axis_index("ch")
        self.above, self.below = outer + 1 < self.groups, outer > 0
        self.sibling = {"ch": 1 - self.core}
        self.to = ({"seq": me + INNER}, {"seq": me - INNER}, self.sibling)
        self.own, self.whole = own, whole
        self.send, self.recv_z, self.recv_c = send, recv_z, recv_c

    def copy(self, source, way, own=False):
        dst = self.whole.at[source, self.core]
        return pltpu.make_async_remote_copy(
            src_ref=self.own if own else dst,
            dst_ref=dst,
            send_sem=self.send.at[source, way],
            recv_sem=(self.recv_c if way == 2 else self.recv_z).at[source],
            device_id=self.to[way],
            device_id_type=MESH,
        )

    def from_sibling(self, source):
        return pltpu.make_async_remote_copy(
            src_ref=self.own,
            dst_ref=self.whole.at[source, 1 - self.core],
            send_sem=self.send.at[source, 2],
            recv_sem=self.recv_c.at[source],
            device_id=self.sibling,
            device_id_type=MESH,
        )

    def keep(self, sem):
        return pltpu.make_async_copy(self.own, self.whole.at[self.outer, self.core], sem)

    def ways(self, step):
        return (
            (self.outer - step, self.outer >= step, self.above, 0),
            (self.outer + step, self.outer + step < self.groups, self.below, 1),
        )

    def start(self):
        pl.when(self.above)(self.copy(self.outer, 0, True).start)
        pl.when(self.below)(self.copy(self.outer, 1, True).start)
        self.copy(self.outer, 2, True).start()

    def step(self, step):
        for source, there, onward, way in self.ways(step):
            pl.when(there)(lambda: self.copy(source, way).wait_recv())
            pl.when(both(there, onward))(lambda: self.copy(source, way).start())
            pl.when(there)(lambda: self.copy(source, 2).start())

    def finish(self):
        for source in range(self.groups):
            self.from_sibling(source).wait_recv()
        pl.when(self.above)(self.copy(self.outer, 0, True).wait_send)
        pl.when(self.below)(self.copy(self.outer, 1, True).wait_send)
        self.copy(self.outer, 2, True).wait_send()
        for step in range(1, self.groups):
            for source, there, onward, way in self.ways(step):
                pl.when(both(there, onward))(lambda: self.copy(source, way).wait_send())
                pl.when(there)(lambda: self.copy(source, 2).wait_send())


def chain_semaphores(groups):
    dma = pltpu.SemaphoreType.DMA
    return [dma((groups, 3)), dma((groups,)), dma((groups,))]


def tokens_body(n, *refs):
    own_ref, column_ref, near_ref = refs[:3]
    all_ref, w_refs = refs[3], refs[4:7]
    send_t, recv_z, recv_c, send_w, recv_w, here = refs[7:]
    groups = n // INNER
    half = groups // 2
    me, outer, by_x, by_y, by_xy = whereabouts()
    base = outer * INNER
    core = lax.axis_index("ch")
    above, below = outer + 1 < groups, outer > 0
    sibling = {"ch": 1 - core}
    barrier = pltpu.get_barrier_semaphore()

    def hello(peer):
        pl.semaphore_signal(barrier, inc=1, device_id=peer, device_id_type=MESH)

    hello({"seq": by_x})
    hello({"seq": by_y})
    hello(sibling)
    pl.when(above)(lambda: hello({"seq": me + INNER}))
    pl.when(below)(lambda: hello({"seq": me - INNER}))
    pl.semaphore_wait(barrier, 3 + above.astype(jnp.int32) + below.astype(jnp.int32))

    chain = Chain(n, own_ref, all_ref, send_t, recv_z, recv_c)

    def part(h):
        return pl.ds(h * half, half)

    flips = ((by_x, by_y), (by_y, by_x))

    def weight_copy(kind, h, far, receive=False):
        source = flips[h][0] if far else me
        if receive:
            source = by_xy if far else flips[h][1]
        return remote(
            near_ref.at[h, kind] if far else column_ref.at[kind, part(h)],
            w_refs[kind].at[part(h), source - base],
            send_w.at[kind, h, far],
            recv_w.at[kind, h, far],
            flips[h][1],
        )

    keep = [chain.keep(here.at[0])]
    for kind in range(3):
        keep.append(
            pltpu.make_async_copy(
                column_ref.at[kind], w_refs[kind].at[:, me - base], here.at[1 + kind]
            )
        )
        for h in range(2):
            keep.append(
                pltpu.make_async_copy(
                    near_ref.at[h, kind],
                    w_refs[kind].at[part(h), flips[h][0] - base],
                    here.at[4 + 2 * kind + h],
                )
            )
    every_w = [(kind, h, far) for kind in range(3) for h in range(2) for far in range(2)]

    chain.start()
    for what in every_w:
        weight_copy(*what).start()
    for copy in keep:
        copy.start()
    for step in range(1, groups):
        chain.step(step)
    for what in every_w:
        weight_copy(*what, receive=True).wait_recv()
    chain.finish()
    for what in every_w:
        weight_copy(*what).wait_send()
    for copy in keep:
        copy.wait()


def gather_tokens(tokens, column, near):
    n = lax.axis_size("seq")
    groups = n // INNER
    kinds, _, rows, units = column.shape
    dma = pltpu.SemaphoreType.DMA
    wide = jax.ShapeDtypeStruct((groups, 2) + tokens.shape, tokens.dtype)
    weight = jax.ShapeDtypeStruct((groups, INNER, rows, units), column.dtype)
    return pl.pallas_call(
        functools.partial(tokens_body, n),
        out_shape=(wide, weight, weight, weight),
        in_specs=[ANY] * 3,
        out_specs=(ANY,) * 4,
        scratch_shapes=chain_semaphores(groups)
        + [dma((kinds, 2, 2)), dma((kinds, 2, 2)), dma((10,))],
        compiler_params=params(6, 16),
        name="gather_tokens",
    )(tokens, column, near)


def reduce_body(n, kinds, *refs):
    p_refs, t_refs = refs[:kinds], refs[kinds : kinds + 3]
    out_refs, far_ref = refs[kinds + 3 : 2 * kinds + 3], refs[2 * kinds + 3]
    summed, got, send_c, recv_c, send_z, recv_z, send_f, recv_f = refs[2 * kinds + 4 :]
    groups = n // INNER
    half = groups // 2
    me, outer, by_x, by_y, by_xy = whereabouts()
    base = outer * INNER
    core = lax.axis_index("ch")
    above, below = outer + 1 < groups, outer > 0
    sibling = {"ch": 1 - core}
    barrier = pltpu.get_barrier_semaphore()

    def hello(peer):
        pl.semaphore_signal(barrier, inc=1, device_id=peer, device_id_type=MESH)

    hello({"seq": by_x})
    hello({"seq": by_y})
    hello(sibling)
    pl.when(above)(lambda: hello({"seq": me + INNER}))
    pl.when(below)(lambda: hello({"seq": me - INNER}))
    pl.semaphore_wait(barrier, 3 + above.astype(jnp.int32) + below.astype(jnp.int32))
    flips = ((by_x, by_y), (by_y, by_x))

    def gradient_copy(kind, h, far):
        source = by_xy if far else flips[h][1]
        return remote(
            t_refs[kind].at[pl.ds(h * half, half), source - base],
            far_ref.at[h, far, kind],
            send_f.at[kind, h, far],
            recv_f.at[kind, h, far],
            flips[h][1],
        )

    def to_sibling(kind, place):
        return pltpu.make_async_remote_copy(
            src_ref=p_refs[kind].at[place, 1 - core],
            dst_ref=summed.at[kind, place],
            send_sem=send_c.at[kind, place],
            recv_sem=recv_c.at[kind, place],
            device_id=sibling,
            device_id_type=MESH,
        )

    def along(kind, place, up):
        last = place == (outer + 1 if up else outer - 1)
        slot = place if up else jnp.where(last, groups, place)
        return remote(
            summed.at[kind, place],
            got.at[kind, slot],
            send_z.at[kind, place],
            recv_z.at[kind, slot],
            me + (INNER if up else -INNER),
        )

    def landed(kind, slot):
        return remote(
            summed.at[kind, 0], got.at[kind, slot], send_z.at[kind, 0], recv_z.at[kind, slot], by_x
        )

    def each(limit, action):
        def one(turn, carry):
            action(turn)
            return carry

        lax.fori_loop(0, limit, one, 0)

    every_f = [(kind, h, far) for far in (1, 0) for kind in range(3) for h in range(2)]
    for kind in range(kinds):
        each(groups, lambda place, kind=kind: to_sibling(kind, place).start())
    for what in every_f:
        gradient_copy(*what).start()

    tall = summed.shape[2]
    chunk = 16

    def rows_of(at):
        return pl.ds(pl.multiple_of(at * chunk, chunk), chunk)

    def ready(kind, place, incoming):
        to_sibling(kind, place).wait_recv()

        def local(at):
            r = rows_of(at)
            summed[kind, place, r] = (
                summed[kind, place, r].astype(F32) + p_refs[kind][place, core, r].astype(F32)
            ).astype(BF16)

        def more(at):
            r = rows_of(at)
            summed[kind, place, r] = (
                summed[kind, place, r].astype(F32)
                + p_refs[kind][place, core, r].astype(F32)
                + got[kind, place, r].astype(F32)
            ).astype(BF16)

        @pl.when(incoming)
        def _():
            landed(kind, place).wait_recv()
            each(tall // chunk, more)

        @pl.when(jnp.logical_not(incoming))
        def _():
            each(tall // chunk, local)

    for kind in range(kinds):

        def climb(turn, kind=kind):
            place = groups - 1 - turn

            @pl.when(place > outer)
            def _():
                ready(kind, place, below)
                along(kind, place, True).start()

        def sink(turn, kind=kind):
            place = turn

            @pl.when(place < outer)
            def _():
                ready(kind, place, above)
                along(kind, place, False).start()

        def turns(turn):
            @pl.when(outer < half)
            def _():
                climb(turn)
                sink(turn)

            @pl.when(outer >= half)
            def _():
                sink(turn)
                climb(turn)

        each(groups - 1, turns)
    for kind in range(kinds):
        to_sibling(kind, outer).wait_recv()

        def own(at, kind=kind):
            r = rows_of(at)
            out_refs[kind][r] = summed[kind, outer, r].astype(F32) + p_refs[kind][
                outer, core, r
            ].astype(F32)

        each(tall // chunk, own)
        for there, slot in ((below, outer), (above, groups)):

            @pl.when(there)
            def _():
                landed(kind, slot).wait_recv()

                def plus(at):
                    r = rows_of(at)
                    out_refs[kind][r] = out_refs[kind][r] + got[kind, slot, r].astype(F32)

                each(tall // chunk, plus)

    for kind in range(kinds):

        def clear(place, kind=kind):
            to_sibling(kind, place).wait_send()

            @pl.when(place > outer)
            def _():
                along(kind, place, True).wait_send()

            @pl.when(place < outer)
            def _():
                along(kind, place, False).wait_send()

        each(groups, clear)
    for what in every_f:
        gradient_copy(*what).wait()


def reduce_tokens(partials, gradients):
    n = lax.axis_size("seq")
    groups = n // INNER
    kinds = len(partials)
    _, _, tall, width = partials[0].shape
    _, _, rows, units = gradients[0].shape
    dma = pltpu.SemaphoreType.DMA
    return pl.pallas_call(
        functools.partial(reduce_body, n, kinds),
        out_shape=(jax.ShapeDtypeStruct((tall, width), F32),) * kinds
        + (jax.ShapeDtypeStruct((2, 2, 3, groups // 2, rows, units), BF16),),
        in_specs=[VMEM] * kinds + [ANY] * 3,
        out_specs=(VMEM,) * kinds + (ANY,),
        scratch_shapes=[
            pltpu.VMEM((kinds, groups, tall, width), BF16),
            pltpu.VMEM((kinds, groups + 1, tall, width), BF16),
            dma((kinds, groups)),
            dma((kinds, groups)),
            dma((kinds, groups)),
            dma((kinds, groups + 1)),
            dma((3, 2, 2)),
            dma((3, 2, 2)),
        ],
        compiler_params=params(7, 60),
        name="reduce_tokens",
    )(*partials, *gradients)


def scatter_body(
    n,
    one_ref,
    mixed_ref,
    dy_ref,
    dxb_ref,
    branch_ref,
    gate_ref,
    dpar_ref,
    gain_one_ref,
    gain_two_ref,
    column_ref,
    out_ref,
    small_out,
    spread_ref,
    made,
    got_q,
    got_p,
    got_z,
    got_s,
    *sems,
):
    send_q, recv_q, send_p, recv_p, send_z, recv_z, send_s, recv_s, send_f, recv_f, here = sems
    groups = n // INNER
    me, outer, by_x, by_y, by_xy = whereabouts()
    rows = one_ref.shape[1]
    part_rows = gate_ref.shape[2]
    total, width = out_ref.shape
    half = width // 2

    def place_of(turn):
        return far_first(groups, outer, turn)

    def base_of(turn):
        return (place_of(turn) - outer) * INNER

    barrier = pltpu.get_barrier_semaphore()

    def hello(peer):
        pl.semaphore_signal(barrier, inc=1, device_id={"seq": peer}, device_id_type=MESH)

    hello(by_x)
    hello(by_y)

    def hello_outer(turn, carry):
        hello(me + base_of(turn))
        return carry

    lax.fori_loop(0, groups - 1, hello_outer, 0)
    core = lax.axis_index("ch")
    masks = [1 << bit for bit in range(n.bit_length() - 1)]
    pl.semaphore_signal(barrier, inc=1, device_id={"ch": 1 - core}, device_id_type=MESH)
    pl.semaphore_wait(barrier, groups + 2)

    flips = ((by_x, by_y), (by_y, by_x))
    units = Units(spread_ref.shape[2], groups, core)

    def exchange(turn, receive=False):
        place = lax.rem(outer + (groups - 1 - turn if receive else turn + 1), groups)
        owner = place if receive else outer
        return Sized(
            units,
            owner,
            lambda width: remote(
                column_ref.at[:, place, :, pl.ds(0, width)],
                spread_ref.at[:, :, units.columns(owner, width)],
                send_f.at[turn],
                recv_f.at[turn],
                me + (place - outer) * INNER,
            ),
        )

    def small(turn):
        place = me
        for at, mask in enumerate(masks):
            flipped = me + mask * (1 - 2 * lax.rem(me // mask, 2))
            place = jnp.where(turn == at, flipped, place)
        other = jnp.where(turn == len(masks), 1 - core, core)
        return pltpu.make_async_remote_copy(
            src_ref=small_out,
            dst_ref=got_s.at[turn],
            send_sem=send_s.at[turn],
            recv_sem=recv_s.at[turn],
            device_id=(place, other),
            device_id_type=MESH,
        )

    small_out[:8] = dpar_ref[...]
    small_out[8:] = jnp.zeros((8, width), F32)
    at = 8
    for gain_ref in (gain_one_ref, gain_two_ref):
        for start in range(0, gain_ref.shape[1], width):
            small_out[at : at + 1] = gain_ref[:, start : start + width]
            at += 1
    small_row = lax.broadcasted_iota(jnp.int32, small_out.shape, 0)

    def cols(h):
        return pl.ds(h * half, half)

    def along_q(turn, h, other):
        source = (by_xy if other else flips[h][1]) + base_of(turn)
        return remote(
            made.at[source, :, cols(h)],
            got_q.at[h, turn, other],
            send_q.at[h, turn, other],
            recv_q.at[h, turn, other],
            flips[h][1],
        )

    def along_p(turn, h):
        return remote(
            made.at[flips[h][0] + base_of(turn), :, cols(h)],
            got_p.at[h, turn],
            send_p.at[h, turn],
            recv_p.at[h, turn],
            flips[h][0],
        )

    def along_z(turn, h):
        place = place_of(turn)
        up = place > outer
        onto = jnp.where(up, outer + 1, outer - 1)
        slot = jnp.where(jnp.logical_and(place == onto, jnp.logical_not(up)), groups, place)
        return remote(
            made.at[me + base_of(turn), :, cols(h)],
            got_z.at[h, slot],
            send_z.at[h, turn],
            recv_z.at[h, slot],
            me + (onto - outer) * INNER,
        )

    def landed(slot, h):
        return remote(
            made.at[me, :, cols(h)], got_z.at[h, slot], send_z.at[h, 0], recv_z.at[h, slot], by_x
        )

    def has_incoming(turn):
        return jnp.where(place_of(turn) > outer, outer > 0, outer < groups - 1)

    def pass_on(turn):
        incoming = has_incoming(turn)
        for h in range(2):

            @pl.when(incoming)
            def _():
                landed(place_of(turn), h).wait_recv()
                add(me + base_of(turn), h, got_z, (h, place_of(turn)))

            along_z(turn, h).start()

    def make(block):
        left = one_ref[block]
        parts = [
            jnp.dot(left, dy_ref[...], preferred_element_type=F32),
            jnp.dot(left, dxb_ref[...], preferred_element_type=F32),
            jnp.dot(mixed_ref[block], branch_ref[...], preferred_element_type=F32),
        ]
        if rows % 16 == 0:
            for at, part in enumerate(parts):
                made[block, at * rows : (at + 1) * rows] = part.astype(BF16)
            for gate in range(2):
                at = 3 * rows + gate * part_rows
                made[block, at : at + part_rows] = gate_ref[block, gate]
        else:
            parts.extend(gate_ref[block, gate].astype(F32) for gate in range(2))
            made[block] = jnp.concatenate(parts, axis=0).astype(BF16)

    step = 32

    def add(block, h, ref, index):
        def one(at, carry):
            r = pl.ds(pl.multiple_of(at * step, step), step)
            made[block, r, cols(h)] = (
                made[block, r, cols(h)].astype(F32) + ref[index + (r,)].astype(F32)
            ).astype(BF16)
            return carry

        lax.fori_loop(0, total // step, one, 0)

    keep = Sized(
        units,
        outer,
        lambda width: pltpu.make_async_copy(
            column_ref.at[:, outer, :, pl.ds(0, width)],
            spread_ref.at[:, :, units.columns(outer, width)],
            here,
        ),
    )
    keep.start()

    def begin(turn, other):
        base = base_of(turn)
        if other:
            make(by_xy + base)
        else:
            for h in range(2):
                make(flips[h][1] + base)
        for h in range(2):
            along_q(turn, h, other).start()

    begin(0, 1)
    begin(0, 0)
    make(me + base_of(0))

    def turn_of(turn, carry):
        pl.when(turn <= len(masks))(lambda: small(turn).start())
        pl.when(turn < groups - 1)(lambda: exchange(turn).start())

        @pl.when(turn < groups)
        def _():
            base = base_of(turn)
            for h in range(2):
                along_q(turn, h, 1).wait_recv()
                add(flips[h][0] + base, h, got_q, (h, turn, 1))
                along_p(turn, h).start()
            pl.when(turn < groups - 1)(lambda: begin(turn + 1, 1))
            for h in range(2):
                along_q(turn, h, 0).wait_recv()
                add(me + base, h, got_q, (h, turn, 0))

            @pl.when(turn < groups - 1)
            def _():
                begin(turn + 1, 0)
                make(me + base_of(turn + 1))

            for h in range(2):
                along_p(turn, h).wait_recv()
                add(me + base, h, got_p, (h, turn))

            @pl.when(jnp.logical_and(turn < groups - 1, jnp.logical_not(has_incoming(turn))))
            def _():
                pass_on(turn)

            @pl.when(jnp.logical_and(turn >= 1, turn < groups - 1))
            def _():
                pl.when(has_incoming(turn - 1))(lambda: pass_on(turn - 1))

            @pl.when(jnp.logical_and(turn == groups - 2, has_incoming(turn)))
            def _():
                pass_on(turn)

        @pl.when(turn <= len(masks))
        def _():
            small(turn).wait()
            counts = jnp.logical_or(turn < len(masks), small_row >= 8)
            small_out[...] = small_out[...] + jnp.where(counts, got_s[turn], 0.0)

        return carry

    assert len(masks) < groups + 2
    lax.fori_loop(0, groups + 2, turn_of, 0)
    for condition, slots in (
        (jnp.logical_and(outer > 0, outer < groups - 1), (outer, groups)),
        (outer == groups - 1, (outer,)),
        (outer == 0, (groups,)),
    ):

        @pl.when(condition)
        def _(slots=slots):
            for h in range(2):
                for slot in slots:
                    landed(slot, h).wait_recv()

                def finish(at, carry):
                    r = pl.ds(pl.multiple_of(at * step, step), step)
                    value = made[me, r, cols(h)].astype(F32)
                    for slot in slots:
                        value = value + got_z[h, slot, r].astype(F32)
                    out_ref[r, cols(h)] = value
                    return carry

                lax.fori_loop(0, total // step, finish, 0)

    def clear(turn, carry):
        for h in range(2):
            along_q(turn, h, 0).wait_send()
            along_q(turn, h, 1).wait_send()
            along_p(turn, h).wait_send()

            @pl.when(turn < groups - 1)
            def _():
                along_z(turn, h).wait_send()

        @pl.when(turn < groups - 1)
        def _():
            exchange(turn, True).wait_recv()
            exchange(turn).wait_send()

        return carry

    lax.fori_loop(0, groups, clear, 0)
    keep.wait()


def scatter_mixer(one, mixed, dy, dxb, branch, gates, dpar, gain_one, gain_two, column, hidden_units):
    n, rows, _ = one.shape
    groups = n // INNER
    width = dy.shape[1]
    total = 3 * rows + 2 * gates.shape[2]
    kinds = column.shape[0]
    turns = n.bit_length()
    dma = pltpu.SemaphoreType.DMA
    return pl.pallas_call(
        functools.partial(scatter_body, n),
        out_shape=(
            jax.ShapeDtypeStruct((total, width), F32),
            jax.ShapeDtypeStruct((16, width), F32),
            jax.ShapeDtypeStruct((kinds, rows, hidden_units), BF16),
        ),
        in_specs=[VMEM] * 9 + [ANY],
        out_specs=(VMEM, VMEM, ANY),
        scratch_shapes=[
            pltpu.VMEM((n, total, width), BF16),
            pltpu.VMEM((2, groups, 2, total, width // 2), BF16),
            pltpu.VMEM((2, groups, total, width // 2), BF16),
            pltpu.VMEM((2, groups + 1, total, width // 2), BF16),
            pltpu.VMEM((turns, 16, width), F32),
            dma((2, groups, 2)),
            dma((2, groups, 2)),
            dma((2, groups)),
            dma((2, groups)),
            dma((2, groups)),
            dma((2, groups + 1)),
            dma((turns,)),
            dma((turns,)),
            dma((groups,)),
            dma((groups,)),
            dma(()),
        ],
        compiler_params=params(2, 62),
        name="scatter_mixer",
    )(one, mixed, dy, dxb, branch, gates, dpar, gain_one, gain_two, column)


GELU_A = 0.7978845608028654
GELU_B = 0.044715


def gelu_parts(v):
    t = jnp.tanh(GELU_A * (v + GELU_B * v * v * v))
    value = 0.5 * v * (1.0 + t)
    slope = 0.5 * (1.0 + t) + 0.5 * v * (1.0 - t * t) * GELU_A * (1.0 + 3.0 * GELU_B * v * v)
    return value, slope


def gates_of(conv_low, gate_ref, par_ref, head, cols, first):
    size = gate_ref.shape[-1]
    weight_x, weight_a = (gate_ref[gate, head].reshape(size, size) for gate in range(2))
    pre_x = jnp.dot(conv_low, weight_x, preferred_element_type=F32)
    pre_a = jnp.dot(conv_low, weight_a, preferred_element_type=F32)
    gate_x = jax.nn.sigmoid(pre_x + par_ref[5:6, cols])
    gate_a = jax.nn.sigmoid(pre_a + par_ref[6:7, cols])
    decay = jnp.exp(-8.0 * gate_a * par_ref[8:9, cols])
    room = 1.0 - decay * decay
    mult = jnp.where(first, 1.0, jnp.sqrt(jnp.maximum(room, 0.001)))
    return gate_x, gate_a, decay, room, mult


FLIPPED = (((1,), (1,)), ((), ()))


def by_columns(ref, cols):
    if len(ref.shape) == 2:
        return ref[:, cols]
    return ref[:, :, cols].reshape(ref.shape[0] * ref.shape[1], -1)


def by_rows(ref, start, size):
    if len(ref.shape) == 2:
        return ref[start : start + size]
    rows = ref.shape[1]
    parts, at = [], start
    while at < start + size:
        block, inside = divmod(at, rows)
        upto = min(rows, inside + start + size - at)
        parts.append(ref[block, inside:upto])
        at += upto - inside
    return jnp.concatenate(parts, axis=0)


def first_row(tokens):
    row = lax.broadcasted_iota(jnp.int32, (tokens, 1), 0)
    return jnp.logical_and(row == 0, lax.axis_index("seq") == 0)


def forward_body(
    n,
    hidden_units,
    gathered,
    one_ref,
    last_ref,
    w_in_ref,
    w_branch_ref,
    w_out_ref,
    gate_ref,
    par_ref,
    x_ref,
    gain_ref,
    column_ref,
    cot_ref,
    xb_ref,
    yp_ref,
    conv_ref,
    state_ref,
    branch_ref,
    edge_ref,
    resid_ref,
    two_ref,
    near_ref,
    cots_ref,
    w_in,
    w_branch,
    w_out,
    mixed,
    mixed_got,
    wide,
    fade,
    mine,
    theirs,
    *sems,
):
    send_tot, recv_tot, send_f, recv_f, send_m, recv_m, loaded, kept = sems[:8]
    tokens, width = xb_ref.shape
    model = one_ref.shape[1]
    me = lax.axis_index("seq")
    size = gate_ref.shape[-1]
    loads = [
        pltpu.make_async_copy(src, dst, loaded.at[at])
        for at, (src, dst) in enumerate(
            ((w_in_ref, w_in), (w_branch_ref, w_branch), (w_out_ref, w_out))
        )
    ]
    core = lax.axis_index("ch")
    half = tokens // 2
    if gathered is None:
        for load in loads:
            load.start()
        greet_all(n, me, True)
        x_start = 0
    else:
        last, columns, rows_before, gather_finish, gates_load = gathered
        last(0)
        loads[0].start()
        rows_before()
        x_start = core * half
    _, _, by_x, by_y, _ = whereabouts()
    part = column_ref.shape[1] // 2
    kinds = column_ref.shape[0]
    units = Units(hidden_units, n // INNER, lax.axis_index("ch"))
    outer = me // INNER
    hosted = [
        [
            Sized(
                units,
                outer,
                lambda width, kind=kind, h=h, part=part: remote(
                    column_ref.at[kind, pl.ds(h * part, part), :, pl.ds(0, width)],
                    near_ref.at[h, kind, :, :, pl.ds(0, width)],
                    send_f.at[kind, h],
                    recv_f.at[kind, h],
                    (by_x, by_y)[h],
                ),
            )
            for h in range(2)
        ]
        for kind in range(kinds)
    ]

    def host(pieces):
        for pair in pieces:
            for copy in pair:
                copy.start()

    chain = Chain(n, cot_ref, cots_ref, *sems[8:])
    keep = chain.keep(kept)
    chain.start()
    keep.start()
    if gathered is None:
        host(hosted[:1])
    loads[0].wait()
    for start in range(0, width, size):
        cols = slice(start, start + size)
        low = jnp.dot(one_ref[...], by_columns(w_in, cols), preferred_element_type=F32).astype(BF16)
        xb_ref[:, cols] = low
        wide[8:, cols] = low.astype(F32)
        low = jnp.dot(last_ref[...], by_columns(w_in, cols), preferred_element_type=F32).astype(BF16)
        wide[:8, cols] = low.astype(F32)[8:]
    if gathered is not None:
        last(1)
        loads[1].start()
        last(3)
        gates_load.start()
        columns()
        host(hosted[:1])
        gates_load.wait()
    loads[1].wait()
    for start in range(0, width, size):
        cols = slice(start, start + size)
        yp_ref[:, cols] = jnp.dot(one_ref[...], by_columns(w_branch, cols), preferred_element_type=F32)

    if gathered is not None:
        last(2)
        loads[2].start()
    edge_ref[:8] = wide[:8]
    first = first_row(tokens)
    for head in range(width // size):
        cols = slice(head * size, (head + 1) * size)
        conv = par_ref[4:5, cols]
        for tap in range(4):
            conv = conv + par_ref[tap : tap + 1, cols] * wide[8 - tap : 8 - tap + tokens, cols]
        conv_low = conv.astype(BF16)
        conv_ref[:, cols] = conv_low
        gate_x, _, decay, _, mult = gates_of(conv_low, gate_ref, par_ref, head, cols, first)
        fade[:, cols] = decay
        state_ref[:, cols] = conv_low.astype(F32) * gate_x * mult

    row = lax.broadcasted_iota(jnp.int32, (8, width), 0)

    def inside(at, carry):
        r = pl.ds(pl.multiple_of(at * 8, 8), 8)
        a, b = fade[r], state_ref[r]
        for by in (1, 2, 4):
            a_back = pltpu.roll(a, by, 0)
            b_back = pltpu.roll(b, by, 0)
            b = jnp.where(row >= by, a * b_back + b, b)
            a = jnp.where(row >= by, a * a_back, a)
        fade[r] = a
        state_ref[r] = b
        return a[7:8] * carry[0], a[7:8] * carry[1] + b[7:8]

    ones, zeros = jnp.ones((1, width), F32), jnp.zeros((1, width), F32)
    tot_a, tot_b = lax.fori_loop(0, tokens // 8, inside, (ones, zeros))
    mine[0:1] = tot_a
    mine[1:2] = tot_b

    def told(place):
        return remote(mine, theirs.at[me], send_tot.at[place], recv_tot.at[me], place)

    def heard(place):
        return remote(mine, theirs.at[place], send_tot.at[place], recv_tot.at[place], place)

    def tell(place, carry):
        told(place).start()
        return carry

    lax.fori_loop(me + 1, n, tell, 0)
    host(hosted[1:])

    def hear(place, carry):
        heard(place).wait_recv()
        return carry

    lax.fori_loop(0, me, hear, 0)
    carry_in = zeros
    for place in range(n):
        gone = place < me
        through = jnp.where(gone, theirs[place, 0:1], 1.0)
        carry_in = through * carry_in + jnp.where(gone, theirs[place, 1:2], 0.0)
    edge_ref[8:] = jnp.broadcast_to(carry_in, (8, width))
    chain.step(1)

    def finish(at, carry):
        r = pl.ds(pl.multiple_of(at * 16, 16), 16)
        a, b = fade[r], state_ref[r]
        top = b[:8] + a[:8] * carry
        low = b[8:] + a[8:] * top[7:8]
        states = jnp.concatenate([top, low], axis=0)
        state_ref[r] = states
        branch_ref[r] = (states * gelu_parts(yp_ref[r])[0]).astype(BF16)
        return low[7:8]

    lax.fori_loop(0, tokens // 16, finish, carry_in)

    def sent(place, carry):
        told(place).wait_send()
        return carry

    lax.fori_loop(me + 1, n, sent, 0)
    loads[2].wait()
    for start in range(0, model, size):
        cols = slice(start, start + size)
        part = lax.dot_general(branch_ref[...], by_rows(w_out, start, size), FLIPPED, preferred_element_type=F32)
        mixed[0, :, cols] = part[:half]
        mixed[1, :, cols] = part[half:]
    exchange = pltpu.make_async_remote_copy(
        src_ref=mixed.at[1 - core],
        dst_ref=mixed_got,
        send_sem=send_m,
        recv_sem=recv_m,
        device_id={"ch": 1 - core},
        device_id_type=MESH,
    )
    exchange.start()
    exchange.wait_recv()

    def norm(at, carry):
        r = pl.ds(pl.multiple_of(at * 16, 16), 16)
        x = x_ref[pl.ds(pl.multiple_of(x_start + at * 16, 16), 16)]
        resid = x.astype(F32) + (mixed[core, r] + mixed_got[r])
        resid_ref[r] = resid
        scale = lax.rsqrt(jnp.mean(resid * resid, axis=-1, keepdims=True) + 1e-06)
        two_ref[r] = (resid * scale * gain_ref[...]).astype(BF16)
        return carry

    lax.fori_loop(0, half // 16, norm, 0)
    exchange.wait_send()
    for step in range(2, n // INNER):
        chain.step(step)
    for pair in hosted:
        for copy in pair:
            copy.wait()
    chain.finish()
    keep.wait()
    if gathered is not None:
        gather_finish()


def first_body(n, hidden_units, *refs):
    given, refs = refs[:12], refs[12:]
    weights, gates, ffn, (x_ref, gains_ref, par_ref, all_cot_ref) = (
        given[:3],
        given[3:5],
        given[5:8],
        given[8:],
    )
    outs, refs = refs[:18], refs[18:]
    scratch, sems = refs[:10], refs[10:]
    gather_sems, forward_sems, gate_sem = sems[:7], sems[7:-1], sems[-1]
    me = lax.axis_index("seq")
    norm_ref, gain_ref = gains_ref.at[pl.ds(0, 1)], gains_ref.at[pl.ds(1, 1)]
    half = x_ref.shape[0] // 2
    start = pl.multiple_of(lax.axis_index("ch") * half, half)
    cot_ref = all_cot_ref.at[pl.ds(start, half)]
    greet_all(n, me, True)
    steps = gather_begin(
        n, (*weights, *gates, *ffn, x_ref, norm_ref, *outs[:8], *gather_sems), True
    )
    gate_s, scratch = scratch[0], scratch[1:]
    full_gates, column_ref, one_ref, _, last_ref = outs[3:8]
    gates_load = pltpu.make_async_copy(full_gates, gate_s, gate_sem)
    forward_body(
        n,
        hidden_units,
        (*steps, gates_load),
        one_ref,
        last_ref,
        *outs[:3],
        gate_s,
        par_ref,
        x_ref,
        gain_ref,
        column_ref,
        cot_ref,
        *outs[8:],
        *scratch,
        *forward_sems,
    )


def mixer_forward(one, last, weights, gates, par, x_half, gain, column, cotangent, hidden_units):
    n = lax.axis_size("seq")
    tokens, model = one.shape
    width = par.shape[1]
    half = tokens // 2
    kinds, groups, rows, units = column.shape
    dma = pltpu.SemaphoreType.DMA
    whole = jax.ShapeDtypeStruct((tokens, width), F32)
    low = jax.ShapeDtypeStruct((tokens, width), BF16)
    return pl.pallas_call(
        functools.partial(forward_body, n, hidden_units, None),
        out_shape=(
            low,
            whole,
            low,
            whole,
            low,
            jax.ShapeDtypeStruct((16, width), F32),
            jax.ShapeDtypeStruct((half, model), F32),
            jax.ShapeDtypeStruct((half, model), BF16),
            jax.ShapeDtypeStruct((2, kinds, groups // 2, rows, units), column.dtype),
            jax.ShapeDtypeStruct((groups, 2) + cotangent.shape, cotangent.dtype),
        ),
        in_specs=[VMEM] * 2 + [HBM] * 3 + [VMEM] * 4 + [HBM, HBM],
        out_specs=(VMEM,) * 8 + (HBM, HBM),
        scratch_shapes=[
            pltpu.VMEM((model, width), BF16),
            pltpu.VMEM((model, width), BF16),
            pltpu.VMEM((model, width), BF16),
            pltpu.VMEM((2, half, model), F32),
            pltpu.VMEM((half, model), F32),
            pltpu.VMEM((tokens + 8, width), F32),
            pltpu.VMEM((tokens, width), F32),
            pltpu.VMEM((2, width), F32),
            pltpu.VMEM((n, 2, width), F32),
            dma((n,)),
            dma((n,)),
            dma((kinds, 2)),
            dma((kinds, 2)),
            dma(()),
            dma(()),
            dma((3,)),
            dma(()),
            *chain_semaphores(groups),
        ],
        compiler_params=params(4, 60),
        name="mixer_forward",
    )(one, last, *weights, gates, par, x_half, gain, column, cotangent)


def gather_forward(weights, gates, ffn, x, gains, par, cotangent):
    n = lax.axis_size("seq")
    groups = n // INNER
    tokens, model = x.shape
    rows, width = weights[0].shape
    half = tokens // 2
    hidden_units = ffn[0].shape[1]
    most = Units(hidden_units, groups, 0).most
    heads, part, size = gates[0].shape
    dma = pltpu.SemaphoreType.DMA
    shape = jax.ShapeDtypeStruct
    whole, low = shape((tokens, width), F32), shape((tokens, width), BF16)
    weight = pltpu.VMEM((n, rows, width), BF16)
    return pl.pallas_call(
        functools.partial(first_body, n, hidden_units),
        out_shape=(
            *(shape((n, rows, width), BF16) for _ in range(3)),
            shape((2, heads, n, part, size), BF16),
            shape((3, groups, rows, most), BF16),
            shape((tokens, model), BF16),
            shape((model, tokens), BF16),
            shape((16, model), BF16),
            low,
            whole,
            low,
            whole,
            low,
            shape((16, width), F32),
            shape((half, model), F32),
            shape((half, model), BF16),
            shape((2, 3, groups // 2, rows, most), BF16),
            shape((groups, 2, half, model), BF16),
        ),
        in_specs=[HBM] * 8 + [VMEM] * 3 + [HBM],
        out_specs=(HBM,) * 5 + (VMEM,) * 11 + (HBM,) * 2,
        scratch_shapes=[
            pltpu.VMEM((2, heads, n, part, size), BF16),
            weight,
            weight,
            weight,
            pltpu.VMEM((2, half, model), F32),
            pltpu.VMEM((half, model), F32),
            pltpu.VMEM((tokens + 8, width), F32),
            pltpu.VMEM((tokens, width), F32),
            pltpu.VMEM((2, width), F32),
            pltpu.VMEM((n, 2, width), F32),
            dma((4, 2, n, 4)),
            dma((4, 2, n)),
            dma((3, groups)),
            dma((3, groups)),
            dma((8,)),
            dma(()),
            dma(()),
            dma((n,)),
            dma((n,)),
            dma((3, 2)),
            dma((3, 2)),
            dma(()),
            dma(()),
            dma((3,)),
            dma(()),
            *chain_semaphores(groups),
            dma(()),
        ],
        compiler_params=params(9, 60),
        name="gather_forward",
    )(*weights, *gates, *ffn, x, gains, par, cotangent)


def backward_body(
    n,
    hidden_units,
    mixed_ref,
    w_in_ref,
    w_branch_ref,
    w_out_ref,
    x_ref,
    gain_ref,
    resid_ref,
    yp_ref,
    state_ref,
    edge_ref,
    conv_ref,
    xb_ref,
    gate_ref,
    par_ref,
    half_ref,
    own_ref,
    dy_ref,
    dxb_ref,
    dgate_ref,
    dpar_ref,
    dx_ref,
    dgain_ref,
    column_ref,
    near_ref,
    own,
    w_in,
    w_branch,
    w_out,
    d_one,
    d_one_got,
    d_one_part,
    fade,
    shift,
    adj,
    gate_x_s,
    gate_a_s,
    dconv,
    wide,
    mine,
    theirs,
    head_rows,
    *sems,
):
    send_rows, recv_rows, send_tot, recv_tot, send_f, recv_f, send_m, recv_m, send_x, recv_x, loaded, own_sem, out_sem = sems
    tokens, width = xb_ref.shape
    model = gain_ref.shape[1]
    me = lax.axis_index("seq")
    size = gate_ref.shape[2]
    loads = [
        pltpu.make_async_copy(src, dst, loaded.at[at])
        for at, (src, dst) in enumerate(
            ((w_out_ref, w_out), (w_in_ref, w_in), (w_branch_ref, w_branch))
        )
    ]
    for load in loads:
        load.start()
    greet_all(n, me, True)
    _, _, by_x, by_y, _ = whereabouts()
    kinds, pieces = half_ref.shape[1:3]
    units = Units(hidden_units, n // INNER, lax.axis_index("ch"))
    outer = me // INNER
    hosted = [
        [
            Sized(
                units,
                outer,
                lambda width, kind=kind, at=at, h=h: remote(
                    half_ref.at[h, kind, at, :, pl.ds(0, width)],
                    near_ref.at[h, kind, at, :, pl.ds(0, width)],
                    send_f.at[kind, at, h],
                    recv_f.at[kind, at, h],
                    (by_x, by_y)[h],
                ),
            )
            for h in range(2)
        ]
        for kind in range(kinds)
        for at in range(pieces)
    ]

    def host(some):
        for pair in some:
            for copy in pair:
                copy.start()

    host(hosted[:2])
    own_load = pltpu.make_async_copy(own_ref, own, own_sem)
    own_load.start()
    first = first_row(tokens)
    fade[tokens:] = jnp.ones((8, width), F32)
    loads[0].wait()
    for head in range(width // size):
        cols = slice(head * size, (head + 1) * size)
        gate_x, gate_a, decay, _, _ = gates_of(conv_ref[:, cols], gate_ref, par_ref, head, cols, first)
        gate_x_s[:, cols] = gate_x
        gate_a_s[:, cols] = gate_a
        fade[:tokens, cols] = decay
        value, slope = gelu_parts(yp_ref[:, cols])
        grad = jnp.dot(mixed_ref[...], w_out[:, cols], preferred_element_type=F32)
        dy_ref[:, cols] = (grad * state_ref[:, cols] * slope).astype(BF16)
        adj[:, cols] = grad * value
        shift[:, cols] = fade[1 : tokens + 1, cols]

    row = lax.broadcasted_iota(jnp.int32, (8, width), 0)
    tiles = tokens // 8

    def inside(turn, carry):
        r = pl.ds(pl.multiple_of((tiles - 1 - turn) * 8, 8), 8)
        a, b = shift[r], adj[r]
        for by in (1, 2, 4):
            a_next = pltpu.roll(a, 8 - by, 0)
            b_next = pltpu.roll(b, 8 - by, 0)
            b = jnp.where(row < 8 - by, a * b_next + b, b)
            a = jnp.where(row < 8 - by, a * a_next, a)
        shift[r] = a
        adj[r] = b
        return a[0:1] * carry[0], a[0:1] * carry[1] + b[0:1]

    ones, zeros = jnp.ones((1, width), F32), jnp.zeros((1, width), F32)
    tot_a, tot_b = lax.fori_loop(0, tiles, inside, (ones, zeros))
    first_fade = fade[0:1]
    mine[0:1] = first_fade * tot_a
    mine[1:2] = first_fade * tot_b

    def told(place):
        return remote(mine, theirs.at[me], send_tot.at[place], recv_tot.at[me], place)

    def heard(place):
        return remote(mine, theirs.at[place], send_tot.at[place], recv_tot.at[place], place)

    def tell(place, carry):
        told(place).start()
        return carry

    lax.fori_loop(0, me, tell, 0)
    host(hosted[2:3])

    def hear(turn, carry):
        heard(n - 1 - turn).wait_recv()
        return carry

    lax.fori_loop(0, n - 1 - me, hear, 0)
    carry_in = zeros
    for place in reversed(range(n)):
        gone = place > me
        through = jnp.where(gone, theirs[place, 0:1], 1.0)
        carry_in = through * carry_in + jnp.where(gone, theirs[place, 1:2], 0.0)

    def finish(turn, carry):
        r = pl.ds(pl.multiple_of((tiles - 1 - turn) * 8, 8), 8)
        value = adj[r] + shift[r] * carry
        adj[r] = value
        return value[0:1]

    lax.fori_loop(0, tiles, finish, carry_in)

    wide[:8] = edge_ref[:8]
    wide[8:] = xb_ref[...].astype(F32)
    at_first = lax.broadcasted_iota(jnp.int32, (tokens, 1), 0) == 0
    for head in range(width // size):
        cols = slice(head * size, (head + 1) * size)
        conv_low = conv_ref[:, cols]
        conv = conv_low.astype(F32)
        gate_x, gate_a, decay = gate_x_s[:, cols], gate_a_s[:, cols], fade[:tokens, cols]
        room = 1.0 - decay * decay
        mult = jnp.where(first, 1.0, jnp.sqrt(jnp.maximum(room, 0.001)))
        back = adj[:, cols]
        before = jnp.where(at_first, edge_ref[8:9, cols], pltpu.roll(state_ref[:, cols], 1, 0))
        d_mult = back * conv * gate_x
        moves = jnp.logical_and(room > 0.001, jnp.logical_not(first))
        d_decay = back * before - jnp.where(moves, d_mult * decay / mult, 0.0)
        d_log = d_decay * decay
        d_pre_x = back * conv * mult * gate_x * (1.0 - gate_x)
        d_pre_a = d_log * (-8.0 * par_ref[8:9, cols]) * gate_a * (1.0 - gate_a)
        dpar_ref[5:6, cols] = jnp.sum(d_pre_x, axis=0, keepdims=True)
        dpar_ref[6:7, cols] = jnp.sum(d_pre_a, axis=0, keepdims=True)
        dpar_ref[7:8, cols] = (
            jnp.sum(d_log * (-8.0 * gate_a), axis=0, keepdims=True) * par_ref[9:10, cols]
        )
        low_x, low_a = d_pre_x.astype(BF16), d_pre_a.astype(BF16)
        d_conv = (
            back * gate_x * mult
            + lax.dot_general(low_x, gate_ref[0, head], FLIPPED, preferred_element_type=F32)
            + lax.dot_general(low_a, gate_ref[1, head], FLIPPED, preferred_element_type=F32)
        )
        dconv[:tokens, cols] = d_conv
        over_rows = (((0,), (0,)), ((), ()))
        for gate, low in enumerate((low_x, low_a)):
            d_gate = lax.dot_general(conv_low, low, over_rows, preferred_element_type=F32)
            dgate_ref[:, gate, :, cols] = d_gate.astype(BF16).reshape(n, size // n, size)
        dpar_ref[4:5, cols] = jnp.sum(d_conv, axis=0, keepdims=True)
        for tap in range(4):
            dpar_ref[tap : tap + 1, cols] = jnp.sum(
                d_conv * wide[8 - tap : 8 - tap + tokens, cols], axis=0, keepdims=True
            )

    rows_copy = remote(
        dconv.at[pl.ds(0, 8)], head_rows, send_rows, recv_rows, lax.rem(me + n - 1, n)
    )
    pl.when(me > 0)(rows_copy.start)
    host(hosted[3:])
    loads[2].wait()
    for start in range(0, model, size):
        cols = slice(start, start + size)
        d_one_part[:, cols] = lax.dot_general(
            dy_ref[...], w_branch[cols], FLIPPED, preferred_element_type=F32
        )

    rows = own.shape[3]
    chunk = 32 if rows % 32 == 0 else rows
    outs = []

    def collect(piece):
        kind, at = divmod(piece, pieces)
        for h in range(2):
            hosted[piece][h].wait()

            def add(turn, carry, h=h):
                r = pl.ds(pl.multiple_of(turn * chunk, chunk), chunk)
                own[h, kind, at, r] = (
                    own[h, kind, at, r].astype(F32) + near_ref[h, kind, at, r].astype(F32)
                ).astype(BF16)
                return carry

            lax.fori_loop(0, rows // chunk, add, 0)
            outs.append(
                pltpu.make_async_copy(
                    own.at[h, kind, at],
                    column_ref.at[kind, h * pieces + at],
                    out_sem.at[kind, at, h],
                )
            )
            outs[-1].start()

    own_load.wait()
    for piece in range(3):
        collect(piece)

    @pl.when(me + 1 < n)
    def _():
        rows_copy.wait_recv()
        dconv[tokens:] = head_rows[...]

    @pl.when(me + 1 == n)
    def _():
        dconv[tokens:] = jnp.zeros((8, width), F32)

    for head in range(width // size):
        cols = slice(head * size, (head + 1) * size)
        total = par_ref[0:1, cols] * dconv[:tokens, cols]
        for tap in range(1, 4):
            total = total + par_ref[tap : tap + 1, cols] * dconv[tap : tap + tokens, cols]
        dxb_ref[:, cols] = total.astype(BF16)

    pl.when(me > 0)(rows_copy.wait_send)

    def sent(place, carry):
        told(place).wait_send()
        return carry

    lax.fori_loop(0, me, sent, 0)
    core = lax.axis_index("ch")
    half = tokens // 2
    loads[1].wait()
    for start in range(0, model, size):
        cols = slice(start, start + size)
        part = (
            d_one_part[:, cols]
            + lax.dot_general(dxb_ref[...], w_in[cols], FLIPPED, preferred_element_type=F32)
        ).astype(BF16)
        d_one[0, :, cols] = part[:half]
        d_one[1, :, cols] = part[half:]
    exchange = pltpu.make_async_remote_copy(
        src_ref=d_one.at[1 - core],
        dst_ref=d_one_got,
        send_sem=send_m,
        recv_sem=recv_m,
        device_id={"ch": 1 - core},
        device_id_type=MESH,
    )
    exchange.start()
    exchange.wait_recv()

    def norm(at, total):
        r = pl.ds(pl.multiple_of(at * 16, 16), 16)
        x = x_ref[pl.ds(pl.multiple_of(core * half + at * 16, 16), 16)].astype(F32)
        scale = lax.rsqrt(jnp.mean(x * x, axis=-1, keepdims=True) + 1e-06)
        grad = d_one[core, r].astype(F32) + d_one_got[r].astype(F32)
        back = grad * gain_ref[...]
        shrink = scale * scale * scale * jnp.mean(x * back, axis=-1, keepdims=True)
        dx_ref[core, r] = resid_ref[r] + (scale * back - x * shrink)
        return total + jnp.sum(grad * (x * scale), axis=0, keepdims=True)

    dgain_ref[...] = lax.fori_loop(0, half // 16, norm, jnp.zeros((1, model), F32))
    share = pltpu.make_async_remote_copy(
        src_ref=dx_ref.at[core],
        dst_ref=dx_ref.at[core],
        send_sem=send_x,
        recv_sem=recv_x,
        device_id={"ch": 1 - core},
        device_id_type=MESH,
    )
    share.start()
    exchange.wait_send()
    for piece in range(3, len(hosted)):
        collect(piece)
    for copy in outs:
        copy.wait()
    pltpu.make_async_remote_copy(
        src_ref=dx_ref.at[core],
        dst_ref=dx_ref.at[1 - core],
        send_sem=send_x,
        recv_sem=recv_x,
        device_id={"ch": 1 - core},
        device_id_type=MESH,
    ).wait_recv()
    share.wait_send()


def mixer_backward(
    mixed, weights, x_half, gain, d_resid, y_pre, states, edge, conv, x_branch, gates, par, halves, own, hidden_units
):
    n = lax.axis_size("seq")
    tokens, width = x_branch.shape
    model = mixed.shape[1]
    size = gates.shape[2]
    half = tokens // 2
    _, kinds, part, rows, units = halves.shape
    dma = pltpu.SemaphoreType.DMA
    whole = pltpu.VMEM((tokens, width), F32)
    longer = pltpu.VMEM((tokens + 8, width), F32)
    weight = pltpu.VMEM((model, width), BF16)
    return pl.pallas_call(
        functools.partial(backward_body, n, hidden_units),
        out_shape=(
            jax.ShapeDtypeStruct((tokens, width), BF16),
            jax.ShapeDtypeStruct((tokens, width), BF16),
            jax.ShapeDtypeStruct((n, 2, size // n, width), BF16),
            jax.ShapeDtypeStruct((8, width), F32),
            jax.ShapeDtypeStruct((2, half, model), F32),
            jax.ShapeDtypeStruct((1, model), F32),
            jax.ShapeDtypeStruct((kinds, 2 * part, rows, units), BF16),
        ),
        in_specs=[VMEM] + [HBM] * 3 + [VMEM] * 10 + [HBM, HBM],
        out_specs=(VMEM,) * 6 + (HBM,),
        scratch_shapes=[
            pltpu.VMEM(halves.shape, BF16),
            pltpu.VMEM(halves.shape, BF16),
            weight,
            weight,
            weight,
            pltpu.VMEM((2, half, model), BF16),
            pltpu.VMEM((half, model), BF16),
            pltpu.VMEM((tokens, model), F32),
            longer,
            whole,
            whole,
            whole,
            whole,
            longer,
            longer,
            pltpu.VMEM((2, width), F32),
            pltpu.VMEM((n, 2, width), F32),
            pltpu.VMEM((8, width), F32),
            dma(()),
            dma(()),
            dma((n,)),
            dma((n,)),
            dma((kinds, part, 2)),
            dma((kinds, part, 2)),
            dma(()),
            dma(()),
            dma(()),
            dma(()),
            dma((3,)),
            dma(()),
            dma((kinds, part, 2)),
        ],
        compiler_params=params(5, 60),
        name="mixer_backward",
    )(mixed, *weights, x_half, gain, d_resid, y_pre, states, edge, conv, x_branch, gates, par, halves, own)


def ffn_body(n, hidden_units, *refs):
    own_ref, cots_ref, column_ref, near_ref, resid_ref, gain_ref = refs[:6]
    block_ref, d_resid_ref, mixed_ref, d_gain_ref, turned_ref = refs[6:11]
    halves_ref, mine_ref, far_ref = refs[11:14]
    tokens, cots, w, extra, hidden, box, sib, got, stage, turned, my_cot = refs[14:25]
    token_sems = refs[25:28]
    send_w, recv_w, keep_w, keep_c, keep_t, keep_m = refs[28:34]
    send_c, recv_s, send_z, recv_r, send_f, recv_f, send_m, recv_m, move, out_sem = refs[34:]
    groups = n // INNER
    half = groups // 2
    me, outer, by_x, by_y, by_xy = whereabouts()
    base = outer * INNER
    core = lax.axis_index("ch")
    above, below = outer + 1 < groups, outer > 0
    sibling = {"ch": 1 - core}
    barrier = pltpu.get_barrier_semaphore()

    def hello(peer):
        pl.semaphore_signal(barrier, inc=1, device_id=peer, device_id_type=MESH)

    hello({"seq": by_x})
    hello({"seq": by_y})
    hello(sibling)
    pl.when(above)(lambda: hello({"seq": me + INNER}))
    pl.when(below)(lambda: hello({"seq": me - INNER}))
    pl.semaphore_wait(barrier, 3 + above.astype(jnp.int32) + below.astype(jnp.int32))
    flips = ((by_x, by_y), (by_y, by_x))
    rows, units = w.shape[3], w.shape[4]
    split = Units(hidden_units, groups, core)
    tall, model = own_ref.shape
    count = 2 * tall
    deep = INNER * rows
    tile = 256

    def part(h):
        return pl.ds(h * half, half)


    chain_t = Chain(n, own_ref, tokens, *token_sems)

    def weight_copy(kind, h, far, receive=False):
        source = flips[h][0] if far else me
        if receive:
            source = by_xy if far else flips[h][1]
        src = near_ref.at[h, kind] if far else column_ref.at[kind, part(h)]
        return Sized(
            split,
            outer,
            lambda width: remote(
                src.at[:, :, pl.ds(0, width)],
                w.at[kind, part(h), source - base, :, pl.ds(0, width)],
                send_w.at[kind, h, far],
                recv_w.at[kind, h, far],
                flips[h][1],
            ),
        )

    keep = [
        [
            pltpu.make_async_copy(
                column_ref.at[kind], w.at[kind, :, me - base], keep_w.at[kind, 0]
            ),
            *(
                pltpu.make_async_copy(
                    near_ref.at[h, kind],
                    w.at[kind, part(h), flips[h][0] - base],
                    keep_w.at[kind, 1 + h],
                )
                for h in range(2)
            ),
        ]
        for kind in range(3)
    ]
    every = [(h, far) for far in range(2) for h in range(2)]
    own_t = chain_t.keep(keep_t)
    load_c = pltpu.make_async_copy(cots_ref, cots, keep_c)
    load_m = pltpu.make_async_copy(cots_ref.at[outer, core], my_cot, keep_m)
    chain_t.start()
    for kind in range(3):
        for h, far in every:
            weight_copy(kind, h, far).start()
    own_t.start()
    load_c.start()
    load_m.start()
    for kind in range(3):
        for copy in keep[kind]:
            copy.start()
    for step in range(1, groups):
        chain_t.step(step)
    chain_t.finish()
    own_t.wait()

    def weights_landed(kind):
        for h, far in every:
            weight_copy(kind, h, far, True).wait_recv()
        for copy in keep[kind]:
            copy.wait()
        if not split.even:

            @pl.when(jnp.logical_not(split.full(outer)))
            def _():
                rest = jnp.zeros((groups, INNER, rows, LANES), BF16)
                w[kind, :, :, :, units - LANES :] = rest

    def columns(kind, at):
        return w[kind, :, :, :, at : at + tile].reshape(model, tile)

    def token_rows(place):
        return pl.ds(pl.multiple_of(place * count, count), count)

    def each(limit, action):
        def one(turn, carry):
            action(turn)
            return carry

        lax.fori_loop(0, limit, one, 0)

    weights_landed(0)
    weights_landed(1)

    def middle(place):
        left = tokens[place].reshape(count, model)
        r = token_rows(place)
        for at in range(0, units, tile):
            c = slice(at, at + tile)
            gate = jnp.dot(left, columns(0, at), preferred_element_type=F32)
            up = jnp.dot(left, columns(1, at), preferred_element_type=F32)
            value, slope = gelu_parts(gate)
            hidden[0, r, c] = (value * up).astype(BF16)
            hidden[1, r, c] = (up * slope).astype(BF16)
            hidden[2, r, c] = value.astype(BF16)

    each(groups, middle)
    def back_hidden(place):
        left = cots[place].reshape(count, model)
        r = token_rows(place)
        for at in range(0, units, tile):
            c = slice(at, at + tile)
            back = jnp.dot(left, columns(2, at), preferred_element_type=F32)
            for kind in (1, 2):
                hidden[kind, r, c] = (back * hidden[kind, r, c].astype(F32)).astype(BF16)


    boxes = (cots, box)

    def partial(kind, place):
        r = token_rows(place)
        for at in range(groups):
            pairs = ((1, 0), (2, 1)) if kind == 0 else ((0, 2),)
            value = 0.0
            for left, right in pairs:
                value = value + lax.dot_general(
                    hidden[left, r],
                    w[right, at].reshape(deep, units),
                    FLIPPED,
                    preferred_element_type=F32,
                )
            value = value.astype(BF16)
            boxes[kind][place, 0, :, at * deep : (at + 1) * deep] = value[:tall]
            boxes[kind][place, 1, :, at * deep : (at + 1) * deep] = value[tall:]
        to_sibling(kind, place).start()

    def to_sibling(kind, place):
        return pltpu.make_async_remote_copy(
            src_ref=boxes[kind].at[place, 1 - core],
            dst_ref=sib.at[kind, place],
            send_sem=send_c.at[kind, place],
            recv_sem=recv_s.at[kind, place],
            device_id=sibling,
            device_id_type=MESH,
        )

    def along(kind, place, up):
        last = place == (outer + 1 if up else outer - 1)
        slot = place if up else jnp.where(last, groups, place)
        return remote(
            boxes[kind].at[place, core],
            got.at[kind, slot],
            send_z.at[kind, place],
            recv_r.at[kind, slot],
            me + (INNER if up else -INNER),
        )

    def landed(kind, slot):
        return remote(
            box.at[0, core], got.at[kind, slot], send_z.at[kind, 0], recv_r.at[kind, slot], by_x
        )

    chunk = 32

    def rows_of(at):
        return pl.ds(pl.multiple_of(at * chunk, chunk), chunk)

    def ready(kind, place, incoming):
        to_sibling(kind, place).wait_recv()

        def add(at, with_got):
            r = rows_of(at)
            value = boxes[kind][place, core, r].astype(F32) + sib[kind, place, r].astype(F32)
            if with_got:
                value = value + got[kind, place, r].astype(F32)
            boxes[kind][place, core, r] = value.astype(BF16)

        @pl.when(incoming)
        def _():
            landed(kind, place).wait_recv()
            each(tall // chunk, lambda at: add(at, True))

        @pl.when(jnp.logical_not(incoming))
        def _():
            each(tall // chunk, lambda at: add(at, False))

    def pass_on(kind, turn):
        ups = groups - 1 - outer
        upper = jnp.where(outer < half, turn < ups, turn >= outer)
        later = jnp.where(outer < half, turn, turn - outer)
        earlier = jnp.where(outer < half, turn - ups, turn)

        @pl.when(upper)
        def _():
            place = groups - 1 - later
            ready(kind, place, below)
            along(kind, place, True).start()

        @pl.when(jnp.logical_not(upper))
        def _():
            ready(kind, earlier, above)
            along(kind, earlier, False).start()

    at_end = jnp.logical_or(outer == 0, outer == groups - 1)

    def partials(kind, start, stop):
        def one(turn, carry):
            partial(kind, far_first(groups, outer, turn))

            @pl.when(jnp.logical_and(at_end, turn >= 1))
            def _():
                pass_on(kind, turn - 1)

            return carry

        lax.fori_loop(start, stop, one, 0)

    def between(kind, turns):
        @pl.when(jnp.logical_not(at_end))
        def _():
            for turn in turns:
                pass_on(kind, turn)

    def totals(kind, use):
        to_sibling(kind, outer).wait_recv()
        for condition, slots in (
            (jnp.logical_and(below, above), (outer, groups)),
            (jnp.logical_and(below, jnp.logical_not(above)), (outer,)),
            (jnp.logical_and(jnp.logical_not(below), above), (groups,)),
        ):

            @pl.when(condition)
            def _(slots=slots):
                for slot in slots:
                    landed(kind, slot).wait_recv()

                def one(at):
                    r = rows_of(at)
                    value = boxes[kind][outer, core, r].astype(F32) + sib[kind, outer, r].astype(F32)
                    for slot in slots:
                        value = value + got[kind, slot, r].astype(F32)
                    use(r, value)

                each(tall // chunk, one)

    def clear(kind):
        def one(place):
            to_sibling(kind, place).wait_send()

            @pl.when(place > outer)
            def _():
                along(kind, place, True).wait_send()

            @pl.when(place < outer)
            def _():
                along(kind, place, False).wait_send()

        each(groups, one)


    made = (w.at[0], w.at[1], extra)

    def gradient_copy(kind, h, far):
        source = by_xy if far else flips[h][1]
        return Sized(
            split,
            outer,
            lambda width: remote(
                made[kind].at[part(h), source - base, :, pl.ds(0, width)],
                far_ref.at[h, far, kind, :, :, pl.ds(0, width)],
                send_f.at[kind, h, far],
                recv_f.at[kind, h, far],
                flips[h][1],
            ),
        )

    def gradients(kinds, source, h):
        for at in range(h * half, (h + 1) * half):
            left = source[:, :, :, at * deep : (at + 1) * deep].reshape(groups * count, deep)
            turned[...] = left.T
            for kind, right in kinds:
                for start in range(0, units, tile):
                    c = slice(start, start + tile)
                    made[kind][at, :, :, c] = (
                        jnp.dot(turned[...], hidden[right, :, c], preferred_element_type=F32)
                        .astype(BF16)
                        .reshape(INNER, rows, tile)
                    )
        for kind, _ in kinds:
            for far in (1, 0):
                gradient_copy(kind, h, far).start()

    def collect(kind, h, far):
        inner = (flips[h][0] if far else me) - base
        gradient_copy(kind, h, far).wait_recv()
        load = pltpu.make_async_copy(far_ref.at[h, far, kind], stage, move)
        load.start()
        load.wait()
        for place in range(half):
            at = h * half + place

            def one(turn, place=place, at=at):
                r = rows_of(turn)
                made[kind][at, inner, r] = (
                    made[kind][at, inner, r].astype(F32) + stage[place, r].astype(F32)
                ).astype(BF16)

            each(rows // chunk, one)
        out_copy(kind, h, far).start()

    def out_copy(kind, h, far):
        inner = (flips[h][0] if far else me) - base
        return pltpu.make_async_copy(
            made[kind].at[part(h), inner],
            (halves_ref if far else mine_ref).at[h, kind],
            out_sem.at[kind, h, far],
        )

    load_c.wait()
    gradients(((2, 0),), cots, 0)
    gradients(((2, 0),), cots, 1)
    weights_landed(2)
    for kind in range(3):
        for h, far in every:
            weight_copy(kind, h, far).wait_send()
    partials(1, 0, groups)
    each(groups, back_hidden)
    load_m.wait()
    partials(0, 0, half)
    between(1, range(1))
    partials(0, half, groups)
    gradients(((0, 1),), tokens, 0)
    between(1, range(1, half))
    gradients(((0, 1),), tokens, 1)
    gradients(((1, 2),), tokens, 0)
    between(1, range(half, groups - 1))
    gradients(((1, 2),), tokens, 1)

    def shared(ref, at, part):
        return pltpu.make_async_remote_copy(
            src_ref=ref.at[core],
            dst_ref=ref.at[part],
            send_sem=send_m.at[at],
            recv_sem=recv_m.at[at],
            device_id=sibling,
            device_id_type=MESH,
        )

    def finish(r, value):
        block_ref[core, r] = (resid_ref[r] + value).astype(BF16)

    d_gain_ref[...] = jnp.zeros((1, model), F32)

    def norm(r, grad):
        resid = resid_ref[r]
        scale = lax.rsqrt(jnp.mean(resid * resid, axis=-1, keepdims=True) + 1e-06)
        back = grad * gain_ref[...]
        shrink = scale * scale * scale * jnp.mean(resid * back, axis=-1, keepdims=True)
        value = my_cot[r].astype(F32) + (scale * back - resid * shrink)
        d_resid_ref[r] = value
        mixed_ref[core, r] = value.astype(BF16)
        d_gain_ref[...] = d_gain_ref[...] + jnp.sum(grad * (resid * scale), axis=0, keepdims=True)

    for far in (1, 0):
        for h in range(2):
            collect(2, h, far)
    between(0, range(1))
    totals(1, finish)
    show = shared(block_ref, 1, core)
    show.start()
    for far in (1, 0):
        for h in range(2):
            collect(0, h, far)
    between(0, range(1, groups - 1))
    totals(0, norm)
    share = shared(mixed_ref, 0, core)
    share.start()
    shared(mixed_ref, 0, 1 - core).wait_recv()
    for start in range(0, model, tile):
        c = slice(start, start + tile)
        turned_ref[c, :tall] = mixed_ref[0, :, c].T
        turned_ref[c, tall:] = mixed_ref[1, :, c].T
    for far in (1, 0):
        for h in range(2):
            collect(1, h, far)
    clear(0)
    clear(1)
    shared(block_ref, 1, 1 - core).wait_recv()
    share.wait_send()
    show.wait_send()
    for kind in range(3):
        for h, far in every:
            gradient_copy(kind, h, far).wait_send()
            out_copy(kind, h, far).wait()


def feed_forward(own, cots, column, near, resid, gain, hidden_units):
    n = lax.axis_size("seq")
    groups = n // INNER
    tall, model = own.shape
    kinds, _, rows, units = column.shape
    half = groups // 2
    dma = pltpu.SemaphoreType.DMA
    part = jax.ShapeDtypeStruct((2, kinds, half, rows, units), BF16)
    return pl.pallas_call(
        functools.partial(ffn_body, n, hidden_units),
        out_shape=(
            jax.ShapeDtypeStruct((2, tall, model), BF16),
            jax.ShapeDtypeStruct((tall, model), F32),
            jax.ShapeDtypeStruct((2, tall, model), BF16),
            jax.ShapeDtypeStruct((1, model), F32),
            jax.ShapeDtypeStruct((model, 2 * tall), BF16),
            part,
            part,
            jax.ShapeDtypeStruct((2, 2, kinds, half, rows, units), BF16),
        ),
        in_specs=[HBM] * 4 + [VMEM] * 2,
        out_specs=(VMEM,) * 5 + (HBM,) * 3,
        scratch_shapes=[
            pltpu.VMEM((groups, 2, tall, model), BF16),
            pltpu.VMEM((groups, 2, tall, model), BF16),
            pltpu.VMEM((kinds, groups, INNER, rows, units), BF16),
            pltpu.VMEM((groups, INNER, rows, units), BF16),
            pltpu.VMEM((3, groups * 2 * tall, units), BF16),
            pltpu.VMEM((groups, 2, tall, model), BF16),
            pltpu.VMEM((2, groups, tall, model), BF16),
            pltpu.VMEM((2, groups + 1, tall, model), BF16),
            pltpu.VMEM((half, rows, units), BF16),
            pltpu.VMEM((INNER * rows, groups * 2 * tall), BF16),
            pltpu.VMEM((tall, model), BF16),
            *chain_semaphores(groups),
            dma((kinds, 2, 2)),
            dma((kinds, 2, 2)),
            dma((kinds, 3)),
            dma(()),
            dma(()),
            dma(()),
            dma((2, groups)),
            dma((2, groups)),
            dma((2, groups)),
            dma((2, groups + 1)),
            dma((kinds, 2, 2)),
            dma((kinds, 2, 2)),
            dma((2,)),
            dma((2,)),
            dma(()),
            dma((kinds, 2, 2)),
        ],
        compiler_params=params(8, 63),
        name="feed_forward",
    )(own, cots, column, near, resid, gain)


def my_half(values):
    half = values.shape[0] // 2
    return lax.dynamic_slice_in_dim(values, lax.axis_index("ch") * half, half, 0)


def join(own):
    other = swap(own, "ch", 1)
    core = lax.axis_index("ch")
    return jnp.concatenate(
        [jnp.where(core == 0, own, other), jnp.where(core == 0, other, own)], axis=0
    )


def tokens_out(partial, half):
    width = partial.shape[1]
    groups = lax.axis_size("seq") // INNER
    outer = lax.axis_index("seq") // INNER
    core = lax.axis_index("ch")
    parts = partial.reshape(groups, 2, half, width)
    theirs = pick(parts, 1 - core, 1).astype(BF16)
    summed = (pick(parts, core, 1).astype(F32) + swap(theirs, "ch", 1).astype(F32)).astype(BF16)
    total = pick(summed, outer).astype(F32)
    for step in range(1, groups):
        total = total + swap(pick(summed, outer ^ step), "seq", step * INNER).astype(F32)
    return total


def feed_forward_parts(n_two, cot_half, all_cot, column, near, resid, ffn_gain, hidden_units):
    f32, bf16 = F32, BF16
    _, groups, depth, units = column.shape
    half_rows, model = n_two.shape
    tok_rows = 2 * half_rows
    _, norm_back_two = jax.vjp(scaled_norm, resid, ffn_gain)
    all_two, *full_ffn = gather_tokens(n_two, column, near)
    all_two, all_cot = (v.reshape(groups * tok_rows, model) for v in (all_two, all_cot))
    own = Units(hidden_units, groups, lax.axis_index("ch")).width(lax.axis_index("seq") // INNER)
    valid = lax.broadcasted_iota(jnp.int32, (1, units), 1) < own
    full_ffn = [jnp.where(valid, w.reshape(model, units), 0) for w in full_ffn]
    gate_pre = jnp.dot(all_two, full_ffn[0], preferred_element_type=f32)
    up_pre = jnp.dot(all_two, full_ffn[1], preferred_element_type=f32)
    gate_act, gelu_back_gate = jax.vjp(gelu_tanh, gate_pre)
    hidden = (gate_act * up_pre).astype(bf16)
    ffn_term = jnp.einsum("tf,df->td", hidden, full_ffn[2], preferred_element_type=f32).astype(bf16)
    d_hidden = jnp.einsum("td,df->tf", all_cot, full_ffn[2], preferred_element_type=f32)
    d_gate = gelu_back_gate(d_hidden * up_pre)[0].astype(bf16)
    d_up = (d_hidden * gate_act).astype(bf16)
    d_n_two = (
        jnp.einsum("tf,df->td", d_gate, full_ffn[0], preferred_element_type=f32)
        + jnp.einsum("tf,df->td", d_up, full_ffn[1], preferred_element_type=f32)
    ).astype(bf16)
    terms = [
        jnp.einsum("td,tf->df", left, right, preferred_element_type=f32)
        .astype(bf16)
        .reshape(groups, INNER, depth, units)
        for left, right in ((all_two, d_gate), (all_two, d_up), (all_cot, hidden))
    ]
    split = [v.reshape(groups, 2, half_rows, model) for v in (d_n_two, ffn_term)]
    if groups <= 4:
        d_n_two, ffn_out, far = reduce_tokens(split, terms)
    else:
        d_n_two, far = reduce_tokens(split[:1], terms)
        ffn_out = tokens_out(ffn_term, half_rows)
    block_out = join((resid + ffn_out).astype(bf16))
    inner = lax.axis_index("seq") % INNER
    by_half = [t.reshape(2, groups // 2, INNER, depth, units) for t in terms]

    def block_at(h, place):
        return jnp.stack([pick(t[h], place, 1) for t in by_half]).astype(f32)

    mine = jnp.stack(
        [(block_at(h, inner) + far[h, 0].astype(f32)).astype(bf16) for h in range(2)]
    )
    halves = jnp.stack(
        [(block_at(h, inner ^ (1, 2)[h]) + far[h, 1].astype(f32)).astype(bf16) for h in range(2)]
    )
    d_resid_norm, d_ffn_gain_term = norm_back_two(d_n_two)
    d_resid = cot_half.astype(f32) + d_resid_norm
    d_mixed = join(d_resid.astype(bf16))
    return block_out, d_resid, d_mixed, d_ffn_gain_term.reshape(1, model), halves, mine


def shards(
    inputs,
    norm_gain,
    branch_weight,
    input_weight,
    channel_params,
    gate_x_blocks,
    gate_a_blocks,
    out_weight,
    ffn_gain,
    ffn_gate,
    ffn_up,
    ffn_down,
    cotangent,
):
    f32 = F32
    bf16 = BF16
    n = lax.axis_size("seq")
    tok_rows, model = inputs.shape
    half_rows = tok_rows // 2
    heads, part, size = gate_x_blocks.shape
    width = heads * size
    depth = ffn_gate.shape[0]
    groups = n // INNER
    hidden_units = ffn_gate.shape[1]
    par = jnp.concatenate(
        [
            channel_params,
            jax.nn.softplus(channel_params[7:8]),
            jax.nn.sigmoid(channel_params[7:8]),
            jnp.zeros((6, width), f32),
        ],
        axis=0,
    )
    mixer_set = [input_weight, branch_weight, out_weight.T]
    gate_set = [gate_x_blocks, gate_a_blocks]
    ffn_set = [ffn_gate, ffn_up, ffn_down.T]
    gains = jnp.stack([norm_gain, ffn_gain])
    gain_one, gain_two = gains[:1], gains[1:]
    if depth % 16 == 0 and part % 16 == 0:
        made = gather_forward(
            mixer_set, gate_set, ffn_set, inputs, gains, par, cotangent
        )
        *full_mixer, full_gates, column, n_one, n_one_turned, _ = made[:8]
        full_mixer = [w.reshape(model, width) for w in full_mixer]
        gates = full_gates.reshape(2, heads, size, size)
        made = made[8:]
    else:
        cot_half = my_half(cotangent)
        *full_mixer, full_gates, column, n_one, n_one_turned, last_rows = gather_weights(
            mixer_set, gate_set, ffn_set, inputs, gain_one
        )
        full_mixer = [w.reshape(model, width) for w in full_mixer]
        gates = full_gates.reshape(2, heads, size, size)
        made = mixer_forward(
            n_one,
            last_rows,
            full_mixer,
            gates,
            par,
            my_half(inputs),
            gain_two,
            column,
            cot_half,
            hidden_units,
        )
    x_branch, y_pre, conv_out, states, branch_out, edge, resid, n_two, near, cots = made
    if groups <= 4 and depth % 16 == 0:
        block_out, d_resid, d_mixed, d_ffn_gain_term, d_mixed_turned, halves, mine, _ = feed_forward(
            n_two, cots, column, near, resid, gain_two, hidden_units
        )
        block_out = block_out.reshape(tok_rows, model)
        d_mixed = d_mixed.reshape(tok_rows, model)
    else:
        block_out, d_resid, d_mixed, d_ffn_gain_term, halves, mine = feed_forward_parts(
            n_two, cot_half, cots, column, near, resid, ffn_gain, hidden_units
        )
        d_mixed_turned = d_mixed.T
    d_y, d_xb, d_gates, d_par, d_inputs, d_norm_gain_term, column_back = mixer_backward(
        d_mixed,
        full_mixer,
        inputs,
        gain_one,
        d_resid,
        y_pre,
        states,
        edge,
        conv_out,
        x_branch,
        gates,
        par,
        halves,
        mine,
        hidden_units,
    )
    d_inputs = d_inputs.reshape(tok_rows, model)
    gain_rows = model // width
    scattered, small, spread = scatter_mixer(
        n_one_turned.reshape(n, depth, tok_rows),
        d_mixed_turned.reshape(n, depth, tok_rows),
        d_y,
        d_xb,
        branch_out,
        d_gates,
        d_par,
        d_norm_gain_term,
        d_ffn_gain_term,
        column_back,
        hidden_units,
    )
    ffn_grads = [spread[kind].astype(f32) for kind in range(3)]
    d_gate_pair = scattered[3 * depth :].reshape(2, part, heads, size).transpose(0, 2, 1, 3)
    return (
        block_out,
        d_inputs,
        small[8 : 8 + gain_rows].reshape(model),
        scattered[:depth],
        scattered[depth : 2 * depth],
        small[:8],
        d_gate_pair[0],
        d_gate_pair[1],
        scattered[2 * depth : 3 * depth].T,
        small[8 + gain_rows : 8 + 2 * gain_rows].reshape(model),
        ffn_grads[0],
        ffn_grads[1],
        ffn_grads[2].T,
    )


def solution(mesh):
    placed = (
        P("seq", None),
        P(),
        P("seq", "ch"),
        P("seq", "ch"),
        P(None, "ch"),
        P("ch", "seq", None),
        P("ch", "seq", None),
        P("ch", "seq"),
        P(),
        P("seq", "ch"),
        P("seq", "ch"),
        P("ch", "seq"),
        P("seq", None),
    )
    return jax.shard_map(
        shards,
        mesh=mesh,
        in_specs=placed,
        out_specs=(
            P("seq", None),
            P("seq", None),
            P(),
            P("seq", "ch"),
            P("seq", "ch"),
            P(None, "ch"),
            P("ch", "seq", None),
            P("ch", "seq", None),
            P("ch", "seq"),
            P(),
            P("seq", "ch"),
            P("seq", "ch"),
            P("ch", "seq"),
        ),
        check_vma=False,
    )
```
